32 devices in a mesh: section: 2 (over x), shard: 4 (over z), seq: 4 (over y, core).
Axes of the slice: x: 2, y: 2, z: 4, core: 2. Of those that a mesh axis runs over, the one named last changes fastest.
Arguments:
- inputs: bfloat16 [2, 1024, 2048], P(None, ('shard', 'seq')), may hold values from -6 to 6
- cotangent: bfloat16 [2, 1024, 2048], P(None, ('shard', 'seq')), may hold values from -6 to 6
- positions: int32 [2, 1024], replicated, may hold values from 0 to 1023, as said below
- gain_attn: bfloat16 [2, 2048], P('section', ('shard', 'seq')), may hold values from 0.5 to 1.5
- w_query: bfloat16 [2, 2048, 2048], P('section', ('shard', 'seq')), may hold values from -0.125 to 0.125
- w_key: bfloat16 [2, 256, 2048], P('section', ('shard', 'seq')), may hold values from -0.125 to 0.125
- w_value: bfloat16 [2, 256, 2048], P('section', ('shard', 'seq')), may hold values from -0.125 to 0.125
- w_out: bfloat16 [2, 2048, 2048], P('section', ('shard', 'seq')), may hold values from -1.75 to 1.75
- gain_ffn: bfloat16 [2, 2048], P('section', ('shard', 'seq')), may hold values from 0.5 to 1.5
- w_gate: bfloat16 [2, 5632, 2048], P('section', ('shard', 'seq')), may hold values from -0.125 to 0.125
- w_up: bfloat16 [2, 5632, 2048], P('section', ('shard', 'seq')), may hold values from -0.125 to 0.125
- w_down: bfloat16 [2, 5632, 2048], P('section', ('shard', 'seq')), may hold values from -0.078125 to 0.078125
Outputs:
- outputs: bfloat16 [2, 2, 1024, 2048], P('section', None, ('shard', 'seq'))
- input_grads: bfloat16 [2, 2, 1024, 2048], P('section', None, ('shard', 'seq'))
- grad_gain_attn: float32 [2, 2048], P('section', ('shard', 'seq'))
- grad_w_query: float32 [2, 2048, 2048], P('section', ('shard', 'seq'))
- grad_w_key: float32 [2, 256, 2048], P('section', ('shard', 'seq'))
- grad_w_value: float32 [2, 256, 2048], P('section', ('shard', 'seq'))
- grad_w_out: float32 [2, 2048, 2048], P('section', ('shard', 'seq'))
- grad_gain_ffn: float32 [2, 2048], P('section', ('shard', 'seq'))
- grad_w_gate: float32 [2, 5632, 2048], P('section', ('shard', 'seq'))
- grad_w_up: float32 [2, 5632, 2048], P('section', ('shard', 'seq'))
- grad_w_down: float32 [2, 5632, 2048], P('section', ('shard', 'seq'))
The draws below stay inside these ranges and needn't reach their ends.
Inputs may be any that keep to these rules, and one draw needn't show every extreme that they name: Each row is a permutation of the positions of a sequence made of blocks of 128 consecutive positions in rising order; the order of the blocks is drawn.
All inputs are finite; a program needn't handle non-finite values.
Results may differ from the reference program's by a relative error of at most 0.03.
Values may be sent and summed in bfloat16 or wider, within the bound.
A program may use at most 384 MiB of HBM per device.

```python
import math
from functools import partial
import jax
import jax.numpy as jnp
from jax import lax

D = 2048
HEADS = 32
KV_HEADS = 4
HEAD_DIM = 64
FF = 5632
MICRO = 2
SECTIONS = 2
LEN = 1024
BLOCK = 128


def draw_positions(key, part):
    key = jax.random.fold_in(key, 11)
    order_keys = jax.random.split(key, MICRO)
    block_count = LEN // BLOCK
    orders = jax.vmap(lambda one_key: jax.random.permutation(one_key, block_count))(order_keys)
    index_all = jnp.arange(LEN, dtype=jnp.int32)
    block_of = index_all // BLOCK
    within = index_all % BLOCK
    return (orders[:, block_of].astype(jnp.int32) * BLOCK + within[None, :]).astype(jnp.int32)


def strengthened(values, stream_key, source, target, blocks, factor):
    owner, partner = [(jnp.arange(values.shape[position]) // (values.shape[position] // blocks)).reshape([-1 if axis == position else 1 for axis in range(values.ndim)]) for position in (source, target)]
    chosen = jax.random.permutation(stream_key, blocks)[partner]
    strong = (owner == chosen) | (owner == (partner + blocks // 2) % blocks)
    return jnp.where(strong, factor * values, values)


def steps_of(stream_key, dims, shards, low, largest):
    level = 1.0
    for axis_at, blocks in shards:
        draws = jax.random.uniform(jax.random.fold_in(jax.random.fold_in(stream_key, 6), axis_at), (blocks,), jnp.float32, low / len(shards), largest / len(shards))
        level = level * jnp.repeat(jnp.exp(draws), dims[axis_at] // blocks).reshape((-1,) + (1,) * (len(dims) - 1 - axis_at))
    return level


def normal_values(own_key, dims, spread, most, shards=(), held_as=jnp.bfloat16):
    values = spread * jax.random.normal(own_key, dims, jnp.float32)
    if shards:
        values = values * steps_of(own_key, dims, shards, -0.22, 0.18)
    return jnp.clip(values, -most, most).astype(held_as)


def gaussian_with(rng, dims, spread, reach, pieces, heavy, kind=jnp.bfloat16):
    values = spread * jax.random.normal(rng, dims, jnp.float32)
    if pieces:
        values = values * steps_of(rng, dims, pieces, -0.22, 0.18)
    return jnp.clip(strengthened(values, jax.random.fold_in(rng, 3), *heavy), -reach, reach).astype(kind)


def setup_inputs(seed: int = 0) -> dict:
    arg_keys = jax.random.split(jax.random.key(seed), 13)
    inputs = gaussian_with(arg_keys[0], (MICRO, LEN, D), 1.0, 6.0, ((1, 16),), (1, 2, 16, 2.0))
    cotangent = normal_values(arg_keys[1], (MICRO, LEN, D), 1.0, 6.0, ((1, 16),))
    positions = draw_positions(jax.random.fold_in(arg_keys[12], 71), 0)
    gain_attn = jnp.clip(1.0 + 0.1 * jax.random.normal(arg_keys[3], (SECTIONS, D), jnp.float32), 0.5, 1.5).astype(jnp.bfloat16)
    w_query = normal_values(arg_keys[4], (SECTIONS, HEADS * HEAD_DIM, D), D ** -0.5, 0.125, ((0, 2), (1, 16)))
    w_key = normal_values(arg_keys[5], (SECTIONS, KV_HEADS * HEAD_DIM, D), D ** -0.5, 0.125, ((0, 2), (1, 16)))
    w_value = normal_values(arg_keys[6], (SECTIONS, KV_HEADS * HEAD_DIM, D), D ** -0.5, 0.125, ((0, 2), (1, 16)))
    w_out = normal_values(arg_keys[7], (SECTIONS, HEADS * HEAD_DIM, D), (max(1, HEADS * HEAD_DIM * 6 // LEN)) ** -0.5, 1.75, ((0, 2), (1, 16)))
    gain_ffn = jnp.clip(1.0 + 0.1 * jax.random.normal(arg_keys[8], (SECTIONS, D), jnp.float32), 0.5, 1.5).astype(jnp.bfloat16)
    w_gate = normal_values(arg_keys[9], (SECTIONS, FF, D), D ** -0.5, 0.125, ((0, 2), (1, 16)))
    w_up = normal_values(arg_keys[10], (SECTIONS, FF, D), D ** -0.5, 0.125, ((0, 2), (1, 16)))
    w_down = normal_values(arg_keys[11], (SECTIONS, FF, D), FF ** -0.5, 0.078125, ((0, 2), (1, 16)))
    return dict(inputs=inputs, cotangent=cotangent, positions=positions, gain_attn=gain_attn, w_query=w_query, w_key=w_key, w_value=w_value, w_out=w_out, gain_ffn=gain_ffn, w_gate=w_gate, w_up=w_up, w_down=w_down)


EPSILON = 1e-05
THETA_BASE = 10000.0
NEG_LARGE = -1e+30
HIGHEST_PREC = lax.Precision.HIGHEST

@jax.custom_vjp
def low(v):
    return lax.optimization_barrier(v.astype(jnp.bfloat16)).astype(jnp.float32)

@jax.custom_vjp
def low_back(v):
    return v

def low_keep(v):
    return (low(v), None)

def low_pass(kept, grad):
    return (grad,)

def back_keep(v):
    return (v, None)

def back_low(kept, grad):
    return (low(grad),)
low.defvjp(low_keep, low_pass)
low_back.defvjp(back_keep, back_low)

def rotate(values, places, direction):
    half_dim = values.shape[-1] // 2
    inv_freq = THETA_BASE ** (-jnp.arange(half_dim, dtype=jnp.float32) * (2.0 / values.shape[-1]))
    angles = places.astype(jnp.float32)[:, None] * inv_freq[None, :]
    cosine = jnp.cos(angles)[:, None, :]
    sine_val = direction * jnp.sin(angles)[:, None, :]
    first = values[..., :half_dim]
    second = values[..., half_dim:]
    return jnp.concatenate([first * cosine - second * sine_val, second * cosine + first * sine_val], -1)

def scaled(values, gain_vec):
    factor = lax.rsqrt(lax.optimization_barrier(jnp.mean(values * values, -1, keepdims=True)) + EPSILON)
    return values * factor * gain_vec

def attend_one(head_item, places):
    query_rows, key_rows, value_rows = head_item
    raw_scores = low_back(jnp.dot(query_rows, key_rows.T, precision=HIGHEST_PREC))
    scores = raw_scores * (1.0 / math.sqrt(query_rows.shape[-1]))
    visible = places[None, :] <= places[:, None]
    scores = jnp.where(visible, scores, NEG_LARGE)
    row_max = lax.optimization_barrier(jnp.max(scores, -1, keepdims=True))
    weight = jnp.exp(scores - row_max)
    row_total = lax.optimization_barrier(jnp.sum(weight, -1, keepdims=True))
    return jnp.dot(low(weight), value_rows, precision=HIGHEST_PREC) / row_total

def layer(values_in, gain_a, w_q, w_k, w_v, w_o, gain_f, w_g, w_u, w_d, places):
    n_tokens = values_in.shape[0]
    normed_one = low(scaled(values_in, gain_a))
    query_pre = low_back(jnp.dot(normed_one, w_q.T, precision=HIGHEST_PREC)).reshape(n_tokens, HEADS, HEAD_DIM)
    key_pre = low_back(jnp.dot(normed_one, w_k.T, precision=HIGHEST_PREC)).reshape(n_tokens, KV_HEADS, HEAD_DIM)
    value_rows = low(low_back(jnp.dot(normed_one, w_v.T, precision=HIGHEST_PREC))).reshape(n_tokens, KV_HEADS, HEAD_DIM)
    query_rot = low(rotate(query_pre, places, 1.0))
    key_rot = low(rotate(key_pre, places, 1.0))
    group_size = HEADS // KV_HEADS
    key_rep = jnp.repeat(key_rot, group_size, axis=1)
    value_rep = jnp.repeat(value_rows, group_size, axis=1)
    per_head = lax.map(jax.checkpoint(partial(attend_one, places=places)), (query_rot.transpose(1, 0, 2), key_rep.transpose(1, 0, 2), value_rep.transpose(1, 0, 2)))
    mixed = low(low_back(per_head.transpose(1, 0, 2).reshape(n_tokens, HEADS * HEAD_DIM)))
    hidden_in = values_in + low_back(jnp.dot(mixed, w_o, precision=HIGHEST_PREC))
    normed_two = low(scaled(hidden_in, gain_f))
    gate_pre = low_back(jnp.dot(normed_two, w_g.T, precision=HIGHEST_PREC))
    up_pre = low_back(jnp.dot(normed_two, w_u.T, precision=HIGHEST_PREC))
    hidden_act = low(jax.nn.silu(gate_pre) * up_pre)
    return hidden_in + jnp.dot(hidden_act, w_d, precision=HIGHEST_PREC)

def reference(inputs, cotangent, positions, gain_attn, w_query, w_key, w_value, w_out, gain_ffn, w_gate, w_up, w_down):
    stacks = (gain_attn, w_query, w_key, w_value, w_out, gain_ffn, w_gate, w_up, w_down)
    first = tuple((array_in[0].astype(jnp.float32) for array_in in stacks))
    second = tuple((array_in[1].astype(jnp.float32) for array_in in stacks))

    def one_batch(grad_sums, batch_item):
        batch_x, batch_grad, places = batch_item

        def section_layer(values_in, *weights):
            return layer(values_in, *weights, places)
        out_one, back_one = jax.vjp(section_layer, batch_x.astype(jnp.float32), *first)
        out_one = out_one.astype(jnp.bfloat16)
        out_two, back_two = jax.vjp(section_layer, out_one.astype(jnp.float32), *second)
        grads_two = back_two(batch_grad.astype(jnp.float32))
        pass_two = grads_two[0].astype(jnp.bfloat16)
        grads_one = back_one(pass_two.astype(jnp.float32))
        pass_one = grads_one[0].astype(jnp.bfloat16)
        grad_sums = tuple((total_in + jnp.stack([grad_first, grad_second]) for total_in, grad_first, grad_second in zip(grad_sums, grads_one[1:], grads_two[1:])))
        return (grad_sums, (out_one, out_two.astype(jnp.bfloat16), pass_one, pass_two))
    start_sums = tuple((jnp.zeros((2,) + array_in.shape[1:], jnp.float32) for array_in in stacks))
    grad_sums, collected = lax.scan(one_batch, start_sums, (inputs, cotangent, positions))
    out_one, out_two, pass_one, pass_two = collected
    outputs = jnp.stack([out_one, out_two])
    input_grads = jnp.stack([pass_one, pass_two])
    return (outputs, input_grads, grad_sums[0], grad_sums[1], grad_sums[2], grad_sums[3], grad_sums[4], grad_sums[5], grad_sums[6], grad_sums[7], grad_sums[8])
```

```python
import functools
import math
import types

import jax
import jax.numpy as jnp
from jax import lax
from jax.experimental import pallas as pl
from jax.experimental.pallas import tpu as pltpu
from jax.sharding import PartitionSpec as P

HEADS = 32
KV_HEADS = 4
HEAD_DIM = 64


EPSILON = 1e-05
THETA_BASE = 10000.0
NEG_LARGE = -1e30


def shifted(value, axis, by):
    count = lax.axis_size(axis)
    pairs = [(i, i + by) for i in range(count) if 0 <= i + by < count]
    return lax.ppermute(value, axis, pairs)


def times_trans(left, right):
    return lax.dot_general(
        left, right, (((1,), (1,)), ((), ())), preferred_element_type=jnp.float32
    )


def outer_sum(left, right):
    return lax.dot_general(
        left, right, (((0,), (0,)), ((), ())), preferred_element_type=jnp.float32
    )


def plain_dot(left, right):
    return jnp.dot(left, right, preferred_element_type=jnp.float32)


def rotate(values, places, direction):
    half_dim = values.shape[-1] // 2
    inv_freq = THETA_BASE ** (-jnp.arange(half_dim, dtype=jnp.float32) * (2.0 / values.shape[-1]))
    angles = places.astype(jnp.float32)[:, None] * inv_freq[None, :]
    cosine = jnp.cos(angles)[:, None, :]
    sine_val = direction * jnp.sin(angles)[:, None, :]
    first = values[..., :half_dim]
    second = values[..., half_dim:]
    return jnp.concatenate(
        [first * cosine - second * sine_val, second * cosine + first * sine_val], -1
    )


def scaled(values, gain_vec):
    factor = lax.rsqrt(jnp.mean(values * values, -1, keepdims=True) + EPSILON)
    return values * factor * gain_vec


def norm_back(values, gain_vec, grad_in):
    factor = lax.rsqrt(jnp.mean(values * values, -1, keepdims=True) + EPSILON)
    gain_grad = jnp.sum(grad_in * values * factor, 0)
    mean_term = jnp.mean(grad_in * gain_vec * values, -1, keepdims=True)
    return (
        gain_grad,
        factor * gain_vec * grad_in - values * (factor * factor * factor) * mean_term,
    )


def ffn_back(grad_rows, kept_rows, gate_pre, up_pre, wg_part, wu_part, wd_part):
    sigmoid_val = jax.nn.sigmoid(gate_pre)
    silu_val = gate_pre * sigmoid_val
    hidden_act = (silu_val * up_pre).astype(jnp.bfloat16)
    grad_down = outer_sum(hidden_act, grad_rows)
    d_act = times_trans(grad_rows, wd_part)
    d_gate = (d_act * up_pre * sigmoid_val * (1.0 + gate_pre * (1.0 - sigmoid_val))).astype(
        jnp.bfloat16
    )
    d_up = (d_act * silu_val).astype(jnp.bfloat16)
    grad_gate = outer_sum(d_gate, kept_rows)
    grad_up = outer_sum(d_up, kept_rows)
    d_normed = plain_dot(d_gate, wg_part) + plain_dot(d_up, wu_part)
    return ((grad_gate, grad_up, grad_down), d_normed)


def body(
    inputs,
    cotangent,
    positions,
    gain_attn,
    w_query,
    w_key,
    w_value,
    w_out,
    gain_ffn,
    w_gate,
    w_up,
    w_down,
):
    n_micro, per_device, model_width = inputs.shape
    n_seq = lax.axis_size("seq")
    n_shard = lax.axis_size("shard")
    section_idx = lax.axis_index("section")
    shard_pos = lax.axis_index("shard")
    member = shard_pos * n_seq + lax.axis_index("seq")
    span_rows = per_device * n_seq
    total_len = span_rows * n_shard
    local_heads = HEADS // n_seq
    kv_repeat = n_seq // KV_HEADS
    q_width = local_heads * HEAD_DIM
    attn_scale = 1.0 / math.sqrt(HEAD_DIM)
    gain_one, gain_two, wq_full, wk_full, wv_full, wo_full = (
        lax.all_gather(gain_attn[0], ("shard", "seq"), axis=0, tiled=True),
        lax.all_gather(gain_ffn[0], ("shard", "seq"), axis=0, tiled=True),
        lax.all_gather(w_query[0], ("shard", "seq"), axis=0, tiled=True),
        lax.all_gather(w_key[0], ("shard", "seq"), axis=0, tiled=True),
        lax.all_gather(w_value[0], ("shard", "seq"), axis=0, tiled=True),
        lax.all_gather(w_out[0], ("shard", "seq"), axis=0, tiled=True),
    )
    gain_a = gain_one.astype(jnp.float32)
    gain_f = gain_two.astype(jnp.float32)
    wg_use, wu_use, wd_use = (w_gate[0], w_up[0], w_down[0])

    def spread_rows(block_in):
        return lax.all_gather(block_in, ("shard", "seq"), axis=0, tiled=True)

    def fold_rows(block_in):
        return lax.psum_scatter(block_in, ("shard", "seq"), scatter_dimension=0, tiled=True)

    def to_heads(block_in):
        return lax.all_to_all(block_in, "seq", split_axis=1, concat_axis=0, tiled=True)

    def to_tokens(block_in):
        return lax.all_to_all(block_in, "seq", split_axis=0, concat_axis=1, tiled=True)

    def over_keys(head_keys, head_values, step_fn, init_state):
        return step_fn(
            init_state,
            (
                lax.all_gather(head_keys, "shard", axis=0, tiled=True),
                lax.all_gather(head_values, "shard", axis=0, tiled=True),
            ),
            jnp.int32(0),
        )

    def place_sets(batch_index):
        place_row = lax.dynamic_index_in_dim(positions, batch_index, 0, keepdims=False)
        token_places = lax.dynamic_slice_in_dim(place_row, member * per_device, per_device)
        span_places = lax.dynamic_slice_in_dim(place_row, shard_pos * span_rows, span_rows)
        return (place_row, token_places, span_places)

    zero_rows = jnp.zeros((per_device, model_width), jnp.bfloat16)
    arrived_x = zero_rows
    results = []
    stored = []
    for tick_index in range(n_micro + 1):
        own_rows = inputs[tick_index] if tick_index < n_micro else zero_rows
        input_now = jnp.where(section_idx == 0, own_rows, arrived_x)
        batch_index = jnp.clip(tick_index - section_idx, 0, n_micro - 1)
        forward_place_row, forward_token_places, forward_span_places = place_sets(batch_index)
        forward_values_in = input_now.astype(jnp.float32)
        forward_normed_one = scaled(forward_values_in, gain_a).astype(jnp.bfloat16)
        queries = rotate(
            times_trans(forward_normed_one, wq_full).reshape(per_device, HEADS, HEAD_DIM),
            forward_token_places,
            1.0,
        ).astype(jnp.bfloat16)
        key_rows = rotate(
            times_trans(forward_normed_one, wk_full).reshape(per_device, KV_HEADS, HEAD_DIM),
            forward_token_places,
            1.0,
        ).astype(jnp.bfloat16)
        value_rows = (
            times_trans(forward_normed_one, wv_full)
            .reshape(per_device, KV_HEADS, HEAD_DIM)
            .astype(jnp.bfloat16)
        )
        key_rows = jnp.repeat(key_rows, kv_repeat, axis=1)
        value_rows = jnp.repeat(value_rows, kv_repeat, axis=1)
        packed = jnp.concatenate(
            [queries.reshape(per_device, n_seq, q_width), key_rows, value_rows], -1
        )
        arrived = to_heads(packed)[:, 0]
        forward_head_query = arrived[:, :q_width].reshape(span_rows, local_heads, HEAD_DIM)
        forward_head_keys = arrived[:, q_width : q_width + HEAD_DIM]
        forward_head_values = arrived[:, q_width + HEAD_DIM :]

        def absorb(state_in, key_piece, start_row):
            run_max, run_total, run_acc = state_in
            piece_keys, piece_values = key_piece
            visible = forward_place_row[None, None, :] <= forward_span_places[None, :, None]
            scores = (
                jnp.einsum(
                    "qhd,kd->hqk",
                    forward_head_query,
                    piece_keys,
                    preferred_element_type=jnp.float32,
                )
                * attn_scale
            )
            scores = jnp.where(visible, scores, NEG_LARGE)
            new_max = jnp.maximum(run_max, jnp.max(scores, -1))
            weight = jnp.where(visible, jnp.exp(scores - new_max[..., None]), 0.0)
            rescale = jnp.exp(run_max - new_max)
            run_total = jnp.sum(weight, -1)
            run_acc = run_acc * rescale.T[..., None] + jnp.einsum(
                "hqk,kd->qhd",
                weight.astype(jnp.bfloat16),
                piece_values,
                preferred_element_type=jnp.float32,
            )
            return (new_max, run_total, run_acc)

        forward_start_state = (
            jnp.full((local_heads, span_rows), NEG_LARGE, jnp.float32),
            jnp.zeros((local_heads, span_rows), jnp.float32),
            jnp.zeros((span_rows, local_heads, HEAD_DIM), jnp.float32),
        )
        run_max, run_total, run_acc = over_keys(
            forward_head_keys, forward_head_values, absorb, forward_start_state
        )
        forward_attended = run_acc / run_total.T[..., None]
        forward_spread = run_max + jnp.log(run_total)
        forward_mixed_tok = to_tokens(
            forward_attended.astype(jnp.bfloat16).reshape(span_rows, 1, q_width)
        ).reshape(per_device, HEADS * HEAD_DIM)
        forward_hidden_in = forward_values_in + plain_dot(forward_mixed_tok, wo_full)
        normed_two = scaled(forward_hidden_in, gain_f).astype(jnp.bfloat16)
        forward_kept_rows = spread_rows(normed_two)
        forward_gate_pre = times_trans(forward_kept_rows, wg_use)
        forward_up_pre = times_trans(forward_kept_rows, wu_use)
        hidden_act = (jax.nn.silu(forward_gate_pre) * forward_up_pre).astype(jnp.bfloat16)
        branch = fold_rows(plain_dot(hidden_act, wd_use))
        result = (forward_hidden_in + branch).astype(jnp.bfloat16)
        forward_saved = (
            input_now,
            forward_head_query,
            forward_head_keys,
            forward_head_values,
            forward_attended,
            forward_spread,
            forward_mixed_tok,
            forward_hidden_in,
            forward_kept_rows,
            forward_gate_pre,
            forward_up_pre,
        )
        result, saved = (result, forward_saved)
        results.append(result)
        stored.append(saved)
        if tick_index < n_micro:
            arrived_x = shifted(result, "section", 1)
    returned = zero_rows
    grads_back = []
    row_lists = []
    gain_total = None
    ffn_total = None
    for tick_index in range(n_micro + 1):
        own_rows = cotangent[tick_index] if tick_index < n_micro else zero_rows
        grad_now = jnp.where(section_idx == 1, own_rows, returned)
        batch_index = jnp.clip(tick_index - 1 + section_idx, 0, n_micro - 1)
        early_saved = stored[max(tick_index - 1, 0)]
        late_saved = stored[min(tick_index + 1, n_micro)]
        saved = jax.tree.map(
            lambda early_val, late_val: jnp.where(section_idx == 0, early_val, late_val),
            early_saved,
            late_saved,
        )
        (
            input_bf,
            head_query,
            backward_head_keys,
            backward_head_values,
            attended,
            spread,
            mixed_tok,
            hidden_in,
            kept_rows,
            gate_pre,
            up_pre,
        ) = saved
        backward_place_row, backward_token_places, backward_span_places = place_sets(batch_index)
        values_in = input_bf.astype(jnp.float32)
        normed_one = scaled(values_in, gain_a).astype(jnp.bfloat16)
        grad_all = spread_rows(grad_now)
        ffn_terms, d_partial = ffn_back(
            grad_all, kept_rows, gate_pre, up_pre, wg_use, wu_use, wd_use
        )
        d_normed_two = fold_rows(d_partial)
        grad_gf, d_hidden = norm_back(hidden_in, gain_f, d_normed_two)
        d_hidden = d_hidden + grad_now.astype(jnp.float32)
        d_branch = d_hidden.astype(jnp.bfloat16)
        d_mixed = times_trans(d_branch, wo_full).astype(jnp.bfloat16)
        d_att = to_heads(d_mixed.reshape(per_device, n_seq, q_width))[:, 0].reshape(
            span_rows, local_heads, HEAD_DIM
        )
        offset = jnp.sum(d_att.astype(jnp.float32) * attended, -1).T

        def collect(state_in, key_piece, start_row):
            piece_keys, piece_values = key_piece
            visible = backward_place_row[None, None, :] <= backward_span_places[None, :, None]
            scores = (
                jnp.einsum(
                    "qhd,kd->hqk", head_query, piece_keys, preferred_element_type=jnp.float32
                )
                * attn_scale
            )
            probs = jnp.where(visible, jnp.exp(scores - spread[..., None]), 0.0)
            d_probs = jnp.einsum(
                "qhd,kd->hqk", d_att, piece_values, preferred_element_type=jnp.float32
            )
            d_score = (probs * (d_probs - offset[..., None]) * attn_scale).astype(jnp.bfloat16)
            d_query_acc = jnp.einsum(
                "hqk,kd->qhd", d_score, piece_keys, preferred_element_type=jnp.float32
            )
            key_part = jnp.einsum(
                "hqk,qhd->kd", d_score, head_query, preferred_element_type=jnp.float32
            )
            value_part = jnp.einsum(
                "hqk,qhd->kd", probs.astype(jnp.bfloat16), d_att, preferred_element_type=jnp.float32
            )
            return (d_query_acc, key_part, value_part)

        start_state = (
            jnp.zeros((span_rows, local_heads, HEAD_DIM), jnp.float32),
            jnp.zeros((total_len, HEAD_DIM), jnp.float32),
            jnp.zeros((total_len, HEAD_DIM), jnp.float32),
        )
        d_query_acc, d_keys_all, d_values_all = over_keys(
            backward_head_keys, backward_head_values, collect, start_state
        )
        own_keys = lax.psum_scatter(
            d_keys_all.astype(jnp.bfloat16), "shard", scatter_dimension=0, tiled=True
        ).astype(jnp.float32)
        own_values = lax.psum_scatter(
            d_values_all.astype(jnp.bfloat16), "shard", scatter_dimension=0, tiled=True
        ).astype(jnp.float32)
        d_query_head = rotate(d_query_acc, backward_span_places, -1.0).astype(jnp.bfloat16)
        d_query = to_tokens(d_query_head.reshape(span_rows, 1, q_width)).reshape(
            per_device, HEADS * HEAD_DIM
        )
        own_keys = rotate(own_keys[:, None, :], backward_span_places, -1.0)[:, 0]
        back_kv = lax.all_to_all(
            jnp.concatenate([own_keys, own_values], -1)[:, None, :].astype(jnp.bfloat16),
            "seq",
            split_axis=0,
            concat_axis=1,
            tiled=True,
        ).astype(jnp.float32)
        back_kv = jnp.sum(back_kv.reshape(per_device, KV_HEADS, kv_repeat, 2 * HEAD_DIM), 2)
        d_key = (
            back_kv[..., :HEAD_DIM].reshape(per_device, KV_HEADS * HEAD_DIM).astype(jnp.bfloat16)
        )
        d_value = (
            back_kv[..., HEAD_DIM:].reshape(per_device, KV_HEADS * HEAD_DIM).astype(jnp.bfloat16)
        )
        d_normed_one = (
            plain_dot(d_query, wq_full) + plain_dot(d_key, wk_full) + plain_dot(d_value, wv_full)
        )
        grad_ga, d_input = norm_back(values_in, gain_a, d_normed_one)
        d_input = d_input + d_hidden
        gain_terms = (grad_ga, grad_gf)
        row_terms = (d_query, d_key, d_value, normed_one, mixed_tok, d_branch)
        d_input, gain_terms, row_terms, ffn_terms = (
            d_input.astype(jnp.bfloat16),
            gain_terms,
            row_terms,
            ffn_terms,
        )
        grads_back.append(d_input)
        row_lists.append(row_terms)
        if tick_index < n_micro:
            returned = shifted(d_input, "section", -1)
        if gain_total is None:
            gain_total = gain_terms
            ffn_total = ffn_terms
        else:
            gain_total = jax.tree.map(jnp.add, gain_total, gain_terms)
            ffn_total = jax.tree.map(jnp.add, ffn_total, ffn_terms)
    joined = [
        jnp.concatenate([row_set[index_val] for row_set in row_lists], 0) for index_val in range(6)
    ]
    grad_wq = outer_sum(joined[0], joined[3])
    grad_wk = outer_sum(joined[1], joined[3])
    grad_wv = outer_sum(joined[2], joined[3])
    grad_wo = outer_sum(joined[4], joined[5])
    attn_owned = (
        lax.psum_scatter(gain_total[0], ("shard", "seq"), scatter_dimension=0, tiled=True),
        lax.psum_scatter(gain_total[1], ("shard", "seq"), scatter_dimension=0, tiled=True),
        lax.psum_scatter(grad_wq, ("shard", "seq"), scatter_dimension=0, tiled=True),
        lax.psum_scatter(grad_wk, ("shard", "seq"), scatter_dimension=0, tiled=True),
        lax.psum_scatter(grad_wv, ("shard", "seq"), scatter_dimension=0, tiled=True),
        lax.psum_scatter(grad_wo, ("shard", "seq"), scatter_dimension=0, tiled=True),
    )
    outputs = lax.dynamic_slice_in_dim(jnp.stack(results), section_idx, n_micro, 0)[None]
    input_grads = lax.dynamic_slice_in_dim(jnp.stack(grads_back), 1 - section_idx, n_micro, 0)[None]
    return (
        outputs,
        input_grads,
        attn_owned[0][None],
        attn_owned[2][None],
        attn_owned[3][None],
        attn_owned[4][None],
        attn_owned[5][None],
        attn_owned[1][None],
        ffn_total[0][None],
        ffn_total[1][None],
        ffn_total[2][None],
    )


LOW = jnp.bfloat16
FULL = jnp.float32
MESH = pl.DeviceIdType.MESH
RING = 4
CHIPS = 2 * RING
SPLIT = 2
PLACE = 128
ORDER = ((2, 1), (1, 1), (3, 1), (0, 1), (2, 0), (1, 0), (3, 0), (0, 0))
IN_VMEM = pl.BlockSpec(memory_space=pltpu.VMEM)
ANYWHERE = pl.BlockSpec(memory_space=pl.ANY)


class Site:
    def __init__(self):
        self.section = lax.axis_index("section")
        self.z = lax.axis_index("shard")
        member = lax.axis_index("seq")
        self.y = lax.div(member, 2)
        self.core = lax.rem(member, 2)
        self.up = (self.section, lax.rem(self.z + 1, RING), member)
        self.down = (self.section, lax.rem(self.z + RING - 1, RING), member)
        self.across = (self.section, self.z, (1 - self.y) * 2 + self.core)
        self.sibling = (self.section, self.z, self.y * 2 + 1 - self.core)
        self.corner = (self.section, self.z, (1 - self.y) * 2 + 1 - self.core)
        self.partner = (1 - self.section, self.z, member)
        self.member = member

    def chip(self, along_z, along_y):
        return lax.rem(self.z + along_z, RING) * 2 + lax.rem(self.y + along_y, 2)


class Links:
    def __init__(self, send, recv, site):
        self.send, self.recv, self.site = send, recv, site
        self.sent = []

    def copy(self, index, src, dst, device):
        return pltpu.make_async_remote_copy(
            src_ref=src,
            dst_ref=dst,
            send_sem=self.send.at[index],
            recv_sem=self.recv.at[index],
            device_id=device,
            device_id_type=MESH,
        )

    def go(self, index, src, dst, device):
        copy = self.copy(index, src, dst, device)
        copy.start()
        self.sent.append(copy)

    def got(self, index, where):
        self.copy(index, where, where, self.site.sibling).wait_recv()
        return where

    def close(self):
        for copy in self.sent:
            copy.wait_send()


def greet(site, corner, partner):
    barrier = pltpu.get_barrier_semaphore()
    devices = [site.up, site.down, site.across, site.sibling]
    devices += [site.corner] * corner + [site.partner] * partner
    for device in devices:
        pl.semaphore_signal(barrier, inc=1, device_id=device, device_id_type=MESH)
    pl.semaphore_wait(barrier, len(devices))


SPREAD_SEMS = 7 * SPLIT + CHIPS
SMALL_SEMS = 7 + CHIPS
FOLD_SEMS = 7 * SPLIT + CHIPS


def spread_steps(site, held, links, use, parts=SPLIT):
    size = held.shape[2] // parts
    other = 1 - site.core
    up, down, across, relay, y_below, y_above, y_far = (k * parts for k in range(7))
    shared = 7 * parts

    def piece(along, part):
        return held.at[site.chip(*along), site.core, pl.ds(part * size, size)]

    def block(along, core):
        return held.at[site.chip(*along), core]

    def go(index, where, device):
        links.go(index, where, where, device)

    def share(slot, along):
        go(shared + slot, block(along, site.core), site.sibling)

    def consume(slot, along):
        links.got(shared + slot, block(along, other))
        use(site.chip(*along))

    own, below, above, far = (0, 0), (3, 0), (1, 0), (2, 0)
    y_own, yb, ya, yf = (0, 1), (3, 1), (1, 1), (2, 1)
    for part in range(parts):
        go(up + part, piece(own, part), site.up)
        go(down + part, piece(own, part), site.down)
        go(across + part, piece(own, part), site.across)
    share(0, own)
    yield
    for part in range(parts):
        came = links.got(up + part, piece(below, part))
        if part % 2 == 0:
            go(relay + part, came, site.up)
        go(y_below + part, came, site.across)
        came = links.got(down + part, piece(above, part))
        if part % 2 == 1:
            go(relay + part, came, site.down)
        go(y_above + part, came, site.across)
    share(1, below)
    share(2, above)
    yield
    for part in range(parts):
        links.got(across + part, piece(y_own, part))
    share(3, y_own)
    consume(0, own)
    for part in range(parts):
        go(y_far + part, links.got(relay + part, piece(far, part)), site.across)
    share(4, far)
    consume(1, below)
    consume(2, above)
    consume(3, y_own)
    for part in range(parts):
        links.got(y_below + part, piece(yb, part))
        links.got(y_above + part, piece(ya, part))
    share(5, yb)
    share(6, ya)
    consume(4, far)
    consume(5, yb)
    consume(6, ya)
    for part in range(parts):
        links.got(y_far + part, piece(yf, part))
    share(7, yf)
    consume(7, yf)


def fold_steps(site, part_of, mine, pass_out, pass_in, stage, land, links):
    rows = mine.shape[1]
    size = rows // SPLIT
    over, relay, up, down = CHIPS, CHIPS + 4 * SPLIT, CHIPS + 5 * SPLIT, CHIPS + 6 * SPLIT

    def came(index, where):
        return links.got(index, where)[...].astype(FULL)

    def compute(step):
        both = part_of(site.chip(*ORDER[step]))
        pass_out[step] = both[:rows].astype(LOW)
        links.go(step, pass_out.at[step], pass_in.at[step], site.sibling)
        mine[step] = both[rows:]

    def settle(step):
        mine[step] += came(step, pass_in.at[step])

    def send_over(step):
        stage[step] = (mine[step] + came(step, pass_in.at[step])).astype(LOW)
        for part in range(SPLIT):
            where = pl.ds(part * size, size)
            links.go(
                over + step * SPLIT + part,
                stage.at[step, where],
                land.at[step, where],
                site.across,
            )

    def pass_on(part):
        where = pl.ds(part * size, size)
        value = mine[4, where] + came(over + part, land.at[0, where])
        stage[4, where] = value.astype(LOW)
        device = site.up if part % 2 == 0 else site.down
        links.go(relay + part, stage.at[4, where], land.at[4, where], device)

    compute(0)
    compute(1)
    send_over(0)
    compute(2)
    send_over(1)
    compute(3)
    send_over(2)
    compute(4)
    send_over(3)
    compute(5)
    settle(4)
    compute(6)
    compute(7)
    for part in range(SPLIT):
        pass_on(part)
    for step in (5, 6, 7):
        settle(step)
    for part in range(SPLIT):
        where = pl.ds(part * size, size)
        for step, base, device in ((5, up, site.up), (6, down, site.down)):
            from_y = over + (step - 4) * SPLIT + part
            value = mine[step, where] + came(from_y, land.at[step - 4, where])
            if part % 2 == step - 5:
                value = value + came(relay + part, land.at[4, where])
            stage[step, where] = value.astype(LOW)
            links.go(base + part, stage.at[step, where], land.at[step, where], device)
    sums = []
    for part in range(SPLIT):
        where = pl.ds(part * size, size)
        value = mine[7, where] + came(over + 3 * SPLIT + part, land.at[3, where])
        value = value + came(up + part, land.at[5, where])
        sums.append(value + came(down + part, land.at[6, where]))
    return jnp.concatenate(sums, 0)


class Cross:
    def __init__(self, site, groups, src, dst, send, recv):
        self.links = Links(send, recv, site)
        self.site, self.groups, self.src, self.dst = site, groups, src, dst
        self.started = 0
        self.landed = set()
        self.start()

    def start(self):
        if self.started < len(self.groups):
            for index in self.groups[self.started]:
                self.links.go(index, self.src[index], self.dst[index], self.site.partner)
            self.started += 1

    def wait(self, index):
        if index in self.landed:
            return
        self.landed.add(index)
        self.links.got(index, self.dst[index])
        if all(other in self.landed for other in self.groups[self.started - 1]):
            self.start()

    def close(self):
        for group in self.groups:
            for index in group:
                self.wait(index)
        self.links.close()


class Weights:
    def __init__(self, site, plan, held, own, other, sems, cross):
        self.site, self.plan, self.cross, self.sems = site, plan, cross, sems
        self.held, self.own, self.other = held, own, other
        self.waits = {}
        for index, (_, _, _, crossed) in enumerate(plan):
            if crossed is None:
                self.start(index)

    def start(self, index):
        _, layer, start, _ = self.plan[index]
        rows = self.own[index].shape[0]
        target = self.held[index]
        target = target if start is None else target.at[pl.ds(start, rows)]
        from_own = pltpu.make_async_copy(self.own[index], target, self.sems.at[index])
        from_other = pltpu.make_async_copy(self.other[index], target, self.sems.at[index])
        pl.when(self.site.section == layer)(from_own.start)
        pl.when(self.site.section != layer)(from_other.start)
        self.waits[index] = from_own

    def settle(self, keys):
        todo = [index for index, item in enumerate(self.plan) if item[0] in keys]
        for index in todo:
            crossed = self.plan[index][3]
            if crossed is not None and index not in self.waits:
                self.cross.wait(crossed)
                self.start(index)
        for index in todo:
            if self.waits[index] is not None:
                self.waits[index].wait()
                self.waits[index] = None


def ring_kernel(spec, *refs):
    refs = list(refs)

    def take(count):
        taken = refs[:count]
        del refs[:count]
        return taken

    plan = spec.plan
    values = take(spec.n_in)
    own, other = take(len(plan)), take(len(plan))
    sources = take(spec.n_cross)
    take(spec.n_after)
    named = types.SimpleNamespace(**dict(zip(spec.names, values + refs)))
    site = Site()
    named.site = site
    greet(site, spec.peers, spec.n_cross or spec.peers)
    cross = weights = None
    if spec.n_cross:
        targets = [getattr(named, key) for key in spec.crossed]
        cross = Cross(
            site, spec.groups, sources, targets, named.cross_send, named.cross_recv
        )
        for index, item in enumerate(plan):
            if item[3] is not None:
                own[index], other[index] = sources[item[3]], targets[item[3]]
    if plan:
        held = [getattr(named, item[0]) for item in plan]
        weights = Weights(site, plan, held, own, other, named.weight_sem, cross)
    total = None
    if spec.fold is not None:
        links = Links(named.fold_send, named.fold_recv, site)
        weights.settle(spec.fold_keys)
        total = fold_steps(
            site,
            functools.partial(spec.fold, named),
            named.mine,
            named.pass_out,
            named.pass_in,
            named.stage,
            named.land,
            links,
        )
    rows = spec.local(named, total)
    if spec.use is not None:
        held = named.held
        held[site.chip(0, 0), site.core] = rows
        kept = []

        def consume(chip):
            if plan:
                weights.settle(spec.use_keys)
            block = held[chip]
            spec.use(named, chip, block.reshape(block.shape[0] * block.shape[1], block.shape[2]))
            source = named.normed if spec.normed else held
            copy = pltpu.make_async_copy(
                source.at[chip], named.rows_all.at[chip], named.keep_sem.at[len(kept)]
            )
            copy.start()
            kept.append(copy)

        links_on = Links(named.spread_send, named.spread_recv, site)
        spreading = spread_steps(site, held, links_on, consume)
        next(spreading)
        if spec.meanwhile is not None:
            spec.meanwhile(named, spreading)
        for _ in spreading:
            pass
        for copy in kept:
            copy.wait()
        links_on.close()
    if spec.fold is not None:
        links.close()
    if cross is not None:
        cross.close()


def ring_call(
    name, ident, inputs, fold_weights, use_weights, outputs, local, fold=None, use=None,
    extra=None, after=(), meanwhile=None, peers=False, normed=False, cross=(),
):
    per_device, width = inputs.pop("like").shape
    out_shape = [jax.ShapeDtypeStruct(*value) for value in outputs.values()]
    out_specs = [IN_VMEM] * len(out_shape)
    names = list(inputs) + list(outputs)
    scratch, plan, own_set, other_set = {}, [], [], []
    crossed = [key for group in cross for key in group]
    cross_set = [value for group in cross for value in group.values()]
    for key, parts in {**fold_weights, **use_weights}.items():
        start = 0
        for part in parts:
            place = start if len(parts) > 1 else None
            if len(part) == 2:
                index = crossed.index(part[0])
                own = other = cross_set[index]
            else:
                index = None
                own, other = part[:2]
            plan.append((key, part[-1], place, index))
            own_set.append(own)
            other_set.append(other)
            start += own.shape[0]
        scratch[key] = pltpu.VMEM((start, width), LOW)
    full = (per_device, width)
    more = dict(extra or {})
    for key, value in zip(crossed, cross_set):
        names.append(key)
        out_shape.append(jax.ShapeDtypeStruct(value.shape, value.dtype))
        out_specs.append(ANYWHERE)
    if cross:
        more.update(
            cross_send=pltpu.SemaphoreType.DMA((len(crossed),)),
            cross_recv=pltpu.SemaphoreType.DMA((len(crossed),)),
        )
    if plan:
        more.update(weight_sem=pltpu.SemaphoreType.DMA((len(plan),)))
    if fold is not None:
        more.update(
            mine=pltpu.VMEM((CHIPS, *full), FULL),
            pass_out=pltpu.VMEM((CHIPS, *full), LOW),
            pass_in=pltpu.VMEM((CHIPS, *full), LOW),
            stage=pltpu.VMEM((CHIPS - 1, *full), LOW),
            land=pltpu.VMEM((CHIPS - 1, *full), LOW),
            fold_send=pltpu.SemaphoreType.DMA((FOLD_SEMS,)),
            fold_recv=pltpu.SemaphoreType.DMA((FOLD_SEMS,)),
        )
    if use is not None:
        names.append("rows_all")
        out_shape.append(jax.ShapeDtypeStruct((CHIPS, 2, *full), LOW))
        out_specs.append(ANYWHERE)
        more.update(
            held=pltpu.VMEM((CHIPS, 2, *full), LOW),
            keep_sem=pltpu.SemaphoreType.DMA((CHIPS,)),
            spread_send=pltpu.SemaphoreType.DMA((SPREAD_SEMS,)),
            spread_recv=pltpu.SemaphoreType.DMA((SPREAD_SEMS,)),
        )
        if normed:
            more.update(normed=pltpu.VMEM((CHIPS, 2, *full), LOW))
    scratch.update(more)
    names += list(scratch)
    groups, at = [], 0
    for group in cross:
        groups.append(list(range(at, at + len(group))))
        at += len(group)
    spec = types.SimpleNamespace(
        names=names, plan=plan, n_in=len(inputs), n_cross=len(crossed), n_after=len(after),
        crossed=crossed, groups=groups, fold=fold, local=local, use=use, meanwhile=meanwhile,
        peers=peers, normed=normed, fold_keys=list(fold_weights), use_keys=list(use_weights),
    )
    return pl.pallas_call(
        functools.partial(ring_kernel, spec),
        out_shape=out_shape,
        in_specs=[IN_VMEM] * len(inputs)
        + [ANYWHERE] * (2 * len(plan) + len(crossed) + len(after)),
        out_specs=out_specs,
        scratch_shapes=list(scratch.values()),
        compiler_params=pltpu.CompilerParams(
            collective_id=ident, has_side_effects=True, vmem_limit_bytes=56 * 2**20
        ),
        cost_estimate=pl.CostEstimate(
            flops=2**35 * ((fold is not None) + (use is not None)),
            bytes_accessed=2**23,
            transcendentals=0,
        ),
        name=name,
    )(*inputs.values(), *own_set, *other_set, *cross_set, *after)


def rows_of(ref, chip, site):
    return jnp.concatenate([ref[chip, 1 - site.core], ref[chip, site.core]], 0)


def fold_mixed(named, chip):
    return plain_dot(rows_of(named.mixed, chip, named.site), named.w_out[...])


def fold_act(named, chip):
    return plain_dot(rows_of(named.act, chip, named.site), named.w_down[...])


def fold_d_qkv(named, chip):
    return plain_dot(rows_of(named.d_qkv, chip, named.site), named.w_in[...])


def fold_d_act(named, chip):
    site = named.site
    return plain_dot(rows_of(named.d_gate, chip, site), named.w_gate[...]) + plain_dot(
        rows_of(named.d_up, chip, site), named.w_up[...]
    )


def use_qkv(named, chip, rows):
    named.qkv[chip] = times_trans(rows, named.w_in[...])


def put(ref, chip, value):
    ref[chip] = value.astype(LOW).reshape(ref.shape[1:])


def use_gate_up(named, chip, rows):
    gate_pre = times_trans(rows, named.w_gate[...])
    up_pre = times_trans(rows, named.w_up[...])
    sig = jax.nn.sigmoid(gate_pre)
    silu_val = gate_pre * sig
    put(named.act, chip, silu_val * up_pre)
    put(named.gate_slope, chip, up_pre * sig * (1.0 + gate_pre * (1.0 - sig)))
    put(named.up_slope, chip, silu_val)


def use_d_act(named, chip, rows):
    d_act = times_trans(rows, named.w_down[...])
    for out, slope in ((named.d_gate, named.gate_slope), (named.d_up, named.up_slope)):
        put(out, chip, d_act * slope[chip].astype(FULL).reshape(d_act.shape))


def use_d_mixed(named, chip, rows):
    named.d_mixed[chip] = times_trans(rows, named.w_out[...]).astype(LOW)


def local_start(named, total):
    return named.x_rows[...]


def gather_small(named, rows_spreading):
    site = named.site
    links_x = Links(named.small_x_send, named.small_x_recv, site)
    links_x.go(0, named.gains_own, named.gains_x, site.partner)
    links_x.go(1, named.kv_own, named.kv_x, site.partner)
    links_x.got(0, named.gains_x)
    own, came = named.gains_own[...], named.gains_x[...]
    first = site.section == 0
    named.gains_all[site.chip(0, 0), site.core] = jnp.concatenate(
        [
            jnp.where(first, own, came)[:2],
            jnp.where(first, came, own)[:2],
            jnp.zeros((4, own.shape[1]), FULL),
        ],
        0,
    )
    links = Links(named.small_send, named.small_recv, site)
    spreading = spread_steps(site, named.gains_all, links, lambda chip: None, 1)
    next(spreading)
    links_x.got(1, named.kv_x)
    named.kv_all[site.member, site.section] = named.kv_own[...]
    named.kv_all[site.member, 1 - site.section] = named.kv_x[...]
    links_kv = Links(named.kv_send, named.kv_recv, site)
    mine = named.kv_all.at[site.member]
    peers = (site.sibling, site.across, site.corner)
    for index, device in enumerate(peers):
        links_kv.go(index, mine, mine, device)
    next(rows_spreading)
    for _ in spreading:
        pass
    for index, device in enumerate(peers):
        links_kv.got(index, named.kv_all.at[device[2]])
    links.close()
    links_kv.close()
    links_x.close()
    named.gain_row[...] = jnp.concatenate(
        [named.gains_all[chip, core, :1] for chip in range(CHIPS) for core in range(2)], 1
    )


def use_first(named, chip, rows):
    normed = scaled(rows.astype(FULL), named.gain_row[...]).astype(LOW)
    named.normed[chip] = normed.reshape(named.normed.shape[1:])
    query = times_trans(normed, named.w_query[...])
    pair = [
        times_trans(normed, named.kv_all[:, 0, index].reshape(HEAD_DIM, normed.shape[1]))
        for index in range(2)
    ]
    named.qkv[chip] = jnp.concatenate([query, *pair], 1)


def local_middle(named, total):
    hidden_in = named.x_rows[...].astype(FULL) + total
    named.hidden_in[...] = hidden_in
    return scaled(hidden_in, named.gain[...]).astype(LOW)


def local_next(named, total):
    result = (named.hidden_in[...] + total).astype(LOW)
    named.result[...] = result
    return scaled(result.astype(FULL), named.gain[...]).astype(LOW)


def local_last(named, total):
    named.result[...] = (named.hidden_in[...] + total).astype(LOW)


def local_top(named, total):
    return named.top_rows[...]


def norm_back_rows(values, gain_vec, grad_in):
    factor = lax.rsqrt(jnp.mean(values * values, -1, keepdims=True) + EPSILON)
    gain_grad = jnp.sum(grad_in * values * factor, 0, keepdims=True)
    mean_term = jnp.mean(grad_in * gain_vec * values, -1, keepdims=True)
    return (
        gain_grad,
        factor * gain_vec * grad_in - values * (factor * factor * factor) * mean_term,
    )


def local_branch(named, total):
    gain_grad, d_hidden = norm_back_rows(named.hidden_in[...], named.gain[...], total)
    d_hidden = d_hidden + named.top_rows[...].astype(FULL)
    named.gain_grad[...] = gain_grad
    named.d_hidden[...] = d_hidden
    return d_hidden.astype(LOW)


def local_input(named, total):
    gain_grad, d_input = norm_back_rows(
        named.x_rows[...].astype(FULL), named.gain[...], total
    )
    d_input = (d_input + named.d_hidden[...]).astype(LOW)
    named.gain_grad[...] = gain_grad
    named.d_input[...] = d_input
    return d_input


def swap_halves(value):
    width = value.shape[1]
    half = HEAD_DIM // 2
    lane = lax.broadcasted_iota(jnp.int32, value.shape, 1)
    return jnp.where(
        lax.rem(lane, HEAD_DIM) < half,
        pltpu.roll(value, width - half, 1),
        pltpu.roll(value, half, 1),
    )


def stacked(pair):
    return jnp.concatenate([pair[:, :HEAD_DIM], pair[:, HEAD_DIM:]], 0)


def side_by_side(turned):
    return jnp.concatenate([turned[:, :PLACE], turned[:, PLACE:]], 0).T


def hide_later(scores, fill):
    last = scores[-PLACE:]
    key = lax.broadcasted_iota(jnp.int32, last.shape, 0)
    query = lax.rem(lax.broadcasted_iota(jnp.int32, last.shape, 1), PLACE)
    last = jnp.where(key <= query, last, fill)
    if scores.shape[0] == PLACE:
        return last
    return jnp.concatenate([scores[:-PLACE], last], 0)


def turn_of(turns, place):
    near, far = pl.ds(0, PLACE), pl.ds(PLACE + place, 1)
    cos_near, sin_near = turns[0, near], turns[1, near]
    cos_far, sin_far = turns[0, far], turns[1, far]
    cosine = cos_near * cos_far - sin_near * sin_far
    sine = sin_near * cos_far + cos_near * sin_far
    lane = lax.broadcasted_iota(jnp.int32, cosine.shape, 1)
    sine = jnp.where(lax.rem(lane, HEAD_DIM) < HEAD_DIM // 2, -sine, sine)
    keyed = lane < HEAD_DIM
    return (
        jnp.concatenate([cosine, jnp.where(keyed, cosine, 1.0)], 1),
        jnp.concatenate([sine, jnp.where(keyed, sine, 0.0)], 1),
    )


def attend_kernel(block_at, qkv, turns, mixed, turned, attended, spread, values_t):
    q_width = 2 * HEAD_DIM
    for place in range(CHIPS):
        at = pl.ds(place * PLACE, PLACE)
        value = qkv[block_at[place]]
        cosine, sine = turn_of(turns, place)
        value = value * cosine + swap_halves(value) * sine
        value = value.astype(LOW)
        scale = jnp.asarray(1.0 / math.sqrt(HEAD_DIM), LOW)
        turned[at, :q_width] = value[:, :q_width] * scale
        turned[at, q_width:] = value[:, q_width:]
        values_t[:, at] = value[:, q_width:].astype(FULL).T[HEAD_DIM:].astype(LOW)
    for place in range(CHIPS):
        at = pl.ds(place * PLACE, PLACE)
        keys = pl.ds(0, (place + 1) * PLACE)
        query = stacked(turned[at, :q_width])
        scores = times_trans(turned[keys, q_width : q_width + HEAD_DIM], query)
        scores = hide_later(scores, NEG_LARGE)
        top = jnp.max(scores, 0, keepdims=True)
        weight = jnp.exp(scores - top)
        total = jnp.sum(weight, 0, keepdims=True)
        out = plain_dot(values_t[:, keys], weight.astype(LOW)) / total
        out = side_by_side(out)
        attended[at] = out
        mixed[block_at[place]] = out.astype(LOW).reshape(mixed.shape[1:])
        spread[pl.ds(place, 1)] = top + jnp.log(total)


def attend_back_kernel(
    block_at, d_mixed, turns, turned, attended, spread, d_qkv, keys_t, d_query, d_key, d_value
):
    q_width = 2 * HEAD_DIM
    d_key[...] = jnp.zeros_like(d_key)
    d_value[...] = jnp.zeros_like(d_value)
    for place in range(CHIPS):
        at = pl.ds(place * PLACE, PLACE)
        keys_t[:, at] = turned[at, q_width:].astype(FULL).T[:HEAD_DIM].astype(LOW)
    for place in range(CHIPS):
        at = pl.ds(place * PLACE, PLACE)
        keys = pl.ds(0, (place + 1) * PLACE)
        d_out = d_mixed[block_at[place]]
        product = (d_out.astype(FULL) * attended[at]).T
        offset = jnp.concatenate(
            [
                jnp.sum(product[:HEAD_DIM], 0, keepdims=True),
                jnp.sum(product[HEAD_DIM:], 0, keepdims=True),
            ],
            1,
        )
        d_out = stacked(d_out)
        query = stacked(turned[at, :q_width])
        scores = times_trans(turned[keys, q_width : q_width + HEAD_DIM], query)
        scores = hide_later(scores, NEG_LARGE)
        probs = jnp.exp(scores - spread[pl.ds(place, 1)])
        d_probs = times_trans(turned[keys, q_width + HEAD_DIM :], d_out)
        d_scores = (probs * (d_probs - offset)).astype(LOW)
        d_key[keys] += plain_dot(d_scores, query)
        d_value[keys] += plain_dot(probs.astype(LOW), d_out)
        d_query[at] = side_by_side(plain_dot(keys_t[:, keys], d_scores)) * (
            1.0 / math.sqrt(HEAD_DIM)
        )
    for place in range(CHIPS):
        at = pl.ds(place * PLACE, PLACE)
        value = jnp.concatenate([d_query[at], d_key[at], d_value[at]], 1)
        cosine, sine = turn_of(turns, place)
        value = value * cosine - swap_halves(value) * sine
        d_qkv[block_at[place]] = value.astype(LOW).reshape(d_qkv.shape[1:])


def plain_call(kernel, name, count, out_shape, scratch):
    return pl.pallas_call(
        kernel,
        out_shape=out_shape,
        in_specs=[pl.BlockSpec(memory_space=pltpu.SMEM)] + [IN_VMEM] * (count - 1),
        out_specs=[IN_VMEM] * len(out_shape),
        scratch_shapes=scratch,
        compiler_params=pltpu.CompilerParams(vmem_limit_bytes=48 * 2**20),
        cost_estimate=pl.CostEstimate(flops=2**33, bytes_accessed=2**23, transcendentals=2**21),
        name=name,
    )


def relay_body(
    inputs,
    cotangent,
    positions,
    gain_attn,
    w_query,
    w_key,
    w_value,
    w_out,
    gain_ffn,
    w_gate,
    w_up,
    w_down,
):
    n_micro, per_device, model_width = inputs.shape
    n_seq = lax.axis_size("seq")
    n_shard = lax.axis_size("shard")
    members = n_seq * n_shard
    total_len = members * per_device
    section_idx = lax.axis_index("section")
    q_width = HEADS // members * HEAD_DIM
    in_width = q_width + 2 * HEAD_DIM
    hidden = w_down.shape[1]
    shape = jax.ShapeDtypeStruct

    def swap(value):
        return lax.ppermute(value, "section", [(0, 1), (1, 0)])

    def pick(first, second):
        return jnp.where(section_idx == 0, first, second)

    rows_in = pick(inputs[0], inputs[1])
    top_in = pick(cotangent[0], cotangent[1])
    places = pick(positions[0], positions[1])

    small = jnp.concatenate([gain_attn, gain_ffn], 0).astype(FULL)
    small = jnp.concatenate([small, jnp.zeros((6, small.shape[1]), FULL)], 0)
    kv_pair = jnp.stack([w_key[0], w_value[0]])

    def w_in_of(layer):
        return [(w_query[0], x_query, layer), (kv_all[layer], kv_all[layer], layer)]

    order = places.reshape(CHIPS, PLACE)[:, 0] // PLACE
    block_at = jnp.sum(
        jnp.where(
            order[None, :] == jnp.arange(CHIPS)[:, None], jnp.arange(CHIPS)[None, :], 0
        ),
        1,
    ).astype(jnp.int32)
    half_dim = HEAD_DIM // 2
    inv_freq = THETA_BASE ** (-jnp.arange(half_dim, dtype=FULL) * (2.0 / HEAD_DIM))
    steps = jnp.concatenate([jnp.arange(PLACE), PLACE * jnp.arange(CHIPS)]).astype(FULL)
    angles = steps[:, None] * jnp.tile(inv_freq, 2 * q_width // HEAD_DIM)[None, :]
    turns = jnp.stack([jnp.cos(angles), jnp.sin(angles)])

    narrow = (CHIPS, 2, per_device, hidden)
    chip_rows = 2 * per_device
    act_outs = dict(act=(narrow, LOW), gate_slope=(narrow, LOW), up_slope=(narrow, LOW))
    back_outs = dict(d_gate=(narrow, LOW), d_up=(narrow, LOW))
    qkv_out = dict(qkv=((CHIPS, chip_rows, in_width), FULL))
    row_low = ((per_device, model_width), LOW)
    row_full = ((per_device, model_width), FULL)
    gain_out = ((1, model_width), FULL)

    def flat(value):
        return value.reshape(total_len, value.shape[-1])

    def attend(qkv):
        mixed, *saved = plain_call(
            attend_kernel,
            "attend",
            3,
            [
                shape((CHIPS, 2, per_device, q_width), LOW),
                shape((total_len, in_width), LOW),
                shape((total_len, q_width), FULL),
                shape((CHIPS, 2 * PLACE), FULL),
            ],
            [pltpu.VMEM((HEAD_DIM, total_len), LOW)],
        )(block_at, qkv, turns)
        return mixed, saved

    def attend_back(saved, d_mixed):
        (d_qkv,) = plain_call(
            attend_back_kernel,
            "attend_back",
            6,
            [shape((CHIPS, 2, per_device, in_width), LOW)],
            [
                pltpu.VMEM((HEAD_DIM, total_len), LOW),
                pltpu.VMEM((total_len, q_width), FULL),
                pltpu.VMEM((total_len, HEAD_DIM), FULL),
                pltpu.VMEM((total_len, HEAD_DIM), FULL),
            ],
        )(block_at, d_mixed, turns, *saved)
        return d_qkv

    def middle(layer, mixed, x_rows, w_gate_set, w_up_set, cross=()):
        return ring_call(
            "attn_out_to_ffn",
            1 + 7 * layer,
            dict(like=x_rows, x_rows=x_rows, mixed=mixed, gain=gains[layer, 1]),
            dict(w_out=[(w_out[0], x_out, layer)]),
            dict(w_gate=[(*w_gate_set, layer)], w_up=[(*w_up_set, layer)]),
            dict(hidden_in=row_full, **act_outs),
            local_middle,
            fold=fold_mixed,
            use=use_gate_up,
            cross=cross,
        )

    def middle_back(layer, d_gate, d_up, hidden_in, top_rows, after=()):
        return ring_call(
            "ffn_back_to_attn",
            2 + 7 * layer,
            dict(
                like=top_rows,
                d_gate=d_gate,
                d_up=d_up,
                hidden_in=hidden_in,
                top_rows=top_rows,
                gain=gains[layer, 1],
            ),
            dict(w_gate=[(w_gate[0], x_gate, layer)], w_up=[(w_up[0], x_up, layer)]),
            dict(w_out=[(w_out[0], x_out, layer)]),
            dict(
                gain_grad=gain_out,
                d_hidden=row_full,
                d_mixed=((CHIPS, chip_rows, q_width), LOW),
            ),
            local_branch,
            fold=fold_d_act,
            use=use_d_mixed,
            after=after,
        )

    qkv, gains_all, kv_all, x_query, x_out, normed_one_a = ring_call(
        "first_rows",
        0,
        dict(like=rows_in, x_rows=rows_in, gains_own=small, kv_own=kv_pair),
        {},
        dict(w_query=[("x_query", 0)]),
        dict(
            **qkv_out,
            gains_all=((CHIPS, 2, *small.shape), FULL),
            kv_all=((n_seq, 2, *kv_pair.shape), LOW),
        ),
        local_start,
        use=use_first,
        extra=dict(
            gain_row=pltpu.VMEM((1, model_width), FULL),
            small_send=pltpu.SemaphoreType.DMA((SMALL_SEMS,)),
            small_recv=pltpu.SemaphoreType.DMA((SMALL_SEMS,)),
            kv_send=pltpu.SemaphoreType.DMA((n_seq - 1,)),
            kv_recv=pltpu.SemaphoreType.DMA((n_seq - 1,)),
            gains_x=pltpu.VMEM(small.shape, FULL),
            kv_x=pltpu.VMEM(kv_pair.shape, LOW),
            small_x_send=pltpu.SemaphoreType.DMA((2,)),
            small_x_recv=pltpu.SemaphoreType.DMA((2,)),
        ),
        normed=True,
        cross=[dict(x_query=w_query[0]), dict(x_out=w_out[0])],
        meanwhile=gather_small,
        peers=True,
    )
    gains = gains_all.reshape(members, -1, gain_attn.shape[1])[:, :4]
    gains = gains.transpose(1, 0, 2).reshape(2, 2, 1, model_width)
    kv_all = kv_all.transpose(1, 2, 0, 3, 4).reshape(2, 2 * HEAD_DIM, model_width)
    mixed_a, saved_a = attend(qkv)
    hidden_a, act_a, gate_slope_a, up_slope_a, x_gate, x_up, x_down, normed_two_a = middle(
        0,
        mixed_a,
        rows_in,
        ("x_gate",),
        ("x_up",),
        [dict(x_gate=w_gate[0], x_up=w_up[0]), dict(x_down=w_down[0])],
    )
    result_a, qkv, normed_one_b = ring_call(
        "ffn_to_next",
        3,
        dict(like=rows_in, act=act_a, hidden_in=hidden_a, gain=gains[1, 0]),
        dict(w_down=[(w_down[0], x_down, 0)]),
        dict(w_in=w_in_of(1)),
        dict(result=row_low, **qkv_out),
        local_next,
        fold=fold_act,
        use=use_qkv,
    )
    mixed_b, saved_b = attend(qkv)
    hidden_b, act_b, gate_slope_b, up_slope_b, normed_two_b = middle(
        1, mixed_b, result_a, (w_gate[0], x_gate), (w_up[0], x_up)
    )

    def join_to(layer, own):
        pairs = [(0, 1)] if layer else [(1, 0)]
        return own, lax.ppermute(own, "section", pairs)

    def ffn_sums(layer, act, top_all, d_gate, d_up, normed_two):
        return [
            join_to(layer, outer_sum(flat(left), flat(right)).astype(LOW))
            for left, right in ((act, top_all), (d_gate, normed_two), (d_up, normed_two))
        ]

    def attn_sums(layer, mixed, branch_all, d_qkv, normed_one):
        g_in = outer_sum(flat(d_qkv), flat(normed_one)).astype(LOW)
        kv = g_in[q_width:].reshape(2, n_seq, -1, model_width)
        kv = lax.all_to_all(kv, "seq", split_axis=1, concat_axis=1, tiled=True)
        kv = jnp.sum(kv.astype(FULL), 1).astype(LOW)
        g_out = outer_sum(flat(mixed), flat(branch_all)).astype(LOW)
        return [join_to(layer, value) for value in (g_out, g_in[:q_width], kv)]

    def came_of(sums):
        return [came for _, came in sums]

    (result_b,) = ring_call(
        "ffn_last",
        4,
        dict(like=rows_in, act=act_b, hidden_in=hidden_b),
        dict(w_down=[(w_down[0], x_down, 1)]),
        {},
        dict(result=row_low),
        local_last,
        fold=fold_act,
    )
    d_gate_b, d_up_b, top_all_b = ring_call(
        "top_rows",
        5,
        dict(like=top_in, top_rows=top_in, gate_slope=gate_slope_b, up_slope=up_slope_b),
        {},
        dict(w_down=[(w_down[0], x_down, 1)]),
        back_outs,
        local_top,
        use=use_d_act,
    )
    ffn_b = ffn_sums(1, act_b, top_all_b, d_gate_b, d_up_b, normed_two_b)
    gain_ffn_b, d_hidden_b, d_mixed, branch_all_b = middle_back(
        1, d_gate_b, d_up_b, hidden_b, top_in
    )
    d_qkv_b = attend_back(saved_b, d_mixed)
    attn_b = attn_sums(1, mixed_b, branch_all_b, d_qkv_b, normed_one_b)
    gain_attn_b, back_b, d_gate_a, d_up_a, top_all_a = ring_call(
        "attn_back_to_prev",
        6,
        dict(
            like=top_in,
            d_qkv=d_qkv_b,
            x_rows=result_a,
            d_hidden=d_hidden_b,
            gain=gains[1, 0],
            gate_slope=gate_slope_a,
            up_slope=up_slope_a,
        ),
        dict(w_in=w_in_of(1)),
        dict(w_down=[(w_down[0], x_down, 0)]),
        dict(gain_grad=gain_out, d_input=row_low, **back_outs),
        local_input,
        fold=fold_d_qkv,
        use=use_d_act,
    )
    ffn_a = ffn_sums(0, act_a, top_all_a, d_gate_a, d_up_a, normed_two_a)
    gain_ffn_a, d_hidden_a, d_mixed, branch_all_a = middle_back(
        0, d_gate_a, d_up_a, hidden_a, back_b, after=came_of(ffn_b)
    )
    d_qkv_a = attend_back(saved_a, d_mixed)
    attn_a = attn_sums(0, mixed_a, branch_all_a, d_qkv_a, normed_one_a)
    gain_attn_a, back_a = ring_call(
        "attn_back_last",
        7,
        dict(like=top_in, d_qkv=d_qkv_a, x_rows=rows_in, d_hidden=d_hidden_a, gain=gains[0, 0]),
        dict(w_in=w_in_of(0)),
        {},
        dict(gain_grad=gain_out, d_input=row_low),
        local_input,
        fold=fold_d_qkv,
        after=came_of(attn_b),
    )

    def joined(first, second):
        came = swap(pick(second, first))
        kept = pick(first, second)
        return pick(jnp.stack([kept, came]), jnp.stack([came, kept]))[None]

    outputs = joined(result_a, result_b)
    input_grads = joined(back_a, back_b)

    g_down, g_gate, g_up, g_out, g_query, g_kv = (
        pick(own_a, own_b).astype(FULL) + pick(came_a, came_b).astype(FULL)
        for (own_a, came_a), (own_b, came_b) in zip(ffn_a + attn_a, ffn_b + attn_b)
    )
    gain_grads = jnp.concatenate([gain_attn_a, gain_ffn_a, gain_attn_b, gain_ffn_b], 0)
    gain_grads = gain_grads.reshape(2, 2, members, -1).transpose(0, 2, 1, 3)
    gain_grads = lax.all_to_all(
        gain_grads.reshape(2 * members, 2, -1),
        ("section", "shard", "seq"),
        split_axis=0,
        concat_axis=0,
        tiled=True,
    )
    gain_grads = jnp.sum(gain_grads, 0, keepdims=True)
    return (
        outputs,
        input_grads,
        gain_grads[:, 0],
        g_query[None],
        g_kv[:1],
        g_kv[1:],
        g_out[None],
        gain_grads[:, 1],
        g_gate[None],
        g_up[None],
        g_down[None],
    )


def fits_relay(mesh):
    shape = mesh.shape
    return shape["section"] == 2 and shape["shard"] == KV_HEADS == RING and shape["seq"] == 4


def solution(mesh):
    in_specs = (
        P(None, ("shard", "seq"), None),
        P(None, ("shard", "seq"), None),
        P(),
        P("section", ("shard", "seq")),
        P("section", ("shard", "seq"), None),
        P("section", ("shard", "seq"), None),
        P("section", ("shard", "seq"), None),
        P("section", ("shard", "seq"), None),
        P("section", ("shard", "seq")),
        P("section", ("shard", "seq"), None),
        P("section", ("shard", "seq"), None),
        P("section", ("shard", "seq"), None),
    )
    out_specs = (
        P("section", None, ("shard", "seq"), None),
        P("section", None, ("shard", "seq"), None),
        P("section", ("shard", "seq")),
        P("section", ("shard", "seq"), None),
        P("section", ("shard", "seq"), None),
        P("section", ("shard", "seq"), None),
        P("section", ("shard", "seq"), None),
        P("section", ("shard", "seq")),
        P("section", ("shard", "seq"), None),
        P("section", ("shard", "seq"), None),
        P("section", ("shard", "seq"), None),
    )
    chosen = relay_body if fits_relay(mesh) else body
    return jax.shard_map(chosen, mesh=mesh, in_specs=in_specs, out_specs=out_specs, check_vma=False)
```

```python
import functools
import math
import types

import jax
import jax.numpy as jnp
from jax import lax
from jax.experimental import pallas as pl
from jax.experimental.pallas import tpu as pltpu
from jax.sharding import PartitionSpec as P

HEADS = 32
KV_HEADS = 4
HEAD_DIM = 64


EPSILON = 1e-05
THETA_BASE = 10000.0
NEG_LARGE = -1e30


def shifted(value, axis, by):
    count = lax.axis_size(axis)
    pairs = [(i, i + by) for i in range(count) if 0 <= i + by < count]
    return lax.ppermute(value, axis, pairs)


def times_trans(left, right):
    return lax.dot_general(
        left, right, (((1,), (1,)), ((), ())), preferred_element_type=jnp.float32
    )


def outer_sum(left, right):
    return lax.dot_general(
        left, right, (((0,), (0,)), ((), ())), preferred_element_type=jnp.float32
    )


def plain_dot(left, right):
    return jnp.dot(left, right, preferred_element_type=jnp.float32)


def rotate(values, places, direction):
    half_dim = values.shape[-1] // 2
    inv_freq = THETA_BASE ** (-jnp.arange(half_dim, dtype=jnp.float32) * (2.0 / values.shape[-1]))
    angles = places.astype(jnp.float32)[:, None] * inv_freq[None, :]
    cosine = jnp.cos(angles)[:, None, :]
    sine_val = direction * jnp.sin(angles)[:, None, :]
    first = values[..., :half_dim]
    second = values[..., half_dim:]
    return jnp.concatenate(
        [first * cosine - second * sine_val, second * cosine + first * sine_val], -1
    )


def scaled(values, gain_vec):
    factor = lax.rsqrt(jnp.mean(values * values, -1, keepdims=True) + EPSILON)
    return values * factor * gain_vec


def norm_back(values, gain_vec, grad_in):
    factor = lax.rsqrt(jnp.mean(values * values, -1, keepdims=True) + EPSILON)
    gain_grad = jnp.sum(grad_in * values * factor, 0)
    mean_term = jnp.mean(grad_in * gain_vec * values, -1, keepdims=True)
    return (
        gain_grad,
        factor * gain_vec * grad_in - values * (factor * factor * factor) * mean_term,
    )


def ffn_back(grad_rows, kept_rows, gate_pre, up_pre, wg_part, wu_part, wd_part):
    sigmoid_val = jax.nn.sigmoid(gate_pre)
    silu_val = gate_pre * sigmoid_val
    hidden_act = (silu_val * up_pre).astype(jnp.bfloat16)
    grad_down = outer_sum(hidden_act, grad_rows)
    d_act = times_trans(grad_rows, wd_part)
    d_gate = (d_act * up_pre * sigmoid_val * (1.0 + gate_pre * (1.0 - sigmoid_val))).astype(
        jnp.bfloat16
    )
    d_up = (d_act * silu_val).astype(jnp.bfloat16)
    grad_gate = outer_sum(d_gate, kept_rows)
    grad_up = outer_sum(d_up, kept_rows)
    d_normed = plain_dot(d_gate, wg_part) + plain_dot(d_up, wu_part)
    return ((grad_gate, grad_up, grad_down), d_normed)


def body(
    inputs,
    cotangent,
    positions,
    gain_attn,
    w_query,
    w_key,
    w_value,
    w_out,
    gain_ffn,
    w_gate,
    w_up,
    w_down,
):
    n_micro, per_device, model_width = inputs.shape
    n_seq = lax.axis_size("seq")
    n_shard = lax.axis_size("shard")
    section_idx = lax.axis_index("section")
    shard_pos = lax.axis_index("shard")
    member = shard_pos * n_seq + lax.axis_index("seq")
    span_rows = per_device * n_seq
    total_len = span_rows * n_shard
    local_heads = HEADS // n_seq
    kv_repeat = n_seq // KV_HEADS
    q_width = local_heads * HEAD_DIM
    attn_scale = 1.0 / math.sqrt(HEAD_DIM)
    gain_one, gain_two, wq_full, wk_full, wv_full, wo_full = (
        lax.all_gather(gain_attn[0], ("shard", "seq"), axis=0, tiled=True),
        lax.all_gather(gain_ffn[0], ("shard", "seq"), axis=0, tiled=True),
        lax.all_gather(w_query[0], ("shard", "seq"), axis=0, tiled=True),
        lax.all_gather(w_key[0], ("shard", "seq"), axis=0, tiled=True),
        lax.all_gather(w_value[0], ("shard", "seq"), axis=0, tiled=True),
        lax.all_gather(w_out[0], ("shard", "seq"), axis=0, tiled=True),
    )
    gain_a = gain_one.astype(jnp.float32)
    gain_f = gain_two.astype(jnp.float32)
    wg_use, wu_use, wd_use = (w_gate[0], w_up[0], w_down[0])

    def spread_rows(block_in):
        return lax.all_gather(block_in, ("shard", "seq"), axis=0, tiled=True)

    def fold_rows(block_in):
        return lax.psum_scatter(block_in, ("shard", "seq"), scatter_dimension=0, tiled=True)

    def to_heads(block_in):
        return lax.all_to_all(block_in, "seq", split_axis=1, concat_axis=0, tiled=True)

    def to_tokens(block_in):
        return lax.all_to_all(block_in, "seq", split_axis=0, concat_axis=1, tiled=True)

    def over_keys(head_keys, head_values, step_fn, init_state):
        return step_fn(
            init_state,
            (
                lax.all_gather(head_keys, "shard", axis=0, tiled=True),
                lax.all_gather(head_values, "shard", axis=0, tiled=True),
            ),
            jnp.int32(0),
        )

    def place_sets(batch_index):
        place_row = lax.dynamic_index_in_dim(positions, batch_index, 0, keepdims=False)
        token_places = lax.dynamic_slice_in_dim(place_row, member * per_device, per_device)
        span_places = lax.dynamic_slice_in_dim(place_row, shard_pos * span_rows, span_rows)
        return (place_row, token_places, span_places)

    zero_rows = jnp.zeros((per_device, model_width), jnp.bfloat16)
    arrived_x = zero_rows
    results = []
    stored = []
    for tick_index in range(n_micro + 1):
        own_rows = inputs[tick_index] if tick_index < n_micro else zero_rows
        input_now = jnp.where(section_idx == 0, own_rows, arrived_x)
        batch_index = jnp.clip(tick_index - section_idx, 0, n_micro - 1)
        forward_place_row, forward_token_places, forward_span_places = place_sets(batch_index)
        forward_values_in = input_now.astype(jnp.float32)
        forward_normed_one = scaled(forward_values_in, gain_a).astype(jnp.bfloat16)
        queries = rotate(
            times_trans(forward_normed_one, wq_full).reshape(per_device, HEADS, HEAD_DIM),
            forward_token_places,
            1.0,
        ).astype(jnp.bfloat16)
        key_rows = rotate(
            times_trans(forward_normed_one, wk_full).reshape(per_device, KV_HEADS, HEAD_DIM),
            forward_token_places,
            1.0,
        ).astype(jnp.bfloat16)
        value_rows = (
            times_trans(forward_normed_one, wv_full)
            .reshape(per_device, KV_HEADS, HEAD_DIM)
            .astype(jnp.bfloat16)
        )
        key_rows = jnp.repeat(key_rows, kv_repeat, axis=1)
        value_rows = jnp.repeat(value_rows, kv_repeat, axis=1)
        packed = jnp.concatenate(
            [queries.reshape(per_device, n_seq, q_width), key_rows, value_rows], -1
        )
        arrived = to_heads(packed)[:, 0]
        forward_head_query = arrived[:, :q_width].reshape(span_rows, local_heads, HEAD_DIM)
        forward_head_keys = arrived[:, q_width : q_width + HEAD_DIM]
        forward_head_values = arrived[:, q_width + HEAD_DIM :]

        def absorb(state_in, key_piece, start_row):
            run_max, run_total, run_acc = state_in
            piece_keys, piece_values = key_piece
            visible = forward_place_row[None, None, :] <= forward_span_places[None, :, None]
            scores = (
                jnp.einsum(
                    "qhd,kd->hqk",
                    forward_head_query,
                    piece_keys,
                    preferred_element_type=jnp.float32,
                )
                * attn_scale
            )
            scores = jnp.where(visible, scores, NEG_LARGE)
            new_max = jnp.maximum(run_max, jnp.max(scores, -1))
            weight = jnp.where(visible, jnp.exp(scores - new_max[..., None]), 0.0)
            rescale = jnp.exp(run_max - new_max)
            run_total = jnp.sum(weight, -1)
            run_acc = run_acc * rescale.T[..., None] + jnp.einsum(
                "hqk,kd->qhd",
                weight.astype(jnp.bfloat16),
                piece_values,
                preferred_element_type=jnp.float32,
            )
            return (new_max, run_total, run_acc)

        forward_start_state = (
            jnp.full((local_heads, span_rows), NEG_LARGE, jnp.float32),
            jnp.zeros((local_heads, span_rows), jnp.float32),
            jnp.zeros((span_rows, local_heads, HEAD_DIM), jnp.float32),
        )
        run_max, run_total, run_acc = over_keys(
            forward_head_keys, forward_head_values, absorb, forward_start_state
        )
        forward_attended = run_acc / run_total.T[..., None]
        forward_spread = run_max + jnp.log(run_total)
        forward_mixed_tok = to_tokens(
            forward_attended.astype(jnp.bfloat16).reshape(span_rows, 1, q_width)
        ).reshape(per_device, HEADS * HEAD_DIM)
        forward_hidden_in = forward_values_in + plain_dot(forward_mixed_tok, wo_full)
        normed_two = scaled(forward_hidden_in, gain_f).astype(jnp.bfloat16)
        forward_kept_rows = spread_rows(normed_two)
        forward_gate_pre = times_trans(forward_kept_rows, wg_use)
        forward_up_pre = times_trans(forward_kept_rows, wu_use)
        hidden_act = (jax.nn.silu(forward_gate_pre) * forward_up_pre).astype(jnp.bfloat16)
        branch = fold_rows(plain_dot(hidden_act, wd_use))
        result = (forward_hidden_in + branch).astype(jnp.bfloat16)
        forward_saved = (
            input_now,
            forward_head_query,
            forward_head_keys,
            forward_head_values,
            forward_attended,
            forward_spread,
            forward_mixed_tok,
            forward_hidden_in,
            forward_kept_rows,
            forward_gate_pre,
            forward_up_pre,
        )
        result, saved = (result, forward_saved)
        results.append(result)
        stored.append(saved)
        if tick_index < n_micro:
            arrived_x = shifted(result, "section", 1)
    returned = zero_rows
    grads_back = []
    row_lists = []
    gain_total = None
    ffn_total = None
    for tick_index in range(n_micro + 1):
        own_rows = cotangent[tick_index] if tick_index < n_micro else zero_rows
        grad_now = jnp.where(section_idx == 1, own_rows, returned)
        batch_index = jnp.clip(tick_index - 1 + section_idx, 0, n_micro - 1)
        early_saved = stored[max(tick_index - 1, 0)]
        late_saved = stored[min(tick_index + 1, n_micro)]
        saved = jax.tree.map(
            lambda early_val, late_val: jnp.where(section_idx == 0, early_val, late_val),
            early_saved,
            late_saved,
        )
        (
            input_bf,
            head_query,
            backward_head_keys,
            backward_head_values,
            attended,
            spread,
            mixed_tok,
            hidden_in,
            kept_rows,
            gate_pre,
            up_pre,
        ) = saved
        backward_place_row, backward_token_places, backward_span_places = place_sets(batch_index)
        values_in = input_bf.astype(jnp.float32)
        normed_one = scaled(values_in, gain_a).astype(jnp.bfloat16)
        grad_all = spread_rows(grad_now)
        ffn_terms, d_partial = ffn_back(
            grad_all, kept_rows, gate_pre, up_pre, wg_use, wu_use, wd_use
        )
        d_normed_two = fold_rows(d_partial)
        grad_gf, d_hidden = norm_back(hidden_in, gain_f, d_normed_two)
        d_hidden = d_hidden + grad_now.astype(jnp.float32)
        d_branch = d_hidden.astype(jnp.bfloat16)
        d_mixed = times_trans(d_branch, wo_full).astype(jnp.bfloat16)
        d_att = to_heads(d_mixed.reshape(per_device, n_seq, q_width))[:, 0].reshape(
            span_rows, local_heads, HEAD_DIM
        )
        offset = jnp.sum(d_att.astype(jnp.float32) * attended, -1).T

        def collect(state_in, key_piece, start_row):
            piece_keys, piece_values = key_piece
            visible = backward_place_row[None, None, :] <= backward_span_places[None, :, None]
            scores = (
                jnp.einsum(
                    "qhd,kd->hqk", head_query, piece_keys, preferred_element_type=jnp.float32
                )
                * attn_scale
            )
            probs = jnp.where(visible, jnp.exp(scores - spread[..., None]), 0.0)
            d_probs = jnp.einsum(
                "qhd,kd->hqk", d_att, piece_values, preferred_element_type=jnp.float32
            )
            d_score = (probs * (d_probs - offset[..., None]) * attn_scale).astype(jnp.bfloat16)
            d_query_acc = jnp.einsum(
                "hqk,kd->qhd", d_score, piece_keys, preferred_element_type=jnp.float32
            )
            key_part = jnp.einsum(
                "hqk,qhd->kd", d_score, head_query, preferred_element_type=jnp.float32
            )
            value_part = jnp.einsum(
                "hqk,qhd->kd", probs.astype(jnp.bfloat16), d_att, preferred_element_type=jnp.float32
            )
            return (d_query_acc, key_part, value_part)

        start_state = (
            jnp.zeros((span_rows, local_heads, HEAD_DIM), jnp.float32),
            jnp.zeros((total_len, HEAD_DIM), jnp.float32),
            jnp.zeros((total_len, HEAD_DIM), jnp.float32),
        )
        d_query_acc, d_keys_all, d_values_all = over_keys(
            backward_head_keys, backward_head_values, collect, start_state
        )
        own_keys = lax.psum_scatter(
            d_keys_all.astype(jnp.bfloat16), "shard", scatter_dimension=0, tiled=True
        ).astype(jnp.float32)
        own_values = lax.psum_scatter(
            d_values_all.astype(jnp.bfloat16), "shard", scatter_dimension=0, tiled=True
        ).astype(jnp.float32)
        d_query_head = rotate(d_query_acc, backward_span_places, -1.0).astype(jnp.bfloat16)
        d_query = to_tokens(d_query_head.reshape(span_rows, 1, q_width)).reshape(
            per_device, HEADS * HEAD_DIM
        )
        own_keys = rotate(own_keys[:, None, :], backward_span_places, -1.0)[:, 0]
        back_kv = lax.all_to_all(
            jnp.concatenate([own_keys, own_values], -1)[:, None, :].astype(jnp.bfloat16),
            "seq",
            split_axis=0,
            concat_axis=1,
            tiled=True,
        ).astype(jnp.float32)
        back_kv = jnp.sum(back_kv.reshape(per_device, KV_HEADS, kv_repeat, 2 * HEAD_DIM), 2)
        d_key = (
            back_kv[..., :HEAD_DIM].reshape(per_device, KV_HEADS * HEAD_DIM).astype(jnp.bfloat16)
        )
        d_value = (
            back_kv[..., HEAD_DIM:].reshape(per_device, KV_HEADS * HEAD_DIM).astype(jnp.bfloat16)
        )
        d_normed_one = (
            plain_dot(d_query, wq_full) + plain_dot(d_key, wk_full) + plain_dot(d_value, wv_full)
        )
        grad_ga, d_input = norm_back(values_in, gain_a, d_normed_one)
        d_input = d_input + d_hidden
        gain_terms = (grad_ga, grad_gf)
        row_terms = (d_query, d_key, d_value, normed_one, mixed_tok, d_branch)
        d_input, gain_terms, row_terms, ffn_terms = (
            d_input.astype(jnp.bfloat16),
            gain_terms,
            row_terms,
            ffn_terms,
        )
        grads_back.append(d_input)
        row_lists.append(row_terms)
        if tick_index < n_micro:
            returned = shifted(d_input, "section", -1)
        if gain_total is None:
            gain_total = gain_terms
            ffn_total = ffn_terms
        else:
            gain_total = jax.tree.map(jnp.add, gain_total, gain_terms)
            ffn_total = jax.tree.map(jnp.add, ffn_total, ffn_terms)
    joined = [
        jnp.concatenate([row_set[index_val] for row_set in row_lists], 0) for index_val in range(6)
    ]
    grad_wq = outer_sum(joined[0], joined[3])
    grad_wk = outer_sum(joined[1], joined[3])
    grad_wv = outer_sum(joined[2], joined[3])
    grad_wo = outer_sum(joined[4], joined[5])
    attn_owned = (
        lax.psum_scatter(gain_total[0], ("shard", "seq"), scatter_dimension=0, tiled=True),
        lax.psum_scatter(gain_total[1], ("shard", "seq"), scatter_dimension=0, tiled=True),
        lax.psum_scatter(grad_wq, ("shard", "seq"), scatter_dimension=0, tiled=True),
        lax.psum_scatter(grad_wk, ("shard", "seq"), scatter_dimension=0, tiled=True),
        lax.psum_scatter(grad_wv, ("shard", "seq"), scatter_dimension=0, tiled=True),
        lax.psum_scatter(grad_wo, ("shard", "seq"), scatter_dimension=0, tiled=True),
    )
    outputs = lax.dynamic_slice_in_dim(jnp.stack(results), section_idx, n_micro, 0)[None]
    input_grads = lax.dynamic_slice_in_dim(jnp.stack(grads_back), 1 - section_idx, n_micro, 0)[None]
    return (
        outputs,
        input_grads,
        attn_owned[0][None],
        attn_owned[2][None],
        attn_owned[3][None],
        attn_owned[4][None],
        attn_owned[5][None],
        attn_owned[1][None],
        ffn_total[0][None],
        ffn_total[1][None],
        ffn_total[2][None],
    )


LOW = jnp.bfloat16
FULL = jnp.float32
MESH = pl.DeviceIdType.MESH
RING = 4
CHIPS = 2 * RING
SPLIT = 2
PLACE = 128
ORDER = ((2, 1), (1, 1), (3, 1), (0, 1), (2, 0), (1, 0), (3, 0), (0, 0))
IN_VMEM = pl.BlockSpec(memory_space=pltpu.VMEM)
IN_HBM = pl.BlockSpec(memory_space=pltpu.HBM)


class Site:
    def __init__(self):
        self.section = lax.axis_index("section")
        self.z = lax.axis_index("shard")
        member = lax.axis_index("seq")
        self.y = lax.div(member, 2)
        self.core = lax.rem(member, 2)
        self.up = (self.section, lax.rem(self.z + 1, RING), member)
        self.down = (self.section, lax.rem(self.z + RING - 1, RING), member)
        self.across = (self.section, self.z, (1 - self.y) * 2 + self.core)
        self.sibling = (self.section, self.z, self.y * 2 + 1 - self.core)
        self.corner = (self.section, self.z, (1 - self.y) * 2 + 1 - self.core)
        self.opposite = (self.section, lax.rem(self.z + 2, RING), member)
        self.partner = (1 - self.section, self.z, member)
        self.member = member

    def chip(self, along_z, along_y):
        return lax.rem(self.z + along_z, RING) * 2 + lax.rem(self.y + along_y, 2)


class Links:
    def __init__(self, send, recv, site):
        self.send, self.recv, self.site = send, recv, site
        self.sent = []

    def copy(self, index, src, dst, device):
        return pltpu.make_async_remote_copy(
            src_ref=src,
            dst_ref=dst,
            send_sem=self.send.at[index],
            recv_sem=self.recv.at[index],
            device_id=device,
            device_id_type=MESH,
        )

    def go(self, index, src, dst, device):
        copy = self.copy(index, src, dst, device)
        copy.start()
        self.sent.append(copy)

    def got(self, index, where):
        self.copy(index, where, where, self.site.sibling).wait_recv()
        return where

    def close(self):
        for copy in self.sent:
            copy.wait_send()


def greet(site, corner, partner):
    barrier = pltpu.get_barrier_semaphore()
    devices = [site.up, site.down, site.across, site.sibling]
    devices += [site.corner] * (corner > 0) + [site.partner] * partner
    devices += [site.opposite] * (corner > 1)
    for device in devices:
        pl.semaphore_signal(barrier, inc=1, device_id=device, device_id_type=MESH)
    pl.semaphore_wait(barrier, len(devices))


SPREAD_SEMS = 7 * SPLIT + CHIPS
SMALL_SEMS = 11
FOLD_SEMS = 7 * SPLIT + CHIPS


def spread_steps(site, held, links, use, parts=SPLIT):
    size = held.shape[2] // parts
    other = 1 - site.core
    up, down, across, relay, y_below, y_above, y_far = (k * parts for k in range(7))
    shared = 7 * parts

    def piece(along, part):
        return held.at[site.chip(*along), site.core, pl.ds(part * size, size)]

    def block(along, core):
        return held.at[site.chip(*along), core]

    def go(index, where, device):
        links.go(index, where, where, device)

    def share(slot, along):
        go(shared + slot, block(along, site.core), site.sibling)

    def consume(slot, along):
        links.got(shared + slot, block(along, other))
        use(site.chip(*along))

    own, below, above, far = (0, 0), (3, 0), (1, 0), (2, 0)
    y_own, yb, ya, yf = (0, 1), (3, 1), (1, 1), (2, 1)
    for part in range(parts):
        go(up + part, piece(own, part), site.up)
        go(down + part, piece(own, part), site.down)
        go(across + part, piece(own, part), site.across)
    share(0, own)
    yield
    for part in range(parts):
        came = links.got(up + part, piece(below, part))
        if part % 2 == 0:
            go(relay + part, came, site.up)
        go(y_below + part, came, site.across)
        came = links.got(down + part, piece(above, part))
        if part % 2 == 1:
            go(relay + part, came, site.down)
        go(y_above + part, came, site.across)
    share(1, below)
    share(2, above)
    yield
    for part in range(parts):
        links.got(across + part, piece(y_own, part))
    share(3, y_own)
    for part in range(parts):
        go(y_far + part, links.got(relay + part, piece(far, part)), site.across)
    share(4, far)
    yield
    consume(0, own)
    consume(1, below)
    for part in range(parts):
        links.got(y_below + part, piece(yb, part))
        links.got(y_above + part, piece(ya, part))
    share(5, yb)
    share(6, ya)
    consume(2, above)
    consume(3, y_own)
    consume(4, far)
    for part in range(parts):
        links.got(y_far + part, piece(yf, part))
    share(7, yf)
    consume(5, yb)
    consume(6, ya)
    consume(7, yf)


def fold_steps(site, part_of, mine, pass_out, pass_in, stage, land, links, idle):
    rows = mine.shape[1]
    size = rows // SPLIT
    over, relay, up, down = CHIPS, CHIPS + 4 * SPLIT, CHIPS + 5 * SPLIT, CHIPS + 6 * SPLIT

    def came(index, where):
        return links.got(index, where)[...].astype(FULL)

    def compute(step):
        both = part_of(site.chip(*ORDER[step]))
        pass_out[step] = both[:rows].astype(LOW)
        links.go(step, pass_out.at[step], pass_in.at[step], site.sibling)
        mine[step] = both[rows:]

    def settle(step):
        mine[step] += came(step, pass_in.at[step])

    def send_over(step):
        stage[step] = (mine[step] + came(step, pass_in.at[step])).astype(LOW)
        for part in range(SPLIT):
            where = pl.ds(part * size, size)
            links.go(
                over + step * SPLIT + part,
                stage.at[step, where],
                land.at[step, where],
                site.across,
            )

    def pass_on(part):
        where = pl.ds(part * size, size)
        value = mine[4, where] + came(over + part, land.at[0, where])
        stage[4, where] = value.astype(LOW)
        device = site.up if part % 2 == 0 else site.down
        links.go(relay + part, stage.at[4, where], land.at[4, where], device)

    compute(0)
    compute(1)
    send_over(0)
    compute(2)
    send_over(1)
    compute(3)
    send_over(2)
    compute(4)
    send_over(3)
    compute(5)
    settle(4)
    compute(6)
    compute(7)
    idle(4)
    for part in range(SPLIT):
        pass_on(part)
    for step in (5, 6, 7):
        settle(step)
    idle(5)
    for part in range(SPLIT):
        where = pl.ds(part * size, size)
        for step, base, device in ((5, up, site.up), (6, down, site.down)):
            from_y = over + (step - 4) * SPLIT + part
            value = mine[step, where] + came(from_y, land.at[step - 4, where])
            if part % 2 == step - 5:
                value = value + came(relay + part, land.at[4, where])
            stage[step, where] = value.astype(LOW)
            links.go(base + part, stage.at[step, where], land.at[step, where], device)
    idle(6)
    sums = []
    for part in range(SPLIT):
        where = pl.ds(part * size, size)
        value = mine[7, where] + came(over + 3 * SPLIT + part, land.at[3, where])
        value = value + came(up + part, land.at[5, where])
        sums.append(value + came(down + part, land.at[6, where]))
    return jnp.concatenate(sums, 0)


class Cross:
    def __init__(self, site, groups, src, dst, ways, send, recv):
        self.links = Links(send, recv, site)
        self.site, self.groups, self.src, self.dst, self.ways = site, groups, src, dst, ways
        self.started = 0
        self.landed = set()

    def where(self, index, receives, action):
        layer = self.ways[index]
        if layer is None:
            action()
        else:
            pl.when((self.site.section == layer) == receives)(action)

    def copy(self, index):
        return self.links.copy(index, self.src[index], self.dst[index], self.site.partner)

    def send(self, index):
        self.where(index, False, self.copy(index).start)

    def start(self):
        if self.started < len(self.groups):
            for index in self.groups[self.started]:
                self.send(index)
            self.started += 1

    def wait(self, index):
        if index in self.landed:
            return
        self.landed.add(index)
        self.where(index, True, self.copy(index).wait_recv)
        if self.started and all(
            other in self.landed for other in self.groups[self.started - 1]
        ):
            self.start()

    def close(self):
        for index in range(len(self.dst)):
            self.wait(index)
        for index in range(len(self.dst)):
            self.where(index, False, self.copy(index).wait_send)


def side_steps(named, side, loads, made):
    tile = 512
    while loads:
        loads.pop().wait()
    for left_key, right_key, out_key in side:
        left = getattr(named, left_key)
        right = getattr(named, right_key)
        count = math.prod(left.shape[:-1])
        for start in range(0, right.shape[-1], tile):
            where = pl.ds(start, tile)
            value = outer_sum(
                left[...].reshape(count, left.shape[-1]),
                right[:, :, :, where].reshape(count, tile),
            ).astype(LOW)
            if out_key is None:
                query = named.g_query.shape[0]
                named.g_query[:, where] = value[:query]
                named.kv_mine[:, :, :, where] = value[query:].reshape(
                    *named.kv_mine.shape[:3], tile
                )
            else:
                getattr(named, out_key)[:, where] = value
            yield
        if out_key is None:
            made("g_query")
            site = named.site
            peers = (site.sibling, site.across, site.corner)
            links = Links(named.kv_send, named.kv_recv, site)
            for index, device in enumerate(peers):
                links.go(
                    index, named.kv_mine.at[:, device[2]], named.kv_came.at[index], device
                )
            yield
            yield
            total = named.kv_mine[:, site.member].astype(FULL)
            for index in range(len(peers)):
                total = total + links.got(index, named.kv_came.at[index])[...].astype(FULL)
            named.g_kv[...] = total.astype(LOW)
            made("g_kv")
            links.close()
        else:
            made(out_key)


class Weights:
    def __init__(self, site, plan, held, own, other, sems, cross):
        self.site, self.plan, self.cross, self.sems = site, plan, cross, sems
        self.held, self.own, self.other = held, own, other
        self.waits = {}
        for index, (_, _, _, crossed) in enumerate(plan):
            if crossed is None:
                self.start(index)

    def start(self, index):
        _, layer, start, _ = self.plan[index]
        rows = self.own[index].shape[0]
        target = self.held[index]
        target = target if start is None else target.at[pl.ds(start, rows)]
        from_own = pltpu.make_async_copy(self.own[index], target, self.sems.at[index])
        from_other = pltpu.make_async_copy(self.other[index], target, self.sems.at[index])
        pl.when(self.site.section == layer)(from_own.start)
        pl.when(self.site.section != layer)(from_other.start)
        self.waits[index] = from_own

    def settle(self, keys):
        todo = [index for index, item in enumerate(self.plan) if item[0] in keys]
        for index in todo:
            crossed = self.plan[index][3]
            if crossed is not None and index not in self.waits:
                self.cross.wait(crossed)
                self.start(index)
        for index in todo:
            if self.waits[index] is not None:
                self.waits[index].wait()
                self.waits[index] = None


def ring_kernel(spec, *refs):
    refs = list(refs)

    def take(count):
        taken = refs[:count]
        del refs[:count]
        return taken

    plan = spec.plan
    values = take(spec.n_in)
    own, other = take(len(plan)), take(len(plan))
    sources = take(spec.n_cross - len(spec.late_cross))
    load_from = take(spec.n_loads)
    take(spec.n_after)
    by_name = dict(zip(spec.names, values + refs))
    places = {key: by_name.pop((key,)) for key in spec.stored}
    named = types.SimpleNamespace(**by_name)
    site = Site()
    named.site = site
    greet(site, spec.peers, spec.n_cross > 0)
    cross = weights = None
    if spec.n_cross:
        targets = [getattr(named, key) for key in spec.crossed]
        sources += [getattr(named, key) for key in spec.late_cross]
        cross = Cross(
            site,
            spec.groups,
            sources,
            targets,
            spec.ways,
            named.cross_send,
            named.cross_recv,
        )
        for index, item in enumerate(plan):
            if item[3] is not None:
                own[index], other[index] = sources[item[3]], targets[item[3]]
    if plan:
        held = [getattr(named, item[0]) for item in plan]
        weights = Weights(site, plan, held, own, other, named.weight_sem, cross)
    loads = [
        pltpu.make_async_copy(source, getattr(named, key), named.load_sem.at[index])
        for index, (key, source) in enumerate(zip(spec.load_keys, load_from))
    ]
    for copy in loads:
        copy.start()
    if spec.before is not None:
        spec.before(named)
    if cross is not None:
        cross.start()

    storing = []

    def made(key):
        if key in places:
            copy = pltpu.make_async_copy(
                getattr(named, key),
                places.pop(key),
                named.stored_sem.at[spec.stored.index(key)],
            )
            copy.start()
            storing.append(copy)
        if key in spec.late_cross:
            cross.send(len(sources) - len(spec.late_cross) + spec.late_cross.index(key))

    working = side_steps(named, spec.side, loads, made)

    def idle(count):
        for _ in range(count if spec.side else 0):
            next(working, None)

    total = None
    if spec.fold is not None:
        links = Links(named.fold_send, named.fold_recv, site)
        weights.settle(spec.fold_keys)
        total = fold_steps(
            site,
            functools.partial(spec.fold, named),
            named.mine,
            named.pass_out,
            named.pass_in,
            named.stage,
            named.land,
            links,
            idle,
        )
    rows = spec.local(named, total)
    for key in spec.local_made:
        made(key)
    folding = None
    if spec.middle is not None:
        folding = spec.middle(named)
        next(folding)
    if spec.second is not None:
        for _ in working:
            pass
        links_second = Links(named.second_send, named.second_recv, site)
        total = fold_steps(
            site,
            functools.partial(spec.second[0], named),
            named.mine_b,
            named.pass_out_b,
            named.pass_in_b,
            named.stage_b,
            named.land_b,
            links_second,
            lambda count: next(folding, None),
        )
        spec.second[1](named, total)
        links_second.close()
        made("result_swap")
        for _ in folding:
            pass
    if spec.side:
        for _ in working:
            pass
    if spec.use is not None:
        held = named.held
        held[site.chip(0, 0), site.core] = rows
        kept, waiting = [], []
        named.ready = False

        def consume(chip):
            if spec.late and not named.ready:
                waiting.append(chip)
                return
            if plan:
                weights.settle(spec.use_keys)
            while loads:
                loads.pop().wait()
            block = held[chip]
            spec.use(named, chip, block.reshape(block.shape[0] * block.shape[1], block.shape[2]))
            source = named.normed if spec.normed else held
            copy = pltpu.make_async_copy(
                source.at[chip], named.rows_all.at[chip], named.keep_sem.at[len(kept)]
            )
            copy.start()
            kept.append(copy)

        links_on = Links(named.spread_send, named.spread_recv, site)
        spreading = spread_steps(site, held, links_on, consume)
        next(spreading)
        if spec.meanwhile is not None:
            spec.meanwhile(named, spreading)
        for _ in spreading:
            pass
        if spec.top:
            for index in spec.groups[0]:
                cross.wait(index)
            place = named.top_all.at[site.chip(0, 0), site.core]
            copy = pltpu.make_async_copy(named.top_rows, place, named.top_sem)
            copy.start()
            copy.wait()
            named.ready = True
            links_top = Links(named.top_send, named.top_recv, site)
            for _ in spread_steps(site, named.top_all, links_top, lambda chip: None):
                for _ in range(3):
                    if waiting:
                        consume(waiting.pop(0))
            links_top.close()
        named.ready = True
        for chip in waiting:
            consume(chip)
        for copy in kept:
            copy.wait()
        links_on.close()
    for key in list(places):
        made(key)
    if spec.after_all is not None:
        spec.after_all(named)
    if spec.fold is not None:
        links.close()
    if cross is not None:
        cross.close()
    for copy in storing:
        copy.wait()


def ring_call(
    name, ident, inputs, fold_weights, use_weights, outputs, local, fold=None, use=None,
    extra=None, after=(), before=None, meanwhile=None, peers=False, normed=False, cross=(),
    late=False, top=None, loads=None, side=(), late_cross=None, second=None, local_made=(), layer=None, two_way=(),
    to_second=(), stored=None, middle=None, after_all=None,
):
    per_device, width = inputs.pop("like").shape
    out_shape = [jax.ShapeDtypeStruct(*value) for value in outputs.values()]
    out_specs = [IN_VMEM] * len(out_shape)
    names = list(inputs) + list(outputs)
    scratch, plan, own_set, other_set = {}, [], [], []
    crossed = [key for group in cross for key in group]
    cross_set = [value for group in cross for value in group.values()]
    for key, parts in {**fold_weights, **use_weights}.items():
        start = 0
        for part in parts:
            place = start if len(parts) > 1 else None
            if len(part) == 2:
                index = crossed.index(part[0])
                own = other = cross_set[index]
            else:
                index = None
                own, other = part[:2]
            plan.append((key, part[-1], place, index))
            own_set.append(own)
            other_set.append(other)
            start += own.shape[0]
        scratch[key] = pltpu.VMEM((start, width), LOW)
    full = (per_device, width)
    late_cross = late_cross or {}
    stored = stored or {}
    extra = dict(extra or {})
    for key, value in stored.items():
        extra[key] = pltpu.VMEM(*value)
    known = dict(zip(names[len(inputs) :], out_shape), **extra)
    more = dict(extra)
    cross_shapes = cross_set + [known[key] for key in late_cross.values()]
    crossed += list(late_cross)
    for key, value in zip(crossed, cross_shapes):
        names.append(key)
        out_shape.append(jax.ShapeDtypeStruct(value.shape, value.dtype))
        out_specs.append(IN_HBM)
    if crossed:
        more.update(
            cross_send=pltpu.SemaphoreType.DMA((len(crossed),)),
            cross_recv=pltpu.SemaphoreType.DMA((len(crossed),)),
        )
    if loads:
        more.update(load_sem=pltpu.SemaphoreType.DMA((len(loads),)))
        for key, value in loads.items():
            scratch[key] = pltpu.VMEM(value.shape, value.dtype)
    if top is not None:
        names.append("top_all")
        out_shape.append(jax.ShapeDtypeStruct((CHIPS, 2, *full), LOW))
        out_specs.append(IN_HBM)
        more.update(
            top_sem=pltpu.SemaphoreType.DMA,
            top_send=pltpu.SemaphoreType.DMA((SPREAD_SEMS,)),
            top_recv=pltpu.SemaphoreType.DMA((SPREAD_SEMS,)),
        )
    if plan:
        more.update(weight_sem=pltpu.SemaphoreType.DMA((len(plan),)))
    if fold is not None:
        more.update(
            mine=pltpu.VMEM((CHIPS, *full), FULL),
            pass_out=pltpu.VMEM((CHIPS, *full), LOW),
            pass_in=pltpu.VMEM((CHIPS, *full), LOW),
            stage=pltpu.VMEM((CHIPS - 1, *full), LOW),
            land=pltpu.VMEM((CHIPS - 1, *full), LOW),
            fold_send=pltpu.SemaphoreType.DMA((FOLD_SEMS,)),
            fold_recv=pltpu.SemaphoreType.DMA((FOLD_SEMS,)),
        )
    if second is not None:
        more.update(
            mine_b=pltpu.VMEM((CHIPS, *full), FULL),
            pass_out_b=pltpu.VMEM((CHIPS, *full), LOW),
            pass_in_b=pltpu.VMEM((CHIPS, *full), LOW),
            stage_b=pltpu.VMEM((CHIPS - 1, *full), LOW),
            land_b=pltpu.VMEM((CHIPS - 1, *full), LOW),
            second_send=pltpu.SemaphoreType.DMA((FOLD_SEMS,)),
            second_recv=pltpu.SemaphoreType.DMA((FOLD_SEMS,)),
        )
    if stored:
        names += [(key,) for key in stored]
        out_shape += [jax.ShapeDtypeStruct(*value) for value in stored.values()]
        out_specs += [IN_HBM] * len(stored)
        more.update(stored_sem=pltpu.SemaphoreType.DMA((len(stored),)))
    if use is not None:
        names.append("rows_all")
        out_shape.append(jax.ShapeDtypeStruct((CHIPS, 2, *full), LOW))
        out_specs.append(IN_HBM)
        more.update(
            held=pltpu.VMEM((CHIPS, 2, *full), LOW),
            keep_sem=pltpu.SemaphoreType.DMA((CHIPS,)),
            spread_send=pltpu.SemaphoreType.DMA((SPREAD_SEMS,)),
            spread_recv=pltpu.SemaphoreType.DMA((SPREAD_SEMS,)),
        )
        if normed:
            more.update(normed=pltpu.VMEM((CHIPS, 2, *full), LOW))
    scratch.update(more)
    names += list(scratch)
    groups, at = [], 0
    for group in cross:
        groups.append(list(range(at, at + len(group))))
        at += len(group)
    sizes = [math.prod(value.shape) * value.dtype.itemsize for value in inputs.values()]
    sizes += [
        math.prod(value.shape) * jnp.dtype(value.dtype).itemsize
        for value, place in zip(out_shape, out_specs)
        if place is IN_VMEM
    ]
    sizes += [
        math.prod(value.shape) * jnp.dtype(value.dtype).itemsize
        for value in scratch.values()
        if isinstance(value, type(pltpu.VMEM((1,), LOW))) and len(value.shape) > 1
    ]
    spec = types.SimpleNamespace(
        names=names, plan=plan, n_in=len(inputs), n_cross=len(crossed), n_after=len(after),
        crossed=crossed, groups=groups, fold=fold, local=local, use=use, meanwhile=meanwhile,
        peers=peers, normed=normed, before=before, late=late, top=top is not None,
        stored=list(stored), middle=middle, after_all=after_all, side=side, ways=[None if key in two_way else 1 if key in to_second else layer for key in crossed], late_cross=list(late_cross.values()), second=second, local_made=local_made,
        n_loads=len(loads or {}), load_keys=list(loads or {}), fold_keys=list(fold_weights), use_keys=list(use_weights),
    )
    return pl.pallas_call(
        functools.partial(ring_kernel, spec),
        out_shape=out_shape,
        in_specs=[IN_VMEM] * len(inputs)
        + [IN_HBM] * (2 * len(plan) + len(cross_set) + len(loads or {}) + len(after)),
        out_specs=out_specs,
        scratch_shapes=list(scratch.values()),
        compiler_params=pltpu.CompilerParams(
            collective_id=ident,
            has_side_effects=True,
            vmem_limit_bytes=int(sum(sizes) * 1.1) + 5 * 2**20,
        ),
        cost_estimate=pl.CostEstimate(
            flops=2**35 * ((fold is not None) + (use is not None)),
            bytes_accessed=2**23,
            transcendentals=0,
        ),
        name=name,
    )(*inputs.values(), *own_set, *other_set, *cross_set, *(loads or {}).values(), *after)


def rows_of(ref, chip, site):
    return jnp.concatenate([ref[chip, 1 - site.core], ref[chip, site.core]], 0)


def fold_mixed(named, chip):
    return plain_dot(rows_of(named.mixed, chip, named.site), named.w_out[...])


def fold_act(named, chip):
    return plain_dot(rows_of(named.act, chip, named.site), named.w_down[...])


def fold_d_qkv(named, chip):
    return plain_dot(rows_of(named.d_qkv, chip, named.site), named.w_in[...])


def fold_d_act(named, chip):
    site = named.site
    return plain_dot(rows_of(named.d_gate, chip, site), named.w_gate[...]) + plain_dot(
        rows_of(named.d_up, chip, site), named.w_up[...]
    )


def use_qkv(named, chip, rows):
    named.qkv[chip] = times_trans(rows, named.w_in[...])


def put(ref, chip, value):
    ref[chip] = value.astype(LOW).reshape(ref.shape[1:])


def use_gate_up(named, chip, rows):
    gate_pre = times_trans(rows, named.w_gate[...])
    up_pre = times_trans(rows, named.w_up[...])
    sig = jax.nn.sigmoid(gate_pre)
    silu_val = gate_pre * sig
    put(named.act, chip, silu_val * up_pre)
    put(named.gate_slope, chip, up_pre * sig * (1.0 + gate_pre * (1.0 - sig)))
    put(named.up_slope, chip, silu_val)


def use_gate_up_back(named, chip, rows):
    gate_pre = times_trans(rows, named.w_gate[...])
    up_pre = times_trans(rows, named.w_up[...])
    sig = jax.nn.sigmoid(gate_pre)
    silu_val = gate_pre * sig
    put(named.act, chip, silu_val * up_pre)
    top = named.top_held[chip].reshape(rows.shape)
    d_act = times_trans(top, named.w_down[...])
    put(named.d_gate, chip, d_act * up_pre * sig * (1.0 + gate_pre * (1.0 - sig)))
    put(named.d_up, chip, d_act * silu_val)


def use_d_act(named, chip, rows):
    d_act = times_trans(rows, named.w_down[...])
    for out, slope in ((named.d_gate, named.gate_slope), (named.d_up, named.up_slope)):
        put(out, chip, d_act * slope[chip].astype(FULL).reshape(d_act.shape))


def use_d_mixed(named, chip, rows):
    named.d_mixed[chip] = times_trans(rows, named.w_out[...]).astype(LOW)


def local_start(named, total):
    return named.x_rows[...]


def gather_small(named):
    site = named.site
    links = Links(named.small_send, named.small_recv, site)
    links.go(0, named.gains_own, named.gains_x, site.partner)
    links.go(1, named.kv_own, named.kv_x, site.partner)
    links.got(0, named.gains_x)
    own, came = named.gains_own[...], named.gains_x[...]
    first = site.section == 0
    named.gains_all[site.z, site.member] = jnp.concatenate(
        [
            jnp.where(first, own, came)[:2],
            jnp.where(first, came, own)[:2],
            jnp.zeros((4, own.shape[1]), FULL),
        ],
        0,
    )
    peers = (site.sibling, site.across, site.corner)
    mine = named.gains_all.at[site.z, site.member]
    for index, device in enumerate(peers):
        links.go(2 + index, mine, mine, device)
    for index, device in enumerate(peers):
        links.got(2 + index, named.gains_all.at[site.z, device[2]])
    shard = named.gains_all.at[site.z]
    for index, device in enumerate((site.up, site.down, site.opposite)):
        links.go(5 + index, shard, shard, device)
    named.links_small = links


def gather_small_end(named, rows_spreading):
    site, links = named.site, named.links_small
    links.got(1, named.kv_x)
    named.kv_all[site.member, site.section] = named.kv_own[...]
    named.kv_all[site.member, 1 - site.section] = named.kv_x[...]
    mine = named.kv_all.at[site.member]
    peers = (site.sibling, site.across, site.corner)
    for index, device in enumerate(peers):
        links.go(8 + index, mine, mine, device)
    next(rows_spreading)
    for index, along_z in enumerate((RING - 1, 1, 2)):
        links.got(5 + index, named.gains_all.at[lax.rem(site.z + along_z, RING)])
    for index, device in enumerate(peers):
        links.got(8 + index, named.kv_all.at[device[2]])
    links.close()
    named.gain_row[...] = jnp.concatenate(
        [named.gains_all[shard, seq, :1] for shard in range(RING) for seq in range(RING)], 1
    )
    named.w_kv[...] = jnp.concatenate(
        [named.kv_all[:, 0, index].reshape(HEAD_DIM, named.w_kv.shape[1]) for index in range(2)],
        0,
    )


def use_first(named, chip, rows):
    normed = scaled(rows.astype(FULL), named.gain_row[...]).astype(LOW)
    named.normed[chip] = normed.reshape(named.normed.shape[1:])
    named.qkv[chip] = jnp.concatenate(
        [times_trans(normed, named.w_query[...]), times_trans(normed, named.w_kv[...])], 1
    )


def local_middle(named, total):
    hidden_in = named.x_rows[...].astype(FULL) + total
    named.hidden_in[...] = hidden_in
    return scaled(hidden_in, named.gain[...]).astype(LOW)


def local_next(named, total):
    result = (named.hidden_in[...] + total).astype(LOW)
    named.result[...] = result
    return scaled(result.astype(FULL), named.gain[...]).astype(LOW)


def local_last(named, total):
    result = (named.hidden_in[...] + total).astype(LOW)
    named.result[...] = result
    named.result_swap[...] = jnp.where(named.site.section == 0, result, named.result_first[...])


def local_top(named, total):
    return named.top_rows[...]


def norm_back_rows(values, gain_vec, grad_in):
    factor = lax.rsqrt(jnp.mean(values * values, -1, keepdims=True) + EPSILON)
    gain_grad = jnp.sum(grad_in * values * factor, 0, keepdims=True)
    mean_term = jnp.mean(grad_in * gain_vec * values, -1, keepdims=True)
    return (
        gain_grad,
        factor * gain_vec * grad_in - values * (factor * factor * factor) * mean_term,
    )


def local_branch(named, total):
    gain_grad, d_hidden = norm_back_rows(named.hidden_in[...], named.gain[...], total)
    d_hidden = d_hidden + named.top_rows[...].astype(FULL)
    named.gain_grad[...] = gain_grad
    named.d_hidden[...] = d_hidden
    return d_hidden.astype(LOW)


def local_input(named, total):
    gain_grad, d_input = norm_back_rows(
        named.x_rows[...].astype(FULL), named.gain[...], total
    )
    d_input = (d_input + named.d_hidden[...]).astype(LOW)
    named.gain_grad[...] = gain_grad
    named.d_input[...] = d_input
    return d_input


def local_input_last(named, total):
    d_input = local_input(named, total)
    named.input_swap[...] = jnp.where(
        named.site.section == 0, named.input_second[...], d_input
    )


def fold_gains(named):
    site = named.site
    links = Links(named.gain_send, named.gain_recv, site)
    own = jnp.concatenate(
        [named.gain_grad[...], named.gain_ffn_a[...], named.gain_attn_b[...],
         named.gain_ffn_b[...], jnp.zeros((4, named.gain_grad.shape[1]), FULL)],
        0,
    )
    width = named.gain_parts.shape[-1]
    for shard in range(RING):
        for seq in range(RING):
            start = (shard * RING + seq) * width
            named.gain_parts[seq, shard] = own[:, start : start + width]
    peers = (site.sibling, site.across, site.corner)
    for index, device in enumerate(peers):
        links.go(index, named.gain_parts.at[device[2]], named.gain_came.at[index], device)
    yield
    total = named.gain_parts[site.member]
    for index in range(3):
        total = total + links.got(index, named.gain_came.at[index])[...]
    named.gain_shards[...] = total
    for index, device in enumerate((site.up, site.down, site.opposite)):
        links.go(
            3 + index, named.gain_shards.at[device[1]], named.gain_last.at[index], device
        )
    yield
    total = named.gain_shards[site.z]
    for index in range(3):
        total = total + links.got(3 + index, named.gain_last.at[index])[...]
    named.gain_own[...] = total
    links.go(6, named.gain_own, named.gain_other, site.partner)
    yield
    total = named.gain_own[...] + links.got(6, named.gain_other)[...]
    named.gain_sums[...] = jnp.where(site.section == 0, total[:2], total[2:4])
    links.close()


def swap_halves(value):
    width = value.shape[1]
    half = HEAD_DIM // 2
    lane = lax.broadcasted_iota(jnp.int32, value.shape, 1)
    return jnp.where(
        lax.rem(lane, HEAD_DIM) < half,
        pltpu.roll(value, width - half, 1),
        pltpu.roll(value, half, 1),
    )


def stacked(pair):
    return jnp.concatenate([pair[:, :HEAD_DIM], pair[:, HEAD_DIM:]], 0)


def side_by_side(turned):
    return jnp.concatenate([turned[:, :PLACE], turned[:, PLACE:]], 0).T


def hide_later(scores, fill):
    last = scores[-PLACE:]
    key = lax.broadcasted_iota(jnp.int32, last.shape, 0)
    query = lax.rem(lax.broadcasted_iota(jnp.int32, last.shape, 1), PLACE)
    last = jnp.where(key <= query, last, fill)
    if scores.shape[0] == PLACE:
        return last
    return jnp.concatenate([scores[:-PLACE], last], 0)


def turn_of(turns, place):
    near, far = pl.ds(0, PLACE), pl.ds(PLACE + place, 1)
    cos_near, sin_near = turns[0, near], turns[1, near]
    cos_far, sin_far = turns[0, far], turns[1, far]
    cosine = cos_near * cos_far - sin_near * sin_far
    sine = sin_near * cos_far + cos_near * sin_far
    lane = lax.broadcasted_iota(jnp.int32, cosine.shape, 1)
    sine = jnp.where(lax.rem(lane, HEAD_DIM) < HEAD_DIM // 2, -sine, sine)
    keyed = lane < HEAD_DIM
    return (
        jnp.concatenate([cosine, jnp.where(keyed, cosine, 1.0)], 1),
        jnp.concatenate([sine, jnp.where(keyed, sine, 0.0)], 1),
    )


def attend_kernel(block_at, qkv, turns, mixed, turned, attended, spread, values_t):
    q_width = 2 * HEAD_DIM
    for place in range(CHIPS):
        at = pl.ds(place * PLACE, PLACE)
        value = qkv[block_at[place]]
        cosine, sine = turn_of(turns, place)
        value = value * cosine + swap_halves(value) * sine
        value = value.astype(LOW)
        scale = jnp.asarray(1.0 / math.sqrt(HEAD_DIM), LOW)
        turned[at, :q_width] = value[:, :q_width] * scale
        turned[at, q_width:] = value[:, q_width:]
        values_t[:, at] = value[:, q_width:].astype(FULL).T[HEAD_DIM:].astype(LOW)
    for place in range(CHIPS):
        at = pl.ds(place * PLACE, PLACE)
        keys = pl.ds(0, (place + 1) * PLACE)
        query = stacked(turned[at, :q_width])
        scores = times_trans(turned[keys, q_width : q_width + HEAD_DIM], query)
        scores = hide_later(scores, NEG_LARGE)
        top = jnp.max(scores, 0, keepdims=True)
        weight = jnp.exp(scores - top)
        total = jnp.sum(weight, 0, keepdims=True)
        out = plain_dot(values_t[:, keys], weight.astype(LOW)) / total
        out = side_by_side(out)
        attended[at] = out
        mixed[block_at[place]] = out.astype(LOW).reshape(mixed.shape[1:])
        spread[pl.ds(place, 1)] = top + jnp.log(total)


def attend_back_kernel(
    block_at, d_mixed, turns, turned, attended, spread, d_qkv, keys_t, d_query, d_key, d_value
):
    q_width = 2 * HEAD_DIM
    d_key[...] = jnp.zeros_like(d_key)
    d_value[...] = jnp.zeros_like(d_value)
    for place in range(CHIPS):
        at = pl.ds(place * PLACE, PLACE)
        keys_t[:, at] = turned[at, q_width:].astype(FULL).T[:HEAD_DIM].astype(LOW)
    for place in range(CHIPS):
        at = pl.ds(place * PLACE, PLACE)
        keys = pl.ds(0, (place + 1) * PLACE)
        d_out = d_mixed[block_at[place]]
        product = (d_out.astype(FULL) * attended[at]).T
        offset = jnp.concatenate(
            [
                jnp.sum(product[:HEAD_DIM], 0, keepdims=True),
                jnp.sum(product[HEAD_DIM:], 0, keepdims=True),
            ],
            1,
        )
        d_out = stacked(d_out)
        query = stacked(turned[at, :q_width])
        scores = times_trans(turned[keys, q_width : q_width + HEAD_DIM], query)
        scores = hide_later(scores, NEG_LARGE)
        probs = jnp.exp(scores - spread[pl.ds(place, 1)])
        d_probs = times_trans(turned[keys, q_width + HEAD_DIM :], d_out)
        d_scores = (probs * (d_probs - offset)).astype(LOW)
        d_key[keys] += plain_dot(d_scores, query)
        d_value[keys] += plain_dot(probs.astype(LOW), d_out)
        d_query[at] = side_by_side(plain_dot(keys_t[:, keys], d_scores)) * (
            1.0 / math.sqrt(HEAD_DIM)
        )
    for place in range(CHIPS):
        at = pl.ds(place * PLACE, PLACE)
        value = jnp.concatenate([d_query[at], d_key[at], d_value[at]], 1)
        cosine, sine = turn_of(turns, place)
        value = value * cosine - swap_halves(value) * sine
        d_qkv[block_at[place]] = value.astype(LOW).reshape(d_qkv.shape[1:])


def join_kernel(count, *refs):
    own, came = (refs[:count], refs[count : 2 * count]), (
        refs[2 * count : 3 * count],
        refs[3 * count : 4 * count],
    )
    outs, refs = refs[4 * count : 5 * count], refs[5 * count :]
    own_at, came_at, sums = refs[:count], refs[count : 2 * count], refs[2 * count : 3 * count]
    sems, out_sem = refs[3 * count :]
    section = lax.axis_index("section")
    waits = []
    for index in range(count):
        for slot, (pair, target) in enumerate(((own, own_at), (came, came_at))):
            copies = [
                pltpu.make_async_copy(
                    pair[layer][index], target[index], sems.at[2 * index + slot]
                )
                for layer in range(2)
            ]
            pl.when(section == 0)(copies[0].start)
            pl.when(section != 0)(copies[1].start)
            waits.append(copies[0])
    done = []
    for index in range(count):
        waits[2 * index].wait()
        waits[2 * index + 1].wait()
        sums[index][...] = own_at[index][...].astype(FULL) + came_at[index][...].astype(FULL)
        copy = pltpu.make_async_copy(sums[index], outs[index], out_sem.at[index])
        copy.start()
        done.append(copy)
    for copy in done:
        copy.wait()


def join_sums(own_a, own_b, came_a, came_b):
    count = len(own_a)
    kept = [pltpu.VMEM(value.shape, LOW) for value in own_a]
    return pl.pallas_call(
        functools.partial(join_kernel, count),
        out_shape=[jax.ShapeDtypeStruct(value.shape, FULL) for value in own_a],
        in_specs=[IN_HBM] * (4 * count),
        out_specs=[IN_HBM] * count,
        scratch_shapes=kept
        + kept
        + [pltpu.VMEM(value.shape, FULL) for value in own_a]
        + [pltpu.SemaphoreType.DMA((2 * count,)), pltpu.SemaphoreType.DMA((count,))],
        compiler_params=pltpu.CompilerParams(vmem_limit_bytes=40 * 2**20),
        cost_estimate=pl.CostEstimate(flops=2**32, bytes_accessed=2**24, transcendentals=0),
        name="join_sums",
    )(*own_a, *own_b, *came_a, *came_b)


def plain_call(kernel, name, count, out_shape, scratch):
    return pl.pallas_call(
        kernel,
        out_shape=out_shape,
        in_specs=[pl.BlockSpec(memory_space=pltpu.SMEM)] + [IN_VMEM] * (count - 1),
        out_specs=[IN_VMEM] * len(out_shape),
        scratch_shapes=scratch,
        compiler_params=pltpu.CompilerParams(vmem_limit_bytes=48 * 2**20),
        cost_estimate=pl.CostEstimate(flops=2**33, bytes_accessed=2**23, transcendentals=2**21),
        name=name,
    )


def relay_body(
    inputs,
    cotangent,
    positions,
    gain_attn,
    w_query,
    w_key,
    w_value,
    w_out,
    gain_ffn,
    w_gate,
    w_up,
    w_down,
):
    n_micro, per_device, model_width = inputs.shape
    n_seq = lax.axis_size("seq")
    n_shard = lax.axis_size("shard")
    members = n_seq * n_shard
    total_len = members * per_device
    section_idx = lax.axis_index("section")
    q_width = HEADS // members * HEAD_DIM
    in_width = q_width + 2 * HEAD_DIM
    hidden = w_down.shape[1]
    shape = jax.ShapeDtypeStruct

    def pick(first, second):
        return jnp.where(section_idx == 0, first, second)

    rows_in = pick(inputs[0], inputs[1])
    top_in = pick(cotangent[0], cotangent[1])
    places = pick(positions[0], positions[1])

    small = jnp.concatenate([gain_attn, gain_ffn], 0).astype(FULL)
    small = jnp.concatenate([small, jnp.zeros((6, small.shape[1]), FULL)], 0)
    kv_pair = jnp.stack([w_key[0], w_value[0]])

    def w_in_of(layer):
        return [(w_query[0], x_query, layer), (kv_all[layer], kv_all[layer], layer)]

    order = places.reshape(CHIPS, PLACE)[:, 0] // PLACE
    block_at = jnp.sum(
        jnp.where(
            order[None, :] == jnp.arange(CHIPS)[:, None], jnp.arange(CHIPS)[None, :], 0
        ),
        1,
    ).astype(jnp.int32)
    half_dim = HEAD_DIM // 2
    inv_freq = THETA_BASE ** (-jnp.arange(half_dim, dtype=FULL) * (2.0 / HEAD_DIM))
    steps = jnp.concatenate([jnp.arange(PLACE), PLACE * jnp.arange(CHIPS)]).astype(FULL)
    angles = steps[:, None] * jnp.tile(inv_freq, 2 * q_width // HEAD_DIM)[None, :]
    turns = jnp.stack([jnp.cos(angles), jnp.sin(angles)])

    narrow = (CHIPS, 2, per_device, hidden)
    chip_rows = 2 * per_device
    back_outs = dict(d_gate=(narrow, LOW), d_up=(narrow, LOW))
    qkv_out = dict(qkv=((CHIPS, chip_rows, in_width), FULL))
    row_low = ((per_device, model_width), LOW)
    row_full = ((per_device, model_width), FULL)
    gain_out = ((1, model_width), FULL)

    def flat(value):
        return value.reshape(total_len, value.shape[-1])

    def attend(qkv):
        mixed, *saved = plain_call(
            attend_kernel,
            "attend",
            3,
            [
                shape((CHIPS, 2, per_device, q_width), LOW),
                shape((total_len, in_width), LOW),
                shape((total_len, q_width), FULL),
                shape((CHIPS, 2 * PLACE), FULL),
            ],
            [pltpu.VMEM((HEAD_DIM, total_len), LOW)],
        )(block_at, qkv, turns)
        return mixed, saved

    def attend_back(saved, d_mixed):
        (d_qkv,) = plain_call(
            attend_back_kernel,
            "attend_back",
            6,
            [shape((CHIPS, 2, per_device, in_width), LOW)],
            [
                pltpu.VMEM((HEAD_DIM, total_len), LOW),
                pltpu.VMEM((total_len, q_width), FULL),
                pltpu.VMEM((total_len, HEAD_DIM), FULL),
                pltpu.VMEM((total_len, HEAD_DIM), FULL),
            ],
        )(block_at, d_mixed, turns, *saved)
        return d_qkv

    wide = ((hidden, model_width), LOW)
    kv_shape = (2, n_seq, w_key.shape[1], model_width)
    in_outs = dict(
        g_out=((q_width, model_width), LOW),
        g_query=((q_width, model_width), LOW),
        g_kv=((2, *kv_shape[2:]), LOW),
    )
    kv_extra = dict(
        kv_mine=pltpu.VMEM(kv_shape, LOW),
        kv_came=pltpu.VMEM((n_seq - 1, 2, *kv_shape[2:]), LOW),
        kv_send=pltpu.SemaphoreType.DMA((n_seq - 1,)),
        kv_recv=pltpu.SemaphoreType.DMA((n_seq - 1,)),
    )
    in_side = (("mixed", "branch_all", "g_out"), ("d_qkv", "normed_one", None))

    def middle_back(
        layer, d_gate, d_up, hidden_in, top_rows, more_in, loads, late_cross, cross=()
    ):
        return ring_call(
            "ffn_back_to_attn",
            2 + 7 * layer,
            dict(
                like=top_rows,
                d_gate=d_gate,
                d_up=d_up,
                hidden_in=hidden_in,
                top_rows=top_rows,
                gain=gains[layer, 1],
                **more_in,
            ),
            dict(w_gate=[(w_gate[0], x_gate, layer)], w_up=[(w_up[0], x_up, layer)]),
            dict(w_out=[(w_out[0], x_out, layer)]),
            dict(
                gain_grad=gain_out,
                d_hidden=row_full,
                d_mixed=((CHIPS, chip_rows, q_width), LOW),
            ),
            local_branch,
            stored=dict(g_down=wide, g_gate=wide, g_up=wide),
            fold=fold_d_act,
            use=use_d_mixed,
            loads=loads,
            side=(
                ("act", "top_all", "g_down"),
                ("d_gate", "normed_two", "g_gate"),
                ("d_up", "normed_two", "g_up"),
            ),
            late_cross=late_cross,
            cross=cross,
            layer=layer,
            to_second=("came_up_b",),
        )

    qkv, gains_all, kv_all, x_query, x_out, normed_one_a = ring_call(
        "first_rows",
        0,
        dict(like=rows_in, x_rows=rows_in, gains_own=small, kv_own=kv_pair),
        {},
        dict(w_query=[("x_query", 0)]),
        dict(
            **qkv_out,
            gains_all=((n_shard, n_seq, *small.shape), FULL),
            kv_all=((n_seq, 2, *kv_pair.shape), LOW),
        ),
        local_start,
        use=use_first,
        extra=dict(
            gain_row=pltpu.VMEM((1, model_width), FULL),
            w_kv=pltpu.VMEM((2 * HEAD_DIM, model_width), LOW),
            small_send=pltpu.SemaphoreType.DMA((SMALL_SEMS,)),
            small_recv=pltpu.SemaphoreType.DMA((SMALL_SEMS,)),
            gains_x=pltpu.VMEM(small.shape, FULL),
            kv_x=pltpu.VMEM(kv_pair.shape, LOW),
        ),
        normed=True,
        cross=[dict(x_query=w_query[0], x_out=w_out[0])],
        before=gather_small,
        meanwhile=gather_small_end,
        peers=2,
    )
    gains = gains_all.reshape(members, -1, gain_attn.shape[1])[:, :4]
    gains = gains.transpose(1, 0, 2).reshape(2, 2, 1, model_width)
    kv_all = kv_all.transpose(1, 2, 0, 3, 4).reshape(2, 2 * HEAD_DIM, model_width)
    mixed_a, saved_a = attend(qkv)
    hidden_a, act_a, x_gate, x_up, x_down, top_all_b, gate_slope_a, up_slope_a, normed_two_a = (
        ring_call(
            "attn_out_to_ffn",
            1,
            dict(
                like=rows_in, x_rows=rows_in, mixed=mixed_a, gain=gains[0, 1], top_rows=top_in
            ),
            dict(w_out=[(w_out[0], x_out, 0)]),
            dict(w_gate=[("x_gate", 0)], w_up=[("x_up", 0)]),
            dict(hidden_in=row_full, act=(narrow, LOW)),
            local_middle,
            fold=fold_mixed,
            use=use_gate_up,
            stored=dict(gate_slope=(narrow, LOW), up_slope=(narrow, LOW)),
            cross=[dict(x_gate=w_gate[0], x_up=w_up[0]), dict(x_down=w_down[0])],
            late=True,
            top=top_in,
        )
    )
    result_a, qkv, normed_one_b = ring_call(
        "ffn_to_next",
        3,
        dict(like=rows_in, act=act_a, hidden_in=hidden_a, gain=gains[1, 0]),
        dict(w_down=[(w_down[0], x_down, 0)]),
        dict(w_in=w_in_of(1)),
        dict(result=row_low, **qkv_out),
        local_next,
        fold=fold_act,
        use=use_qkv,
    )
    mixed_b, saved_b = attend(qkv)
    hidden_b, act_b, d_gate_b, d_up_b, normed_two_b = ring_call(
        "attn_out_to_ffn_and_back",
        5,
        dict(like=rows_in, x_rows=result_a, mixed=mixed_b, gain=gains[1, 1]),
        dict(w_out=[(w_out[0], x_out, 1)]),
        dict(
            w_gate=[(w_gate[0], x_gate, 1)],
            w_up=[(w_up[0], x_up, 1)],
            w_down=[(w_down[0], x_down, 1)],
        ),
        dict(hidden_in=row_full, act=(narrow, LOW), **back_outs),
        local_middle,
        fold=fold_mixed,
        use=use_gate_up_back,
        loads=dict(top_held=top_all_b),
    )

    (
        gain_ffn_b, d_hidden_b, d_mixed, came_down_b, own_down_b, own_gate_b, own_up_b,
        branch_all_b,
    ) = middle_back(
        1, d_gate_b, d_up_b, hidden_b, top_in, dict(act=act_b),
        dict(top_all=top_all_b, normed_two=normed_two_b),
        dict(came_down="g_down"),
    )
    d_qkv_b = attend_back(saved_b, d_mixed)
    (
        gain_attn_b, back_b, d_gate_a, d_up_a, came_gate_b, came_out_b, came_query_b,
        came_kv_b, own_out_b, own_query_b, own_kv_b, top_all_a,
    ) = ring_call(
        "attn_back_to_prev",
        6,
        dict(
            like=top_in,
            d_qkv=d_qkv_b,
            x_rows=result_a,
            d_hidden=d_hidden_b,
            gain=gains[1, 0],
        ),
        dict(w_in=w_in_of(1)),
        dict(w_down=[(w_down[0], x_down, 0)]),
        dict(gain_grad=gain_out, d_input=row_low, **back_outs),
        local_input,
        fold=fold_d_qkv,
        use=use_d_act,
        extra=kv_extra,
        peers=1,
        stored=in_outs,
        loads=dict(
            mixed=mixed_b,
            branch_all=branch_all_b,
            normed_one=normed_one_b,
            gate_slope=gate_slope_a,
            up_slope=up_slope_a,
        ),
        side=in_side,
        cross=[dict(came_gate=own_gate_b)],
        layer=1,
        late_cross=dict(came_out="g_out", came_query="g_query", came_kv="g_kv"),
    )
    (
        gain_ffn_a, d_hidden_a, d_mixed, came_up_b, came_down_a, came_gate_a, own_down_a,
        own_gate_a, own_up_a, branch_all_a,
    ) = middle_back(
        0, d_gate_a, d_up_a, hidden_a, back_b, {},
        dict(act=act_a, top_all=top_all_a, normed_two=normed_two_a),
        dict(came_down="g_down", came_gate="g_gate"),
        [dict(came_up_b=own_up_b)],
    )
    d_qkv_a = attend_back(saved_a, d_mixed)
    (
        _, back_a, result_b, gain_sums, came_up_a, came_out_a, came_query_a, came_kv_a,
        input_came, result_came, own_out_a, own_query_a, own_kv_a,
    ) = ring_call(
        "attn_back_last",
        7,
        dict(
            like=top_in,
            d_qkv=d_qkv_a,
            x_rows=rows_in,
            d_hidden=d_hidden_a,
            gain=gains[0, 0],
            act=act_b,
            hidden_in=hidden_b,
            result_first=result_a,
            input_second=back_b,
            gain_ffn_a=gain_ffn_a,
            gain_attn_b=gain_attn_b,
            gain_ffn_b=gain_ffn_b,
        ),
        dict(w_in=w_in_of(0), w_down=[(w_down[0], x_down, 1)]),
        {},
        dict(
            gain_grad=gain_out,
            d_input=row_low,
            result=row_low,
            gain_sums=((2, gain_attn.shape[1]), FULL),
        ),

        local_input_last,
        fold=fold_d_qkv,
        extra=dict(
            **kv_extra,
            input_swap=pltpu.VMEM(*row_low),
            result_swap=pltpu.VMEM(*row_low),
            gain_parts=pltpu.VMEM((n_seq, n_shard, *small.shape), FULL),
            gain_came=pltpu.VMEM((n_seq - 1, n_shard, *small.shape), FULL),
            gain_shards=pltpu.VMEM((n_shard, *small.shape), FULL),
            gain_last=pltpu.VMEM((n_shard - 1, *small.shape), FULL),
            gain_own=pltpu.VMEM(small.shape, FULL),
            gain_other=pltpu.VMEM(small.shape, FULL),
            gain_send=pltpu.SemaphoreType.DMA((7,)),
            gain_recv=pltpu.SemaphoreType.DMA((7,)),
        ),
        stored=in_outs,
        middle=fold_gains,
        peers=2,
        loads=dict(mixed=mixed_a, branch_all=branch_all_a, normed_one=normed_one_a),
        side=in_side,
        cross=[dict(came_up=own_up_a)],
        layer=0,
        two_way=("input_came", "result_came"),
        late_cross=dict(
            came_out="g_out",
            came_query="g_query",
            came_kv="g_kv",
            input_came="input_swap",
            result_came="result_swap",
        ),
        second=(fold_act, local_last),
        local_made=("input_swap",),
    )

    def joined(first, second, came):
        kept = pick(first, second)
        return pick(jnp.stack([kept, came]), jnp.stack([came, kept]))[None]

    outputs = joined(result_a, result_b, result_came)
    input_grads = joined(back_a, back_b, input_came)

    g_down, g_gate, g_up, g_out, g_query, g_kv = join_sums(
        (own_down_a, own_gate_a, own_up_a, own_out_a, own_query_a, own_kv_a),
        (own_down_b, own_gate_b, own_up_b, own_out_b, own_query_b, own_kv_b),
        (came_down_a, came_gate_a, came_up_a, came_out_a, came_query_a, came_kv_a),
        (came_down_b, came_gate_b, came_up_b, came_out_b, came_query_b, came_kv_b),
    )
    return (
        outputs,
        input_grads,
        gain_sums[:1],
        g_query[None],
        g_kv[:1],
        g_kv[1:],
        g_out[None],
        gain_sums[1:],
        g_gate[None],
        g_up[None],
        g_down[None],
    )


def fits_relay(mesh):
    shape = mesh.shape
    return shape["section"] == 2 and shape["shard"] == KV_HEADS == RING and shape["seq"] == 4


def solution(mesh):
    in_specs = (
        P(None, ("shard", "seq"), None),
        P(None, ("shard", "seq"), None),
        P(),
        P("section", ("shard", "seq")),
        P("section", ("shard", "seq"), None),
        P("section", ("shard", "seq"), None),
        P("section", ("shard", "seq"), None),
        P("section", ("shard", "seq"), None),
        P("section", ("shard", "seq")),
        P("section", ("shard", "seq"), None),
        P("section", ("shard", "seq"), None),
        P("section", ("shard", "seq"), None),
    )
    out_specs = (
        P("section", None, ("shard", "seq"), None),
        P("section", None, ("shard", "seq"), None),
        P("section", ("shard", "seq")),
        P("section", ("shard", "seq"), None),
        P("section", ("shard", "seq"), None),
        P("section", ("shard", "seq"), None),
        P("section", ("shard", "seq"), None),
        P("section", ("shard", "seq")),
        P("section", ("shard", "seq"), None),
        P("section", ("shard", "seq"), None),
        P("section", ("shard", "seq"), None),
    )
    chosen = relay_body if fits_relay(mesh) else body
    return jax.shard_map(chosen, mesh=mesh, in_specs=in_specs, out_specs=out_specs, check_vma=False)
```

```python
import functools
import math
import types

import jax
import jax.numpy as jnp
from jax import lax
from jax.experimental import pallas as pl
from jax.experimental.pallas import tpu as pltpu
from jax.sharding import PartitionSpec as P

HEADS = 32
KV_HEADS = 4
HEAD_DIM = 64


EPSILON = 1e-05
THETA_BASE = 10000.0
NEG_LARGE = -1e30


def shifted(value, axis, by):
    count = lax.axis_size(axis)
    pairs = [(i, i + by) for i in range(count) if 0 <= i + by < count]
    return lax.ppermute(value, axis, pairs)


def times_trans(left, right):
    return lax.dot_general(
        left, right, (((1,), (1,)), ((), ())), preferred_element_type=jnp.float32
    )


def outer_sum(left, right):
    return lax.dot_general(
        left, right, (((0,), (0,)), ((), ())), preferred_element_type=jnp.float32
    )


def plain_dot(left, right):
    return jnp.dot(left, right, preferred_element_type=jnp.float32)


def rotate(values, places, direction):
    half_dim = values.shape[-1] // 2
    inv_freq = THETA_BASE ** (-jnp.arange(half_dim, dtype=jnp.float32) * (2.0 / values.shape[-1]))
    angles = places.astype(jnp.float32)[:, None] * inv_freq[None, :]
    cosine = jnp.cos(angles)[:, None, :]
    sine_val = direction * jnp.sin(angles)[:, None, :]
    first = values[..., :half_dim]
    second = values[..., half_dim:]
    return jnp.concatenate(
        [first * cosine - second * sine_val, second * cosine + first * sine_val], -1
    )


def scaled(values, gain_vec):
    factor = lax.rsqrt(jnp.mean(values * values, -1, keepdims=True) + EPSILON)
    return values * factor * gain_vec


def norm_back(values, gain_vec, grad_in):
    factor = lax.rsqrt(jnp.mean(values * values, -1, keepdims=True) + EPSILON)
    gain_grad = jnp.sum(grad_in * values * factor, 0)
    mean_term = jnp.mean(grad_in * gain_vec * values, -1, keepdims=True)
    return (
        gain_grad,
        factor * gain_vec * grad_in - values * (factor * factor * factor) * mean_term,
    )


def ffn_back(grad_rows, kept_rows, gate_pre, up_pre, wg_part, wu_part, wd_part):
    sigmoid_val = jax.nn.sigmoid(gate_pre)
    silu_val = gate_pre * sigmoid_val
    hidden_act = (silu_val * up_pre).astype(jnp.bfloat16)
    grad_down = outer_sum(hidden_act, grad_rows)
    d_act = times_trans(grad_rows, wd_part)
    d_gate = (d_act * up_pre * sigmoid_val * (1.0 + gate_pre * (1.0 - sigmoid_val))).astype(
        jnp.bfloat16
    )
    d_up = (d_act * silu_val).astype(jnp.bfloat16)
    grad_gate = outer_sum(d_gate, kept_rows)
    grad_up = outer_sum(d_up, kept_rows)
    d_normed = plain_dot(d_gate, wg_part) + plain_dot(d_up, wu_part)
    return ((grad_gate, grad_up, grad_down), d_normed)


def body(
    inputs,
    cotangent,
    positions,
    gain_attn,
    w_query,
    w_key,
    w_value,
    w_out,
    gain_ffn,
    w_gate,
    w_up,
    w_down,
):
    n_micro, per_device, model_width = inputs.shape
    n_seq = lax.axis_size("seq")
    n_shard = lax.axis_size("shard")
    section_idx = lax.axis_index("section")
    shard_pos = lax.axis_index("shard")
    member = shard_pos * n_seq + lax.axis_index("seq")
    span_rows = per_device * n_seq
    total_len = span_rows * n_shard
    local_heads = HEADS // n_seq
    kv_repeat = n_seq // KV_HEADS
    q_width = local_heads * HEAD_DIM
    attn_scale = 1.0 / math.sqrt(HEAD_DIM)
    gain_one, gain_two, wq_full, wk_full, wv_full, wo_full = (
        lax.all_gather(gain_attn[0], ("shard", "seq"), axis=0, tiled=True),
        lax.all_gather(gain_ffn[0], ("shard", "seq"), axis=0, tiled=True),
        lax.all_gather(w_query[0], ("shard", "seq"), axis=0, tiled=True),
        lax.all_gather(w_key[0], ("shard", "seq"), axis=0, tiled=True),
        lax.all_gather(w_value[0], ("shard", "seq"), axis=0, tiled=True),
        lax.all_gather(w_out[0], ("shard", "seq"), axis=0, tiled=True),
    )
    gain_a = gain_one.astype(jnp.float32)
    gain_f = gain_two.astype(jnp.float32)
    wg_use, wu_use, wd_use = (w_gate[0], w_up[0], w_down[0])

    def spread_rows(block_in):
        return lax.all_gather(block_in, ("shard", "seq"), axis=0, tiled=True)

    def fold_rows(block_in):
        return lax.psum_scatter(block_in, ("shard", "seq"), scatter_dimension=0, tiled=True)

    def to_heads(block_in):
        return lax.all_to_all(block_in, "seq", split_axis=1, concat_axis=0, tiled=True)

    def to_tokens(block_in):
        return lax.all_to_all(block_in, "seq", split_axis=0, concat_axis=1, tiled=True)

    def over_keys(head_keys, head_values, step_fn, init_state):
        return step_fn(
            init_state,
            (
                lax.all_gather(head_keys, "shard", axis=0, tiled=True),
                lax.all_gather(head_values, "shard", axis=0, tiled=True),
            ),
            jnp.int32(0),
        )

    def place_sets(batch_index):
        place_row = lax.dynamic_index_in_dim(positions, batch_index, 0, keepdims=False)
        token_places = lax.dynamic_slice_in_dim(place_row, member * per_device, per_device)
        span_places = lax.dynamic_slice_in_dim(place_row, shard_pos * span_rows, span_rows)
        return (place_row, token_places, span_places)

    zero_rows = jnp.zeros((per_device, model_width), jnp.bfloat16)
    arrived_x = zero_rows
    results = []
    stored = []
    for tick_index in range(n_micro + 1):
        own_rows = inputs[tick_index] if tick_index < n_micro else zero_rows
        input_now = jnp.where(section_idx == 0, own_rows, arrived_x)
        batch_index = jnp.clip(tick_index - section_idx, 0, n_micro - 1)
        forward_place_row, forward_token_places, forward_span_places = place_sets(batch_index)
        forward_values_in = input_now.astype(jnp.float32)
        forward_normed_one = scaled(forward_values_in, gain_a).astype(jnp.bfloat16)
        queries = rotate(
            times_trans(forward_normed_one, wq_full).reshape(per_device, HEADS, HEAD_DIM),
            forward_token_places,
            1.0,
        ).astype(jnp.bfloat16)
        key_rows = rotate(
            times_trans(forward_normed_one, wk_full).reshape(per_device, KV_HEADS, HEAD_DIM),
            forward_token_places,
            1.0,
        ).astype(jnp.bfloat16)
        value_rows = (
            times_trans(forward_normed_one, wv_full)
            .reshape(per_device, KV_HEADS, HEAD_DIM)
            .astype(jnp.bfloat16)
        )
        key_rows = jnp.repeat(key_rows, kv_repeat, axis=1)
        value_rows = jnp.repeat(value_rows, kv_repeat, axis=1)
        packed = jnp.concatenate(
            [queries.reshape(per_device, n_seq, q_width), key_rows, value_rows], -1
        )
        arrived = to_heads(packed)[:, 0]
        forward_head_query = arrived[:, :q_width].reshape(span_rows, local_heads, HEAD_DIM)
        forward_head_keys = arrived[:, q_width : q_width + HEAD_DIM]
        forward_head_values = arrived[:, q_width + HEAD_DIM :]

        def absorb(state_in, key_piece, start_row):
            run_max, run_total, run_acc = state_in
            piece_keys, piece_values = key_piece
            visible = forward_place_row[None, None, :] <= forward_span_places[None, :, None]
            scores = (
                jnp.einsum(
                    "qhd,kd->hqk",
                    forward_head_query,
                    piece_keys,
                    preferred_element_type=jnp.float32,
                )
                * attn_scale
            )
            scores = jnp.where(visible, scores, NEG_LARGE)
            new_max = jnp.maximum(run_max, jnp.max(scores, -1))
            weight = jnp.where(visible, jnp.exp(scores - new_max[..., None]), 0.0)
            rescale = jnp.exp(run_max - new_max)
            run_total = jnp.sum(weight, -1)
            run_acc = run_acc * rescale.T[..., None] + jnp.einsum(
                "hqk,kd->qhd",
                weight.astype(jnp.bfloat16),
                piece_values,
                preferred_element_type=jnp.float32,
            )
            return (new_max, run_total, run_acc)

        forward_start_state = (
            jnp.full((local_heads, span_rows), NEG_LARGE, jnp.float32),
            jnp.zeros((local_heads, span_rows), jnp.float32),
            jnp.zeros((span_rows, local_heads, HEAD_DIM), jnp.float32),
        )
        run_max, run_total, run_acc = over_keys(
            forward_head_keys, forward_head_values, absorb, forward_start_state
        )
        forward_attended = run_acc / run_total.T[..., None]
        forward_spread = run_max + jnp.log(run_total)
        forward_mixed_tok = to_tokens(
            forward_attended.astype(jnp.bfloat16).reshape(span_rows, 1, q_width)
        ).reshape(per_device, HEADS * HEAD_DIM)
        forward_hidden_in = forward_values_in + plain_dot(forward_mixed_tok, wo_full)
        normed_two = scaled(forward_hidden_in, gain_f).astype(jnp.bfloat16)
        forward_kept_rows = spread_rows(normed_two)
        forward_gate_pre = times_trans(forward_kept_rows, wg_use)
        forward_up_pre = times_trans(forward_kept_rows, wu_use)
        hidden_act = (jax.nn.silu(forward_gate_pre) * forward_up_pre).astype(jnp.bfloat16)
        branch = fold_rows(plain_dot(hidden_act, wd_use))
        result = (forward_hidden_in + branch).astype(jnp.bfloat16)
        forward_saved = (
            input_now,
            forward_head_query,
            forward_head_keys,
            forward_head_values,
            forward_attended,
            forward_spread,
            forward_mixed_tok,
            forward_hidden_in,
            forward_kept_rows,
            forward_gate_pre,
            forward_up_pre,
        )
        result, saved = (result, forward_saved)
        results.append(result)
        stored.append(saved)
        if tick_index < n_micro:
            arrived_x = shifted(result, "section", 1)
    returned = zero_rows
    grads_back = []
    row_lists = []
    gain_total = None
    ffn_total = None
    for tick_index in range(n_micro + 1):
        own_rows = cotangent[tick_index] if tick_index < n_micro else zero_rows
        grad_now = jnp.where(section_idx == 1, own_rows, returned)
        batch_index = jnp.clip(tick_index - 1 + section_idx, 0, n_micro - 1)
        early_saved = stored[max(tick_index - 1, 0)]
        late_saved = stored[min(tick_index + 1, n_micro)]
        saved = jax.tree.map(
            lambda early_val, late_val: jnp.where(section_idx == 0, early_val, late_val),
            early_saved,
            late_saved,
        )
        (
            input_bf,
            head_query,
            backward_head_keys,
            backward_head_values,
            attended,
            spread,
            mixed_tok,
            hidden_in,
            kept_rows,
            gate_pre,
            up_pre,
        ) = saved
        backward_place_row, backward_token_places, backward_span_places = place_sets(batch_index)
        values_in = input_bf.astype(jnp.float32)
        normed_one = scaled(values_in, gain_a).astype(jnp.bfloat16)
        grad_all = spread_rows(grad_now)
        ffn_terms, d_partial = ffn_back(
            grad_all, kept_rows, gate_pre, up_pre, wg_use, wu_use, wd_use
        )
        d_normed_two = fold_rows(d_partial)
        grad_gf, d_hidden = norm_back(hidden_in, gain_f, d_normed_two)
        d_hidden = d_hidden + grad_now.astype(jnp.float32)
        d_branch = d_hidden.astype(jnp.bfloat16)
        d_mixed = times_trans(d_branch, wo_full).astype(jnp.bfloat16)
        d_att = to_heads(d_mixed.reshape(per_device, n_seq, q_width))[:, 0].reshape(
            span_rows, local_heads, HEAD_DIM
        )
        offset = jnp.sum(d_att.astype(jnp.float32) * attended, -1).T

        def collect(state_in, key_piece, start_row):
            piece_keys, piece_values = key_piece
            visible = backward_place_row[None, None, :] <= backward_span_places[None, :, None]
            scores = (
                jnp.einsum(
                    "qhd,kd->hqk", head_query, piece_keys, preferred_element_type=jnp.float32
                )
                * attn_scale
            )
            probs = jnp.where(visible, jnp.exp(scores - spread[..., None]), 0.0)
            d_probs = jnp.einsum(
                "qhd,kd->hqk", d_att, piece_values, preferred_element_type=jnp.float32
            )
            d_score = (probs * (d_probs - offset[..., None]) * attn_scale).astype(jnp.bfloat16)
            d_query_acc = jnp.einsum(
                "hqk,kd->qhd", d_score, piece_keys, preferred_element_type=jnp.float32
            )
            key_part = jnp.einsum(
                "hqk,qhd->kd", d_score, head_query, preferred_element_type=jnp.float32
            )
            value_part = jnp.einsum(
                "hqk,qhd->kd", probs.astype(jnp.bfloat16), d_att, preferred_element_type=jnp.float32
            )
            return (d_query_acc, key_part, value_part)

        start_state = (
            jnp.zeros((span_rows, local_heads, HEAD_DIM), jnp.float32),
            jnp.zeros((total_len, HEAD_DIM), jnp.float32),
            jnp.zeros((total_len, HEAD_DIM), jnp.float32),
        )
        d_query_acc, d_keys_all, d_values_all = over_keys(
            backward_head_keys, backward_head_values, collect, start_state
        )
        own_keys = lax.psum_scatter(
            d_keys_all.astype(jnp.bfloat16), "shard", scatter_dimension=0, tiled=True
        ).astype(jnp.float32)
        own_values = lax.psum_scatter(
            d_values_all.astype(jnp.bfloat16), "shard", scatter_dimension=0, tiled=True
        ).astype(jnp.float32)
        d_query_head = rotate(d_query_acc, backward_span_places, -1.0).astype(jnp.bfloat16)
        d_query = to_tokens(d_query_head.reshape(span_rows, 1, q_width)).reshape(
            per_device, HEADS * HEAD_DIM
        )
        own_keys = rotate(own_keys[:, None, :], backward_span_places, -1.0)[:, 0]
        back_kv = lax.all_to_all(
            jnp.concatenate([own_keys, own_values], -1)[:, None, :].astype(jnp.bfloat16),
            "seq",
            split_axis=0,
            concat_axis=1,
            tiled=True,
        ).astype(jnp.float32)
        back_kv = jnp.sum(back_kv.reshape(per_device, KV_HEADS, kv_repeat, 2 * HEAD_DIM), 2)
        d_key = (
            back_kv[..., :HEAD_DIM].reshape(per_device, KV_HEADS * HEAD_DIM).astype(jnp.bfloat16)
        )
        d_value = (
            back_kv[..., HEAD_DIM:].reshape(per_device, KV_HEADS * HEAD_DIM).astype(jnp.bfloat16)
        )
        d_normed_one = (
            plain_dot(d_query, wq_full) + plain_dot(d_key, wk_full) + plain_dot(d_value, wv_full)
        )
        grad_ga, d_input = norm_back(values_in, gain_a, d_normed_one)
        d_input = d_input + d_hidden
        gain_terms = (grad_ga, grad_gf)
        row_terms = (d_query, d_key, d_value, normed_one, mixed_tok, d_branch)
        d_input, gain_terms, row_terms, ffn_terms = (
            d_input.astype(jnp.bfloat16),
            gain_terms,
            row_terms,
            ffn_terms,
        )
        grads_back.append(d_input)
        row_lists.append(row_terms)
        if tick_index < n_micro:
            returned = shifted(d_input, "section", -1)
        if gain_total is None:
            gain_total = gain_terms
            ffn_total = ffn_terms
        else:
            gain_total = jax.tree.map(jnp.add, gain_total, gain_terms)
            ffn_total = jax.tree.map(jnp.add, ffn_total, ffn_terms)
    joined = [
        jnp.concatenate([row_set[index_val] for row_set in row_lists], 0) for index_val in range(6)
    ]
    grad_wq = outer_sum(joined[0], joined[3])
    grad_wk = outer_sum(joined[1], joined[3])
    grad_wv = outer_sum(joined[2], joined[3])
    grad_wo = outer_sum(joined[4], joined[5])
    attn_owned = (
        lax.psum_scatter(gain_total[0], ("shard", "seq"), scatter_dimension=0, tiled=True),
        lax.psum_scatter(gain_total[1], ("shard", "seq"), scatter_dimension=0, tiled=True),
        lax.psum_scatter(grad_wq, ("shard", "seq"), scatter_dimension=0, tiled=True),
        lax.psum_scatter(grad_wk, ("shard", "seq"), scatter_dimension=0, tiled=True),
        lax.psum_scatter(grad_wv, ("shard", "seq"), scatter_dimension=0, tiled=True),
        lax.psum_scatter(grad_wo, ("shard", "seq"), scatter_dimension=0, tiled=True),
    )
    outputs = lax.dynamic_slice_in_dim(jnp.stack(results), section_idx, n_micro, 0)[None]
    input_grads = lax.dynamic_slice_in_dim(jnp.stack(grads_back), 1 - section_idx, n_micro, 0)[None]
    return (
        outputs,
        input_grads,
        attn_owned[0][None],
        attn_owned[2][None],
        attn_owned[3][None],
        attn_owned[4][None],
        attn_owned[5][None],
        attn_owned[1][None],
        ffn_total[0][None],
        ffn_total[1][None],
        ffn_total[2][None],
    )


LOW = jnp.bfloat16
FULL = jnp.float32
MESH = pl.DeviceIdType.MESH
RING = 4
CHIPS = 2 * RING
SPLIT = 2
PLACE = 128
ORDER = ((2, 1), (1, 1), (3, 1), (0, 1), (2, 0), (1, 0), (3, 0), (0, 0))
IN_VMEM = pl.BlockSpec(memory_space=pltpu.VMEM)
IN_HBM = pl.BlockSpec(memory_space=pltpu.HBM)
IN_SMEM = pl.BlockSpec(memory_space=pltpu.SMEM)


class Site:
    def __init__(self):
        self.section = lax.axis_index("section")
        self.z = lax.axis_index("shard")
        member = lax.axis_index("seq")
        self.y = lax.div(member, 2)
        self.core = lax.rem(member, 2)
        self.up = (self.section, lax.rem(self.z + 1, RING), member)
        self.down = (self.section, lax.rem(self.z + RING - 1, RING), member)
        self.across = (self.section, self.z, (1 - self.y) * 2 + self.core)
        self.sibling = (self.section, self.z, self.y * 2 + 1 - self.core)
        self.corner = (self.section, self.z, (1 - self.y) * 2 + 1 - self.core)
        self.opposite = (self.section, lax.rem(self.z + 2, RING), member)
        self.partner = (1 - self.section, self.z, member)
        self.member = member

    def chip(self, along_z, along_y):
        return lax.rem(self.z + along_z, RING) * 2 + lax.rem(self.y + along_y, 2)


class Links:
    def __init__(self, send, recv, site):
        self.send, self.recv, self.site = send, recv, site
        self.sent = []

    def copy(self, index, src, dst, device):
        return pltpu.make_async_remote_copy(
            src_ref=src,
            dst_ref=dst,
            send_sem=self.send.at[index],
            recv_sem=self.recv.at[index],
            device_id=device,
            device_id_type=MESH,
        )

    def go(self, index, src, dst, device):
        copy = self.copy(index, src, dst, device)
        copy.start()
        self.sent.append(copy)

    def got(self, index, where):
        self.copy(index, where, where, self.site.sibling).wait_recv()
        return where

    def close(self):
        for copy in self.sent:
            copy.wait_send()


def greet(site):
    barrier = pltpu.get_barrier_semaphore()
    devices = (
        site.up, site.down, site.across, site.sibling, site.corner, site.opposite, site.partner
    )
    for device in devices:
        pl.semaphore_signal(barrier, inc=1, device_id=device, device_id_type=MESH)
    pl.semaphore_wait(barrier, len(devices))


SPREAD_SEMS = 7 * SPLIT + CHIPS
FOLD_SEMS = 7 * SPLIT + CHIPS
SMALL_SEMS = 11
COPY_SEMS = 48
CROSS_SEMS = 10


class Spread:
    def __init__(self, site, held, links, use):
        self.site, self.held, self.links, self.use = site, held, links, use
        self.size = held.shape[2] // SPLIT
        self.up, self.down, self.over, self.relay, self.y_below, self.y_above, self.y_far = (
            k * SPLIT for k in range(7)
        )
        self.along = ((0, 0), (3, 0), (1, 0), (0, 1), (2, 0), (3, 1), (1, 1), (2, 1))

    def piece(self, slot, part):
        site = self.site
        rows = pl.ds(part * self.size, self.size)
        return self.held.at[site.chip(*self.along[slot]), site.core, rows]

    def block(self, slot, core):
        return self.held.at[self.site.chip(*self.along[slot]), core]

    def go(self, index, where, device):
        self.links.go(index, where, where, device)

    def share(self, slot):
        self.go(7 * SPLIT + slot, self.block(slot, self.site.core), self.site.sibling)

    def consume(self, *slots):
        for slot in slots:
            self.links.got(7 * SPLIT + slot, self.block(slot, 1 - self.site.core))
            self.use(self.site.chip(*self.along[slot]))

    def own(self, part):
        where = self.piece(0, part)
        self.go(self.up + part, where, self.site.up)
        self.go(self.down + part, where, self.site.down)
        self.go(self.over + part, where, self.site.across)

    def relays(self, part):
        came = self.links.got(self.up + part, self.piece(1, part))
        if part % 2 == 0:
            self.go(self.relay + part, came, self.site.up)
        self.go(self.y_below + part, came, self.site.across)
        came = self.links.got(self.down + part, self.piece(2, part))
        if part % 2 == 1:
            self.go(self.relay + part, came, self.site.down)
        self.go(self.y_above + part, came, self.site.across)

    def far(self, part):
        came = self.links.got(self.relay + part, self.piece(4, part))
        self.go(self.y_far + part, came, self.site.across)

    def after_relays(self):
        self.share(1)
        self.share(2)
        for part in range(SPLIT):
            self.links.got(self.over + part, self.piece(3, part))
        self.share(3)

    def tail(self, consume=True):
        def take(*slots):
            if consume:
                self.consume(*slots)

        self.share(4)
        take(0, 1)
        for part in range(SPLIT):
            self.links.got(self.y_below + part, self.piece(5, part))
            self.links.got(self.y_above + part, self.piece(6, part))
        self.share(5)
        self.share(6)
        take(2, 3, 4)
        for part in range(SPLIT):
            self.links.got(self.y_far + part, self.piece(7, part))
        self.share(7)
        take(5, 6, 7)
        if not consume:
            for slot in range(CHIPS):
                self.links.got(7 * SPLIT + slot, self.block(slot, 1 - self.site.core))

    def rest(self, consume=True):
        self.after_relays()
        for part in range(SPLIT):
            self.far(part)
        self.tail(consume)


class Fold:
    def __init__(self, site, part_of, buffers, links):
        self.site, self.part_of, self.links = site, part_of, links
        self.mine, self.pass_out, self.pass_in, self.stage, self.land = buffers
        self.rows = self.mine.shape[1]
        self.size = self.rows // SPLIT
        self.over = CHIPS
        self.relay, self.up, self.down = (CHIPS + (4 + k) * SPLIT for k in range(3))

    def where(self, part):
        return pl.ds(part * self.size, self.size)

    def came(self, index, where):
        return self.links.got(index, where)[...].astype(FULL)

    def compute(self, step):
        both = self.part_of(self.site.chip(*ORDER[step]))
        self.pass_out[step] = both[: self.rows].astype(LOW)
        self.links.go(step, self.pass_out.at[step], self.pass_in.at[step], self.site.sibling)
        self.mine[step] = both[self.rows :]

    def settle(self, step):
        self.mine[step] += self.came(step, self.pass_in.at[step])

    def send(self, index, slot, part, value, device):
        where = self.where(part)
        self.stage[slot, where] = value.astype(LOW)
        self.links.go(index, self.stage.at[slot, where], self.land.at[slot, where], device)

    def send_over(self, step, part):
        value = self.mine[step, self.where(part)]
        self.send(self.over + step * SPLIT + part, step, part, value, self.site.across)

    def start(self):
        self.compute(0)
        self.compute(1)
        for step in range(4):
            self.settle(step)
            self.send_over(step, 0)
            self.compute(step + 2)
        for step in range(4):
            self.send_over(step, 1)
        self.compute(6)
        self.compute(7)
        for step in range(4, CHIPS):
            self.settle(step)

    def pass_on(self, part):
        where = self.where(part)
        value = self.mine[4, where] + self.came(self.over + part, self.land.at[0, where])
        device = self.site.up if part % 2 == 0 else self.site.down
        self.send(self.relay + part, 4, part, value, device)

    def up_down(self, part):
        where = self.where(part)
        for step, base, device in ((5, self.up, self.site.up), (6, self.down, self.site.down)):
            from_y = self.over + (step - 4) * SPLIT + part
            value = self.mine[step, where] + self.came(from_y, self.land.at[step - 4, where])
            if part % 2 == step - 5:
                value = value + self.came(self.relay + part, self.land.at[4, where])
            self.send(base + part, step, part, value, device)

    def final(self, part):
        where = self.where(part)
        value = self.mine[7, where] + self.came(
            self.over + 3 * SPLIT + part, self.land.at[3, where]
        )
        value = value + self.came(self.up + part, self.land.at[5, where])
        return value + self.came(self.down + part, self.land.at[6, where])


def fold_spread(fold, spread, local, idle):
    def finish(part):
        rows = local(fold.final(part), fold.where(part))
        if spread is not None:
            site = spread.site
            spread.held[site.chip(0, 0), site.core, fold.where(part)] = rows
            spread.own(part)

    fold.start()
    idle(3)
    fold.pass_on(0)
    idle(2)
    fold.up_down(0)
    fold.pass_on(1)
    idle(3)
    finish(0)
    fold.up_down(1)
    idle(3)
    if spread is not None:
        spread.relays(0)
    finish(1)
    if spread is not None:
        spread.share(0)
        spread.far(0)
        idle(2)
        spread.relays(1)
        spread.after_relays()
        spread.far(1)
        idle(10)
        spread.tail()
        spread.links.close()
    else:
        idle(10)
    fold.links.close()


class Cross:
    def __init__(self, n):
        self.site = n.site
        self.links = Links(n.cross_send, n.cross_recv, n.site)
        self.begun = []

    def where(self, layer, receives, action):
        if layer is None:
            action()
        else:
            pl.when((self.site.section == layer) == receives)(action)

    def send(self, src, dst, layer=None):
        copy = self.links.copy(len(self.begun), src, dst, self.site.partner)
        self.begun.append([copy, layer, False])
        self.where(layer, False, copy.start)
        return len(self.begun) - 1

    def wait(self, index):
        copy, layer, landed = self.begun[index]
        if not landed:
            self.begun[index][2] = True
            self.where(layer, True, copy.wait_recv)

    def close(self):
        for index in range(len(self.begun)):
            self.wait(index)
        for copy, layer, _ in self.begun:
            self.where(layer, False, copy.wait_send)


class Copies:
    def __init__(self, n):
        self.n, self.count, self.open = n, 0, []

    def sem(self):
        self.count += 1
        return self.n.copy_sem.at[self.count - 1]

    def start(self, src, dst):
        copy = pltpu.make_async_copy(src, dst, self.sem())
        copy.start()
        self.open.append(copy)
        return copy

    def pick(self, own, other, dst, layer):
        sem = self.sem()
        from_own = pltpu.make_async_copy(own, dst, sem)
        from_other = pltpu.make_async_copy(other, dst, sem)
        pl.when(self.n.site.section == layer)(from_own.start)
        pl.when(self.n.site.section != layer)(from_other.start)
        self.open.append(from_own)
        return from_own

    def wait(self, *copies):
        for copy in copies:
            if any(copy is other for other in self.open):
                self.open = [other for other in self.open if other is not copy]
                copy.wait()

    def close(self):
        self.wait(*list(self.open))


def kernel_of(body, names, *refs):
    n = types.SimpleNamespace(**dict(zip(names, refs)))
    n.site = Site()
    n.copies = Copies(n)
    n.cross = Cross(n)
    body(n)
    n.cross.close()
    n.copies.close()


def launch(name, ident, body, scalars, inputs, outputs, scratch):
    scratch = dict(
        scratch,
        copy_sem=pltpu.SemaphoreType.DMA((COPY_SEMS,)),
        cross_send=pltpu.SemaphoreType.DMA((CROSS_SEMS,)),
        cross_recv=pltpu.SemaphoreType.DMA((CROSS_SEMS,)),
    )
    names = [*scalars, *inputs, *outputs, *scratch]
    results = pl.pallas_call(
        functools.partial(kernel_of, body, names),
        out_shape=[jax.ShapeDtypeStruct(*value) for value in outputs.values()],
        in_specs=[IN_SMEM] * len(scalars) + [IN_HBM] * len(inputs),
        out_specs=[IN_HBM] * len(outputs),
        scratch_shapes=list(scratch.values()),
        compiler_params=pltpu.CompilerParams(
            collective_id=ident, has_side_effects=True, vmem_limit_bytes=60 * 2**20
        ),
        cost_estimate=pl.CostEstimate(flops=2**37, bytes_accessed=2**23, transcendentals=0),
        name=name,
    )(*scalars.values(), *inputs.values())
    return types.SimpleNamespace(**dict(zip(outputs, results)))


def fold_buffers(full):
    return dict(
        mine=pltpu.VMEM((CHIPS, *full), FULL),
        pass_out=pltpu.VMEM((CHIPS, *full), LOW),
        pass_in=pltpu.VMEM((CHIPS, *full), LOW),
        stage=pltpu.VMEM((CHIPS - 1, *full), LOW),
        land=pltpu.VMEM((CHIPS - 1, *full), LOW),
        fold_send=pltpu.SemaphoreType.DMA((FOLD_SEMS,)),
        fold_recv=pltpu.SemaphoreType.DMA((FOLD_SEMS,)),
    )


def fold_of(n, part_of):
    buffers = (n.mine, n.pass_out, n.pass_in, n.stage, n.land)
    return Fold(n.site, part_of, buffers, Links(n.fold_send, n.fold_recv, n.site))


def spread_of(n, held, send, recv, use, kept=None):
    def take(chip):
        block = held[chip]
        use(chip, block.reshape(block.shape[0] * block.shape[1], block.shape[2]))
        if kept is not None:
            n.copies.start(held.at[chip], kept.at[chip])

    return Spread(n.site, held, Links(send, recv, n.site), take)


def spread_sems(*names):
    return {name: pltpu.SemaphoreType.DMA((SPREAD_SEMS,)) for name in names}


def no_idle(count):
    pass


def rows_of(ref, chip, site):
    return jnp.concatenate([ref[chip, 1 - site.core], ref[chip, site.core]], 0)


def put(ref, chip, value):
    ref[chip] = value.astype(LOW).reshape(ref.shape[1:])


def gate_chunk(n, chip, rows):
    gate_pre = times_trans(rows, n.w_g[...])
    up_pre = times_trans(rows, n.w_u[...])
    sig = jax.nn.sigmoid(gate_pre)
    silu_val = gate_pre * sig
    put(n.act, chip, silu_val * up_pre)
    return up_pre * sig * (1.0 + gate_pre * (1.0 - sig)), silu_val


def norm_back_rows(values, gain_vec, grad_in):
    factor = lax.rsqrt(jnp.mean(values * values, -1, keepdims=True) + EPSILON)
    gain_grad = jnp.sum(grad_in * values * factor, 0, keepdims=True)
    mean_term = jnp.mean(grad_in * gain_vec * values, -1, keepdims=True)
    return (
        gain_grad,
        factor * gain_vec * grad_in - values * (factor * factor * factor) * mean_term,
    )


def swap_halves(value):
    width = value.shape[1]
    half = HEAD_DIM // 2
    lane = lax.broadcasted_iota(jnp.int32, value.shape, 1)
    return jnp.where(
        lax.rem(lane, HEAD_DIM) < half,
        pltpu.roll(value, width - half, 1),
        pltpu.roll(value, half, 1),
    )


def stacked(pair):
    return jnp.concatenate([pair[:, :HEAD_DIM], pair[:, HEAD_DIM:]], 0)


def side_by_side(turned):
    return jnp.concatenate([turned[:, :PLACE], turned[:, PLACE:]], 0).T


def hide_later(scores, fill):
    last = scores[-PLACE:]
    key = lax.broadcasted_iota(jnp.int32, last.shape, 0)
    query = lax.rem(lax.broadcasted_iota(jnp.int32, last.shape, 1), PLACE)
    last = jnp.where(key <= query, last, fill)
    if scores.shape[0] == PLACE:
        return last
    return jnp.concatenate([scores[:-PLACE], last], 0)


def turn_of(turns, place):
    near, far = pl.ds(0, PLACE), pl.ds(PLACE + place, 1)
    cos_near, sin_near = turns[0, near], turns[1, near]
    cos_far, sin_far = turns[0, far], turns[1, far]
    cosine = cos_near * cos_far - sin_near * sin_far
    sine = sin_near * cos_far + cos_near * sin_far
    lane = lax.broadcasted_iota(jnp.int32, cosine.shape, 1)
    sine = jnp.where(lax.rem(lane, HEAD_DIM) < HEAD_DIM // 2, -sine, sine)
    keyed = lane < HEAD_DIM
    return (
        jnp.concatenate([cosine, jnp.where(keyed, cosine, 1.0)], 1),
        jnp.concatenate([sine, jnp.where(keyed, sine, 0.0)], 1),
    )


def attend(n):
    q_width = 2 * HEAD_DIM
    scale = jnp.asarray(1.0 / math.sqrt(HEAD_DIM), LOW)
    for place in range(CHIPS):
        at = pl.ds(place * PLACE, PLACE)
        value = n.qkv[n.block_at[place]]
        cosine, sine = turn_of(n.turns_v, place)
        value = (value * cosine + swap_halves(value) * sine).astype(LOW)
        n.turned_v[at, :q_width] = value[:, :q_width] * scale
        n.turned_v[at, q_width:] = value[:, q_width:]
        n.values_t[:, at] = value[:, q_width:].astype(FULL).T[HEAD_DIM:].astype(LOW)
    for place in range(CHIPS):
        at = pl.ds(place * PLACE, PLACE)
        keys = pl.ds(0, (place + 1) * PLACE)
        query = stacked(n.turned_v[at, :q_width])
        scores = times_trans(n.turned_v[keys, q_width : q_width + HEAD_DIM], query)
        scores = hide_later(scores, NEG_LARGE)
        top = jnp.max(scores, 0, keepdims=True)
        weight = jnp.exp(scores - top)
        total = jnp.sum(weight, 0, keepdims=True)
        out = plain_dot(n.values_t[:, keys], weight.astype(LOW)) / total
        n.attended_v[place] = side_by_side(out)
        n.spread_v[pl.ds(place, 1)] = top + jnp.log(total)
    for block in range(CHIPS):
        put(n.mixed_v, block, n.attended_v[n.order[block]])
    n.copies.start(n.turned_v, n.turned)
    n.copies.start(n.attended_v, n.attended)
    n.copies.start(n.spread_v, n.spread)
    n.copies.start(n.mixed_v, n.mixed)


def attend_back(n):
    q_width = 2 * HEAD_DIM
    n.d_key[...] = jnp.zeros_like(n.d_key)
    n.d_value[...] = jnp.zeros_like(n.d_value)
    for place in range(CHIPS):
        at = pl.ds(place * PLACE, PLACE)
        n.keys_t[:, at] = n.turned_v[at, q_width:].astype(FULL).T[:HEAD_DIM].astype(LOW)
    for place in range(CHIPS):
        at = pl.ds(place * PLACE, PLACE)
        keys = pl.ds(0, (place + 1) * PLACE)
        d_out = n.d_mixed[n.block_at[place]]
        product = (d_out.astype(FULL) * n.attended_v[place]).T
        offset = jnp.concatenate(
            [
                jnp.sum(product[:HEAD_DIM], 0, keepdims=True),
                jnp.sum(product[HEAD_DIM:], 0, keepdims=True),
            ],
            1,
        )
        d_out = stacked(d_out)
        query = stacked(n.turned_v[at, :q_width])
        scores = times_trans(n.turned_v[keys, q_width : q_width + HEAD_DIM], query)
        scores = hide_later(scores, NEG_LARGE)
        probs = jnp.exp(scores - n.spread_v[pl.ds(place, 1)])
        d_probs = times_trans(n.turned_v[keys, q_width + HEAD_DIM :], d_out)
        d_scores = (probs * (d_probs - offset)).astype(LOW)
        n.d_key[keys] += plain_dot(d_scores, query)
        n.d_value[keys] += plain_dot(probs.astype(LOW), d_out)
        n.d_query[at] = side_by_side(plain_dot(n.keys_t[:, keys], d_scores)) * (
            1.0 / math.sqrt(HEAD_DIM)
        )
    for place in range(CHIPS):
        at = pl.ds(place * PLACE, PLACE)
        value = jnp.concatenate([n.d_query[at], n.d_key[at], n.d_value[at]], 1)
        cosine, sine = turn_of(n.turns_v, place)
        value = value * cosine - swap_halves(value) * sine
        n.d_turned[place] = value.astype(LOW)
    for block in range(CHIPS):
        put(n.d_qkv, block, n.d_turned[n.order[block]])


def gather_small(n):
    site = n.site
    links = n.links_small = Links(n.small_send, n.small_recv, site)
    links.go(0, n.gains_mine, n.gains_x, site.partner)
    links.go(1, n.kv_mine, n.kv_x, site.partner)
    links.got(0, n.gains_x)
    own, came = n.gains_mine[...], n.gains_x[...]
    first = site.section == 0
    n.gains_all[site.z, site.member] = jnp.concatenate(
        [
            jnp.where(first, own, came)[:2],
            jnp.where(first, came, own)[:2],
            jnp.zeros((4, own.shape[1]), FULL),
        ],
        0,
    )
    peers = (site.sibling, site.across, site.corner)
    mine = n.gains_all.at[site.z, site.member]
    for index, device in enumerate(peers):
        links.go(2 + index, mine, mine, device)
    for index, device in enumerate(peers):
        links.got(2 + index, n.gains_all.at[site.z, device[2]])
    shard = n.gains_all.at[site.z]
    for index, device in enumerate((site.up, site.down, site.opposite)):
        links.go(5 + index, shard, shard, device)


def gather_small_keys(n):
    site, links = n.site, n.links_small
    links.got(1, n.kv_x)
    n.kv_all[site.member, site.section] = n.kv_mine[...]
    n.kv_all[site.member, 1 - site.section] = n.kv_x[...]
    mine = n.kv_all.at[site.member]
    for index, device in enumerate((site.sibling, site.across, site.corner)):
        links.go(8 + index, mine, mine, device)


def gather_small_end(n):
    site, links = n.site, n.links_small
    for index, along_z in enumerate((RING - 1, 1, 2)):
        links.got(5 + index, n.gains_all.at[lax.rem(site.z + along_z, RING)])
    for index, device in enumerate((site.sibling, site.across, site.corner)):
        links.got(8 + index, n.kv_all.at[device[2]])
    links.close()
    n.gains_v[...] = jnp.concatenate(
        [n.gains_all[shard, seq] for shard in range(RING) for seq in range(RING)], 1
    )
    for layer in range(2):
        for index in range(2):
            rows = n.kv_all[:, layer, index]
            n.w_kv[layer, pl.ds(index * HEAD_DIM, HEAD_DIM)] = rows.reshape(
                HEAD_DIM, rows.shape[-1]
            )
    n.copies.start(n.gains_v, n.gains)
    n.copies.start(n.w_kv, n.kv_rows)


def forward_first(n):
    site, copies, cross = n.site, n.copies, n.cross
    own = (site.chip(0, 0), site.core)
    small = [copies.start(n.gains_own, n.gains_mine), copies.start(n.kv_own, n.kv_mine)]
    rows_copy = copies.start(n.x_rows, n.held.at[own])
    top_copy = copies.start(n.top_rows, n.top_all.at[own])
    turns_copy = copies.start(n.turns, n.turns_v)
    greet(site)
    copies.wait(*small)
    gather_small(n)
    at_query = cross.send(n.w_query, n.x_query)
    at_out = cross.send(n.w_out, n.x_out)
    copies.wait(rows_copy)

    def use_first(chip, rows):
        normed = scaled(rows.astype(FULL), n.gains_v[:1]).astype(LOW)
        n.normed[chip] = normed.reshape(n.normed.shape[1:])
        n.qkv[chip] = jnp.concatenate(
            [times_trans(normed, n.w_q[...]), times_trans(normed, n.w_kv[0])], 1
        )
        copies.start(n.normed.at[chip], n.rows_one.at[chip])

    spread = spread_of(n, n.held, n.spread_send, n.spread_recv, use_first)
    for part in range(SPLIT):
        spread.own(part)
    spread.share(0)
    gather_small_keys(n)
    for part in range(SPLIT):
        spread.relays(part)
    gather_small_end(n)
    spread.after_relays()
    cross.wait(at_query)
    at_gate = cross.send(n.w_gate, n.x_gate)
    query_copy = copies.pick(n.w_query, n.x_query, n.w_q, 0)
    for part in range(SPLIT):
        spread.far(part)
    copies.wait(query_copy)
    spread.tail()
    spread.links.close()
    copies.wait(top_copy, turns_copy)
    top = spread_of(n, n.top_all, n.top_send, n.top_recv, None)
    for part in range(SPLIT):
        top.own(part)
    cross.wait(at_out)
    at_up = cross.send(n.w_up, n.x_up)
    out_copy = copies.pick(n.w_out, n.x_out, n.w_o, 0)
    attend(n)
    top.share(0)
    for part in range(SPLIT):
        top.relays(part)
    copies.wait(out_copy)

    def part_of(chip):
        return plain_dot(rows_of(n.mixed_v, chip, site), n.w_o[...])

    def local(total, where):
        hidden_in = n.held[(*own, where)].astype(FULL) + total
        n.hidden_v[where] = hidden_in
        return scaled(hidden_in, n.gains_v[1:2]).astype(LOW)

    def use_gate(chip, rows):
        gate_slope, up_slope = gate_chunk(n, chip, rows)
        put(n.gate_slope_v, chip, gate_slope)
        put(n.up_slope_v, chip, up_slope)

    started = []

    def idle(count):
        started.append(count)
        if len(started) == 5:
            top.after_relays()
            for part in range(SPLIT):
                top.far(part)
        if len(started) == 6:
            cross.wait(at_gate)
            started.append(cross.send(n.w_down, n.x_down))
            cross.wait(at_up)
            gate_copies = (
                copies.pick(n.w_gate, n.x_gate, n.w_g, 0),
                copies.pick(n.w_up, n.x_up, n.w_u, 0),
            )
            copies.wait(*gate_copies)

    spread = spread_of(
        n, n.held_two, n.spread_two_send, n.spread_two_recv, use_gate, n.rows_two
    )
    fold_spread(fold_of(n, part_of), spread, local, idle)
    copies.start(n.hidden_v, n.hidden)
    for source, target in (
        (n.act, n.act_all), (n.gate_slope_v, n.gate_slope), (n.up_slope_v, n.up_slope)
    ):
        copies.start(source, target)
    top.tail(consume=False)
    top.links.close()


def forward_second(n):
    site, copies = n.site, n.copies
    first = [
        copies.start(n.act_prev, n.act_prev_v),
        copies.pick(n.w_down, n.x_down, n.w_d_prev, 0),
    ]
    rows_copies = [copies.start(n.hidden_prev, n.hidden_prev_v), copies.start(n.gains, n.gains_v)]
    qkv_copies = [
        copies.pick(n.w_query, n.x_query, n.w_in.at[pl.ds(0, 2 * HEAD_DIM)], 1),
        copies.start(n.kv_rows.at[1], n.w_in.at[pl.ds(2 * HEAD_DIM, 2 * HEAD_DIM)]),
        copies.start(n.turns, n.turns_v),
    ]
    later = [
        copies.pick(n.w_out, n.x_out, n.w_o, 1),
        copies.pick(n.w_gate, n.x_gate, n.w_g, 1),
        copies.pick(n.w_up, n.x_up, n.w_u, 1),
        copies.pick(n.w_down, n.x_down, n.w_d, 1),
        copies.start(n.top_all, n.top_held),
    ]
    greet(site)
    copies.wait(*first, *rows_copies)

    def part_of(chip):
        return plain_dot(rows_of(n.act_prev_v, chip, site), n.w_d_prev[...])

    def local(total, where):
        result = (n.hidden_prev_v[where] + total).astype(LOW)
        n.result_v[where] = result
        return scaled(result.astype(FULL), n.gains_v[2:3]).astype(LOW)

    def use_qkv(chip, rows):
        n.qkv[chip] = times_trans(rows, n.w_in[...])

    def settle(count):
        copies.wait(*qkv_copies)

    spread = spread_of(n, n.held, n.spread_send, n.spread_recv, use_qkv, n.rows_one)
    fold_spread(fold_of(n, part_of), spread, local, settle)
    copies.start(n.result_v, n.result)
    attend(n)
    copies.wait(*later)

    def part_of_two(chip):
        return plain_dot(rows_of(n.mixed_v, chip, site), n.w_o[...])

    def local_two(total, where):
        hidden_in = n.result_v[where].astype(FULL) + total
        n.hidden_v[where] = hidden_in
        return scaled(hidden_in, n.gains_v[3:4]).astype(LOW)

    def use_gate(chip, rows):
        gate_slope, up_slope = gate_chunk(n, chip, rows)
        d_act = times_trans(n.top_held[chip].reshape(rows.shape), n.w_d[...])
        put(n.d_gate_v, chip, d_act * gate_slope)
        put(n.d_up_v, chip, d_act * up_slope)

    spread = spread_of(
        n, n.held_two, n.spread_two_send, n.spread_two_recv, use_gate, n.rows_two
    )
    fold_spread(fold_of(n, part_of_two), spread, local_two, no_idle)
    for source, target in (
        (n.hidden_v, n.hidden), (n.act, n.act_all), (n.d_gate_v, n.d_gate), (n.d_up_v, n.d_up)
    ):
        copies.start(source, target)


def products(n, left, right, store, tile=512):
    count = math.prod(left.shape[:-1])
    for start in range(0, right.shape[-1], tile):
        where = pl.ds(start, tile)
        value = outer_sum(
            left[...].reshape(count, left.shape[-1]), right[:, :, :, where].reshape(count, tile)
        )
        store(where, value.astype(LOW))
        yield


def ffn_products(n, loads, made):
    n.copies.wait(*loads)
    for left, right, out in (
        (n.act, n.top_held, n.g_down_v),
        (n.d_gate_v, n.normed, n.g_gate_v),
        (n.d_up_v, n.normed, n.g_up_v),
    ):

        def store(where, value):
            out[:, where] = value

        yield from products(n, left, right, store)
        made(out)


def in_products(n, loads, made):
    site = n.site
    n.copies.wait(*loads)

    def store_out(where, value):
        n.g_out_v[:, where] = value

    def store_in(where, value):
        query = n.g_query_v.shape[0]
        n.g_query_v[:, where] = value[:query]
        n.kv_mine[:, :, :, where] = value[query:].reshape(
            *n.kv_mine.shape[:3], value.shape[1]
        )

    yield from products(n, n.d_qkv, n.normed, store_in)
    made(n.g_query_v)
    peers = (site.sibling, site.across, site.corner)
    links = Links(n.kv_send, n.kv_recv, site)
    for index, device in enumerate(peers):
        links.go(index, n.kv_mine.at[:, device[2]], n.kv_came.at[index], device)
    yield from products(n, n.mixed_v, n.held, store_out)
    made(n.g_out_v)
    total = n.kv_mine[:, site.member].astype(FULL)
    for index in range(len(peers)):
        total = total + links.got(index, n.kv_came.at[index])[...].astype(FULL)
    n.g_kv_v[...] = total.astype(LOW)
    made(n.g_kv_v)
    links.close()


def fold_gains(n):
    site = n.site
    links = Links(n.gain_send, n.gain_recv, site)
    own = jnp.concatenate(
        [n.gain_grads[...], n.gain_later_v[...], jnp.zeros((4, n.gain_grads.shape[1]), FULL)], 0
    )
    width = n.gain_parts.shape[-1]
    for shard in range(RING):
        for seq in range(RING):
            start = (shard * RING + seq) * width
            n.gain_parts[seq, shard] = own[:, start : start + width]
    peers = (site.sibling, site.across, site.corner)
    for index, device in enumerate(peers):
        links.go(index, n.gain_parts.at[device[2]], n.gain_came.at[index], device)
    yield
    total = n.gain_parts[site.member]
    for index in range(3):
        total = total + links.got(index, n.gain_came.at[index])[...]
    n.gain_shards[...] = total
    for index, device in enumerate((site.up, site.down, site.opposite)):
        links.go(
            3 + index, n.gain_shards.at[device[1]], n.gain_last.at[index], device
        )
    yield
    total = n.gain_shards[site.z]
    for index in range(3):
        total = total + links.got(3 + index, n.gain_last.at[index])[...]
    n.gain_own[...] = total
    links.go(6, n.gain_own, n.gain_other, site.partner)
    yield
    total = n.gain_own[...] + links.got(6, n.gain_other)[...]
    n.gain_sums_v[...] = jnp.where(site.section == 0, total[:2], total[2:4])
    links.close()
    n.copies.start(n.gain_sums_v, n.gain_sums)


def backward(layer, n):
    site, copies, cross = n.site, n.copies, n.cross
    first = [
        copies.start(n.d_gate, n.d_gate_v),
        copies.start(n.d_up, n.d_up_v),
        copies.pick(n.w_gate, n.x_gate, n.w_g, layer),
        copies.pick(n.w_up, n.x_up, n.w_u, layer),
    ]
    rows_copies = [
        copies.start(n.hidden, n.hidden_v),
        copies.start(n.top_rows, n.top_v),
        copies.start(n.gains, n.gains_v),
        copies.pick(n.w_out, n.x_out, n.w_o, layer),
    ]
    loads = [
        copies.start(n.act_all, n.act),
        copies.start(n.top_all, n.top_held),
        copies.start(n.rows_two, n.normed),
    ]
    attn_copies = [
        copies.start(n.turns, n.turns_v),
        copies.start(n.turned, n.turned_v),
        copies.start(n.attended, n.attended_v),
        copies.start(n.spread, n.spread_v),
        copies.start(n.mixed, n.mixed_v),
        copies.pick(n.w_query, n.x_query, n.w_in.at[pl.ds(0, 2 * HEAD_DIM)], layer),
        copies.start(n.kv_rows.at[layer], n.w_in.at[pl.ds(2 * HEAD_DIM, 2 * HEAD_DIM)]),
        copies.start(n.x_rows, n.x_v),
    ]
    if layer == 1:
        next_copies = [
            copies.pick(n.w_down, n.x_down, n.w_d, 0),
            copies.start(n.gate_slope, n.gate_slope_v),
            copies.start(n.up_slope, n.up_slope_v),
        ]
    else:
        next_copies = [
            copies.pick(n.w_down, n.x_down, n.w_d, 1),
            copies.start(n.act_last, n.act_last_v),
            copies.start(n.hidden_last, n.hidden_last_v),
            copies.start(n.gain_later, n.gain_later_v),
        ]
    greet(site)
    if layer == 1:
        cross.send(n.x_rows, n.came_result_first, 0)
    else:
        cross.send(n.own_up_later, n.came_up_later, 1)
        cross.send(n.top_rows, n.came_input_later, 1)
    copies.wait(*first, *rows_copies)

    def made(out):
        target, came = {
            id(n.g_down_v): (n.own_down, n.came_down),
            id(n.g_gate_v): (n.own_gate, n.came_gate),
            id(n.g_up_v): (n.own_up, None if layer == 1 else n.came_up),
            id(n.g_out_v): (n.own_out, n.came_out),
            id(n.g_query_v): (n.own_query, n.came_query),
            id(n.g_kv_v): (n.own_kv, n.came_kv),
        }[id(out)]
        copies.start(out, target)
        if came is not None:
            cross.send(out, came, layer)

    def step_on(working):
        def idle(count):
            for _ in range(count):
                next(working, None)

        return idle

    def part_of(chip):
        return plain_dot(rows_of(n.d_gate_v, chip, site), n.w_g[...]) + plain_dot(
            rows_of(n.d_up_v, chip, site), n.w_u[...]
        )

    def add_gain(row, value, where):
        row = pl.ds(row, 1)
        n.gain_grads[row] = value if where.start == 0 else n.gain_grads[row] + value

    def local(total, where):
        gain_grad, d_hidden = norm_back_rows(
            n.hidden_v[where], n.gains_v[2 * layer + 1 : 2 * layer + 2], total
        )
        d_hidden = d_hidden + n.top_v[where].astype(FULL)
        add_gain(1, gain_grad, where)
        n.d_hidden[where] = d_hidden
        return d_hidden.astype(LOW)

    def use_d_mixed(chip, rows):
        n.d_mixed[chip] = times_trans(rows, n.w_o[...]).astype(LOW)

    working = ffn_products(n, loads, made)
    spread = spread_of(n, n.held, n.spread_send, n.spread_recv, use_d_mixed)
    fold_spread(fold_of(n, part_of), spread, local, step_on(working))
    for _ in working:
        pass
    normed_copy = copies.start(n.rows_one, n.normed)
    copies.wait(*attn_copies)
    attend_back(n)
    copies.wait(*next_copies)

    def part_of_two(chip):
        return plain_dot(rows_of(n.d_qkv, chip, site), n.w_in[...])

    def local_two(total, where):
        gain_grad, d_input = norm_back_rows(
            n.x_v[where].astype(FULL), n.gains_v[2 * layer : 2 * layer + 1], total
        )
        d_input = (d_input + n.d_hidden[where]).astype(LOW)
        add_gain(0, gain_grad, where)
        n.d_input_v[where] = d_input
        return d_input

    working = in_products(n, [normed_copy], made)
    if layer == 1:

        def use_d_act(chip, rows):
            d_act = times_trans(rows, n.w_d[...])
            for out, slope in ((n.d_gate_v, n.gate_slope_v), (n.d_up_v, n.up_slope_v)):
                put(out, chip, d_act * slope[chip].astype(FULL).reshape(d_act.shape))

        spread = spread_of(
            n, n.held_two, n.spread_two_send, n.spread_two_recv, use_d_act, n.top_next
        )
        fold_spread(fold_of(n, part_of_two), spread, local_two, step_on(working))
        for _ in working:
            pass
        for source, target in (
            (n.d_gate_v, n.d_gate_next), (n.d_up_v, n.d_up_next), (n.d_input_v, n.d_input),
            (n.gain_grads, n.gain_out),
        ):
            copies.start(source, target)
        return
    fold_spread(fold_of(n, part_of_two), None, local_two, step_on(working))
    for _ in working:
        pass
    copies.start(n.d_input_v, n.d_input)
    cross.send(n.d_input_v, n.came_input, 0)

    def part_of_last(chip):
        return plain_dot(rows_of(n.act_last_v, chip, site), n.w_d[...])

    def local_last(total, where):
        n.result_v[where] = (n.hidden_last_v[where] + total).astype(LOW)

    buffers = (n.mine, n.pass_out, n.pass_in_two, n.stage, n.land_two)
    links = Links(n.last_send, n.last_recv, site)
    gains_on = fold_gains(n)
    next(gains_on)
    fold_spread(
        Fold(site, part_of_last, buffers, links), None, local_last,
        lambda count: next(gains_on, None),
    )
    for _ in gains_on:
        pass
    copies.start(n.result_v, n.result)
    cross.send(n.result_v, n.came_result, 1)


def join_kernel(count, *refs):
    own, came = (refs[:count], refs[count : 2 * count]), (
        refs[2 * count : 3 * count],
        refs[3 * count : 4 * count],
    )
    outs, refs = refs[4 * count : 5 * count], refs[5 * count :]
    own_at, came_at, sums = refs[:count], refs[count : 2 * count], refs[2 * count : 3 * count]
    sems, out_sem = refs[3 * count :]
    section = lax.axis_index("section")
    waits = []
    for index in range(count):
        for slot, (pair, target) in enumerate(((own, own_at), (came, came_at))):
            copies = [
                pltpu.make_async_copy(
                    pair[layer][index], target[index], sems.at[2 * index + slot]
                )
                for layer in range(2)
            ]
            pl.when(section == 0)(copies[0].start)
            pl.when(section != 0)(copies[1].start)
            waits.append(copies[0])
    done = []
    for index in range(count):
        waits[2 * index].wait()
        waits[2 * index + 1].wait()
        sums[index][...] = own_at[index][...].astype(FULL) + came_at[index][...].astype(FULL)
        copy = pltpu.make_async_copy(sums[index], outs[index], out_sem.at[index])
        copy.start()
        done.append(copy)
    for copy in done:
        copy.wait()


def join_sums(own_a, own_b, came_a, came_b):
    count = len(own_a)
    kept = [pltpu.VMEM(value.shape, LOW) for value in own_a]
    return pl.pallas_call(
        functools.partial(join_kernel, count),
        out_shape=[jax.ShapeDtypeStruct(value.shape, FULL) for value in own_a],
        in_specs=[IN_HBM] * (4 * count),
        out_specs=[IN_HBM] * count,
        scratch_shapes=kept
        + kept
        + [pltpu.VMEM(value.shape, FULL) for value in own_a]
        + [pltpu.SemaphoreType.DMA((2 * count,)), pltpu.SemaphoreType.DMA((count,))],
        compiler_params=pltpu.CompilerParams(vmem_limit_bytes=40 * 2**20),
        cost_estimate=pl.CostEstimate(flops=2**32, bytes_accessed=2**24, transcendentals=0),
        name="join_sums",
    )(*own_a, *own_b, *came_a, *came_b)


def relay_body(
    inputs,
    cotangent,
    positions,
    gain_attn,
    w_query,
    w_key,
    w_value,
    w_out,
    gain_ffn,
    w_gate,
    w_up,
    w_down,
):
    n_micro, per_device, model_width = inputs.shape
    n_seq = lax.axis_size("seq")
    n_shard = lax.axis_size("shard")
    members = n_seq * n_shard
    total_len = members * per_device
    section_idx = lax.axis_index("section")
    q_width = HEADS // members * HEAD_DIM
    in_width = q_width + 2 * HEAD_DIM
    hidden = w_down.shape[1]
    vmem = pltpu.VMEM

    def pick(first, second):
        return jnp.where(section_idx == 0, first, second)

    x_rows = pick(inputs[0], inputs[1])
    top_rows = pick(cotangent[0], cotangent[1])
    places = pick(positions[0], positions[1])
    gains_own = jnp.concatenate(
        [gain_attn, gain_ffn, jnp.zeros((6, gain_attn.shape[1]), gain_attn.dtype)], 0
    ).astype(FULL)
    kv_own = jnp.stack([w_key[0], w_value[0]])
    own = dict(
        w_query=w_query[0], w_out=w_out[0], w_gate=w_gate[0], w_up=w_up[0], w_down=w_down[0]
    )

    order = (places.reshape(CHIPS, PLACE)[:, 0] // PLACE).astype(jnp.int32)
    numbers = jnp.arange(CHIPS, dtype=jnp.int32)
    block_at = jnp.sum(
        jnp.where(order[None, :] == numbers[:, None], numbers[None, :], 0), 1
    ).astype(jnp.int32)
    scalars = dict(block_at=block_at, order=order)
    half_dim = HEAD_DIM // 2
    inv_freq = THETA_BASE ** (-jnp.arange(half_dim, dtype=FULL) * (2.0 / HEAD_DIM))
    steps = jnp.concatenate([jnp.arange(PLACE), PLACE * jnp.arange(CHIPS)]).astype(FULL)
    angles = steps[:, None] * jnp.tile(inv_freq, 2 * q_width // HEAD_DIM)[None, :]
    turns = jnp.stack([jnp.cos(angles), jnp.sin(angles)])

    rows = (per_device, model_width)
    row_low, row_full = (rows, LOW), (rows, FULL)
    all_rows = ((CHIPS, 2, *rows), LOW)
    narrow = ((CHIPS, 2, per_device, hidden), LOW)
    wide = ((hidden, model_width), LOW)
    quarter = ((q_width, model_width), LOW)
    gain_row = ((8, model_width), FULL)
    kv_shape = (2, w_key.shape[1], model_width)
    small = gains_own.shape
    saved = dict(
        turned=((total_len, in_width), LOW),
        attended=((CHIPS, PLACE, q_width), FULL),
        spread=((CHIPS, 2 * PLACE), FULL),
        mixed=((CHIPS, 2, per_device, q_width), LOW),
    )
    saved_v = dict(
        turned_v=vmem(*saved["turned"]),
        attended_v=vmem(*saved["attended"]),
        spread_v=vmem(*saved["spread"]),
        mixed_v=vmem(*saved["mixed"]),
        turns_v=vmem(turns.shape, FULL),
    )
    attend_v = dict(
        **saved_v,
        qkv=vmem((CHIPS, PLACE, in_width), FULL),
        values_t=vmem((HEAD_DIM, total_len), LOW),
    )
    gates_v = dict(w_g=vmem(*wide), w_u=vmem(*wide))

    first = launch(
        "forward_first",
        0,
        forward_first,
        scalars,
        dict(
            x_rows=x_rows, top_rows=top_rows, gains_own=gains_own, kv_own=kv_own, turns=turns,
            **own,
        ),
        dict(
            x_query=quarter,
            x_out=quarter,
            x_gate=wide,
            x_up=wide,
            x_down=wide,
            gains=gain_row,
            kv_rows=((2, 2 * HEAD_DIM, model_width), LOW),
            top_all=all_rows,
            rows_one=all_rows,
            rows_two=all_rows,
            hidden=row_full,
            act_all=narrow,
            gate_slope=narrow,
            up_slope=narrow,
            **saved,
        ),
        dict(
            gains_mine=vmem(small, FULL),
            gains_x=vmem(small, FULL),
            gains_all=vmem((n_shard, n_seq, *small), FULL),
            gains_v=vmem(*gain_row),
            kv_mine=vmem(kv_shape, LOW),
            kv_x=vmem(kv_shape, LOW),
            kv_all=vmem((n_seq, 2, *kv_shape), LOW),
            w_kv=vmem((2, 2 * HEAD_DIM, model_width), LOW),
            small_send=pltpu.SemaphoreType.DMA((SMALL_SEMS,)),
            small_recv=pltpu.SemaphoreType.DMA((SMALL_SEMS,)),
            held=vmem(*all_rows),
            held_two=vmem(*all_rows),
            normed=vmem(*all_rows),
            w_q=vmem(*quarter),
            w_o=vmem(*quarter),
            hidden_v=vmem(*row_full),
            act=vmem(*narrow),
            gate_slope_v=vmem(*narrow),
            up_slope_v=vmem(*narrow),
            **gates_v,
            **attend_v,
            **fold_buffers(rows),
            **spread_sems(
                "spread_send", "spread_recv", "spread_two_send", "spread_two_recv", "top_send",
                "top_recv",
            ),
        ),
    )
    crossed = dict(
        **own,
        x_query=first.x_query,
        x_out=first.x_out,
        x_gate=first.x_gate,
        x_up=first.x_up,
        x_down=first.x_down,
        gains=first.gains,
        kv_rows=first.kv_rows,
        turns=turns,
    )
    second = launch(
        "forward_second",
        1,
        forward_second,
        scalars,
        dict(
            act_prev=first.act_all, hidden_prev=first.hidden, top_all=first.top_all, **crossed
        ),
        dict(
            result=row_low,
            rows_one=all_rows,
            rows_two=all_rows,
            hidden=row_full,
            act_all=narrow,
            d_gate=narrow,
            d_up=narrow,
            **saved,
        ),
        dict(
            act_prev_v=vmem(*narrow),
            hidden_prev_v=vmem(*row_full),
            gains_v=vmem(*gain_row),
            w_d_prev=vmem(*wide),
            w_in=vmem((in_width, model_width), LOW),
            w_o=vmem(*quarter),
            w_d=vmem(*wide),
            top_held=vmem(*all_rows),
            held=vmem(*all_rows),
            held_two=vmem(*all_rows),
            result_v=vmem(*row_low),
            hidden_v=vmem(*row_full),
            act=vmem(*narrow),
            d_gate_v=vmem(*narrow),
            d_up_v=vmem(*narrow),
            **gates_v,
            **attend_v,
            **fold_buffers(rows),
            **spread_sems("spread_send", "spread_recv", "spread_two_send", "spread_two_recv"),
        ),
    )

    kv_pair = ((2, *kv_shape[1:]), LOW)
    own_sums = dict(
        own_down=wide, own_gate=wide, own_up=wide, own_out=quarter, own_query=quarter,
        own_kv=kv_pair,
    )
    came_sums = dict(
        came_down=wide, came_gate=wide, came_out=quarter, came_query=quarter, came_kv=kv_pair
    )
    back_v = dict(
        d_gate_v=vmem(*narrow),
        d_up_v=vmem(*narrow),
        act=vmem(*narrow),
        hidden_v=vmem(*row_full),
        top_v=vmem(*row_low),
        x_v=vmem(*row_low),
        d_hidden=vmem(*row_full),
        d_input_v=vmem(*row_low),
        gains_v=vmem(*gain_row),
        gain_grads=vmem((2, model_width), FULL),
        w_o=vmem(*quarter),
        w_in=vmem((in_width, model_width), LOW),
        w_d=vmem(*wide),
        top_held=vmem(*all_rows),
        normed=vmem(*all_rows),
        held=vmem(*all_rows),
        d_mixed=vmem((CHIPS, PLACE, q_width), LOW),
        d_qkv=vmem((CHIPS, 2, per_device, in_width), LOW),
        d_turned=vmem((CHIPS, PLACE, in_width), LOW),
        d_query=vmem((total_len, q_width), FULL),
        d_key=vmem((total_len, HEAD_DIM), FULL),
        d_value=vmem((total_len, HEAD_DIM), FULL),
        keys_t=vmem((HEAD_DIM, total_len), LOW),
        g_down_v=vmem(*wide),
        g_gate_v=vmem(*wide),
        g_up_v=vmem(*wide),
        g_out_v=vmem(*quarter),
        g_query_v=vmem(*quarter),
        g_kv_v=vmem(*kv_pair),
        kv_mine=vmem((2, n_seq, *kv_shape[1:]), LOW),
        kv_came=vmem((n_seq - 1, 2, *kv_shape[1:]), LOW),
        kv_send=pltpu.SemaphoreType.DMA((n_seq - 1,)),
        kv_recv=pltpu.SemaphoreType.DMA((n_seq - 1,)),
        **gates_v,
        **saved_v,
        **fold_buffers(rows),
    )

    def back_in(done, layer_rows, top, d_gate, d_up, top_all):
        return dict(
            d_gate=d_gate,
            d_up=d_up,
            hidden=done.hidden,
            top_rows=top,
            x_rows=layer_rows,
            act_all=done.act_all,
            top_all=top_all,
            rows_one=done.rows_one,
            rows_two=done.rows_two,
            **{key: getattr(done, key) for key in saved},
            **crossed,
        )

    third = launch(
        "backward_second",
        2,
        functools.partial(backward, 1),
        scalars,
        dict(
            **back_in(
                second, second.result, top_rows, second.d_gate, second.d_up, first.top_all
            ),
            gate_slope=first.gate_slope,
            up_slope=first.up_slope,
        ),
        dict(
            d_gate_next=narrow,
            d_up_next=narrow,
            top_next=all_rows,
            d_input=row_low,
            gain_out=((2, model_width), FULL),
            came_result_first=row_low,
            **own_sums,
            **came_sums,
        ),
        dict(
            gate_slope_v=vmem(*narrow),
            up_slope_v=vmem(*narrow),
            held_two=vmem(*all_rows),
            **back_v,
            **spread_sems("spread_send", "spread_recv", "spread_two_send", "spread_two_recv"),
        ),
    )
    fourth = launch(
        "backward_first",
        3,
        functools.partial(backward, 0),
        scalars,
        dict(
            **back_in(
                first, x_rows, third.d_input, third.d_gate_next, third.d_up_next, third.top_next
            ),
            own_up_later=third.own_up,
            gain_later=third.gain_out,
            act_last=second.act_all,
            hidden_last=second.hidden,
        ),
        dict(
            d_input=row_low,
            result=row_low,
            gain_sums=((2, small[1]), FULL),
            came_up=wide,
            came_up_later=wide,
            came_input=row_low,
            came_input_later=row_low,
            came_result=row_low,
            **own_sums,
            **came_sums,
        ),
        dict(
            act_last_v=vmem(*narrow),
            hidden_last_v=vmem(*row_full),
            gain_later_v=vmem((2, model_width), FULL),
            result_v=vmem(*row_low),
            pass_in_two=vmem((CHIPS, *rows), LOW),
            land_two=vmem((CHIPS - 1, *rows), LOW),
            last_send=pltpu.SemaphoreType.DMA((FOLD_SEMS,)),
            last_recv=pltpu.SemaphoreType.DMA((FOLD_SEMS,)),
            gain_parts=vmem((n_seq, n_shard, *small), FULL),
            gain_came=vmem((n_seq - 1, n_shard, *small), FULL),
            gain_shards=vmem((n_shard, *small), FULL),
            gain_last=vmem((n_shard - 1, *small), FULL),
            gain_own=vmem(small, FULL),
            gain_other=vmem(small, FULL),
            gain_sums_v=vmem((2, small[1]), FULL),
            gain_send=pltpu.SemaphoreType.DMA((7,)),
            gain_recv=pltpu.SemaphoreType.DMA((7,)),
            **back_v,
            **spread_sems("spread_send", "spread_recv"),
        ),
    )

    def joined(kept, came):
        return pick(jnp.stack([kept, came]), jnp.stack([came, kept]))[None]

    outputs = joined(
        pick(second.result, fourth.result),
        pick(third.came_result_first, fourth.came_result),
    )
    input_grads = joined(
        pick(fourth.d_input, third.d_input), pick(fourth.came_input, fourth.came_input_later)
    )
    g_down, g_gate, g_up, g_out, g_query, g_kv = join_sums(
        [fourth.own_down, fourth.own_gate, fourth.own_up, fourth.own_out, fourth.own_query, fourth.own_kv],
        [third.own_down, third.own_gate, third.own_up, third.own_out, third.own_query, third.own_kv],
        [fourth.came_down, fourth.came_gate, fourth.came_up, fourth.came_out, fourth.came_query, fourth.came_kv],
        [third.came_down, third.came_gate, fourth.came_up_later, third.came_out, third.came_query, third.came_kv],
    )
    return (
        outputs,
        input_grads,
        fourth.gain_sums[:1],
        g_query[None],
        g_kv[:1],
        g_kv[1:],
        g_out[None],
        fourth.gain_sums[1:],
        g_gate[None],
        g_up[None],
        g_down[None],
    )


def fits_relay(mesh):
    shape = mesh.shape
    return shape["section"] == 2 and shape["shard"] == KV_HEADS == RING and shape["seq"] == 4


def solution(mesh):
    in_specs = (
        P(None, ("shard", "seq"), None),
        P(None, ("shard", "seq"), None),
        P(),
        P("section", ("shard", "seq")),
        P("section", ("shard", "seq"), None),
        P("section", ("shard", "seq"), None),
        P("section", ("shard", "seq"), None),
        P("section", ("shard", "seq"), None),
        P("section", ("shard", "seq")),
        P("section", ("shard", "seq"), None),
        P("section", ("shard", "seq"), None),
        P("section", ("shard", "seq"), None),
    )
    out_specs = (
        P("section", None, ("shard", "seq"), None),
        P("section", None, ("shard", "seq"), None),
        P("section", ("shard", "seq")),
        P("section", ("shard", "seq"), None),
        P("section", ("shard", "seq"), None),
        P("section", ("shard", "seq"), None),
        P("section", ("shard", "seq"), None),
        P("section", ("shard", "seq")),
        P("section", ("shard", "seq"), None),
        P("section", ("shard", "seq"), None),
        P("section", ("shard", "seq"), None),
    )
    chosen = relay_body if fits_relay(mesh) else body
    return jax.shard_map(chosen, mesh=mesh, in_specs=in_specs, out_specs=out_specs, check_vma=False)
```

```python
import functools
import math
import types

import jax
import jax.numpy as jnp
from jax import lax
from jax.experimental import pallas as pl
from jax.experimental.pallas import tpu as pltpu
from jax.sharding import PartitionSpec as P

HEADS = 32
KV_HEADS = 4
HEAD_DIM = 64


EPSILON = 1e-05
THETA_BASE = 10000.0
NEG_LARGE = -1e30


def shifted(value, axis, by):
    count = lax.axis_size(axis)
    pairs = [(i, i + by) for i in range(count) if 0 <= i + by < count]
    return lax.ppermute(value, axis, pairs)


def times_trans(left, right):
    return lax.dot_general(
        left, right, (((1,), (1,)), ((), ())), preferred_element_type=jnp.float32
    )


def outer_sum(left, right):
    return lax.dot_general(
        left, right, (((0,), (0,)), ((), ())), preferred_element_type=jnp.float32
    )


def plain_dot(left, right):
    return jnp.dot(left, right, preferred_element_type=jnp.float32)


def rotate(values, places, direction):
    half_dim = values.shape[-1] // 2
    inv_freq = THETA_BASE ** (-jnp.arange(half_dim, dtype=jnp.float32) * (2.0 / values.shape[-1]))
    angles = places.astype(jnp.float32)[:, None] * inv_freq[None, :]
    cosine = jnp.cos(angles)[:, None, :]
    sine_val = direction * jnp.sin(angles)[:, None, :]
    first = values[..., :half_dim]
    second = values[..., half_dim:]
    return jnp.concatenate(
        [first * cosine - second * sine_val, second * cosine + first * sine_val], -1
    )


def scaled(values, gain_vec):
    factor = lax.rsqrt(jnp.mean(values * values, -1, keepdims=True) + EPSILON)
    return values * factor * gain_vec


def norm_back(values, gain_vec, grad_in):
    factor = lax.rsqrt(jnp.mean(values * values, -1, keepdims=True) + EPSILON)
    gain_grad = jnp.sum(grad_in * values * factor, 0)
    mean_term = jnp.mean(grad_in * gain_vec * values, -1, keepdims=True)
    return (
        gain_grad,
        factor * gain_vec * grad_in - values * (factor * factor * factor) * mean_term,
    )


def ffn_back(grad_rows, kept_rows, gate_pre, up_pre, wg_part, wu_part, wd_part):
    sigmoid_val = jax.nn.sigmoid(gate_pre)
    silu_val = gate_pre * sigmoid_val
    hidden_act = (silu_val * up_pre).astype(jnp.bfloat16)
    grad_down = outer_sum(hidden_act, grad_rows)
    d_act = times_trans(grad_rows, wd_part)
    d_gate = (d_act * up_pre * sigmoid_val * (1.0 + gate_pre * (1.0 - sigmoid_val))).astype(
        jnp.bfloat16
    )
    d_up = (d_act * silu_val).astype(jnp.bfloat16)
    grad_gate = outer_sum(d_gate, kept_rows)
    grad_up = outer_sum(d_up, kept_rows)
    d_normed = plain_dot(d_gate, wg_part) + plain_dot(d_up, wu_part)
    return ((grad_gate, grad_up, grad_down), d_normed)


def body(
    inputs,
    cotangent,
    positions,
    gain_attn,
    w_query,
    w_key,
    w_value,
    w_out,
    gain_ffn,
    w_gate,
    w_up,
    w_down,
):
    n_micro, per_device, model_width = inputs.shape
    n_seq = lax.axis_size("seq")
    n_shard = lax.axis_size("shard")
    section_idx = lax.axis_index("section")
    shard_pos = lax.axis_index("shard")
    member = shard_pos * n_seq + lax.axis_index("seq")
    span_rows = per_device * n_seq
    total_len = span_rows * n_shard
    local_heads = HEADS // n_seq
    kv_repeat = n_seq // KV_HEADS
    q_width = local_heads * HEAD_DIM
    attn_scale = 1.0 / math.sqrt(HEAD_DIM)
    gain_one, gain_two, wq_full, wk_full, wv_full, wo_full = (
        lax.all_gather(gain_attn[0], ("shard", "seq"), axis=0, tiled=True),
        lax.all_gather(gain_ffn[0], ("shard", "seq"), axis=0, tiled=True),
        lax.all_gather(w_query[0], ("shard", "seq"), axis=0, tiled=True),
        lax.all_gather(w_key[0], ("shard", "seq"), axis=0, tiled=True),
        lax.all_gather(w_value[0], ("shard", "seq"), axis=0, tiled=True),
        lax.all_gather(w_out[0], ("shard", "seq"), axis=0, tiled=True),
    )
    gain_a = gain_one.astype(jnp.float32)
    gain_f = gain_two.astype(jnp.float32)
    wg_use, wu_use, wd_use = (w_gate[0], w_up[0], w_down[0])

    def spread_rows(block_in):
        return lax.all_gather(block_in, ("shard", "seq"), axis=0, tiled=True)

    def fold_rows(block_in):
        return lax.psum_scatter(block_in, ("shard", "seq"), scatter_dimension=0, tiled=True)

    def to_heads(block_in):
        return lax.all_to_all(block_in, "seq", split_axis=1, concat_axis=0, tiled=True)

    def to_tokens(block_in):
        return lax.all_to_all(block_in, "seq", split_axis=0, concat_axis=1, tiled=True)

    def over_keys(head_keys, head_values, step_fn, init_state):
        return step_fn(
            init_state,
            (
                lax.all_gather(head_keys, "shard", axis=0, tiled=True),
                lax.all_gather(head_values, "shard", axis=0, tiled=True),
            ),
            jnp.int32(0),
        )

    def place_sets(batch_index):
        place_row = lax.dynamic_index_in_dim(positions, batch_index, 0, keepdims=False)
        token_places = lax.dynamic_slice_in_dim(place_row, member * per_device, per_device)
        span_places = lax.dynamic_slice_in_dim(place_row, shard_pos * span_rows, span_rows)
        return (place_row, token_places, span_places)

    zero_rows = jnp.zeros((per_device, model_width), jnp.bfloat16)
    arrived_x = zero_rows
    results = []
    stored = []
    for tick_index in range(n_micro + 1):
        own_rows = inputs[tick_index] if tick_index < n_micro else zero_rows
        input_now = jnp.where(section_idx == 0, own_rows, arrived_x)
        batch_index = jnp.clip(tick_index - section_idx, 0, n_micro - 1)
        forward_place_row, forward_token_places, forward_span_places = place_sets(batch_index)
        forward_values_in = input_now.astype(jnp.float32)
        forward_normed_one = scaled(forward_values_in, gain_a).astype(jnp.bfloat16)
        queries = rotate(
            times_trans(forward_normed_one, wq_full).reshape(per_device, HEADS, HEAD_DIM),
            forward_token_places,
            1.0,
        ).astype(jnp.bfloat16)
        key_rows = rotate(
            times_trans(forward_normed_one, wk_full).reshape(per_device, KV_HEADS, HEAD_DIM),
            forward_token_places,
            1.0,
        ).astype(jnp.bfloat16)
        value_rows = (
            times_trans(forward_normed_one, wv_full)
            .reshape(per_device, KV_HEADS, HEAD_DIM)
            .astype(jnp.bfloat16)
        )
        key_rows = jnp.repeat(key_rows, kv_repeat, axis=1)
        value_rows = jnp.repeat(value_rows, kv_repeat, axis=1)
        packed = jnp.concatenate(
            [queries.reshape(per_device, n_seq, q_width), key_rows, value_rows], -1
        )
        arrived = to_heads(packed)[:, 0]
        forward_head_query = arrived[:, :q_width].reshape(span_rows, local_heads, HEAD_DIM)
        forward_head_keys = arrived[:, q_width : q_width + HEAD_DIM]
        forward_head_values = arrived[:, q_width + HEAD_DIM :]

        def absorb(state_in, key_piece, start_row):
            run_max, run_total, run_acc = state_in
            piece_keys, piece_values = key_piece
            visible = forward_place_row[None, None, :] <= forward_span_places[None, :, None]
            scores = (
                jnp.einsum(
                    "qhd,kd->hqk",
                    forward_head_query,
                    piece_keys,
                    preferred_element_type=jnp.float32,
                )
                * attn_scale
            )
            scores = jnp.where(visible, scores, NEG_LARGE)
            new_max = jnp.maximum(run_max, jnp.max(scores, -1))
            weight = jnp.where(visible, jnp.exp(scores - new_max[..., None]), 0.0)
            rescale = jnp.exp(run_max - new_max)
            run_total = jnp.sum(weight, -1)
            run_acc = run_acc * rescale.T[..., None] + jnp.einsum(
                "hqk,kd->qhd",
                weight.astype(jnp.bfloat16),
                piece_values,
                preferred_element_type=jnp.float32,
            )
            return (new_max, run_total, run_acc)

        forward_start_state = (
            jnp.full((local_heads, span_rows), NEG_LARGE, jnp.float32),
            jnp.zeros((local_heads, span_rows), jnp.float32),
            jnp.zeros((span_rows, local_heads, HEAD_DIM), jnp.float32),
        )
        run_max, run_total, run_acc = over_keys(
            forward_head_keys, forward_head_values, absorb, forward_start_state
        )
        forward_attended = run_acc / run_total.T[..., None]
        forward_spread = run_max + jnp.log(run_total)
        forward_mixed_tok = to_tokens(
            forward_attended.astype(jnp.bfloat16).reshape(span_rows, 1, q_width)
        ).reshape(per_device, HEADS * HEAD_DIM)
        forward_hidden_in = forward_values_in + plain_dot(forward_mixed_tok, wo_full)
        normed_two = scaled(forward_hidden_in, gain_f).astype(jnp.bfloat16)
        forward_kept_rows = spread_rows(normed_two)
        forward_gate_pre = times_trans(forward_kept_rows, wg_use)
        forward_up_pre = times_trans(forward_kept_rows, wu_use)
        hidden_act = (jax.nn.silu(forward_gate_pre) * forward_up_pre).astype(jnp.bfloat16)
        branch = fold_rows(plain_dot(hidden_act, wd_use))
        result = (forward_hidden_in + branch).astype(jnp.bfloat16)
        forward_saved = (
            input_now,
            forward_head_query,
            forward_head_keys,
            forward_head_values,
            forward_attended,
            forward_spread,
            forward_mixed_tok,
            forward_hidden_in,
            forward_kept_rows,
            forward_gate_pre,
            forward_up_pre,
        )
        result, saved = (result, forward_saved)
        results.append(result)
        stored.append(saved)
        if tick_index < n_micro:
            arrived_x = shifted(result, "section", 1)
    returned = zero_rows
    grads_back = []
    row_lists = []
    gain_total = None
    ffn_total = None
    for tick_index in range(n_micro + 1):
        own_rows = cotangent[tick_index] if tick_index < n_micro else zero_rows
        grad_now = jnp.where(section_idx == 1, own_rows, returned)
        batch_index = jnp.clip(tick_index - 1 + section_idx, 0, n_micro - 1)
        early_saved = stored[max(tick_index - 1, 0)]
        late_saved = stored[min(tick_index + 1, n_micro)]
        saved = jax.tree.map(
            lambda early_val, late_val: jnp.where(section_idx == 0, early_val, late_val),
            early_saved,
            late_saved,
        )
        (
            input_bf,
            head_query,
            backward_head_keys,
            backward_head_values,
            attended,
            spread,
            mixed_tok,
            hidden_in,
            kept_rows,
            gate_pre,
            up_pre,
        ) = saved
        backward_place_row, backward_token_places, backward_span_places = place_sets(batch_index)
        values_in = input_bf.astype(jnp.float32)
        normed_one = scaled(values_in, gain_a).astype(jnp.bfloat16)
        grad_all = spread_rows(grad_now)
        ffn_terms, d_partial = ffn_back(
            grad_all, kept_rows, gate_pre, up_pre, wg_use, wu_use, wd_use
        )
        d_normed_two = fold_rows(d_partial)
        grad_gf, d_hidden = norm_back(hidden_in, gain_f, d_normed_two)
        d_hidden = d_hidden + grad_now.astype(jnp.float32)
        d_branch = d_hidden.astype(jnp.bfloat16)
        d_mixed = times_trans(d_branch, wo_full).astype(jnp.bfloat16)
        d_att = to_heads(d_mixed.reshape(per_device, n_seq, q_width))[:, 0].reshape(
            span_rows, local_heads, HEAD_DIM
        )
        offset = jnp.sum(d_att.astype(jnp.float32) * attended, -1).T

        def collect(state_in, key_piece, start_row):
            piece_keys, piece_values = key_piece
            visible = backward_place_row[None, None, :] <= backward_span_places[None, :, None]
            scores = (
                jnp.einsum(
                    "qhd,kd->hqk", head_query, piece_keys, preferred_element_type=jnp.float32
                )
                * attn_scale
            )
            probs = jnp.where(visible, jnp.exp(scores - spread[..., None]), 0.0)
            d_probs = jnp.einsum(
                "qhd,kd->hqk", d_att, piece_values, preferred_element_type=jnp.float32
            )
            d_score = (probs * (d_probs - offset[..., None]) * attn_scale).astype(jnp.bfloat16)
            d_query_acc = jnp.einsum(
                "hqk,kd->qhd", d_score, piece_keys, preferred_element_type=jnp.float32
            )
            key_part = jnp.einsum(
                "hqk,qhd->kd", d_score, head_query, preferred_element_type=jnp.float32
            )
            value_part = jnp.einsum(
                "hqk,qhd->kd", probs.astype(jnp.bfloat16), d_att, preferred_element_type=jnp.float32
            )
            return (d_query_acc, key_part, value_part)

        start_state = (
            jnp.zeros((span_rows, local_heads, HEAD_DIM), jnp.float32),
            jnp.zeros((total_len, HEAD_DIM), jnp.float32),
            jnp.zeros((total_len, HEAD_DIM), jnp.float32),
        )
        d_query_acc, d_keys_all, d_values_all = over_keys(
            backward_head_keys, backward_head_values, collect, start_state
        )
        own_keys = lax.psum_scatter(
            d_keys_all.astype(jnp.bfloat16), "shard", scatter_dimension=0, tiled=True
        ).astype(jnp.float32)
        own_values = lax.psum_scatter(
            d_values_all.astype(jnp.bfloat16), "shard", scatter_dimension=0, tiled=True
        ).astype(jnp.float32)
        d_query_head = rotate(d_query_acc, backward_span_places, -1.0).astype(jnp.bfloat16)
        d_query = to_tokens(d_query_head.reshape(span_rows, 1, q_width)).reshape(
            per_device, HEADS * HEAD_DIM
        )
        own_keys = rotate(own_keys[:, None, :], backward_span_places, -1.0)[:, 0]
        back_kv = lax.all_to_all(
            jnp.concatenate([own_keys, own_values], -1)[:, None, :].astype(jnp.bfloat16),
            "seq",
            split_axis=0,
            concat_axis=1,
            tiled=True,
        ).astype(jnp.float32)
        back_kv = jnp.sum(back_kv.reshape(per_device, KV_HEADS, kv_repeat, 2 * HEAD_DIM), 2)
        d_key = (
            back_kv[..., :HEAD_DIM].reshape(per_device, KV_HEADS * HEAD_DIM).astype(jnp.bfloat16)
        )
        d_value = (
            back_kv[..., HEAD_DIM:].reshape(per_device, KV_HEADS * HEAD_DIM).astype(jnp.bfloat16)
        )
        d_normed_one = (
            plain_dot(d_query, wq_full) + plain_dot(d_key, wk_full) + plain_dot(d_value, wv_full)
        )
        grad_ga, d_input = norm_back(values_in, gain_a, d_normed_one)
        d_input = d_input + d_hidden
        gain_terms = (grad_ga, grad_gf)
        row_terms = (d_query, d_key, d_value, normed_one, mixed_tok, d_branch)
        d_input, gain_terms, row_terms, ffn_terms = (
            d_input.astype(jnp.bfloat16),
            gain_terms,
            row_terms,
            ffn_terms,
        )
        grads_back.append(d_input)
        row_lists.append(row_terms)
        if tick_index < n_micro:
            returned = shifted(d_input, "section", -1)
        if gain_total is None:
            gain_total = gain_terms
            ffn_total = ffn_terms
        else:
            gain_total = jax.tree.map(jnp.add, gain_total, gain_terms)
            ffn_total = jax.tree.map(jnp.add, ffn_total, ffn_terms)
    joined = [
        jnp.concatenate([row_set[index_val] for row_set in row_lists], 0) for index_val in range(6)
    ]
    grad_wq = outer_sum(joined[0], joined[3])
    grad_wk = outer_sum(joined[1], joined[3])
    grad_wv = outer_sum(joined[2], joined[3])
    grad_wo = outer_sum(joined[4], joined[5])
    attn_owned = (
        lax.psum_scatter(gain_total[0], ("shard", "seq"), scatter_dimension=0, tiled=True),
        lax.psum_scatter(gain_total[1], ("shard", "seq"), scatter_dimension=0, tiled=True),
        lax.psum_scatter(grad_wq, ("shard", "seq"), scatter_dimension=0, tiled=True),
        lax.psum_scatter(grad_wk, ("shard", "seq"), scatter_dimension=0, tiled=True),
        lax.psum_scatter(grad_wv, ("shard", "seq"), scatter_dimension=0, tiled=True),
        lax.psum_scatter(grad_wo, ("shard", "seq"), scatter_dimension=0, tiled=True),
    )
    outputs = lax.dynamic_slice_in_dim(jnp.stack(results), section_idx, n_micro, 0)[None]
    input_grads = lax.dynamic_slice_in_dim(jnp.stack(grads_back), 1 - section_idx, n_micro, 0)[None]
    return (
        outputs,
        input_grads,
        attn_owned[0][None],
        attn_owned[2][None],
        attn_owned[3][None],
        attn_owned[4][None],
        attn_owned[5][None],
        attn_owned[1][None],
        ffn_total[0][None],
        ffn_total[1][None],
        ffn_total[2][None],
    )


LOW = jnp.bfloat16
FULL = jnp.float32
MESH = pl.DeviceIdType.MESH
RING = 4
CHIPS = 2 * RING
SPLIT = 2
LAG = (0, 0, 1, 2, 3)
PLACE = 128
ORDER = ((2, 1), (1, 1), (3, 1), (0, 1), (2, 0), (1, 0), (3, 0), (0, 0))
IN_VMEM = pl.BlockSpec(memory_space=pltpu.VMEM)
IN_HBM = pl.BlockSpec(memory_space=pltpu.HBM)
IN_SMEM = pl.BlockSpec(memory_space=pltpu.SMEM)


class Site:
    def __init__(self):
        self.section = lax.axis_index("section")
        self.z = lax.axis_index("shard")
        member = lax.axis_index("seq")
        self.y = lax.div(member, 2)
        self.core = lax.rem(member, 2)
        self.up = (self.section, lax.rem(self.z + 1, RING), member)
        self.down = (self.section, lax.rem(self.z + RING - 1, RING), member)
        self.across = (self.section, self.z, (1 - self.y) * 2 + self.core)
        self.sibling = (self.section, self.z, self.y * 2 + 1 - self.core)
        self.corner = (self.section, self.z, (1 - self.y) * 2 + 1 - self.core)
        self.opposite = (self.section, lax.rem(self.z + 2, RING), member)
        self.partner = (1 - self.section, self.z, member)
        self.member = member

    def chip(self, along_z, along_y):
        return lax.rem(self.z + along_z, RING) * 2 + lax.rem(self.y + along_y, 2)


class Links:
    def __init__(self, send, recv, site):
        self.send, self.recv, self.site = send, recv, site
        self.sent = []

    def copy(self, index, src, dst, device):
        return pltpu.make_async_remote_copy(
            src_ref=src,
            dst_ref=dst,
            send_sem=self.send.at[index],
            recv_sem=self.recv.at[index],
            device_id=device,
            device_id_type=MESH,
        )

    def go(self, index, src, dst, device):
        copy = self.copy(index, src, dst, device)
        copy.start()
        self.sent.append(copy)

    def got(self, index, where):
        self.copy(index, where, where, self.site.sibling).wait_recv()
        return where

    def close(self):
        for copy in self.sent:
            copy.wait_send()


def greet(site):
    barrier = pltpu.get_barrier_semaphore()
    devices = (
        site.up, site.down, site.across, site.sibling, site.corner, site.opposite, site.partner
    )
    for device in devices:
        pl.semaphore_signal(barrier, inc=1, device_id=device, device_id_type=MESH)
    pl.semaphore_wait(barrier, len(devices))


SPREAD_SEMS = 7 * SPLIT + CHIPS
FOLD_SEMS = 7 * SPLIT + CHIPS
SMALL_SEMS = 11
COPY_SEMS = 48
CROSS_SEMS = 32
PIECE = 128


class Spread:
    def __init__(self, site, held, links, use):
        self.site, self.held, self.links, self.use = site, held, links, use
        self.size = held.shape[2] // SPLIT
        self.up, self.down, self.over, self.relay, self.y_below, self.y_above, self.y_far = (
            k * SPLIT for k in range(7)
        )
        self.along = ((0, 0), (3, 0), (1, 0), (0, 1), (2, 0), (3, 1), (1, 1), (2, 1))

    def piece(self, slot, part):
        site = self.site
        rows = pl.ds(part * self.size, self.size)
        return self.held.at[site.chip(*self.along[slot]), site.core, rows]

    def block(self, slot, core):
        return self.held.at[self.site.chip(*self.along[slot]), core]

    def go(self, index, where, device):
        self.links.go(index, where, where, device)

    def share(self, slot):
        self.go(7 * SPLIT + slot, self.block(slot, self.site.core), self.site.sibling)

    def consume(self, *slots):
        for slot in slots:
            self.links.got(7 * SPLIT + slot, self.block(slot, 1 - self.site.core))
            self.use(self.site.chip(*self.along[slot]))

    def own(self, part):
        where = self.piece(0, part)
        self.go(self.up + part, where, self.site.up)
        self.go(self.down + part, where, self.site.down)
        self.go(self.over + part, where, self.site.across)

    def relays(self, part):
        came = self.links.got(self.up + part, self.piece(1, part))
        if part % 2 == 0:
            self.go(self.relay + part, came, self.site.up)
        self.go(self.y_below + part, came, self.site.across)
        came = self.links.got(self.down + part, self.piece(2, part))
        if part % 2 == 1:
            self.go(self.relay + part, came, self.site.down)
        self.go(self.y_above + part, came, self.site.across)

    def far(self, part):
        came = self.links.got(self.relay + part, self.piece(4, part))
        self.go(self.y_far + part, came, self.site.across)

    def after_relays(self):
        self.share(1)
        self.share(2)
        for part in range(SPLIT):
            self.links.got(self.over + part, self.piece(3, part))
        self.share(3)

    def tail(self, consume=True, first=0):
        def take(*slots):
            if consume:
                self.consume(*slots)

        self.share(4)
        take(*range(first, 3))
        for part in range(SPLIT):
            self.links.got(self.y_below + part, self.piece(5, part))
            self.links.got(self.y_above + part, self.piece(6, part))
        self.share(5)
        self.share(6)
        take(3, 4)
        for part in range(SPLIT):
            self.links.got(self.y_far + part, self.piece(7, part))
        self.share(7)
        take(5, 6, 7)
        if not consume:
            for slot in range(CHIPS):
                self.links.got(7 * SPLIT + slot, self.block(slot, 1 - self.site.core))

    def rest(self, consume=True):
        self.after_relays()
        for part in range(SPLIT):
            self.far(part)
        self.tail(consume)


class Fold:
    def __init__(self, site, part_of, buffers, links):
        self.site, self.part_of, self.links = site, part_of, links
        self.mine, self.pass_out, self.pass_in, self.stage, self.land = buffers
        self.rows = self.mine.shape[1]
        self.size = self.rows // SPLIT
        self.over = CHIPS
        self.relay, self.up, self.down = (CHIPS + (4 + k) * SPLIT for k in range(3))

    def where(self, part):
        return pl.ds(part * self.size, self.size)

    def came(self, index, where):
        return self.links.got(index, where)[...].astype(FULL)

    def compute(self, step):
        both = self.part_of(self.site.chip(*ORDER[step]))
        self.pass_out[step] = both[: self.rows].astype(LOW)
        self.links.go(step, self.pass_out.at[step], self.pass_in.at[step], self.site.sibling)
        self.mine[step] = both[self.rows :]

    def settle(self, step):
        self.mine[step] += self.came(step, self.pass_in.at[step])

    def send(self, index, slot, part, value, device):
        where = self.where(part)
        self.stage[slot, where] = value.astype(LOW)
        self.links.go(index, self.stage.at[slot, where], self.land.at[slot, where], device)

    def send_over(self, step, part):
        value = self.mine[step, self.where(part)]
        self.send(self.over + step * SPLIT + part, step, part, value, self.site.across)

    def start(self):
        self.compute(0)
        self.compute(1)
        for step in range(4):
            self.settle(step)
            self.send_over(step, 0)
            self.compute(step + 2)
        for part in range(1, SPLIT):
            for step in range(4):
                self.send_over(step, part)
        self.compute(6)
        self.compute(7)
        for step in range(4, CHIPS):
            self.settle(step)

    def pass_on(self, part):
        where = self.where(part)
        value = self.mine[4, where] + self.came(self.over + part, self.land.at[0, where])
        device = self.site.up if part % 2 == 0 else self.site.down
        self.send(self.relay + part, 4, part, value, device)

    def up_down(self, part):
        where = self.where(part)
        for step, base, device in ((5, self.up, self.site.up), (6, self.down, self.site.down)):
            from_y = self.over + (step - 4) * SPLIT + part
            value = self.mine[step, where] + self.came(from_y, self.land.at[step - 4, where])
            if part % 2 == step - 5:
                value = value + self.came(self.relay + part, self.land.at[4, where])
            self.send(base + part, step, part, value, device)

    def final(self, part):
        where = self.where(part)
        value = self.mine[7, where] + self.came(
            self.over + 3 * SPLIT + part, self.land.at[3, where]
        )
        value = value + self.came(self.up + part, self.land.at[5, where])
        return value + self.came(self.down + part, self.land.at[6, where])


def fold_spread(fold, spread, local, idle):
    def finish(part):
        rows = local(fold.final(part), fold.where(part))
        if spread is not None:
            site = spread.site
            spread.held[site.chip(0, 0), site.core, fold.where(part)] = rows
            spread.own(part)

    fold.start()
    idle(3)
    last = SPLIT - 1
    for tick in range(SPLIT + LAG[-1]):
        steps = [tick - lag for lag in LAG]
        if 0 <= steps[0] < SPLIT:
            fold.pass_on(steps[0])
        if 0 <= steps[1] < SPLIT:
            fold.up_down(steps[1])
        if 0 <= steps[2] < SPLIT:
            finish(steps[2])
        if spread is not None:
            if steps[2] == last:
                spread.share(0)
            if 0 <= steps[3] < SPLIT:
                spread.relays(steps[3])
            if steps[3] == last:
                spread.after_relays()
            if 0 <= steps[4] < SPLIT:
                spread.far(steps[4])
            if steps[2] == last + 1:
                spread.consume(0)
        idle(3)
    if spread is not None:
        idle(10)
        spread.tail(first=1)
        spread.links.close()
    else:
        idle(10)
    fold.links.close()


class Cross:
    def __init__(self, n):
        self.site = n.site
        self.links = Links(n.cross_send, n.cross_recv, n.site)
        self.begun = []
        self.count = 0

    def where(self, layer, receives, action):
        if layer is None:
            action()
        else:
            pl.when((self.site.section == layer) == receives)(action)

    def send(self, src, dst, layer=None):
        rows = src.shape[0]
        pieces = []
        start = 0
        while start < rows:
            size = min(PIECE, rows - start)
            where = pl.ds(start, size)
            pieces.append(
                self.links.copy(self.count, src.at[where], dst.at[where], self.site.partner)
            )
            self.count += 1
            start += size

        def begin():
            for copy in pieces:
                copy.start()

        self.where(layer, False, begin)
        self.begun.append([pieces, layer, False])
        return len(self.begun) - 1

    def wait(self, index):
        pieces, layer, landed = self.begun[index]

        def arrive():
            for copy in pieces:
                copy.wait_recv()

        if not landed:
            self.begun[index][2] = True
            self.where(layer, True, arrive)

    def close(self):
        for index in range(len(self.begun)):
            self.wait(index)
        for pieces, layer, _ in self.begun:

            def leave():
                for copy in pieces:
                    copy.wait_send()

            self.where(layer, False, leave)


class Copies:
    def __init__(self, n):
        self.n, self.count, self.open = n, 0, []

    def sem(self):
        self.count += 1
        return self.n.copy_sem.at[self.count - 1]

    def start(self, src, dst):
        copy = pltpu.make_async_copy(src, dst, self.sem())
        copy.start()
        self.open.append(copy)
        return copy

    def pick(self, own, other, dst, layer):
        sem = self.sem()
        from_own = pltpu.make_async_copy(own, dst, sem)
        from_other = pltpu.make_async_copy(other, dst, sem)
        pl.when(self.n.site.section == layer)(from_own.start)
        pl.when(self.n.site.section != layer)(from_other.start)
        self.open.append(from_own)
        return from_own

    def wait(self, *copies):
        for copy in copies:
            if any(copy is other for other in self.open):
                self.open = [other for other in self.open if other is not copy]
                copy.wait()

    def close(self):
        self.wait(*list(self.open))


def kernel_of(body, names, *refs):
    n = types.SimpleNamespace(**dict(zip(names, refs)))
    n.site = Site()
    n.copies = Copies(n)
    n.cross = Cross(n)
    body(n)
    n.cross.close()
    n.copies.close()


def launch(name, ident, body, scalars, inputs, outputs, scratch):
    scratch = dict(
        scratch,
        copy_sem=pltpu.SemaphoreType.DMA((COPY_SEMS,)),
        cross_send=pltpu.SemaphoreType.DMA((CROSS_SEMS,)),
        cross_recv=pltpu.SemaphoreType.DMA((CROSS_SEMS,)),
    )
    names = [*scalars, *inputs, *outputs, *scratch]
    results = pl.pallas_call(
        functools.partial(kernel_of, body, names),
        out_shape=[jax.ShapeDtypeStruct(*value) for value in outputs.values()],
        in_specs=[IN_SMEM] * len(scalars) + [IN_HBM] * len(inputs),
        out_specs=[IN_HBM] * len(outputs),
        scratch_shapes=list(scratch.values()),
        compiler_params=pltpu.CompilerParams(
            collective_id=ident, has_side_effects=True, vmem_limit_bytes=60 * 2**20
        ),
        cost_estimate=pl.CostEstimate(flops=2**37, bytes_accessed=2**23, transcendentals=0),
        name=name,
    )(*scalars.values(), *inputs.values())
    return types.SimpleNamespace(**dict(zip(outputs, results)))


def fold_buffers(full):
    return dict(
        mine=pltpu.VMEM((CHIPS, *full), FULL),
        pass_out=pltpu.VMEM((CHIPS, *full), LOW),
        pass_in=pltpu.VMEM((CHIPS, *full), LOW),
        stage=pltpu.VMEM((CHIPS - 1, *full), LOW),
        land=pltpu.VMEM((CHIPS - 1, *full), LOW),
        fold_send=pltpu.SemaphoreType.DMA((FOLD_SEMS,)),
        fold_recv=pltpu.SemaphoreType.DMA((FOLD_SEMS,)),
    )


def fold_of(n, part_of):
    buffers = (n.mine, n.pass_out, n.pass_in, n.stage, n.land)
    return Fold(n.site, part_of, buffers, Links(n.fold_send, n.fold_recv, n.site))


def spread_of(n, held, send, recv, use, kept=None):
    def take(chip):
        block = held[chip]
        use(chip, block.reshape(block.shape[0] * block.shape[1], block.shape[2]))
        if kept is not None:
            n.copies.start(held.at[chip], kept.at[chip])

    return Spread(n.site, held, Links(send, recv, n.site), take)


def spread_sems(*names):
    return {name: pltpu.SemaphoreType.DMA((SPREAD_SEMS,)) for name in names}


def no_idle(count):
    pass


def rows_of(ref, chip, site):
    return jnp.concatenate([ref[chip, 1 - site.core], ref[chip, site.core]], 0)


def put(ref, chip, value):
    ref[chip] = value.astype(LOW).reshape(ref.shape[1:])


def gate_chunk(n, chip, rows):
    gate_pre = times_trans(rows, n.w_g[...])
    up_pre = times_trans(rows, n.w_u[...])
    sig = jax.nn.sigmoid(gate_pre)
    silu_val = gate_pre * sig
    put(n.act, chip, silu_val * up_pre)
    return up_pre * sig * (1.0 + gate_pre * (1.0 - sig)), silu_val


def norm_back_rows(values, gain_vec, grad_in):
    factor = lax.rsqrt(jnp.mean(values * values, -1, keepdims=True) + EPSILON)
    gain_grad = jnp.sum(grad_in * values * factor, 0, keepdims=True)
    mean_term = jnp.mean(grad_in * gain_vec * values, -1, keepdims=True)
    return (
        gain_grad,
        factor * gain_vec * grad_in - values * (factor * factor * factor) * mean_term,
    )


def swap_halves(value):
    width = value.shape[1]
    half = HEAD_DIM // 2
    lane = lax.broadcasted_iota(jnp.int32, value.shape, 1)
    return jnp.where(
        lax.rem(lane, HEAD_DIM) < half,
        pltpu.roll(value, width - half, 1),
        pltpu.roll(value, half, 1),
    )


def stacked(pair):
    return jnp.concatenate([pair[:, :HEAD_DIM], pair[:, HEAD_DIM:]], 0)


def side_by_side(turned):
    return jnp.concatenate([turned[:, :PLACE], turned[:, PLACE:]], 0).T


def hide_later(scores, fill):
    last = scores[-PLACE:]
    key = lax.broadcasted_iota(jnp.int32, last.shape, 0)
    query = lax.rem(lax.broadcasted_iota(jnp.int32, last.shape, 1), PLACE)
    last = jnp.where(key <= query, last, fill)
    if scores.shape[0] == PLACE:
        return last
    return jnp.concatenate([scores[:-PLACE], last], 0)


def turn_of(turns, place):
    near, far = pl.ds(0, PLACE), pl.ds(PLACE + place, 1)
    cos_near, sin_near = turns[0, near], turns[1, near]
    cos_far, sin_far = turns[0, far], turns[1, far]
    cosine = cos_near * cos_far - sin_near * sin_far
    sine = sin_near * cos_far + cos_near * sin_far
    lane = lax.broadcasted_iota(jnp.int32, cosine.shape, 1)
    sine = jnp.where(lax.rem(lane, HEAD_DIM) < HEAD_DIM // 2, -sine, sine)
    keyed = lane < HEAD_DIM
    return (
        jnp.concatenate([cosine, jnp.where(keyed, cosine, 1.0)], 1),
        jnp.concatenate([sine, jnp.where(keyed, sine, 0.0)], 1),
    )


def attend(n):
    q_width = 2 * HEAD_DIM
    scale = jnp.asarray(1.0 / math.sqrt(HEAD_DIM), LOW)
    for place in range(CHIPS):
        at = pl.ds(place * PLACE, PLACE)
        value = n.qkv[n.block_at[place]]
        cosine, sine = turn_of(n.turns_v, place)
        value = (value * cosine + swap_halves(value) * sine).astype(LOW)
        n.turned_v[at, :q_width] = value[:, :q_width] * scale
        n.turned_v[at, q_width:] = value[:, q_width:]
        n.values_t[:, at] = value[:, q_width:].astype(FULL).T[HEAD_DIM:].astype(LOW)
    for place in range(CHIPS):
        at = pl.ds(place * PLACE, PLACE)
        keys = pl.ds(0, (place + 1) * PLACE)
        query = stacked(n.turned_v[at, :q_width])
        scores = times_trans(n.turned_v[keys, q_width : q_width + HEAD_DIM], query)
        scores = hide_later(scores, NEG_LARGE)
        top = jnp.max(scores, 0, keepdims=True)
        weight = jnp.exp(scores - top)
        total = jnp.sum(weight, 0, keepdims=True)
        out = plain_dot(n.values_t[:, keys], weight.astype(LOW)) / total
        n.attended_v[place] = side_by_side(out)
        n.spread_v[pl.ds(place, 1)] = top + jnp.log(total)
    for block in range(CHIPS):
        put(n.mixed_v, block, n.attended_v[n.order[block]])
    n.copies.start(n.turned_v, n.turned)
    n.copies.start(n.attended_v, n.attended)
    n.copies.start(n.spread_v, n.spread)
    n.copies.start(n.mixed_v, n.mixed)


def attend_back(n):
    q_width = 2 * HEAD_DIM
    n.d_key[...] = jnp.zeros_like(n.d_key)
    n.d_value[...] = jnp.zeros_like(n.d_value)
    for place in range(CHIPS):
        at = pl.ds(place * PLACE, PLACE)
        n.keys_t[:, at] = n.turned_v[at, q_width:].astype(FULL).T[:HEAD_DIM].astype(LOW)
    for place in range(CHIPS):
        at = pl.ds(place * PLACE, PLACE)
        keys = pl.ds(0, (place + 1) * PLACE)
        d_out = n.d_mixed[n.block_at[place]]
        product = (d_out.astype(FULL) * n.attended_v[place]).T
        offset = jnp.concatenate(
            [
                jnp.sum(product[:HEAD_DIM], 0, keepdims=True),
                jnp.sum(product[HEAD_DIM:], 0, keepdims=True),
            ],
            1,
        )
        d_out = stacked(d_out)
        query = stacked(n.turned_v[at, :q_width])
        scores = times_trans(n.turned_v[keys, q_width : q_width + HEAD_DIM], query)
        scores = hide_later(scores, NEG_LARGE)
        probs = jnp.exp(scores - n.spread_v[pl.ds(place, 1)])
        d_probs = times_trans(n.turned_v[keys, q_width + HEAD_DIM :], d_out)
        d_scores = (probs * (d_probs - offset)).astype(LOW)
        n.d_key[keys] += plain_dot(d_scores, query)
        n.d_value[keys] += plain_dot(probs.astype(LOW), d_out)
        n.d_query[at] = side_by_side(plain_dot(n.keys_t[:, keys], d_scores)) * (
            1.0 / math.sqrt(HEAD_DIM)
        )
    for place in range(CHIPS):
        at = pl.ds(place * PLACE, PLACE)
        value = jnp.concatenate([n.d_query[at], n.d_key[at], n.d_value[at]], 1)
        cosine, sine = turn_of(n.turns_v, place)
        value = value * cosine - swap_halves(value) * sine
        n.d_turned[place] = value.astype(LOW)
    for block in range(CHIPS):
        put(n.d_qkv, block, n.d_turned[n.order[block]])


def gather_small(n):
    site = n.site
    links = n.links_small = Links(n.small_send, n.small_recv, site)
    links.go(0, n.gains_mine, n.gains_x, site.partner)
    links.go(1, n.kv_mine, n.kv_x, site.partner)
    links.got(0, n.gains_x)
    own, came = n.gains_mine[...], n.gains_x[...]
    first = site.section == 0
    n.gains_all[site.z, site.member] = jnp.concatenate(
        [
            jnp.where(first, own, came)[:2],
            jnp.where(first, came, own)[:2],
            jnp.zeros((4, own.shape[1]), FULL),
        ],
        0,
    )
    peers = (site.sibling, site.across, site.corner)
    mine = n.gains_all.at[site.z, site.member]
    for index, device in enumerate(peers):
        links.go(2 + index, mine, mine, device)
    for index, device in enumerate(peers):
        links.got(2 + index, n.gains_all.at[site.z, device[2]])
    shard = n.gains_all.at[site.z]
    for index, device in enumerate((site.up, site.down, site.opposite)):
        links.go(5 + index, shard, shard, device)


def gather_small_keys(n):
    site, links = n.site, n.links_small
    links.got(1, n.kv_x)
    n.kv_all[site.member, site.section] = n.kv_mine[...]
    n.kv_all[site.member, 1 - site.section] = n.kv_x[...]
    mine = n.kv_all.at[site.member]
    for index, device in enumerate((site.sibling, site.across, site.corner)):
        links.go(8 + index, mine, mine, device)


def gather_small_end(n):
    site, links = n.site, n.links_small
    for index, along_z in enumerate((RING - 1, 1, 2)):
        links.got(5 + index, n.gains_all.at[lax.rem(site.z + along_z, RING)])
    for index, device in enumerate((site.sibling, site.across, site.corner)):
        links.got(8 + index, n.kv_all.at[device[2]])
    links.close()
    n.gains_v[...] = jnp.concatenate(
        [n.gains_all[shard, seq] for shard in range(RING) for seq in range(RING)], 1
    )
    for layer in range(2):
        for index in range(2):
            rows = n.kv_all[:, layer, index]
            n.w_kv[layer, pl.ds(index * HEAD_DIM, HEAD_DIM)] = rows.reshape(
                HEAD_DIM, rows.shape[-1]
            )
    n.copies.start(n.gains_v, n.gains)
    n.copies.start(n.w_kv, n.kv_rows)


def forward_first(n):
    site, copies, cross = n.site, n.copies, n.cross
    own = (site.chip(0, 0), site.core)
    small = [
        copies.start(n.gains_own, n.gains_mine),
        copies.start(n.w_key, n.kv_mine.at[0]),
        copies.start(n.w_value, n.kv_mine.at[1]),
    ]
    rows_copy = copies.pick(n.inputs.at[0], n.inputs.at[1], n.held.at[own], 0)
    top_copy = copies.pick(n.cotangent.at[0], n.cotangent.at[1], n.top_v, 0)
    turns_copy = copies.start(n.turns, n.turns_v)
    greet(site)
    copies.wait(*small)
    gather_small(n)
    at_query, at_out, at_gate, at_up, _ = (
        cross.send(*pair)
        for pair in (
            (n.w_query, n.x_query),
            (n.w_out, n.x_out),
            (n.w_gate, n.x_gate),
            (n.w_up, n.x_up),
            (n.w_down, n.x_down),
        )
    )
    copies.wait(rows_copy)

    def use_first(chip, rows):
        normed = scaled(rows.astype(FULL), n.gains_v[:1]).astype(LOW)
        n.normed[chip] = normed.reshape(n.normed.shape[1:])
        n.qkv[chip] = jnp.concatenate(
            [times_trans(normed, n.w_q[...]), times_trans(normed, n.w_kv[0])], 1
        )
        copies.start(n.normed.at[chip], n.rows_one.at[chip])

    spread = spread_of(n, n.held, n.spread_send, n.spread_recv, use_first)
    for part in range(SPLIT):
        spread.own(part)
    spread.share(0)
    gather_small_keys(n)
    for part in range(SPLIT):
        spread.relays(part)
    gather_small_end(n)
    spread.after_relays()
    cross.wait(at_query)
    query_copy = copies.pick(n.w_query, n.x_query, n.w_q, 0)
    for part in range(SPLIT):
        spread.far(part)
    copies.wait(query_copy)
    copies.wait(top_copy, turns_copy)
    top_copy = copies.start(n.top_v, n.top_all.at[own])
    spread.tail()
    spread.links.close()
    copies.wait(top_copy)
    top = spread_of(n, n.top_all, n.top_send, n.top_recv, None)
    for part in range(SPLIT):
        top.own(part)
    cross.wait(at_out)
    out_copy = copies.pick(n.w_out, n.x_out, n.w_o, 0)
    attend(n)
    top.share(0)
    copies.wait(out_copy)

    def part_of(chip):
        return plain_dot(rows_of(n.mixed_v, chip, site), n.w_o[...])

    def local(total, where):
        hidden_in = n.held[(*own, where)].astype(FULL) + total
        n.hidden_v[where] = hidden_in
        return scaled(hidden_in, n.gains_v[1:2]).astype(LOW)

    waiting = []

    def use_later(chip, rows):
        waiting.append(chip)

    def use_gate(chip):
        rows = n.held_two[chip].reshape(-1, n.held_two.shape[-1])
        gate_slope, up_slope = gate_chunk(n, chip, rows)
        put(n.gate_slope_v, chip, gate_slope)
        put(n.up_slope_v, chip, up_slope)

    def idle(count):
        if count == 10:
            for part in range(SPLIT):
                top.relays(part)

    spread = spread_of(
        n, n.held_two, n.spread_two_send, n.spread_two_recv, use_later, n.rows_two
    )
    fold_spread(fold_of(n, part_of), spread, local, idle)
    copies.start(n.hidden_v, n.hidden)
    top.after_relays()
    for part in range(SPLIT):
        top.far(part)
    cross.wait(at_gate)
    cross.wait(at_up)
    copies.wait(
        copies.pick(n.w_gate, n.x_gate, n.w_g, 0), copies.pick(n.w_up, n.x_up, n.w_u, 0)
    )
    for chip in waiting:
        use_gate(chip)
    for source, target in (
        (n.act, n.act_all), (n.gate_slope_v, n.gate_slope), (n.up_slope_v, n.up_slope)
    ):
        copies.start(source, target)
    top.tail(consume=False)
    top.links.close()


def forward_second(n):
    site, copies = n.site, n.copies
    first = [
        copies.start(n.act_prev, n.act_prev_v),
        copies.pick(n.w_down, n.x_down, n.w_d_prev, 0),
    ]
    rows_copies = [copies.start(n.hidden_prev, n.hidden_prev_v), copies.start(n.gains, n.gains_v)]
    qkv_copies = [
        copies.pick(n.w_query, n.x_query, n.w_in.at[pl.ds(0, 2 * HEAD_DIM)], 1),
        copies.start(n.kv_rows.at[1], n.w_in.at[pl.ds(2 * HEAD_DIM, 2 * HEAD_DIM)]),
        copies.start(n.turns, n.turns_v),
    ]
    later = [
        copies.pick(n.w_out, n.x_out, n.w_o, 1),
        copies.pick(n.w_gate, n.x_gate, n.w_g, 1),
        copies.pick(n.w_up, n.x_up, n.w_u, 1),
        copies.pick(n.w_down, n.x_down, n.w_d, 1),
        copies.start(n.top_all, n.top_held),
    ]
    greet(site)
    copies.wait(*first, *rows_copies)

    def part_of(chip):
        return plain_dot(rows_of(n.act_prev_v, chip, site), n.w_d_prev[...])

    def local(total, where):
        result = (n.hidden_prev_v[where] + total).astype(LOW)
        n.result_v[where] = result
        return scaled(result.astype(FULL), n.gains_v[2:3]).astype(LOW)

    def use_qkv(chip, rows):
        n.qkv[chip] = times_trans(rows, n.w_in[...])

    def settle(count):
        copies.wait(*qkv_copies)

    spread = spread_of(n, n.held, n.spread_send, n.spread_recv, use_qkv, n.rows_one)
    fold_spread(fold_of(n, part_of), spread, local, settle)
    copies.start(n.result_v, n.result)
    attend(n)
    copies.wait(*later)

    def part_of_two(chip):
        return plain_dot(rows_of(n.mixed_v, chip, site), n.w_o[...])

    def local_two(total, where):
        hidden_in = n.result_v[where].astype(FULL) + total
        n.hidden_v[where] = hidden_in
        return scaled(hidden_in, n.gains_v[3:4]).astype(LOW)

    def use_gate(chip, rows):
        gate_slope, up_slope = gate_chunk(n, chip, rows)
        d_act = times_trans(n.top_held[chip].reshape(rows.shape), n.w_d[...])
        put(n.d_gate_v, chip, d_act * gate_slope)
        put(n.d_up_v, chip, d_act * up_slope)

    spread = spread_of(
        n, n.held_two, n.spread_two_send, n.spread_two_recv, use_gate, n.rows_two
    )
    fold_spread(fold_of(n, part_of_two), spread, local_two, no_idle)
    for source, target in (
        (n.hidden_v, n.hidden), (n.act, n.act_all), (n.d_gate_v, n.d_gate), (n.d_up_v, n.d_up)
    ):
        copies.start(source, target)


def products(n, left, right, store, tile=512):
    count = math.prod(left.shape[:-1])
    for start in range(0, right.shape[-1], tile):
        where = pl.ds(start, tile)
        value = outer_sum(
            left[...].reshape(count, left.shape[-1]), right[:, :, :, where].reshape(count, tile)
        )
        store(where, value.astype(LOW))
        yield


def ffn_products(n, loads, made):
    n.copies.wait(*loads)
    for left, right, out in (
        (n.act, n.top_held, n.g_down_v),
        (n.d_gate_v, n.normed, n.g_gate_v),
        (n.d_up_v, n.normed, n.g_up_v),
    ):

        def store(where, value):
            out[:, where] = value

        yield from products(n, left, right, store)
        made(out)


def in_products(n, loads, made):
    site = n.site
    n.copies.wait(*loads)

    def store_out(where, value):
        n.g_out_v[:, where] = value

    def store_in(where, value):
        query = n.g_query_v.shape[0]
        n.g_query_v[:, where] = value[:query]
        n.kv_mine[:, :, :, where] = value[query:].reshape(
            *n.kv_mine.shape[:3], value.shape[1]
        )

    yield from products(n, n.d_qkv, n.normed, store_in)
    made(n.g_query_v)
    peers = (site.sibling, site.across, site.corner)
    links = Links(n.kv_send, n.kv_recv, site)
    for index, device in enumerate(peers):
        links.go(index, n.kv_mine.at[:, device[2]], n.kv_came.at[index], device)
    yield from products(n, n.mixed_v, n.held, store_out)
    made(n.g_out_v)
    total = n.kv_mine[:, site.member].astype(FULL)
    for index in range(len(peers)):
        total = total + links.got(index, n.kv_came.at[index])[...].astype(FULL)
    n.g_kv_v[...] = total.astype(LOW)
    made(n.g_kv_v)
    links.close()


def fold_gains(n):
    site = n.site
    links = Links(n.gain_send, n.gain_recv, site)
    own = jnp.concatenate(
        [n.gain_grads[...], n.gain_later_v[...], jnp.zeros((4, n.gain_grads.shape[1]), FULL)], 0
    )
    width = n.gain_parts.shape[-1]
    for shard in range(RING):
        for seq in range(RING):
            start = (shard * RING + seq) * width
            n.gain_parts[seq, shard] = own[:, start : start + width]
    peers = (site.sibling, site.across, site.corner)
    for index, device in enumerate(peers):
        links.go(index, n.gain_parts.at[device[2]], n.gain_came.at[index], device)
    yield
    total = n.gain_parts[site.member]
    for index in range(3):
        total = total + links.got(index, n.gain_came.at[index])[...]
    n.gain_shards[...] = total
    for index, device in enumerate((site.up, site.down, site.opposite)):
        links.go(
            3 + index, n.gain_shards.at[device[1]], n.gain_last.at[index], device
        )
    yield
    total = n.gain_shards[site.z]
    for index in range(3):
        total = total + links.got(3 + index, n.gain_last.at[index])[...]
    n.gain_own[...] = total
    links.go(6, n.gain_own, n.gain_other, site.partner)
    yield
    total = n.gain_own[...] + links.got(6, n.gain_other)[...]
    n.gain_sums_v[...] = jnp.where(site.section == 0, total[:2], total[2:4])
    links.close()
    n.copies.start(n.gain_sums_v, n.gain_sums)


def backward(layer, n):
    site, copies, cross = n.site, n.copies, n.cross
    first = [
        copies.start(n.d_gate, n.d_gate_v),
        copies.start(n.d_up, n.d_up_v),
        copies.pick(n.w_gate, n.x_gate, n.w_g, layer),
        copies.pick(n.w_up, n.x_up, n.w_u, layer),
    ]
    rows_copies = [
        copies.start(n.hidden, n.hidden_v),
        copies.pick(n.cotangent.at[0], n.cotangent.at[1], n.top_v, 0)
        if layer == 1
        else copies.start(n.top_rows, n.top_v),
        copies.start(n.gains, n.gains_v),
        copies.pick(n.w_out, n.x_out, n.w_o, layer),
    ]
    loads = [
        copies.start(n.act_all, n.act),
        copies.start(n.top_all, n.top_held),
        copies.start(n.rows_two, n.normed),
    ]
    attn_copies = [
        copies.start(n.turns, n.turns_v),
        copies.start(n.turned, n.turned_v),
        copies.start(n.attended, n.attended_v),
        copies.start(n.spread, n.spread_v),
        copies.start(n.mixed, n.mixed_v),
        copies.pick(n.w_query, n.x_query, n.w_in.at[pl.ds(0, 2 * HEAD_DIM)], layer),
        copies.start(n.kv_rows.at[layer], n.w_in.at[pl.ds(2 * HEAD_DIM, 2 * HEAD_DIM)]),
        copies.start(n.x_rows, n.x_v)
        if layer == 1
        else copies.pick(n.inputs.at[0], n.inputs.at[1], n.x_v, 0),
    ]
    if layer == 1:
        next_copies = [
            copies.pick(n.w_down, n.x_down, n.w_d, 0),
            copies.start(n.gate_slope, n.gate_slope_v),
            copies.start(n.up_slope, n.up_slope_v),
        ]
    else:
        next_copies = [
            copies.pick(n.w_down, n.x_down, n.w_d, 1),
            copies.start(n.act_last, n.act_last_v),
            copies.start(n.hidden_last, n.hidden_last_v),
            copies.start(n.gain_later, n.gain_later_v),
        ]
    greet(site)
    if layer == 1:
        cross.send(n.x_rows, n.came_result_first, 0)
    else:
        cross.send(n.own_up_later, n.came_up_later, 1)
        cross.send(n.top_rows, n.came_input_later, 1)
    copies.wait(*first, *rows_copies)

    def made(out):
        target, came = {
            id(n.g_down_v): (n.own_down, n.came_down),
            id(n.g_gate_v): (n.own_gate, n.came_gate),
            id(n.g_up_v): (n.own_up, None if layer == 1 else n.came_up),
            id(n.g_out_v): (n.own_out, n.came_out),
            id(n.g_query_v): (n.own_query, n.came_query),
            id(n.g_kv_v): (n.own_kv, n.came_kv),
        }[id(out)]
        copies.start(out, target)
        if came is not None:
            cross.send(out, came, layer)

    def step_on(working):
        def idle(count):
            for _ in range(count):
                next(working, None)

        return idle

    def part_of(chip):
        return plain_dot(rows_of(n.d_gate_v, chip, site), n.w_g[...]) + plain_dot(
            rows_of(n.d_up_v, chip, site), n.w_u[...]
        )

    def add_gain(row, value, where):
        row = pl.ds(row, 1)
        n.gain_grads[row] = value if where.start == 0 else n.gain_grads[row] + value

    def local(total, where):
        gain_grad, d_hidden = norm_back_rows(
            n.hidden_v[where], n.gains_v[2 * layer + 1 : 2 * layer + 2], total
        )
        d_hidden = d_hidden + n.top_v[where].astype(FULL)
        add_gain(1, gain_grad, where)
        n.d_hidden[where] = d_hidden
        return d_hidden.astype(LOW)

    def use_d_mixed(chip, rows):
        n.d_mixed[chip] = times_trans(rows, n.w_o[...]).astype(LOW)

    working = ffn_products(n, loads, made)
    if layer == 0:
        step_on(working)(5)
    spread = spread_of(n, n.held, n.spread_send, n.spread_recv, use_d_mixed)
    fold_spread(fold_of(n, part_of), spread, local, step_on(working))
    for _ in working:
        pass
    normed_copy = copies.start(n.rows_one, n.normed)
    copies.wait(*attn_copies)
    attend_back(n)
    copies.wait(*next_copies)

    def part_of_two(chip):
        return plain_dot(rows_of(n.d_qkv, chip, site), n.w_in[...])

    def local_two(total, where):
        gain_grad, d_input = norm_back_rows(
            n.x_v[where].astype(FULL), n.gains_v[2 * layer : 2 * layer + 1], total
        )
        d_input = (d_input + n.d_hidden[where]).astype(LOW)
        add_gain(0, gain_grad, where)
        n.d_input_v[where] = d_input
        return d_input

    working = in_products(n, [normed_copy], made)
    if layer == 1:

        def use_d_act(chip, rows):
            d_act = times_trans(rows, n.w_d[...])
            for out, slope in ((n.d_gate_v, n.gate_slope_v), (n.d_up_v, n.up_slope_v)):
                put(out, chip, d_act * slope[chip].astype(FULL).reshape(d_act.shape))

        spread = spread_of(
            n, n.held_two, n.spread_two_send, n.spread_two_recv, use_d_act, n.top_next
        )
        fold_spread(fold_of(n, part_of_two), spread, local_two, step_on(working))
        for _ in working:
            pass
        for source, target in (
            (n.d_gate_v, n.d_gate_next), (n.d_up_v, n.d_up_next), (n.d_input_v, n.d_input),
            (n.gain_grads, n.gain_out),
        ):
            copies.start(source, target)
        return
    fold_spread(fold_of(n, part_of_two), None, local_two, step_on(working))
    for _ in working:
        pass
    copies.start(n.d_input_v, n.d_input)
    cross.send(n.d_input_v, n.came_input, 0)

    def part_of_last(chip):
        return plain_dot(rows_of(n.act_last_v, chip, site), n.w_d[...])

    def local_last(total, where):
        n.result_v[where] = (n.hidden_last_v[where] + total).astype(LOW)

    buffers = (n.mine, n.pass_out, n.pass_in_two, n.stage, n.land_two)
    links = Links(n.last_send, n.last_recv, site)
    gains_on = fold_gains(n)
    next(gains_on)
    fold_spread(
        Fold(site, part_of_last, buffers, links), None, local_last,
        lambda count: next(gains_on, None),
    )
    for _ in gains_on:
        pass
    copies.start(n.result_v, n.result)
    cross.send(n.result_v, n.came_result, 1)


def join_kernel(count, *refs):
    def take(number):
        nonlocal refs
        taken, refs = refs[:number], refs[number:]
        return taken

    own, came = (take(count), take(count)), (take(count), take(count))
    rows = (take(4), take(4))
    outs, row_outs = take(count + 1), take(2)
    own_at, came_at, sums = take(count), take(count), take(count)
    row_at, sems, out_sem, row_sem = refs
    section = lax.axis_index("section")

    def either(first, second):
        pl.when(section == 0)(first.start)
        pl.when(section != 0)(second.start)
        return first

    waits = []
    for index in range(count):
        for slot, (pair, target) in enumerate(((own, own_at), (came, came_at))):
            waits.append(
                either(
                    *(
                        pltpu.make_async_copy(
                            pair[layer][index], target[index], sems.at[2 * index + slot]
                        )
                        for layer in range(2)
                    )
                )
            )
    done = []
    row_waits = []
    for index, (own_a, own_b, came_a, came_b) in enumerate(rows):
        for slot, (first, second) in enumerate(((own_a, came_b), (came_a, own_b))):
            target, sem = row_at.at[index, slot], row_sem.at[2 * index + slot]
            row_waits.append(
                either(
                    pltpu.make_async_copy(first, target, sem),
                    pltpu.make_async_copy(second, target, sem),
                )
            )
    for copy in row_waits:
        copy.wait()
    for index, out in enumerate(row_outs):
        copy = pltpu.make_async_copy(row_at.at[index], out, row_sem.at[index])
        copy.start()
        done.append(copy)
    for index in range(count):
        waits[2 * index].wait()
        waits[2 * index + 1].wait()
        sums[index][...] = own_at[index][...].astype(FULL) + came_at[index][...].astype(FULL)
        if index < count - 1:
            parts = [(sums[index], outs[index])]
        else:
            parts = [(sums[index].at[pl.ds(k, 1)], outs[index + k]) for k in range(2)]
        for source, target in parts:
            copy = pltpu.make_async_copy(source, target, out_sem.at[len(done) - 2])
            copy.start()
            done.append(copy)
    for copy in done:
        copy.wait()


def join_all(own_a, own_b, came_a, came_b, results, input_grads):
    count = len(own_a)
    kept = [pltpu.VMEM(value.shape, LOW) for value in own_a]
    shapes = [value.shape for value in own_a]
    shapes = shapes[:-1] + [(1, *shapes[-1][1:])] * 2
    row_shape = jax.ShapeDtypeStruct((2, *results[0].shape), LOW)
    return pl.pallas_call(
        functools.partial(join_kernel, count),
        out_shape=[jax.ShapeDtypeStruct(value, FULL) for value in shapes] + [row_shape] * 2,
        in_specs=[IN_HBM] * (4 * count + 8),
        out_specs=[IN_HBM] * (count + 3),
        scratch_shapes=kept
        + kept
        + [pltpu.VMEM(value.shape, FULL) for value in own_a]
        + [
            pltpu.VMEM((2, *row_shape.shape), LOW),
            pltpu.SemaphoreType.DMA((2 * count,)),
            pltpu.SemaphoreType.DMA((count + 1,)),
            pltpu.SemaphoreType.DMA((4,)),
        ],
        compiler_params=pltpu.CompilerParams(vmem_limit_bytes=58 * 2**20),
        cost_estimate=pl.CostEstimate(flops=2**32, bytes_accessed=2**24, transcendentals=0),
        name="join_all",
    )(*own_a, *own_b, *came_a, *came_b, *results, *input_grads)


def relay_body(
    inputs,
    cotangent,
    positions,
    gain_attn,
    w_query,
    w_key,
    w_value,
    w_out,
    gain_ffn,
    w_gate,
    w_up,
    w_down,
):
    n_micro, per_device, model_width = inputs.shape
    n_seq = lax.axis_size("seq")
    n_shard = lax.axis_size("shard")
    members = n_seq * n_shard
    total_len = members * per_device
    section_idx = lax.axis_index("section")
    q_width = HEADS // members * HEAD_DIM
    in_width = q_width + 2 * HEAD_DIM
    hidden = w_down.shape[1]
    vmem = pltpu.VMEM

    def pick(first, second):
        return jnp.where(section_idx == 0, first, second)

    places = pick(positions[0], positions[1])
    gains_own = jnp.concatenate(
        [gain_attn, gain_ffn, jnp.zeros((6, gain_attn.shape[1]), gain_attn.dtype)], 0
    ).astype(FULL)
    own = dict(
        w_query=w_query[0], w_out=w_out[0], w_gate=w_gate[0], w_up=w_up[0], w_down=w_down[0]
    )

    order = (places.reshape(CHIPS, PLACE)[:, 0] // PLACE).astype(jnp.int32)
    numbers = jnp.arange(CHIPS, dtype=jnp.int32)
    block_at = jnp.sum(
        jnp.where(order[None, :] == numbers[:, None], numbers[None, :], 0), 1
    ).astype(jnp.int32)
    scalars = dict(block_at=block_at, order=order)
    half_dim = HEAD_DIM // 2
    inv_freq = THETA_BASE ** (-jnp.arange(half_dim, dtype=FULL) * (2.0 / HEAD_DIM))
    steps = jnp.concatenate([jnp.arange(PLACE), PLACE * jnp.arange(CHIPS)]).astype(FULL)
    angles = steps[:, None] * jnp.tile(inv_freq, 2 * q_width // HEAD_DIM)[None, :]
    turns = jnp.stack([jnp.cos(angles), jnp.sin(angles)])

    rows = (per_device, model_width)
    row_low, row_full = (rows, LOW), (rows, FULL)
    all_rows = ((CHIPS, 2, *rows), LOW)
    narrow = ((CHIPS, 2, per_device, hidden), LOW)
    wide = ((hidden, model_width), LOW)
    quarter = ((q_width, model_width), LOW)
    gain_row = ((8, model_width), FULL)
    kv_shape = (2, w_key.shape[1], model_width)
    small = gains_own.shape
    saved = dict(
        turned=((total_len, in_width), LOW),
        attended=((CHIPS, PLACE, q_width), FULL),
        spread=((CHIPS, 2 * PLACE), FULL),
        mixed=((CHIPS, 2, per_device, q_width), LOW),
    )
    saved_v = dict(
        turned_v=vmem(*saved["turned"]),
        attended_v=vmem(*saved["attended"]),
        spread_v=vmem(*saved["spread"]),
        mixed_v=vmem(*saved["mixed"]),
        turns_v=vmem(turns.shape, FULL),
    )
    attend_v = dict(
        **saved_v,
        qkv=vmem((CHIPS, PLACE, in_width), FULL),
        values_t=vmem((HEAD_DIM, total_len), LOW),
    )
    gates_v = dict(w_g=vmem(*wide), w_u=vmem(*wide))

    first = launch(
        "forward_first",
        0,
        forward_first,
        scalars,
        dict(
            inputs=inputs, cotangent=cotangent, gains_own=gains_own, w_key=w_key[0],
            w_value=w_value[0], turns=turns, **own,
        ),
        dict(
            x_query=quarter,
            x_out=quarter,
            x_gate=wide,
            x_up=wide,
            x_down=wide,
            gains=gain_row,
            kv_rows=((2, 2 * HEAD_DIM, model_width), LOW),
            top_all=all_rows,
            rows_one=all_rows,
            rows_two=all_rows,
            hidden=row_full,
            act_all=narrow,
            gate_slope=narrow,
            up_slope=narrow,
            **saved,
        ),
        dict(
            gains_mine=vmem(small, FULL),
            gains_x=vmem(small, FULL),
            gains_all=vmem((n_shard, n_seq, *small), FULL),
            gains_v=vmem(*gain_row),
            kv_mine=vmem(kv_shape, LOW),
            kv_x=vmem(kv_shape, LOW),
            kv_all=vmem((n_seq, 2, *kv_shape), LOW),
            w_kv=vmem((2, 2 * HEAD_DIM, model_width), LOW),
            small_send=pltpu.SemaphoreType.DMA((SMALL_SEMS,)),
            small_recv=pltpu.SemaphoreType.DMA((SMALL_SEMS,)),
            held=vmem(*all_rows),
            held_two=vmem(*all_rows),
            normed=vmem(*all_rows),
            w_q=vmem(*quarter),
            w_o=vmem(*quarter),
            hidden_v=vmem(*row_full),
            top_v=vmem(*row_low),
            act=vmem(*narrow),
            gate_slope_v=vmem(*narrow),
            up_slope_v=vmem(*narrow),
            **gates_v,
            **attend_v,
            **fold_buffers(rows),
            **spread_sems(
                "spread_send", "spread_recv", "spread_two_send", "spread_two_recv", "top_send",
                "top_recv",
            ),
        ),
    )
    crossed = dict(
        **own,
        x_query=first.x_query,
        x_out=first.x_out,
        x_gate=first.x_gate,
        x_up=first.x_up,
        x_down=first.x_down,
        gains=first.gains,
        kv_rows=first.kv_rows,
        turns=turns,
    )
    second = launch(
        "forward_second",
        1,
        forward_second,
        scalars,
        dict(
            act_prev=first.act_all, hidden_prev=first.hidden, top_all=first.top_all, **crossed
        ),
        dict(
            result=row_low,
            rows_one=all_rows,
            rows_two=all_rows,
            hidden=row_full,
            act_all=narrow,
            d_gate=narrow,
            d_up=narrow,
            **saved,
        ),
        dict(
            act_prev_v=vmem(*narrow),
            hidden_prev_v=vmem(*row_full),
            gains_v=vmem(*gain_row),
            w_d_prev=vmem(*wide),
            w_in=vmem((in_width, model_width), LOW),
            w_o=vmem(*quarter),
            w_d=vmem(*wide),
            top_held=vmem(*all_rows),
            held=vmem(*all_rows),
            held_two=vmem(*all_rows),
            result_v=vmem(*row_low),
            hidden_v=vmem(*row_full),
            act=vmem(*narrow),
            d_gate_v=vmem(*narrow),
            d_up_v=vmem(*narrow),
            **gates_v,
            **attend_v,
            **fold_buffers(rows),
            **spread_sems("spread_send", "spread_recv", "spread_two_send", "spread_two_recv"),
        ),
    )

    kv_pair = ((2, *kv_shape[1:]), LOW)
    own_sums = dict(
        own_down=wide, own_gate=wide, own_up=wide, own_out=quarter, own_query=quarter,
        own_kv=kv_pair,
    )
    came_sums = dict(
        came_down=wide, came_gate=wide, came_out=quarter, came_query=quarter, came_kv=kv_pair
    )
    back_v = dict(
        d_gate_v=vmem(*narrow),
        d_up_v=vmem(*narrow),
        act=vmem(*narrow),
        hidden_v=vmem(*row_full),
        top_v=vmem(*row_low),
        x_v=vmem(*row_low),
        d_hidden=vmem(*row_full),
        d_input_v=vmem(*row_low),
        gains_v=vmem(*gain_row),
        gain_grads=vmem((2, model_width), FULL),
        w_o=vmem(*quarter),
        w_in=vmem((in_width, model_width), LOW),
        w_d=vmem(*wide),
        top_held=vmem(*all_rows),
        normed=vmem(*all_rows),
        held=vmem(*all_rows),
        d_mixed=vmem((CHIPS, PLACE, q_width), LOW),
        d_qkv=vmem((CHIPS, 2, per_device, in_width), LOW),
        d_turned=vmem((CHIPS, PLACE, in_width), LOW),
        d_query=vmem((total_len, q_width), FULL),
        d_key=vmem((total_len, HEAD_DIM), FULL),
        d_value=vmem((total_len, HEAD_DIM), FULL),
        keys_t=vmem((HEAD_DIM, total_len), LOW),
        g_down_v=vmem(*wide),
        g_gate_v=vmem(*wide),
        g_up_v=vmem(*wide),
        g_out_v=vmem(*quarter),
        g_query_v=vmem(*quarter),
        g_kv_v=vmem(*kv_pair),
        kv_mine=vmem((2, n_seq, *kv_shape[1:]), LOW),
        kv_came=vmem((n_seq - 1, 2, *kv_shape[1:]), LOW),
        kv_send=pltpu.SemaphoreType.DMA((n_seq - 1,)),
        kv_recv=pltpu.SemaphoreType.DMA((n_seq - 1,)),
        **gates_v,
        **saved_v,
        **fold_buffers(rows),
    )

    def back_in(done, d_gate, d_up, top_all):
        return dict(
            d_gate=d_gate,
            d_up=d_up,
            hidden=done.hidden,
            act_all=done.act_all,
            top_all=top_all,
            rows_one=done.rows_one,
            rows_two=done.rows_two,
            **{key: getattr(done, key) for key in saved},
            **crossed,
        )

    third = launch(
        "backward_second",
        2,
        functools.partial(backward, 1),
        scalars,
        dict(
            **back_in(second, second.d_gate, second.d_up, first.top_all),
            x_rows=second.result,
            cotangent=cotangent,
            gate_slope=first.gate_slope,
            up_slope=first.up_slope,
        ),
        dict(
            d_gate_next=narrow,
            d_up_next=narrow,
            top_next=all_rows,
            d_input=row_low,
            gain_out=((2, model_width), FULL),
            came_result_first=row_low,
            **own_sums,
            **came_sums,
        ),
        dict(
            gate_slope_v=vmem(*narrow),
            up_slope_v=vmem(*narrow),
            held_two=vmem(*all_rows),
            **back_v,
            **spread_sems("spread_send", "spread_recv", "spread_two_send", "spread_two_recv"),
        ),
    )
    fourth = launch(
        "backward_first",
        3,
        functools.partial(backward, 0),
        scalars,
        dict(
            **back_in(first, third.d_gate_next, third.d_up_next, third.top_next),
            inputs=inputs,
            top_rows=third.d_input,
            own_up_later=third.own_up,
            gain_later=third.gain_out,
            act_last=second.act_all,
            hidden_last=second.hidden,
        ),
        dict(
            d_input=row_low,
            result=row_low,
            gain_sums=((2, small[1]), FULL),
            came_up=wide,
            came_up_later=wide,
            came_input=row_low,
            came_input_later=row_low,
            came_result=row_low,
            **own_sums,
            **came_sums,
        ),
        dict(
            act_last_v=vmem(*narrow),
            hidden_last_v=vmem(*row_full),
            gain_later_v=vmem((2, model_width), FULL),
            result_v=vmem(*row_low),
            pass_in_two=vmem((CHIPS, *rows), LOW),
            land_two=vmem((CHIPS - 1, *rows), LOW),
            last_send=pltpu.SemaphoreType.DMA((FOLD_SEMS,)),
            last_recv=pltpu.SemaphoreType.DMA((FOLD_SEMS,)),
            gain_parts=vmem((n_seq, n_shard, *small), FULL),
            gain_came=vmem((n_seq - 1, n_shard, *small), FULL),
            gain_shards=vmem((n_shard, *small), FULL),
            gain_last=vmem((n_shard - 1, *small), FULL),
            gain_own=vmem(small, FULL),
            gain_other=vmem(small, FULL),
            gain_sums_v=vmem((2, small[1]), FULL),
            gain_send=pltpu.SemaphoreType.DMA((7,)),
            gain_recv=pltpu.SemaphoreType.DMA((7,)),
            **back_v,
            **spread_sems("spread_send", "spread_recv"),
        ),
    )

    def sums(of, done):
        return [getattr(done, f"{of}_{key}") for key in ("down", "gate", "up", "out", "query", "kv")]

    third.came_up = fourth.came_up_later
    g_down, g_gate, g_up, g_out, g_query, g_key, g_value, outputs, input_grads = join_all(
        sums("own", fourth),
        sums("own", third),
        sums("came", fourth),
        sums("came", third),
        (second.result, fourth.result, third.came_result_first, fourth.came_result),
        (fourth.d_input, third.d_input, fourth.came_input, fourth.came_input_later),
    )
    return (
        outputs[None],
        input_grads[None],
        fourth.gain_sums[:1],
        g_query[None],
        g_key,
        g_value,
        g_out[None],
        fourth.gain_sums[1:],
        g_gate[None],
        g_up[None],
        g_down[None],
    )


def fits_relay(mesh):
    shape = mesh.shape
    return shape["section"] == 2 and shape["shard"] == KV_HEADS == RING and shape["seq"] == 4


def solution(mesh):
    in_specs = (
        P(None, ("shard", "seq"), None),
        P(None, ("shard", "seq"), None),
        P(),
        P("section", ("shard", "seq")),
        P("section", ("shard", "seq"), None),
        P("section", ("shard", "seq"), None),
        P("section", ("shard", "seq"), None),
        P("section", ("shard", "seq"), None),
        P("section", ("shard", "seq")),
        P("section", ("shard", "seq"), None),
        P("section", ("shard", "seq"), None),
        P("section", ("shard", "seq"), None),
    )
    out_specs = (
        P("section", None, ("shard", "seq"), None),
        P("section", None, ("shard", "seq"), None),
        P("section", ("shard", "seq")),
        P("section", ("shard", "seq"), None),
        P("section", ("shard", "seq"), None),
        P("section", ("shard", "seq"), None),
        P("section", ("shard", "seq"), None),
        P("section", ("shard", "seq")),
        P("section", ("shard", "seq"), None),
        P("section", ("shard", "seq"), None),
        P("section", ("shard", "seq"), None),
    )
    chosen = relay_body if fits_relay(mesh) else body
    return jax.shard_map(chosen, mesh=mesh, in_specs=in_specs, out_specs=out_specs, check_vma=False)
```

```python
import functools
import math
import types

import jax
import jax.numpy as jnp
from jax import lax
from jax.experimental import pallas as pl
from jax.experimental.pallas import tpu as pltpu
from jax.sharding import PartitionSpec as P

HEADS = 32
KV_HEADS = 4
HEAD_DIM = 64


EPSILON = 1e-05
THETA_BASE = 10000.0
NEG_LARGE = -1e30


def shifted(value, axis, by):
    count = lax.axis_size(axis)
    pairs = [(i, i + by) for i in range(count) if 0 <= i + by < count]
    return lax.ppermute(value, axis, pairs)


def times_trans(left, right):
    return lax.dot_general(
        left, right, (((1,), (1,)), ((), ())), preferred_element_type=jnp.float32
    )


def outer_sum(left, right):
    return lax.dot_general(
        left, right, (((0,), (0,)), ((), ())), preferred_element_type=jnp.float32
    )


def plain_dot(left, right):
    return jnp.dot(left, right, preferred_element_type=jnp.float32)


def rotate(values, places, direction):
    half_dim = values.shape[-1] // 2
    inv_freq = THETA_BASE ** (-jnp.arange(half_dim, dtype=jnp.float32) * (2.0 / values.shape[-1]))
    angles = places.astype(jnp.float32)[:, None] * inv_freq[None, :]
    cosine = jnp.cos(angles)[:, None, :]
    sine_val = direction * jnp.sin(angles)[:, None, :]
    first = values[..., :half_dim]
    second = values[..., half_dim:]
    return jnp.concatenate(
        [first * cosine - second * sine_val, second * cosine + first * sine_val], -1
    )


def scaled(values, gain_vec):
    factor = lax.rsqrt(jnp.mean(values * values, -1, keepdims=True) + EPSILON)
    return values * factor * gain_vec


def norm_back(values, gain_vec, grad_in):
    factor = lax.rsqrt(jnp.mean(values * values, -1, keepdims=True) + EPSILON)
    gain_grad = jnp.sum(grad_in * values * factor, 0)
    mean_term = jnp.mean(grad_in * gain_vec * values, -1, keepdims=True)
    return (
        gain_grad,
        factor * gain_vec * grad_in - values * (factor * factor * factor) * mean_term,
    )


def ffn_back(grad_rows, kept_rows, gate_pre, up_pre, wg_part, wu_part, wd_part):
    sigmoid_val = jax.nn.sigmoid(gate_pre)
    silu_val = gate_pre * sigmoid_val
    hidden_act = (silu_val * up_pre).astype(jnp.bfloat16)
    grad_down = outer_sum(hidden_act, grad_rows)
    d_act = times_trans(grad_rows, wd_part)
    d_gate = (d_act * up_pre * sigmoid_val * (1.0 + gate_pre * (1.0 - sigmoid_val))).astype(
        jnp.bfloat16
    )
    d_up = (d_act * silu_val).astype(jnp.bfloat16)
    grad_gate = outer_sum(d_gate, kept_rows)
    grad_up = outer_sum(d_up, kept_rows)
    d_normed = plain_dot(d_gate, wg_part) + plain_dot(d_up, wu_part)
    return ((grad_gate, grad_up, grad_down), d_normed)


def body(
    inputs,
    cotangent,
    positions,
    gain_attn,
    w_query,
    w_key,
    w_value,
    w_out,
    gain_ffn,
    w_gate,
    w_up,
    w_down,
):
    n_micro, per_device, model_width = inputs.shape
    n_seq = lax.axis_size("seq")
    n_shard = lax.axis_size("shard")
    section_idx = lax.axis_index("section")
    shard_pos = lax.axis_index("shard")
    member = shard_pos * n_seq + lax.axis_index("seq")
    span_rows = per_device * n_seq
    total_len = span_rows * n_shard
    local_heads = HEADS // n_seq
    kv_repeat = n_seq // KV_HEADS
    q_width = local_heads * HEAD_DIM
    attn_scale = 1.0 / math.sqrt(HEAD_DIM)
    gain_one, gain_two, wq_full, wk_full, wv_full, wo_full = (
        lax.all_gather(gain_attn[0], ("shard", "seq"), axis=0, tiled=True),
        lax.all_gather(gain_ffn[0], ("shard", "seq"), axis=0, tiled=True),
        lax.all_gather(w_query[0], ("shard", "seq"), axis=0, tiled=True),
        lax.all_gather(w_key[0], ("shard", "seq"), axis=0, tiled=True),
        lax.all_gather(w_value[0], ("shard", "seq"), axis=0, tiled=True),
        lax.all_gather(w_out[0], ("shard", "seq"), axis=0, tiled=True),
    )
    gain_a = gain_one.astype(jnp.float32)
    gain_f = gain_two.astype(jnp.float32)
    wg_use, wu_use, wd_use = (w_gate[0], w_up[0], w_down[0])

    def spread_rows(block_in):
        return lax.all_gather(block_in, ("shard", "seq"), axis=0, tiled=True)

    def fold_rows(block_in):
        return lax.psum_scatter(block_in, ("shard", "seq"), scatter_dimension=0, tiled=True)

    def to_heads(block_in):
        return lax.all_to_all(block_in, "seq", split_axis=1, concat_axis=0, tiled=True)

    def to_tokens(block_in):
        return lax.all_to_all(block_in, "seq", split_axis=0, concat_axis=1, tiled=True)

    def over_keys(head_keys, head_values, step_fn, init_state):
        return step_fn(
            init_state,
            (
                lax.all_gather(head_keys, "shard", axis=0, tiled=True),
                lax.all_gather(head_values, "shard", axis=0, tiled=True),
            ),
            jnp.int32(0),
        )

    def place_sets(batch_index):
        place_row = lax.dynamic_index_in_dim(positions, batch_index, 0, keepdims=False)
        token_places = lax.dynamic_slice_in_dim(place_row, member * per_device, per_device)
        span_places = lax.dynamic_slice_in_dim(place_row, shard_pos * span_rows, span_rows)
        return (place_row, token_places, span_places)

    zero_rows = jnp.zeros((per_device, model_width), jnp.bfloat16)
    arrived_x = zero_rows
    results = []
    stored = []
    for tick_index in range(n_micro + 1):
        own_rows = inputs[tick_index] if tick_index < n_micro else zero_rows
        input_now = jnp.where(section_idx == 0, own_rows, arrived_x)
        batch_index = jnp.clip(tick_index - section_idx, 0, n_micro - 1)
        forward_place_row, forward_token_places, forward_span_places = place_sets(batch_index)
        forward_values_in = input_now.astype(jnp.float32)
        forward_normed_one = scaled(forward_values_in, gain_a).astype(jnp.bfloat16)
        queries = rotate(
            times_trans(forward_normed_one, wq_full).reshape(per_device, HEADS, HEAD_DIM),
            forward_token_places,
            1.0,
        ).astype(jnp.bfloat16)
        key_rows = rotate(
            times_trans(forward_normed_one, wk_full).reshape(per_device, KV_HEADS, HEAD_DIM),
            forward_token_places,
            1.0,
        ).astype(jnp.bfloat16)
        value_rows = (
            times_trans(forward_normed_one, wv_full)
            .reshape(per_device, KV_HEADS, HEAD_DIM)
            .astype(jnp.bfloat16)
        )
        key_rows = jnp.repeat(key_rows, kv_repeat, axis=1)
        value_rows = jnp.repeat(value_rows, kv_repeat, axis=1)
        packed = jnp.concatenate(
            [queries.reshape(per_device, n_seq, q_width), key_rows, value_rows], -1
        )
        arrived = to_heads(packed)[:, 0]
        forward_head_query = arrived[:, :q_width].reshape(span_rows, local_heads, HEAD_DIM)
        forward_head_keys = arrived[:, q_width : q_width + HEAD_DIM]
        forward_head_values = arrived[:, q_width + HEAD_DIM :]

        def absorb(state_in, key_piece, start_row):
            run_max, run_total, run_acc = state_in
            piece_keys, piece_values = key_piece
            visible = forward_place_row[None, None, :] <= forward_span_places[None, :, None]
            scores = (
                jnp.einsum(
                    "qhd,kd->hqk",
                    forward_head_query,
                    piece_keys,
                    preferred_element_type=jnp.float32,
                )
                * attn_scale
            )
            scores = jnp.where(visible, scores, NEG_LARGE)
            new_max = jnp.maximum(run_max, jnp.max(scores, -1))
            weight = jnp.where(visible, jnp.exp(scores - new_max[..., None]), 0.0)
            rescale = jnp.exp(run_max - new_max)
            run_total = jnp.sum(weight, -1)
            run_acc = run_acc * rescale.T[..., None] + jnp.einsum(
                "hqk,kd->qhd",
                weight.astype(jnp.bfloat16),
                piece_values,
                preferred_element_type=jnp.float32,
            )
            return (new_max, run_total, run_acc)

        forward_start_state = (
            jnp.full((local_heads, span_rows), NEG_LARGE, jnp.float32),
            jnp.zeros((local_heads, span_rows), jnp.float32),
            jnp.zeros((span_rows, local_heads, HEAD_DIM), jnp.float32),
        )
        run_max, run_total, run_acc = over_keys(
            forward_head_keys, forward_head_values, absorb, forward_start_state
        )
        forward_attended = run_acc / run_total.T[..., None]
        forward_spread = run_max + jnp.log(run_total)
        forward_mixed_tok = to_tokens(
            forward_attended.astype(jnp.bfloat16).reshape(span_rows, 1, q_width)
        ).reshape(per_device, HEADS * HEAD_DIM)
        forward_hidden_in = forward_values_in + plain_dot(forward_mixed_tok, wo_full)
        normed_two = scaled(forward_hidden_in, gain_f).astype(jnp.bfloat16)
        forward_kept_rows = spread_rows(normed_two)
        forward_gate_pre = times_trans(forward_kept_rows, wg_use)
        forward_up_pre = times_trans(forward_kept_rows, wu_use)
        hidden_act = (jax.nn.silu(forward_gate_pre) * forward_up_pre).astype(jnp.bfloat16)
        branch = fold_rows(plain_dot(hidden_act, wd_use))
        result = (forward_hidden_in + branch).astype(jnp.bfloat16)
        forward_saved = (
            input_now,
            forward_head_query,
            forward_head_keys,
            forward_head_values,
            forward_attended,
            forward_spread,
            forward_mixed_tok,
            forward_hidden_in,
            forward_kept_rows,
            forward_gate_pre,
            forward_up_pre,
        )
        result, saved = (result, forward_saved)
        results.append(result)
        stored.append(saved)
        if tick_index < n_micro:
            arrived_x = shifted(result, "section", 1)
    returned = zero_rows
    grads_back = []
    row_lists = []
    gain_total = None
    ffn_total = None
    for tick_index in range(n_micro + 1):
        own_rows = cotangent[tick_index] if tick_index < n_micro else zero_rows
        grad_now = jnp.where(section_idx == 1, own_rows, returned)
        batch_index = jnp.clip(tick_index - 1 + section_idx, 0, n_micro - 1)
        early_saved = stored[max(tick_index - 1, 0)]
        late_saved = stored[min(tick_index + 1, n_micro)]
        saved = jax.tree.map(
            lambda early_val, late_val: jnp.where(section_idx == 0, early_val, late_val),
            early_saved,
            late_saved,
        )
        (
            input_bf,
            head_query,
            backward_head_keys,
            backward_head_values,
            attended,
            spread,
            mixed_tok,
            hidden_in,
            kept_rows,
            gate_pre,
            up_pre,
        ) = saved
        backward_place_row, backward_token_places, backward_span_places = place_sets(batch_index)
        values_in = input_bf.astype(jnp.float32)
        normed_one = scaled(values_in, gain_a).astype(jnp.bfloat16)
        grad_all = spread_rows(grad_now)
        ffn_terms, d_partial = ffn_back(
            grad_all, kept_rows, gate_pre, up_pre, wg_use, wu_use, wd_use
        )
        d_normed_two = fold_rows(d_partial)
        grad_gf, d_hidden = norm_back(hidden_in, gain_f, d_normed_two)
        d_hidden = d_hidden + grad_now.astype(jnp.float32)
        d_branch = d_hidden.astype(jnp.bfloat16)
        d_mixed = times_trans(d_branch, wo_full).astype(jnp.bfloat16)
        d_att = to_heads(d_mixed.reshape(per_device, n_seq, q_width))[:, 0].reshape(
            span_rows, local_heads, HEAD_DIM
        )
        offset = jnp.sum(d_att.astype(jnp.float32) * attended, -1).T

        def collect(state_in, key_piece, start_row):
            piece_keys, piece_values = key_piece
            visible = backward_place_row[None, None, :] <= backward_span_places[None, :, None]
            scores = (
                jnp.einsum(
                    "qhd,kd->hqk", head_query, piece_keys, preferred_element_type=jnp.float32
                )
                * attn_scale
            )
            probs = jnp.where(visible, jnp.exp(scores - spread[..., None]), 0.0)
            d_probs = jnp.einsum(
                "qhd,kd->hqk", d_att, piece_values, preferred_element_type=jnp.float32
            )
            d_score = (probs * (d_probs - offset[..., None]) * attn_scale).astype(jnp.bfloat16)
            d_query_acc = jnp.einsum(
                "hqk,kd->qhd", d_score, piece_keys, preferred_element_type=jnp.float32
            )
            key_part = jnp.einsum(
                "hqk,qhd->kd", d_score, head_query, preferred_element_type=jnp.float32
            )
            value_part = jnp.einsum(
                "hqk,qhd->kd", probs.astype(jnp.bfloat16), d_att, preferred_element_type=jnp.float32
            )
            return (d_query_acc, key_part, value_part)

        start_state = (
            jnp.zeros((span_rows, local_heads, HEAD_DIM), jnp.float32),
            jnp.zeros((total_len, HEAD_DIM), jnp.float32),
            jnp.zeros((total_len, HEAD_DIM), jnp.float32),
        )
        d_query_acc, d_keys_all, d_values_all = over_keys(
            backward_head_keys, backward_head_values, collect, start_state
        )
        own_keys = lax.psum_scatter(
            d_keys_all.astype(jnp.bfloat16), "shard", scatter_dimension=0, tiled=True
        ).astype(jnp.float32)
        own_values = lax.psum_scatter(
            d_values_all.astype(jnp.bfloat16), "shard", scatter_dimension=0, tiled=True
        ).astype(jnp.float32)
        d_query_head = rotate(d_query_acc, backward_span_places, -1.0).astype(jnp.bfloat16)
        d_query = to_tokens(d_query_head.reshape(span_rows, 1, q_width)).reshape(
            per_device, HEADS * HEAD_DIM
        )
        own_keys = rotate(own_keys[:, None, :], backward_span_places, -1.0)[:, 0]
        back_kv = lax.all_to_all(
            jnp.concatenate([own_keys, own_values], -1)[:, None, :].astype(jnp.bfloat16),
            "seq",
            split_axis=0,
            concat_axis=1,
            tiled=True,
        ).astype(jnp.float32)
        back_kv = jnp.sum(back_kv.reshape(per_device, KV_HEADS, kv_repeat, 2 * HEAD_DIM), 2)
        d_key = (
            back_kv[..., :HEAD_DIM].reshape(per_device, KV_HEADS * HEAD_DIM).astype(jnp.bfloat16)
        )
        d_value = (
            back_kv[..., HEAD_DIM:].reshape(per_device, KV_HEADS * HEAD_DIM).astype(jnp.bfloat16)
        )
        d_normed_one = (
            plain_dot(d_query, wq_full) + plain_dot(d_key, wk_full) + plain_dot(d_value, wv_full)
        )
        grad_ga, d_input = norm_back(values_in, gain_a, d_normed_one)
        d_input = d_input + d_hidden
        gain_terms = (grad_ga, grad_gf)
        row_terms = (d_query, d_key, d_value, normed_one, mixed_tok, d_branch)
        d_input, gain_terms, row_terms, ffn_terms = (
            d_input.astype(jnp.bfloat16),
            gain_terms,
            row_terms,
            ffn_terms,
        )
        grads_back.append(d_input)
        row_lists.append(row_terms)
        if tick_index < n_micro:
            returned = shifted(d_input, "section", -1)
        if gain_total is None:
            gain_total = gain_terms
            ffn_total = ffn_terms
        else:
            gain_total = jax.tree.map(jnp.add, gain_total, gain_terms)
            ffn_total = jax.tree.map(jnp.add, ffn_total, ffn_terms)
    joined = [
        jnp.concatenate([row_set[index_val] for row_set in row_lists], 0) for index_val in range(6)
    ]
    grad_wq = outer_sum(joined[0], joined[3])
    grad_wk = outer_sum(joined[1], joined[3])
    grad_wv = outer_sum(joined[2], joined[3])
    grad_wo = outer_sum(joined[4], joined[5])
    attn_owned = (
        lax.psum_scatter(gain_total[0], ("shard", "seq"), scatter_dimension=0, tiled=True),
        lax.psum_scatter(gain_total[1], ("shard", "seq"), scatter_dimension=0, tiled=True),
        lax.psum_scatter(grad_wq, ("shard", "seq"), scatter_dimension=0, tiled=True),
        lax.psum_scatter(grad_wk, ("shard", "seq"), scatter_dimension=0, tiled=True),
        lax.psum_scatter(grad_wv, ("shard", "seq"), scatter_dimension=0, tiled=True),
        lax.psum_scatter(grad_wo, ("shard", "seq"), scatter_dimension=0, tiled=True),
    )
    outputs = lax.dynamic_slice_in_dim(jnp.stack(results), section_idx, n_micro, 0)[None]
    input_grads = lax.dynamic_slice_in_dim(jnp.stack(grads_back), 1 - section_idx, n_micro, 0)[None]
    return (
        outputs,
        input_grads,
        attn_owned[0][None],
        attn_owned[2][None],
        attn_owned[3][None],
        attn_owned[4][None],
        attn_owned[5][None],
        attn_owned[1][None],
        ffn_total[0][None],
        ffn_total[1][None],
        ffn_total[2][None],
    )


LOW = jnp.bfloat16
FULL = jnp.float32
MESH = pl.DeviceIdType.MESH
RING = 4
CHIPS = 2 * RING
SPLIT = 2
LAG = (0, 0, 1, 2, 3)
PLACE = 128
ORDER = ((2, 1), (1, 1), (3, 1), (0, 1), (2, 0), (1, 0), (3, 0), (0, 0))
IN_VMEM = pl.BlockSpec(memory_space=pltpu.VMEM)
IN_HBM = pl.BlockSpec(memory_space=pltpu.HBM)
IN_SMEM = pl.BlockSpec(memory_space=pltpu.SMEM)


class Site:
    def __init__(self):
        self.section = lax.axis_index("section")
        self.z = lax.axis_index("shard")
        member = lax.axis_index("seq")
        self.y = lax.div(member, 2)
        self.core = lax.rem(member, 2)
        self.up = (self.section, lax.rem(self.z + 1, RING), member)
        self.down = (self.section, lax.rem(self.z + RING - 1, RING), member)
        self.across = (self.section, self.z, (1 - self.y) * 2 + self.core)
        self.sibling = (self.section, self.z, self.y * 2 + 1 - self.core)
        self.corner = (self.section, self.z, (1 - self.y) * 2 + 1 - self.core)
        self.opposite = (self.section, lax.rem(self.z + 2, RING), member)
        self.partner = (1 - self.section, self.z, member)
        self.member = member

    def chip(self, along_z, along_y):
        return lax.rem(self.z + along_z, RING) * 2 + lax.rem(self.y + along_y, 2)


class Links:
    def __init__(self, send, recv, site):
        self.send, self.recv, self.site = send, recv, site
        self.sent = []

    def copy(self, index, src, dst, device):
        return pltpu.make_async_remote_copy(
            src_ref=src,
            dst_ref=dst,
            send_sem=self.send.at[index],
            recv_sem=self.recv.at[index],
            device_id=device,
            device_id_type=MESH,
        )

    def go(self, index, src, dst, device):
        copy = self.copy(index, src, dst, device)
        copy.start()
        self.sent.append(copy)

    def got(self, index, where):
        self.copy(index, where, where, self.site.sibling).wait_recv()
        return where

    def close(self):
        for copy in self.sent:
            copy.wait_send()


def greet(site):
    barrier = pltpu.get_barrier_semaphore()
    devices = (
        site.up, site.down, site.across, site.sibling, site.corner, site.opposite, site.partner
    )
    for device in devices:
        pl.semaphore_signal(barrier, inc=1, device_id=device, device_id_type=MESH)
    pl.semaphore_wait(barrier, len(devices))


SPREAD_SEMS = 7 * SPLIT + CHIPS
FOLD_SEMS = 7 * SPLIT + CHIPS
SMALL_SEMS = 11
COPY_SEMS = 48
CROSS_SEMS = 32
PIECE = 128


class Spread:
    def __init__(self, site, held, links, use):
        self.site, self.held, self.links, self.use = site, held, links, use
        self.size = held.shape[2] // SPLIT
        self.up, self.down, self.over, self.relay, self.y_below, self.y_above, self.y_far = (
            k * SPLIT for k in range(7)
        )
        self.along = ((0, 0), (3, 0), (1, 0), (0, 1), (2, 0), (3, 1), (1, 1), (2, 1))

    def piece(self, slot, part):
        site = self.site
        rows = pl.ds(part * self.size, self.size)
        return self.held.at[site.chip(*self.along[slot]), site.core, rows]

    def block(self, slot, core):
        return self.held.at[self.site.chip(*self.along[slot]), core]

    def go(self, index, where, device):
        self.links.go(index, where, where, device)

    def share(self, slot):
        self.go(7 * SPLIT + slot, self.block(slot, self.site.core), self.site.sibling)

    def consume(self, *slots):
        for slot in slots:
            self.links.got(7 * SPLIT + slot, self.block(slot, 1 - self.site.core))
            self.use(self.site.chip(*self.along[slot]))

    def ways(self, part):
        ways = (
            (self.up + part, 1, self.site.up, self.y_below + part),
            (self.down + part, 2, self.site.down, self.y_above + part),
        )
        return ways if part % 2 == 0 else ways[::-1]

    def own(self, part):
        where = self.piece(0, part)
        for index, _, device, _ in self.ways(part):
            self.go(index, where, device)
        self.go(self.over + part, where, self.site.across)

    def relays(self, part):
        for turn, (index, slot, device, over) in enumerate(self.ways(part)):
            came = self.links.got(index, self.piece(slot, part))
            if turn == 0:
                self.go(self.relay + part, came, device)
            self.go(over, came, self.site.across)

    def far(self, part):
        came = self.links.got(self.relay + part, self.piece(4, part))
        self.go(self.y_far + part, came, self.site.across)

    def after_relays(self):
        self.share(1)
        self.share(2)
        for part in range(SPLIT):
            self.links.got(self.over + part, self.piece(3, part))
        self.share(3)

    def tail(self, consume=True, first=0):
        def take(*slots):
            if consume:
                self.consume(*slots)

        self.share(4)
        take(*range(first, 3))
        for part in range(SPLIT):
            self.links.got(self.y_below + part, self.piece(5, part))
            self.links.got(self.y_above + part, self.piece(6, part))
        self.share(5)
        self.share(6)
        take(3, 4)
        for part in range(SPLIT):
            self.links.got(self.y_far + part, self.piece(7, part))
        self.share(7)
        take(5, 6, 7)
        if not consume:
            for slot in range(CHIPS):
                self.links.got(7 * SPLIT + slot, self.block(slot, 1 - self.site.core))

    def rest(self, consume=True):
        self.after_relays()
        for part in range(SPLIT):
            self.far(part)
        self.tail(consume)


class Fold:
    def __init__(self, site, part_of, buffers, links):
        self.site, self.part_of, self.links = site, part_of, links
        self.mine, self.pass_out, self.pass_in, self.stage, self.land = buffers
        self.rows = self.mine.shape[1]
        self.size = self.rows // SPLIT
        self.over = CHIPS
        self.relay, self.up, self.down = (CHIPS + (4 + k) * SPLIT for k in range(3))

    def where(self, part):
        return pl.ds(part * self.size, self.size)

    def came(self, index, where):
        return self.links.got(index, where)[...].astype(FULL)

    def compute(self, step):
        both = self.part_of(self.site.chip(*ORDER[step]))
        self.pass_out[step] = both[: self.rows].astype(LOW)
        self.links.go(step, self.pass_out.at[step], self.pass_in.at[step], self.site.sibling)
        self.mine[step] = both[self.rows :]

    def settle(self, step):
        self.mine[step] += self.came(step, self.pass_in.at[step])

    def send(self, index, slot, part, value, device):
        where = self.where(part)
        self.stage[slot, where] = value.astype(LOW)
        self.links.go(index, self.stage.at[slot, where], self.land.at[slot, where], device)

    def send_over(self, step, part):
        value = self.mine[step, self.where(part)]
        self.send(self.over + step * SPLIT + part, step, part, value, self.site.across)

    def start(self):
        self.compute(0)
        self.compute(1)
        for step in range(4):
            self.settle(step)
            self.send_over(step, 0)
            self.compute(step + 2)
        for part in range(1, SPLIT):
            for step in range(4):
                self.send_over(step, part)
        self.compute(6)
        self.compute(7)
        for step in range(4, CHIPS):
            self.settle(step)

    def pass_on(self, part):
        where = self.where(part)
        value = self.mine[4, where] + self.came(self.over + part, self.land.at[0, where])
        device = self.site.up if part % 2 == 0 else self.site.down
        self.send(self.relay + part, 4, part, value, device)

    def up_down(self, part):
        where = self.where(part)
        ways = ((5, self.up, self.site.up), (6, self.down, self.site.down))
        for step, base, device in ways if part % 2 else ways[::-1]:
            from_y = self.over + (step - 4) * SPLIT + part
            value = self.mine[step, where] + self.came(from_y, self.land.at[step - 4, where])
            if part % 2 == step - 5:
                value = value + self.came(self.relay + part, self.land.at[4, where])
            self.send(base + part, step, part, value, device)

    def final(self, part):
        where = self.where(part)
        value = self.mine[7, where] + self.came(
            self.over + 3 * SPLIT + part, self.land.at[3, where]
        )
        value = value + self.came(self.up + part, self.land.at[5, where])
        return value + self.came(self.down + part, self.land.at[6, where])


def fold_spread(fold, spread, local, idle):
    def finish(part):
        rows = local(fold.final(part), fold.where(part))
        if spread is not None:
            site = spread.site
            spread.held[site.chip(0, 0), site.core, fold.where(part)] = rows
            spread.own(part)

    fold.start()
    idle(3)
    last = SPLIT - 1
    for tick in range(SPLIT + LAG[-1]):
        steps = [tick - lag for lag in LAG]
        if 0 <= steps[0] < SPLIT:
            fold.pass_on(steps[0])
        if 0 <= steps[1] < SPLIT:
            fold.up_down(steps[1])
        if 0 <= steps[2] < SPLIT:
            finish(steps[2])
        if spread is not None:
            if steps[2] == last:
                spread.share(0)
            if 0 <= steps[3] < SPLIT:
                spread.relays(steps[3])
            if steps[3] == last:
                spread.after_relays()
            if 0 <= steps[4] < SPLIT:
                spread.far(steps[4])
            if steps[2] == last + 1:
                spread.consume(0)
        idle(3)
    if spread is not None:
        idle(10)
        spread.tail(first=1)
        spread.links.close()
    else:
        idle(10)
    fold.links.close()


class Cross:
    def __init__(self, n):
        self.site = n.site
        self.links = Links(n.cross_send, n.cross_recv, n.site)
        self.begun = []
        self.count = 0

    def where(self, layer, receives, action):
        if layer is None:
            action()
        else:
            pl.when((self.site.section == layer) == receives)(action)

    def send(self, src, dst, layer=None):
        rows = src.shape[0]
        pieces = []
        start = 0
        while start < rows:
            size = min(PIECE, rows - start)
            where = pl.ds(start, size)
            pieces.append(
                self.links.copy(self.count, src.at[where], dst.at[where], self.site.partner)
            )
            self.count += 1
            start += size

        def begin():
            for copy in pieces:
                copy.start()

        self.where(layer, False, begin)
        self.begun.append([pieces, layer, False])
        return len(self.begun) - 1

    def wait(self, index):
        pieces, layer, landed = self.begun[index]

        def arrive():
            for copy in pieces:
                copy.wait_recv()

        if not landed:
            self.begun[index][2] = True
            self.where(layer, True, arrive)

    def close(self):
        for index in range(len(self.begun)):
            self.wait(index)
        for pieces, layer, _ in self.begun:

            def leave():
                for copy in pieces:
                    copy.wait_send()

            self.where(layer, False, leave)


class Copies:
    def __init__(self, n):
        self.n, self.count, self.open = n, 0, []

    def sem(self):
        self.count += 1
        return self.n.copy_sem.at[self.count - 1]

    def start(self, src, dst):
        copy = pltpu.make_async_copy(src, dst, self.sem())
        copy.start()
        self.open.append(copy)
        return copy

    def pick(self, own, other, dst, layer):
        sem = self.sem()
        from_own = pltpu.make_async_copy(own, dst, sem)
        from_other = pltpu.make_async_copy(other, dst, sem)
        pl.when(self.n.site.section == layer)(from_own.start)
        pl.when(self.n.site.section != layer)(from_other.start)
        self.open.append(from_own)
        return from_own

    def wait(self, *copies):
        for copy in copies:
            if any(copy is other for other in self.open):
                self.open = [other for other in self.open if other is not copy]
                copy.wait()

    def close(self):
        self.wait(*list(self.open))


def kernel_of(body, names, *refs):
    n = types.SimpleNamespace(**dict(zip(names, refs)))
    n.site = Site()
    n.copies = Copies(n)
    n.cross = Cross(n)
    body(n)
    n.cross.close()
    n.copies.close()


def launch(name, ident, body, scalars, inputs, outputs, scratch):
    scratch = dict(
        scratch,
        copy_sem=pltpu.SemaphoreType.DMA((COPY_SEMS,)),
        cross_send=pltpu.SemaphoreType.DMA((CROSS_SEMS,)),
        cross_recv=pltpu.SemaphoreType.DMA((CROSS_SEMS,)),
    )
    names = [*scalars, *inputs, *outputs, *scratch]
    results = pl.pallas_call(
        functools.partial(kernel_of, body, names),
        out_shape=[jax.ShapeDtypeStruct(*value) for value in outputs.values()],
        in_specs=[IN_SMEM] * len(scalars) + [IN_HBM] * len(inputs),
        out_specs=[IN_HBM] * len(outputs),
        scratch_shapes=list(scratch.values()),
        compiler_params=pltpu.CompilerParams(
            collective_id=ident, has_side_effects=True, vmem_limit_bytes=60 * 2**20
        ),
        cost_estimate=pl.CostEstimate(flops=2**37, bytes_accessed=2**23, transcendentals=0),
        name=name,
    )(*scalars.values(), *inputs.values())
    return types.SimpleNamespace(**dict(zip(outputs, results)))


def fold_buffers(full):
    return dict(
        mine=pltpu.VMEM((CHIPS, *full), FULL),
        pass_out=pltpu.VMEM((CHIPS, *full), LOW),
        pass_in=pltpu.VMEM((CHIPS, *full), LOW),
        stage=pltpu.VMEM((CHIPS - 1, *full), LOW),
        land=pltpu.VMEM((CHIPS - 1, *full), LOW),
        fold_send=pltpu.SemaphoreType.DMA((FOLD_SEMS,)),
        fold_recv=pltpu.SemaphoreType.DMA((FOLD_SEMS,)),
    )


def fold_of(n, part_of):
    buffers = (n.mine, n.pass_out, n.pass_in, n.stage, n.land)
    return Fold(n.site, part_of, buffers, Links(n.fold_send, n.fold_recv, n.site))


def spread_of(n, held, send, recv, use, kept=None):
    def take(chip):
        block = held[chip]
        use(chip, block.reshape(block.shape[0] * block.shape[1], block.shape[2]))
        if kept is not None:
            n.copies.start(held.at[chip], kept.at[chip])

    return Spread(n.site, held, Links(send, recv, n.site), take)


def spread_sems(*names):
    return {name: pltpu.SemaphoreType.DMA((SPREAD_SEMS,)) for name in names}


def no_idle(count):
    pass


def rows_of(ref, chip, site):
    return jnp.concatenate([ref[chip, 1 - site.core], ref[chip, site.core]], 0)


def put(ref, chip, value):
    ref[chip] = value.astype(LOW).reshape(ref.shape[1:])


def gate_chunk(n, chip, rows):
    gate_pre = times_trans(rows, n.w_g[...])
    up_pre = times_trans(rows, n.w_u[...])
    sig = jax.nn.sigmoid(gate_pre)
    silu_val = gate_pre * sig
    put(n.act, chip, silu_val * up_pre)
    return up_pre * sig * (1.0 + gate_pre * (1.0 - sig)), silu_val


def norm_back_rows(values, gain_vec, grad_in):
    factor = lax.rsqrt(jnp.mean(values * values, -1, keepdims=True) + EPSILON)
    gain_grad = jnp.sum(grad_in * values * factor, 0, keepdims=True)
    mean_term = jnp.mean(grad_in * gain_vec * values, -1, keepdims=True)
    return (
        gain_grad,
        factor * gain_vec * grad_in - values * (factor * factor * factor) * mean_term,
    )


def swap_halves(value):
    width = value.shape[1]
    half = HEAD_DIM // 2
    lane = lax.broadcasted_iota(jnp.int32, value.shape, 1)
    return jnp.where(
        lax.rem(lane, HEAD_DIM) < half,
        pltpu.roll(value, width - half, 1),
        pltpu.roll(value, half, 1),
    )


def stacked(pair):
    return jnp.concatenate([pair[:, :HEAD_DIM], pair[:, HEAD_DIM:]], 0)


def side_by_side(turned):
    return jnp.concatenate([turned[:, :PLACE], turned[:, PLACE:]], 0).T


def hide_later(scores, fill):
    last = scores[-PLACE:]
    key = lax.broadcasted_iota(jnp.int32, last.shape, 0)
    query = lax.rem(lax.broadcasted_iota(jnp.int32, last.shape, 1), PLACE)
    last = jnp.where(key <= query, last, fill)
    if scores.shape[0] == PLACE:
        return last
    return jnp.concatenate([scores[:-PLACE], last], 0)


def turn_of(turns, place):
    near, far = pl.ds(0, PLACE), pl.ds(PLACE + place, 1)
    cos_near, sin_near = turns[0, near], turns[1, near]
    cos_far, sin_far = turns[0, far], turns[1, far]
    cosine = cos_near * cos_far - sin_near * sin_far
    sine = sin_near * cos_far + cos_near * sin_far
    lane = lax.broadcasted_iota(jnp.int32, cosine.shape, 1)
    sine = jnp.where(lax.rem(lane, HEAD_DIM) < HEAD_DIM // 2, -sine, sine)
    keyed = lane < HEAD_DIM
    return (
        jnp.concatenate([cosine, jnp.where(keyed, cosine, 1.0)], 1),
        jnp.concatenate([sine, jnp.where(keyed, sine, 0.0)], 1),
    )


def attend(n):
    q_width = 2 * HEAD_DIM
    scale = jnp.asarray(1.0 / math.sqrt(HEAD_DIM), LOW)
    for place in range(CHIPS):
        at = pl.ds(place * PLACE, PLACE)
        value = n.qkv[n.block_at[place]]
        cosine, sine = turn_of(n.turns_v, place)
        value = (value * cosine + swap_halves(value) * sine).astype(LOW)
        n.turned_v[at, :q_width] = value[:, :q_width] * scale
        n.turned_v[at, q_width:] = value[:, q_width:]
        n.values_t[:, at] = value[:, q_width:].astype(FULL).T[HEAD_DIM:].astype(LOW)
    for place in range(CHIPS):
        at = pl.ds(place * PLACE, PLACE)
        keys = pl.ds(0, (place + 1) * PLACE)
        query = stacked(n.turned_v[at, :q_width])
        scores = times_trans(n.turned_v[keys, q_width : q_width + HEAD_DIM], query)
        scores = hide_later(scores, NEG_LARGE)
        top = jnp.max(scores, 0, keepdims=True)
        weight = jnp.exp(scores - top)
        total = jnp.sum(weight, 0, keepdims=True)
        out = plain_dot(n.values_t[:, keys], weight.astype(LOW)) / total
        n.attended_v[place] = side_by_side(out)
        n.spread_v[pl.ds(place, 1)] = top + jnp.log(total)
    for block in range(CHIPS):
        put(n.mixed_v, block, n.attended_v[n.order[block]])


def keep_attention(n):
    n.copies.start(n.turned_v, n.turned)
    n.copies.start(n.attended_v, n.attended)
    n.copies.start(n.spread_v, n.spread)
    n.copies.start(n.mixed_v, n.mixed)


def attend_back(n):
    q_width = 2 * HEAD_DIM
    n.d_key[...] = jnp.zeros_like(n.d_key)
    n.d_value[...] = jnp.zeros_like(n.d_value)
    for place in range(CHIPS):
        at = pl.ds(place * PLACE, PLACE)
        n.keys_t[:, at] = n.turned_v[at, q_width:].astype(FULL).T[:HEAD_DIM].astype(LOW)
    for place in range(CHIPS):
        at = pl.ds(place * PLACE, PLACE)
        keys = pl.ds(0, (place + 1) * PLACE)
        d_out = n.d_mixed[n.block_at[place]]
        product = (d_out.astype(FULL) * n.attended_v[place]).T
        offset = jnp.concatenate(
            [
                jnp.sum(product[:HEAD_DIM], 0, keepdims=True),
                jnp.sum(product[HEAD_DIM:], 0, keepdims=True),
            ],
            1,
        )
        d_out = stacked(d_out)
        query = stacked(n.turned_v[at, :q_width])
        scores = times_trans(n.turned_v[keys, q_width : q_width + HEAD_DIM], query)
        scores = hide_later(scores, NEG_LARGE)
        probs = jnp.exp(scores - n.spread_v[pl.ds(place, 1)])
        d_probs = times_trans(n.turned_v[keys, q_width + HEAD_DIM :], d_out)
        d_scores = (probs * (d_probs - offset)).astype(LOW)
        n.d_key[keys] += plain_dot(d_scores, query)
        n.d_value[keys] += plain_dot(probs.astype(LOW), d_out)
        n.d_query[at] = side_by_side(plain_dot(n.keys_t[:, keys], d_scores)) * (
            1.0 / math.sqrt(HEAD_DIM)
        )
    for place in range(CHIPS):
        at = pl.ds(place * PLACE, PLACE)
        value = jnp.concatenate([n.d_query[at], n.d_key[at], n.d_value[at]], 1)
        cosine, sine = turn_of(n.turns_v, place)
        value = value * cosine - swap_halves(value) * sine
        n.d_turned[place] = value.astype(LOW)
    for block in range(CHIPS):
        put(n.d_qkv, block, n.d_turned[n.order[block]])


def gather_small(n):
    site = n.site
    links = n.links_small = Links(n.small_send, n.small_recv, site)
    links.go(0, n.gains_mine, n.gains_x, site.partner)
    links.go(1, n.kv_mine, n.kv_x, site.partner)
    links.got(0, n.gains_x)
    own, came = n.gains_mine[...], n.gains_x[...]
    first = site.section == 0
    n.gains_all[site.z, site.member] = jnp.concatenate(
        [
            jnp.where(first, own, came)[:2],
            jnp.where(first, came, own)[:2],
            jnp.zeros((4, own.shape[1]), FULL),
        ],
        0,
    )
    peers = (site.sibling, site.across, site.corner)
    mine = n.gains_all.at[site.z, site.member]
    for index, device in enumerate(peers):
        links.go(2 + index, mine, mine, device)
    for index, device in enumerate(peers):
        links.got(2 + index, n.gains_all.at[site.z, device[2]])
    shard = n.gains_all.at[site.z]
    for index, device in enumerate((site.up, site.down, site.opposite)):
        links.go(5 + index, shard, shard, device)


def gather_small_keys(n):
    site, links = n.site, n.links_small
    links.got(1, n.kv_x)
    n.kv_all[site.member, site.section] = n.kv_mine[...]
    n.kv_all[site.member, 1 - site.section] = n.kv_x[...]
    mine = n.kv_all.at[site.member]
    for index, device in enumerate((site.sibling, site.across, site.corner)):
        links.go(8 + index, mine, mine, device)


def gather_small_end(n):
    site, links = n.site, n.links_small
    for index, along_z in enumerate((RING - 1, 1, 2)):
        links.got(5 + index, n.gains_all.at[lax.rem(site.z + along_z, RING)])
    for index, device in enumerate((site.sibling, site.across, site.corner)):
        links.got(8 + index, n.kv_all.at[device[2]])
    links.close()
    n.gains_v[...] = jnp.concatenate(
        [n.gains_all[shard, seq] for shard in range(RING) for seq in range(RING)], 1
    )
    for layer in range(2):
        for index in range(2):
            rows = n.kv_all[:, layer, index]
            n.w_kv[layer, pl.ds(index * HEAD_DIM, HEAD_DIM)] = rows.reshape(
                HEAD_DIM, rows.shape[-1]
            )
    n.copies.start(n.gains_v, n.gains)
    n.copies.start(n.w_kv, n.kv_rows)


def forward_first(n):
    site, copies, cross = n.site, n.copies, n.cross
    own = (site.chip(0, 0), site.core)
    small = [
        copies.start(n.gains_own, n.gains_mine),
        copies.start(n.w_key, n.kv_mine.at[0]),
        copies.start(n.w_value, n.kv_mine.at[1]),
    ]
    rows_copy = copies.pick(n.inputs.at[0], n.inputs.at[1], n.held.at[own], 0)
    top_copy = copies.pick(n.cotangent.at[0], n.cotangent.at[1], n.top_v, 0)
    turns_copy = copies.start(n.turns, n.turns_v)
    greet(site)
    copies.wait(*small)
    gather_small(n)
    at_query, at_out, at_gate, at_up, _ = (
        cross.send(*pair)
        for pair in (
            (n.w_query, n.x_query),
            (n.w_out, n.x_out),
            (n.w_gate, n.x_gate),
            (n.w_up, n.x_up),
            (n.w_down, n.x_down),
        )
    )
    copies.wait(rows_copy)

    def use_first(chip, rows):
        normed = scaled(rows.astype(FULL), n.gains_v[:1]).astype(LOW)
        n.normed[chip] = normed.reshape(n.normed.shape[1:])
        n.qkv[chip] = jnp.concatenate(
            [times_trans(normed, n.w_q[...]), times_trans(normed, n.w_kv[0])], 1
        )
        copies.start(n.normed.at[chip], n.rows_one.at[chip])

    spread = spread_of(n, n.held, n.spread_send, n.spread_recv, use_first)
    for part in range(SPLIT):
        spread.own(part)
    spread.share(0)
    gather_small_keys(n)
    for part in range(SPLIT):
        spread.relays(part)
    gather_small_end(n)
    spread.after_relays()
    cross.wait(at_query)
    query_copy = copies.pick(n.w_query, n.x_query, n.w_q, 0)
    for part in range(SPLIT):
        spread.far(part)
    copies.wait(query_copy)
    copies.wait(top_copy, turns_copy)
    top_copy = copies.start(n.top_v, n.top_all.at[own])
    spread.tail()
    spread.links.close()
    copies.wait(top_copy)
    top = spread_of(n, n.top_all, n.top_send, n.top_recv, None)
    for part in range(SPLIT):
        top.own(part)
    cross.wait(at_out)
    out_copy = copies.pick(n.w_out, n.x_out, n.w_o, 0)
    attend(n)
    keep_attention(n)
    top.share(0)
    copies.wait(out_copy)

    def part_of(chip):
        return plain_dot(rows_of(n.mixed_v, chip, site), n.w_o[...])

    def local(total, where):
        hidden_in = n.held[(*own, where)].astype(FULL) + total
        n.hidden_v[where] = hidden_in
        return scaled(hidden_in, n.gains_v[1:2]).astype(LOW)

    waiting = []

    def use_later(chip, rows):
        waiting.append(chip)

    def use_gate(chip):
        rows = n.held_two[chip].reshape(-1, n.held_two.shape[-1])
        gate_slope, up_slope = gate_chunk(n, chip, rows)
        put(n.gate_slope_v, chip, gate_slope)
        put(n.up_slope_v, chip, up_slope)

    def idle(count):
        if count == 10:
            for part in range(SPLIT):
                top.relays(part)

    spread = spread_of(
        n, n.held_two, n.spread_two_send, n.spread_two_recv, use_later, n.rows_two
    )
    fold_spread(fold_of(n, part_of), spread, local, idle)
    copies.start(n.hidden_v, n.hidden)
    top.after_relays()
    for part in range(SPLIT):
        top.far(part)
    cross.wait(at_gate)
    cross.wait(at_up)
    copies.wait(
        copies.pick(n.w_gate, n.x_gate, n.w_g, 0), copies.pick(n.w_up, n.x_up, n.w_u, 0)
    )
    for chip in waiting:
        use_gate(chip)
    for source, target in (
        (n.act, n.act_all), (n.gate_slope_v, n.gate_slope), (n.up_slope_v, n.up_slope)
    ):
        copies.start(source, target)
    top.tail(consume=False)
    top.links.close()


def second_layer(n):
    site, copies = n.site, n.copies
    first = [
        copies.start(n.act_prev, n.act_prev_v),
        copies.pick(n.w_down, n.x_down, n.w_d_prev, 0),
    ]
    rows_copies = [copies.start(n.hidden_prev, n.hidden_prev_v), copies.start(n.gains, n.gains_v)]
    qkv_copies = [
        copies.pick(n.w_query, n.x_query, n.w_in.at[pl.ds(0, 2 * HEAD_DIM)], 1),
        copies.start(n.kv_rows.at[1], n.w_in.at[pl.ds(2 * HEAD_DIM, 2 * HEAD_DIM)]),
        copies.start(n.turns, n.turns_v),
    ]
    later = [
        copies.pick(n.w_out, n.x_out, n.w_o, 1),
        copies.pick(n.w_gate, n.x_gate, n.w_g, 1),
        copies.pick(n.w_up, n.x_up, n.w_u, 1),
        copies.pick(n.w_down, n.x_down, n.w_d, 1),
        copies.start(n.top_all, n.top_held),
    ]
    back_copies = [copies.pick(n.cotangent.at[0], n.cotangent.at[1], n.top_v, 0)]
    next_copies = [
        copies.start(n.gate_slope, n.gate_slope_v),
        copies.start(n.up_slope, n.up_slope_v),
    ]
    greet(site)
    copies.wait(*first, *rows_copies)

    def part_of(chip):
        return plain_dot(rows_of(n.act_prev_v, chip, site), n.w_d_prev[...])

    def local(total, where):
        result = (n.hidden_prev_v[where] + total).astype(LOW)
        n.result_v[where] = result
        return scaled(result.astype(FULL), n.gains_v[2:3]).astype(LOW)

    def use_qkv(chip, rows):
        n.qkv[chip] = times_trans(rows, n.w_in[...])

    def settle(count):
        copies.wait(*qkv_copies)

    spread = spread_of(n, n.held, n.spread_send, n.spread_recv, use_qkv)
    fold_spread(fold_of(n, part_of), spread, local, settle)
    copies.start(n.result_v, n.result)
    n.cross.send(n.result_v, n.came_result_first, 0)
    attend(n)
    copies.wait(*later)

    def part_of_two(chip):
        return plain_dot(rows_of(n.mixed_v, chip, site), n.w_o[...])

    def local_two(total, where):
        hidden_in = n.result_v[where].astype(FULL) + total
        n.hidden_v[where] = hidden_in
        return scaled(hidden_in, n.gains_v[3:4]).astype(LOW)

    def use_gate(chip, rows):
        gate_slope, up_slope = gate_chunk(n, chip, rows)
        d_act = times_trans(n.top_held[chip].reshape(rows.shape), n.w_d[...])
        put(n.d_gate_v, chip, d_act * gate_slope)
        put(n.d_up_v, chip, d_act * up_slope)

    spread = spread_of(
        n, n.held_two, n.spread_two_send, n.spread_two_recv, use_gate
    )
    fold_spread(fold_of(n, part_of_two), spread, local_two, no_idle)
    copies.start(n.hidden_v, n.hidden)
    copies.start(n.act, n.act_all)
    copies.wait(*back_copies)
    backward(
        1, n, [], [], n.held_two, n.normed, n.held, None, next_copies, n.w_d_prev, n.result_v
    )


def products(n, left, right, store, tile=512):
    count = math.prod(left.shape[:-1])
    for start in range(0, right.shape[-1], tile):
        where = pl.ds(start, tile)
        value = outer_sum(
            left[...].reshape(count, left.shape[-1]), right[:, :, :, where].reshape(count, tile)
        )
        store(where, value.astype(LOW))
        yield


def ffn_products(n, loads, made, normed_two):
    n.copies.wait(*loads)
    for left, right, out in (
        (n.act, n.top_held, n.g_down_v),
        (n.d_gate_v, normed_two, n.g_gate_v),
        (n.d_up_v, normed_two, n.g_up_v),
    ):

        def store(where, value):
            out[:, where] = value

        yield from products(n, left, right, store)
        made(out)


def in_products(n, loads, made, normed_one, branch):
    site = n.site
    n.copies.wait(*loads)

    def store_out(where, value):
        n.g_out_v[:, where] = value

    def store_in(where, value):
        query = n.g_query_v.shape[0]
        n.g_query_v[:, where] = value[:query]
        n.kv_mine[:, :, :, where] = value[query:].reshape(
            *n.kv_mine.shape[:3], value.shape[1]
        )

    yield from products(n, n.d_qkv, normed_one, store_in)
    made(n.g_query_v)
    peers = (site.sibling, site.across, site.corner)
    links = Links(n.kv_send, n.kv_recv, site)
    for index, device in enumerate(peers):
        links.go(index, n.kv_mine.at[:, device[2]], n.kv_came.at[index], device)
    yield from products(n, n.mixed_v, branch, store_out)
    made(n.g_out_v)
    total = n.kv_mine[:, site.member].astype(FULL)
    for index in range(len(peers)):
        total = total + links.got(index, n.kv_came.at[index])[...].astype(FULL)
    n.g_kv_v[...] = total.astype(LOW)
    made(n.g_kv_v)
    links.close()


def fold_gains(n):
    site = n.site
    links = Links(n.gain_send, n.gain_recv, site)
    own = jnp.concatenate(
        [n.gain_grads[...], n.gain_later_v[...], jnp.zeros((4, n.gain_grads.shape[1]), FULL)], 0
    )
    width = n.gain_parts.shape[-1]
    for shard in range(RING):
        for seq in range(RING):
            start = (shard * RING + seq) * width
            n.gain_parts[seq, shard] = own[:, start : start + width]
    peers = (site.sibling, site.across, site.corner)
    for index, device in enumerate(peers):
        links.go(index, n.gain_parts.at[device[2]], n.gain_came.at[index], device)
    yield
    total = n.gain_parts[site.member]
    for index in range(3):
        total = total + links.got(index, n.gain_came.at[index])[...]
    n.gain_shards[...] = total
    for index, device in enumerate((site.up, site.down, site.opposite)):
        links.go(
            3 + index, n.gain_shards.at[device[1]], n.gain_last.at[index], device
        )
    yield
    total = n.gain_shards[site.z]
    for index in range(3):
        total = total + links.got(3 + index, n.gain_last.at[index])[...]
    n.gain_own[...] = total
    links.go(6, n.gain_own, n.gain_other, site.partner)
    yield
    total = n.gain_own[...] + links.got(6, n.gain_other)[...]
    n.gain_sums_v[...] = jnp.where(site.section == 0, total[:2], total[2:4])
    links.close()
    n.copies.start(n.gain_sums_v, n.gain_sums)


def first_layer_back(n):
    site, copies, cross = n.site, n.copies, n.cross
    first = [
        copies.start(n.d_gate, n.d_gate_v),
        copies.start(n.d_up, n.d_up_v),
        copies.pick(n.w_gate, n.x_gate, n.w_g, 0),
        copies.pick(n.w_up, n.x_up, n.w_u, 0),
    ]
    loads = [copies.start(n.act_all, n.act), copies.start(n.top_all, n.top_held)]
    rows_copies = [
        copies.start(n.hidden, n.hidden_v),
        copies.start(n.top_rows, n.top_v),
        copies.start(n.gains, n.gains_v),
        copies.pick(n.w_out, n.x_out, n.w_o, 0),
    ]
    loads.append(copies.start(n.rows_two, n.normed))
    attn_copies = [
        copies.start(n.turns, n.turns_v),
        copies.start(n.turned, n.turned_v),
        copies.start(n.attended, n.attended_v),
        copies.start(n.spread, n.spread_v),
        copies.start(n.mixed, n.mixed_v),
        copies.pick(n.w_query, n.x_query, n.w_in.at[pl.ds(0, 2 * HEAD_DIM)], 0),
        copies.start(n.kv_rows.at[0], n.w_in.at[pl.ds(2 * HEAD_DIM, 2 * HEAD_DIM)]),
        copies.pick(n.inputs.at[0], n.inputs.at[1], n.x_v, 0),
    ]
    next_copies = [
        copies.pick(n.w_down, n.x_down, n.w_d, 1),
        copies.start(n.act_last, n.act_last_v),
        copies.start(n.hidden_last, n.hidden_last_v),
        copies.start(n.gain_later, n.gain_later_v),
    ]
    greet(site)
    cross.send(n.own_up_later, n.came_up_later, 1)
    cross.send(n.top_rows, n.came_input_later, 1)
    copies.wait(*first, *rows_copies)
    backward(
        0, n, loads, attn_copies, n.normed, n.held, n.normed, n.rows_one, next_copies, n.w_d, n.x_v
    )


def backward(
    layer, n, loads, attn_copies, normed_two, branch, normed_one, rows_one, next_copies, w_next,
    x_rows,
):
    site, copies, cross = n.site, n.copies, n.cross

    def made(out):
        target, came = {
            id(n.g_down_v): (n.own_down, n.came_down),
            id(n.g_gate_v): (n.own_gate, n.came_gate),
            id(n.g_up_v): (n.own_up, None if layer == 1 else n.came_up),
            id(n.g_out_v): (n.own_out, n.came_out),
            id(n.g_query_v): (n.own_query, n.came_query),
            id(n.g_kv_v): (n.own_kv, n.came_kv),
        }[id(out)]
        copies.start(out, target)
        if came is not None:
            cross.send(out, came, layer)

    def step_on(working):
        def idle(count):
            for _ in range(count):
                next(working, None)

        return idle

    def part_of(chip):
        return plain_dot(rows_of(n.d_gate_v, chip, site), n.w_g[...]) + plain_dot(
            rows_of(n.d_up_v, chip, site), n.w_u[...]
        )

    def add_gain(row, value, where):
        row = pl.ds(row, 1)
        n.gain_grads[row] = value if where.start == 0 else n.gain_grads[row] + value

    def local(total, where):
        gain_grad, d_hidden = norm_back_rows(
            n.hidden_v[where], n.gains_v[2 * layer + 1 : 2 * layer + 2], total
        )
        d_hidden = d_hidden + n.top_v[where].astype(FULL)
        add_gain(1, gain_grad, where)
        n.d_hidden[where] = d_hidden
        return d_hidden.astype(LOW)

    def use_d_mixed(chip, rows):
        n.d_mixed[chip] = times_trans(rows, n.w_o[...]).astype(LOW)

    working = ffn_products(n, loads, made, normed_two)
    if layer == 0:
        step_on(working)(5)
    spread = spread_of(n, branch, n.back_send, n.back_recv, use_d_mixed)
    fold_spread(fold_of(n, part_of), spread, local, step_on(working))
    for _ in working:
        pass
    one_copies = [] if rows_one is None else [copies.start(rows_one, normed_one)]
    copies.wait(*attn_copies)
    attend_back(n)
    copies.wait(*next_copies)

    def part_of_two(chip):
        return plain_dot(rows_of(n.d_qkv, chip, site), n.w_in[...])

    def local_two(total, where):
        gain_grad, d_input = norm_back_rows(
            x_rows[where].astype(FULL), n.gains_v[2 * layer : 2 * layer + 1], total
        )
        d_input = (d_input + n.d_hidden[where]).astype(LOW)
        add_gain(0, gain_grad, where)
        n.d_input_v[where] = d_input
        return d_input

    working = in_products(n, one_copies, made, normed_one, branch)
    if layer == 1:

        def use_d_act(chip, rows):
            d_act = times_trans(rows, w_next[...])
            for out, slope in ((n.d_gate_v, n.gate_slope_v), (n.d_up_v, n.up_slope_v)):
                put(out, chip, d_act * slope[chip].astype(FULL).reshape(d_act.shape))

        spread = spread_of(
            n, n.held_two, n.back_two_send, n.back_two_recv, use_d_act, n.top_next
        )
        fold_spread(fold_of(n, part_of_two), spread, local_two, step_on(working))
        for _ in working:
            pass
        for source, target in (
            (n.d_gate_v, n.d_gate_next), (n.d_up_v, n.d_up_next), (n.d_input_v, n.d_input),
            (n.gain_grads, n.gain_out),
        ):
            copies.start(source, target)
        return
    fold_spread(fold_of(n, part_of_two), None, local_two, step_on(working))
    for _ in working:
        pass
    copies.start(n.d_input_v, n.d_input)
    cross.send(n.d_input_v, n.came_input, 0)

    def part_of_last(chip):
        return plain_dot(rows_of(n.act_last_v, chip, site), w_next[...])

    def local_last(total, where):
        n.result_v[where] = (n.hidden_last_v[where] + total).astype(LOW)

    buffers = (n.mine, n.pass_out, n.pass_in_two, n.stage, n.land_two)
    links = Links(n.last_send, n.last_recv, site)
    gains_on = fold_gains(n)
    next(gains_on)
    fold_spread(
        Fold(site, part_of_last, buffers, links), None, local_last,
        lambda count: next(gains_on, None),
    )
    for _ in gains_on:
        pass
    copies.start(n.result_v, n.result)
    cross.send(n.result_v, n.came_result, 1)


def join_kernel(count, *refs):
    def take(number):
        nonlocal refs
        taken, refs = refs[:number], refs[number:]
        return taken

    own, came = (take(count), take(count)), (take(count), take(count))
    rows = (take(4), take(4))
    outs, row_outs = take(count + 1), take(2)
    own_at, came_at, sums = take(count), take(count), take(count)
    row_at, sems, out_sem, row_sem = refs
    section = lax.axis_index("section")

    def either(first, second):
        pl.when(section == 0)(first.start)
        pl.when(section != 0)(second.start)
        return first

    waits = []
    for index in range(count):
        for slot, (pair, target) in enumerate(((own, own_at), (came, came_at))):
            waits.append(
                either(
                    *(
                        pltpu.make_async_copy(
                            pair[layer][index], target[index], sems.at[2 * index + slot]
                        )
                        for layer in range(2)
                    )
                )
            )
    done = []
    row_waits = []
    for index, (own_a, own_b, came_a, came_b) in enumerate(rows):
        for slot, (first, second) in enumerate(((own_a, came_b), (came_a, own_b))):
            target, sem = row_at.at[index, slot], row_sem.at[2 * index + slot]
            row_waits.append(
                either(
                    pltpu.make_async_copy(first, target, sem),
                    pltpu.make_async_copy(second, target, sem),
                )
            )
    for copy in row_waits:
        copy.wait()
    for index, out in enumerate(row_outs):
        copy = pltpu.make_async_copy(row_at.at[index], out, row_sem.at[index])
        copy.start()
        done.append(copy)
    for index in range(count):
        waits[2 * index].wait()
        waits[2 * index + 1].wait()
        sums[index][...] = own_at[index][...].astype(FULL) + came_at[index][...].astype(FULL)
        if index < count - 1:
            parts = [(sums[index], outs[index])]
        else:
            parts = [(sums[index].at[pl.ds(k, 1)], outs[index + k]) for k in range(2)]
        for source, target in parts:
            copy = pltpu.make_async_copy(source, target, out_sem.at[len(done) - 2])
            copy.start()
            done.append(copy)
    for copy in done:
        copy.wait()


def join_all(own_a, own_b, came_a, came_b, results, input_grads):
    count = len(own_a)
    kept = [pltpu.VMEM(value.shape, LOW) for value in own_a]
    shapes = [value.shape for value in own_a]
    shapes = shapes[:-1] + [(1, *shapes[-1][1:])] * 2
    row_shape = jax.ShapeDtypeStruct((2, *results[0].shape), LOW)
    return pl.pallas_call(
        functools.partial(join_kernel, count),
        out_shape=[jax.ShapeDtypeStruct(value, FULL) for value in shapes] + [row_shape] * 2,
        in_specs=[IN_HBM] * (4 * count + 8),
        out_specs=[IN_HBM] * (count + 3),
        scratch_shapes=kept
        + kept
        + [pltpu.VMEM(value.shape, FULL) for value in own_a]
        + [
            pltpu.VMEM((2, *row_shape.shape), LOW),
            pltpu.SemaphoreType.DMA((2 * count,)),
            pltpu.SemaphoreType.DMA((count + 1,)),
            pltpu.SemaphoreType.DMA((4,)),
        ],
        compiler_params=pltpu.CompilerParams(vmem_limit_bytes=58 * 2**20),
        cost_estimate=pl.CostEstimate(flops=2**32, bytes_accessed=2**24, transcendentals=0),
        name="join_all",
    )(*own_a, *own_b, *came_a, *came_b, *results, *input_grads)


def relay_body(
    inputs,
    cotangent,
    positions,
    gain_attn,
    w_query,
    w_key,
    w_value,
    w_out,
    gain_ffn,
    w_gate,
    w_up,
    w_down,
):
    n_micro, per_device, model_width = inputs.shape
    n_seq = lax.axis_size("seq")
    n_shard = lax.axis_size("shard")
    members = n_seq * n_shard
    total_len = members * per_device
    section_idx = lax.axis_index("section")
    q_width = HEADS // members * HEAD_DIM
    in_width = q_width + 2 * HEAD_DIM
    hidden = w_down.shape[1]
    vmem = pltpu.VMEM

    def pick(first, second):
        return jnp.where(section_idx == 0, first, second)

    places = pick(positions[0], positions[1])
    gains_own = jnp.concatenate(
        [gain_attn, gain_ffn, jnp.zeros((6, gain_attn.shape[1]), gain_attn.dtype)], 0
    ).astype(FULL)
    own = dict(
        w_query=w_query[0], w_out=w_out[0], w_gate=w_gate[0], w_up=w_up[0], w_down=w_down[0]
    )

    order = (places.reshape(CHIPS, PLACE)[:, 0] // PLACE).astype(jnp.int32)
    numbers = jnp.arange(CHIPS, dtype=jnp.int32)
    block_at = jnp.sum(
        jnp.where(order[None, :] == numbers[:, None], numbers[None, :], 0), 1
    ).astype(jnp.int32)
    scalars = dict(block_at=block_at, order=order)
    half_dim = HEAD_DIM // 2
    inv_freq = THETA_BASE ** (-jnp.arange(half_dim, dtype=FULL) * (2.0 / HEAD_DIM))
    steps = jnp.concatenate([jnp.arange(PLACE), PLACE * jnp.arange(CHIPS)]).astype(FULL)
    angles = steps[:, None] * jnp.tile(inv_freq, 2 * q_width // HEAD_DIM)[None, :]
    turns = jnp.stack([jnp.cos(angles), jnp.sin(angles)])

    rows = (per_device, model_width)
    row_low, row_full = (rows, LOW), (rows, FULL)
    all_rows = ((CHIPS, 2, *rows), LOW)
    narrow = ((CHIPS, 2, per_device, hidden), LOW)
    wide = ((hidden, model_width), LOW)
    quarter = ((q_width, model_width), LOW)
    gain_row = ((8, model_width), FULL)
    kv_shape = (2, w_key.shape[1], model_width)
    small = gains_own.shape
    saved = dict(
        turned=((total_len, in_width), LOW),
        attended=((CHIPS, PLACE, q_width), FULL),
        spread=((CHIPS, 2 * PLACE), FULL),
        mixed=((CHIPS, 2, per_device, q_width), LOW),
    )
    saved_v = dict(
        turned_v=vmem(*saved["turned"]),
        attended_v=vmem(*saved["attended"]),
        spread_v=vmem(*saved["spread"]),
        mixed_v=vmem(*saved["mixed"]),
        turns_v=vmem(turns.shape, FULL),
    )
    attend_v_only = dict(
        qkv=vmem((CHIPS, PLACE, in_width), FULL),
        values_t=vmem((HEAD_DIM, total_len), LOW),
    )
    attend_v = dict(**saved_v, **attend_v_only)
    gates_v = dict(w_g=vmem(*wide), w_u=vmem(*wide))

    first = launch(
        "forward_first",
        0,
        forward_first,
        scalars,
        dict(
            inputs=inputs, cotangent=cotangent, gains_own=gains_own, w_key=w_key[0],
            w_value=w_value[0], turns=turns, **own,
        ),
        dict(
            x_query=quarter,
            x_out=quarter,
            x_gate=wide,
            x_up=wide,
            x_down=wide,
            gains=gain_row,
            kv_rows=((2, 2 * HEAD_DIM, model_width), LOW),
            top_all=all_rows,
            rows_one=all_rows,
            rows_two=all_rows,
            hidden=row_full,
            act_all=narrow,
            gate_slope=narrow,
            up_slope=narrow,
            **saved,
        ),
        dict(
            gains_mine=vmem(small, FULL),
            gains_x=vmem(small, FULL),
            gains_all=vmem((n_shard, n_seq, *small), FULL),
            gains_v=vmem(*gain_row),
            kv_mine=vmem(kv_shape, LOW),
            kv_x=vmem(kv_shape, LOW),
            kv_all=vmem((n_seq, 2, *kv_shape), LOW),
            w_kv=vmem((2, 2 * HEAD_DIM, model_width), LOW),
            small_send=pltpu.SemaphoreType.DMA((SMALL_SEMS,)),
            small_recv=pltpu.SemaphoreType.DMA((SMALL_SEMS,)),
            held=vmem(*all_rows),
            held_two=vmem(*all_rows),
            normed=vmem(*all_rows),
            w_q=vmem(*quarter),
            w_o=vmem(*quarter),
            hidden_v=vmem(*row_full),
            top_v=vmem(*row_low),
            act=vmem(*narrow),
            gate_slope_v=vmem(*narrow),
            up_slope_v=vmem(*narrow),
            **gates_v,
            **attend_v,
            **fold_buffers(rows),
            **spread_sems(
                "spread_send", "spread_recv", "spread_two_send", "spread_two_recv", "top_send",
                "top_recv",
            ),
        ),
    )
    crossed = dict(
        **own,
        x_query=first.x_query,
        x_out=first.x_out,
        x_gate=first.x_gate,
        x_up=first.x_up,
        x_down=first.x_down,
        gains=first.gains,
        kv_rows=first.kv_rows,
        turns=turns,
    )
    kv_pair = ((2, *kv_shape[1:]), LOW)
    own_sums = dict(
        own_down=wide, own_gate=wide, own_up=wide, own_out=quarter, own_query=quarter,
        own_kv=kv_pair,
    )
    came_sums = dict(
        came_down=wide, came_gate=wide, came_out=quarter, came_query=quarter, came_kv=kv_pair
    )
    back_v = dict(
        d_gate_v=vmem(*narrow),
        d_up_v=vmem(*narrow),
        act=vmem(*narrow),
        hidden_v=vmem(*row_full),
        top_v=vmem(*row_low),
        x_v=vmem(*row_low),
        d_hidden=vmem(*row_full),
        d_input_v=vmem(*row_low),
        gains_v=vmem(*gain_row),
        gain_grads=vmem((2, model_width), FULL),
        w_o=vmem(*quarter),
        w_in=vmem((in_width, model_width), LOW),
        w_d=vmem(*wide),
        top_held=vmem(*all_rows),
        normed=vmem(*all_rows),
        held=vmem(*all_rows),
        d_mixed=vmem((CHIPS, PLACE, q_width), LOW),
        d_qkv=vmem((CHIPS, 2, per_device, in_width), LOW),
        d_turned=vmem((CHIPS, PLACE, in_width), LOW),
        d_query=vmem((total_len, q_width), FULL),
        d_key=vmem((total_len, HEAD_DIM), FULL),
        d_value=vmem((total_len, HEAD_DIM), FULL),
        keys_t=vmem((HEAD_DIM, total_len), LOW),
        g_down_v=vmem(*wide),
        g_gate_v=vmem(*wide),
        g_up_v=vmem(*wide),
        g_out_v=vmem(*quarter),
        g_query_v=vmem(*quarter),
        g_kv_v=vmem(*kv_pair),
        kv_mine=vmem((2, n_seq, *kv_shape[1:]), LOW),
        kv_came=vmem((n_seq - 1, 2, *kv_shape[1:]), LOW),
        kv_send=pltpu.SemaphoreType.DMA((n_seq - 1,)),
        kv_recv=pltpu.SemaphoreType.DMA((n_seq - 1,)),
        **gates_v,
        **saved_v,
        **fold_buffers(rows),
    )

    def back_in(done, d_gate, d_up, top_all):
        return dict(
            d_gate=d_gate,
            d_up=d_up,
            hidden=done.hidden,
            act_all=done.act_all,
            top_all=top_all,
            rows_one=done.rows_one,
            rows_two=done.rows_two,
            **{key: getattr(done, key) for key in saved},
            **crossed,
        )

    merged_v = dict(
        back_v,
        act_prev_v=vmem(*narrow),
        hidden_prev_v=vmem(*row_full),
        w_d_prev=vmem(*wide),
        held_two=vmem(*all_rows),
        result_v=vmem(*row_low),
        gate_slope_v=vmem(*narrow),
        up_slope_v=vmem(*narrow),
        **attend_v_only,
        **spread_sems(
            "spread_send", "spread_recv", "spread_two_send", "spread_two_recv", "back_send",
            "back_recv", "back_two_send", "back_two_recv",
        ),
    )
    del merged_v["x_v"]
    third = launch(
        "second_layer",
        1,
        second_layer,
        scalars,
        dict(
            act_prev=first.act_all,
            hidden_prev=first.hidden,
            top_all=first.top_all,
            cotangent=cotangent,
            gate_slope=first.gate_slope,
            up_slope=first.up_slope,
            **crossed,
        ),
        dict(
            result=row_low,
            hidden=row_full,
            act_all=narrow,
            d_gate_next=narrow,
            d_up_next=narrow,
            top_next=all_rows,
            d_input=row_low,
            gain_out=((2, model_width), FULL),
            came_result_first=row_low,
            **own_sums,
            **came_sums,
        ),
        merged_v,
    )
    fourth = launch(
        "first_layer_back",
        2,
        first_layer_back,
        scalars,
        dict(
            **back_in(first, third.d_gate_next, third.d_up_next, third.top_next),
            inputs=inputs,
            top_rows=third.d_input,
            own_up_later=third.own_up,
            gain_later=third.gain_out,
            act_last=third.act_all,
            hidden_last=third.hidden,
        ),
        dict(
            d_input=row_low,
            result=row_low,
            gain_sums=((2, small[1]), FULL),
            came_up=wide,
            came_up_later=wide,
            came_input=row_low,
            came_input_later=row_low,
            came_result=row_low,
            **own_sums,
            **came_sums,
        ),
        dict(
            act_last_v=vmem(*narrow),
            hidden_last_v=vmem(*row_full),
            gain_later_v=vmem((2, model_width), FULL),
            result_v=vmem(*row_low),
            pass_in_two=vmem((CHIPS, *rows), LOW),
            land_two=vmem((CHIPS - 1, *rows), LOW),
            last_send=pltpu.SemaphoreType.DMA((FOLD_SEMS,)),
            last_recv=pltpu.SemaphoreType.DMA((FOLD_SEMS,)),
            gain_parts=vmem((n_seq, n_shard, *small), FULL),
            gain_came=vmem((n_seq - 1, n_shard, *small), FULL),
            gain_shards=vmem((n_shard, *small), FULL),
            gain_last=vmem((n_shard - 1, *small), FULL),
            gain_own=vmem(small, FULL),
            gain_other=vmem(small, FULL),
            gain_sums_v=vmem((2, small[1]), FULL),
            gain_send=pltpu.SemaphoreType.DMA((7,)),
            gain_recv=pltpu.SemaphoreType.DMA((7,)),
            **back_v,
            **spread_sems("back_send", "back_recv"),
        ),
    )

    def sums(of, done):
        return [getattr(done, f"{of}_{key}") for key in ("down", "gate", "up", "out", "query", "kv")]

    third.came_up = fourth.came_up_later
    g_down, g_gate, g_up, g_out, g_query, g_key, g_value, outputs, input_grads = join_all(
        sums("own", fourth),
        sums("own", third),
        sums("came", fourth),
        sums("came", third),
        (third.result, fourth.result, third.came_result_first, fourth.came_result),
        (fourth.d_input, third.d_input, fourth.came_input, fourth.came_input_later),
    )
    return (
        outputs[None],
        input_grads[None],
        fourth.gain_sums[:1],
        g_query[None],
        g_key,
        g_value,
        g_out[None],
        fourth.gain_sums[1:],
        g_gate[None],
        g_up[None],
        g_down[None],
    )


def fits_relay(mesh):
    shape = mesh.shape
    return shape["section"] == 2 and shape["shard"] == KV_HEADS == RING and shape["seq"] == 4


def solution(mesh):
    in_specs = (
        P(None, ("shard", "seq"), None),
        P(None, ("shard", "seq"), None),
        P(),
        P("section", ("shard", "seq")),
        P("section", ("shard", "seq"), None),
        P("section", ("shard", "seq"), None),
        P("section", ("shard", "seq"), None),
        P("section", ("shard", "seq"), None),
        P("section", ("shard", "seq")),
        P("section", ("shard", "seq"), None),
        P("section", ("shard", "seq"), None),
        P("section", ("shard", "seq"), None),
    )
    out_specs = (
        P("section", None, ("shard", "seq"), None),
        P("section", None, ("shard", "seq"), None),
        P("section", ("shard", "seq")),
        P("section", ("shard", "seq"), None),
        P("section", ("shard", "seq"), None),
        P("section", ("shard", "seq"), None),
        P("section", ("shard", "seq"), None),
        P("section", ("shard", "seq")),
        P("section", ("shard", "seq"), None),
        P("section", ("shard", "seq"), None),
        P("section", ("shard", "seq"), None),
    )
    chosen = relay_body if fits_relay(mesh) else body
    return jax.shard_map(chosen, mesh=mesh, in_specs=in_specs, out_specs=out_specs, check_vma=False)
```

```python
import functools
import math
import types

import jax
import jax.numpy as jnp
from jax import lax
from jax.experimental import pallas as pl
from jax.experimental.pallas import tpu as pltpu
from jax.sharding import PartitionSpec as P

HEADS = 32
KV_HEADS = 4
HEAD_DIM = 64


EPSILON = 1e-05
THETA_BASE = 10000.0
NEG_LARGE = -1e30


def shifted(value, axis, by):
    count = lax.axis_size(axis)
    pairs = [(i, i + by) for i in range(count) if 0 <= i + by < count]
    return lax.ppermute(value, axis, pairs)


def times_trans(left, right):
    return lax.dot_general(
        left, right, (((1,), (1,)), ((), ())), preferred_element_type=jnp.float32
    )


def outer_sum(left, right):
    return lax.dot_general(
        left, right, (((0,), (0,)), ((), ())), preferred_element_type=jnp.float32
    )


def plain_dot(left, right):
    return jnp.dot(left, right, preferred_element_type=jnp.float32)


def rotate(values, places, direction):
    half_dim = values.shape[-1] // 2
    inv_freq = THETA_BASE ** (-jnp.arange(half_dim, dtype=jnp.float32) * (2.0 / values.shape[-1]))
    angles = places.astype(jnp.float32)[:, None] * inv_freq[None, :]
    cosine = jnp.cos(angles)[:, None, :]
    sine_val = direction * jnp.sin(angles)[:, None, :]
    first = values[..., :half_dim]
    second = values[..., half_dim:]
    return jnp.concatenate(
        [first * cosine - second * sine_val, second * cosine + first * sine_val], -1
    )


def scaled(values, gain_vec):
    factor = lax.rsqrt(jnp.mean(values * values, -1, keepdims=True) + EPSILON)
    return values * factor * gain_vec


def norm_back(values, gain_vec, grad_in):
    factor = lax.rsqrt(jnp.mean(values * values, -1, keepdims=True) + EPSILON)
    gain_grad = jnp.sum(grad_in * values * factor, 0)
    mean_term = jnp.mean(grad_in * gain_vec * values, -1, keepdims=True)
    return (
        gain_grad,
        factor * gain_vec * grad_in - values * (factor * factor * factor) * mean_term,
    )


def ffn_back(grad_rows, kept_rows, gate_pre, up_pre, wg_part, wu_part, wd_part):
    sigmoid_val = jax.nn.sigmoid(gate_pre)
    silu_val = gate_pre * sigmoid_val
    hidden_act = (silu_val * up_pre).astype(jnp.bfloat16)
    grad_down = outer_sum(hidden_act, grad_rows)
    d_act = times_trans(grad_rows, wd_part)
    d_gate = (d_act * up_pre * sigmoid_val * (1.0 + gate_pre * (1.0 - sigmoid_val))).astype(
        jnp.bfloat16
    )
    d_up = (d_act * silu_val).astype(jnp.bfloat16)
    grad_gate = outer_sum(d_gate, kept_rows)
    grad_up = outer_sum(d_up, kept_rows)
    d_normed = plain_dot(d_gate, wg_part) + plain_dot(d_up, wu_part)
    return ((grad_gate, grad_up, grad_down), d_normed)


def body(
    inputs,
    cotangent,
    positions,
    gain_attn,
    w_query,
    w_key,
    w_value,
    w_out,
    gain_ffn,
    w_gate,
    w_up,
    w_down,
):
    n_micro, per_device, model_width = inputs.shape
    n_seq = lax.axis_size("seq")
    n_shard = lax.axis_size("shard")
    section_idx = lax.axis_index("section")
    shard_pos = lax.axis_index("shard")
    member = shard_pos * n_seq + lax.axis_index("seq")
    span_rows = per_device * n_seq
    total_len = span_rows * n_shard
    local_heads = HEADS // n_seq
    kv_repeat = n_seq // KV_HEADS
    q_width = local_heads * HEAD_DIM
    attn_scale = 1.0 / math.sqrt(HEAD_DIM)
    gain_one, gain_two, wq_full, wk_full, wv_full, wo_full = (
        lax.all_gather(gain_attn[0], ("shard", "seq"), axis=0, tiled=True),
        lax.all_gather(gain_ffn[0], ("shard", "seq"), axis=0, tiled=True),
        lax.all_gather(w_query[0], ("shard", "seq"), axis=0, tiled=True),
        lax.all_gather(w_key[0], ("shard", "seq"), axis=0, tiled=True),
        lax.all_gather(w_value[0], ("shard", "seq"), axis=0, tiled=True),
        lax.all_gather(w_out[0], ("shard", "seq"), axis=0, tiled=True),
    )
    gain_a = gain_one.astype(jnp.float32)
    gain_f = gain_two.astype(jnp.float32)
    wg_use, wu_use, wd_use = (w_gate[0], w_up[0], w_down[0])

    def spread_rows(block_in):
        return lax.all_gather(block_in, ("shard", "seq"), axis=0, tiled=True)

    def fold_rows(block_in):
        return lax.psum_scatter(block_in, ("shard", "seq"), scatter_dimension=0, tiled=True)

    def to_heads(block_in):
        return lax.all_to_all(block_in, "seq", split_axis=1, concat_axis=0, tiled=True)

    def to_tokens(block_in):
        return lax.all_to_all(block_in, "seq", split_axis=0, concat_axis=1, tiled=True)

    def over_keys(head_keys, head_values, step_fn, init_state):
        return step_fn(
            init_state,
            (
                lax.all_gather(head_keys, "shard", axis=0, tiled=True),
                lax.all_gather(head_values, "shard", axis=0, tiled=True),
            ),
            jnp.int32(0),
        )

    def place_sets(batch_index):
        place_row = lax.dynamic_index_in_dim(positions, batch_index, 0, keepdims=False)
        token_places = lax.dynamic_slice_in_dim(place_row, member * per_device, per_device)
        span_places = lax.dynamic_slice_in_dim(place_row, shard_pos * span_rows, span_rows)
        return (place_row, token_places, span_places)

    zero_rows = jnp.zeros((per_device, model_width), jnp.bfloat16)
    arrived_x = zero_rows
    results = []
    stored = []
    for tick_index in range(n_micro + 1):
        own_rows = inputs[tick_index] if tick_index < n_micro else zero_rows
        input_now = jnp.where(section_idx == 0, own_rows, arrived_x)
        batch_index = jnp.clip(tick_index - section_idx, 0, n_micro - 1)
        forward_place_row, forward_token_places, forward_span_places = place_sets(batch_index)
        forward_values_in = input_now.astype(jnp.float32)
        forward_normed_one = scaled(forward_values_in, gain_a).astype(jnp.bfloat16)
        queries = rotate(
            times_trans(forward_normed_one, wq_full).reshape(per_device, HEADS, HEAD_DIM),
            forward_token_places,
            1.0,
        ).astype(jnp.bfloat16)
        key_rows = rotate(
            times_trans(forward_normed_one, wk_full).reshape(per_device, KV_HEADS, HEAD_DIM),
            forward_token_places,
            1.0,
        ).astype(jnp.bfloat16)
        value_rows = (
            times_trans(forward_normed_one, wv_full)
            .reshape(per_device, KV_HEADS, HEAD_DIM)
            .astype(jnp.bfloat16)
        )
        key_rows = jnp.repeat(key_rows, kv_repeat, axis=1)
        value_rows = jnp.repeat(value_rows, kv_repeat, axis=1)
        packed = jnp.concatenate(
            [queries.reshape(per_device, n_seq, q_width), key_rows, value_rows], -1
        )
        arrived = to_heads(packed)[:, 0]
        forward_head_query = arrived[:, :q_width].reshape(span_rows, local_heads, HEAD_DIM)
        forward_head_keys = arrived[:, q_width : q_width + HEAD_DIM]
        forward_head_values = arrived[:, q_width + HEAD_DIM :]

        def absorb(state_in, key_piece, start_row):
            run_max, run_total, run_acc = state_in
            piece_keys, piece_values = key_piece
            visible = forward_place_row[None, None, :] <= forward_span_places[None, :, None]
            scores = (
                jnp.einsum(
                    "qhd,kd->hqk",
                    forward_head_query,
                    piece_keys,
                    preferred_element_type=jnp.float32,
                )
                * attn_scale
            )
            scores = jnp.where(visible, scores, NEG_LARGE)
            new_max = jnp.maximum(run_max, jnp.max(scores, -1))
            weight = jnp.where(visible, jnp.exp(scores - new_max[..., None]), 0.0)
            rescale = jnp.exp(run_max - new_max)
            run_total = jnp.sum(weight, -1)
            run_acc = run_acc * rescale.T[..., None] + jnp.einsum(
                "hqk,kd->qhd",
                weight.astype(jnp.bfloat16),
                piece_values,
                preferred_element_type=jnp.float32,
            )
            return (new_max, run_total, run_acc)

        forward_start_state = (
            jnp.full((local_heads, span_rows), NEG_LARGE, jnp.float32),
            jnp.zeros((local_heads, span_rows), jnp.float32),
            jnp.zeros((span_rows, local_heads, HEAD_DIM), jnp.float32),
        )
        run_max, run_total, run_acc = over_keys(
            forward_head_keys, forward_head_values, absorb, forward_start_state
        )
        forward_attended = run_acc / run_total.T[..., None]
        forward_spread = run_max + jnp.log(run_total)
        forward_mixed_tok = to_tokens(
            forward_attended.astype(jnp.bfloat16).reshape(span_rows, 1, q_width)
        ).reshape(per_device, HEADS * HEAD_DIM)
        forward_hidden_in = forward_values_in + plain_dot(forward_mixed_tok, wo_full)
        normed_two = scaled(forward_hidden_in, gain_f).astype(jnp.bfloat16)
        forward_kept_rows = spread_rows(normed_two)
        forward_gate_pre = times_trans(forward_kept_rows, wg_use)
        forward_up_pre = times_trans(forward_kept_rows, wu_use)
        hidden_act = (jax.nn.silu(forward_gate_pre) * forward_up_pre).astype(jnp.bfloat16)
        branch = fold_rows(plain_dot(hidden_act, wd_use))
        result = (forward_hidden_in + branch).astype(jnp.bfloat16)
        forward_saved = (
            input_now,
            forward_head_query,
            forward_head_keys,
            forward_head_values,
            forward_attended,
            forward_spread,
            forward_mixed_tok,
            forward_hidden_in,
            forward_kept_rows,
            forward_gate_pre,
            forward_up_pre,
        )
        result, saved = (result, forward_saved)
        results.append(result)
        stored.append(saved)
        if tick_index < n_micro:
            arrived_x = shifted(result, "section", 1)
    returned = zero_rows
    grads_back = []
    row_lists = []
    gain_total = None
    ffn_total = None
    for tick_index in range(n_micro + 1):
        own_rows = cotangent[tick_index] if tick_index < n_micro else zero_rows
        grad_now = jnp.where(section_idx == 1, own_rows, returned)
        batch_index = jnp.clip(tick_index - 1 + section_idx, 0, n_micro - 1)
        early_saved = stored[max(tick_index - 1, 0)]
        late_saved = stored[min(tick_index + 1, n_micro)]
        saved = jax.tree.map(
            lambda early_val, late_val: jnp.where(section_idx == 0, early_val, late_val),
            early_saved,
            late_saved,
        )
        (
            input_bf,
            head_query,
            backward_head_keys,
            backward_head_values,
            attended,
            spread,
            mixed_tok,
            hidden_in,
            kept_rows,
            gate_pre,
            up_pre,
        ) = saved
        backward_place_row, backward_token_places, backward_span_places = place_sets(batch_index)
        values_in = input_bf.astype(jnp.float32)
        normed_one = scaled(values_in, gain_a).astype(jnp.bfloat16)
        grad_all = spread_rows(grad_now)
        ffn_terms, d_partial = ffn_back(
            grad_all, kept_rows, gate_pre, up_pre, wg_use, wu_use, wd_use
        )
        d_normed_two = fold_rows(d_partial)
        grad_gf, d_hidden = norm_back(hidden_in, gain_f, d_normed_two)
        d_hidden = d_hidden + grad_now.astype(jnp.float32)
        d_branch = d_hidden.astype(jnp.bfloat16)
        d_mixed = times_trans(d_branch, wo_full).astype(jnp.bfloat16)
        d_att = to_heads(d_mixed.reshape(per_device, n_seq, q_width))[:, 0].reshape(
            span_rows, local_heads, HEAD_DIM
        )
        offset = jnp.sum(d_att.astype(jnp.float32) * attended, -1).T

        def collect(state_in, key_piece, start_row):
            piece_keys, piece_values = key_piece
            visible = backward_place_row[None, None, :] <= backward_span_places[None, :, None]
            scores = (
                jnp.einsum(
                    "qhd,kd->hqk", head_query, piece_keys, preferred_element_type=jnp.float32
                )
                * attn_scale
            )
            probs = jnp.where(visible, jnp.exp(scores - spread[..., None]), 0.0)
            d_probs = jnp.einsum(
                "qhd,kd->hqk", d_att, piece_values, preferred_element_type=jnp.float32
            )
            d_score = (probs * (d_probs - offset[..., None]) * attn_scale).astype(jnp.bfloat16)
            d_query_acc = jnp.einsum(
                "hqk,kd->qhd", d_score, piece_keys, preferred_element_type=jnp.float32
            )
            key_part = jnp.einsum(
                "hqk,qhd->kd", d_score, head_query, preferred_element_type=jnp.float32
            )
            value_part = jnp.einsum(
                "hqk,qhd->kd", probs.astype(jnp.bfloat16), d_att, preferred_element_type=jnp.float32
            )
            return (d_query_acc, key_part, value_part)

        start_state = (
            jnp.zeros((span_rows, local_heads, HEAD_DIM), jnp.float32),
            jnp.zeros((total_len, HEAD_DIM), jnp.float32),
            jnp.zeros((total_len, HEAD_DIM), jnp.float32),
        )
        d_query_acc, d_keys_all, d_values_all = over_keys(
            backward_head_keys, backward_head_values, collect, start_state
        )
        own_keys = lax.psum_scatter(
            d_keys_all.astype(jnp.bfloat16), "shard", scatter_dimension=0, tiled=True
        ).astype(jnp.float32)
        own_values = lax.psum_scatter(
            d_values_all.astype(jnp.bfloat16), "shard", scatter_dimension=0, tiled=True
        ).astype(jnp.float32)
        d_query_head = rotate(d_query_acc, backward_span_places, -1.0).astype(jnp.bfloat16)
        d_query = to_tokens(d_query_head.reshape(span_rows, 1, q_width)).reshape(
            per_device, HEADS * HEAD_DIM
        )
        own_keys = rotate(own_keys[:, None, :], backward_span_places, -1.0)[:, 0]
        back_kv = lax.all_to_all(
            jnp.concatenate([own_keys, own_values], -1)[:, None, :].astype(jnp.bfloat16),
            "seq",
            split_axis=0,
            concat_axis=1,
            tiled=True,
        ).astype(jnp.float32)
        back_kv = jnp.sum(back_kv.reshape(per_device, KV_HEADS, kv_repeat, 2 * HEAD_DIM), 2)
        d_key = (
            back_kv[..., :HEAD_DIM].reshape(per_device, KV_HEADS * HEAD_DIM).astype(jnp.bfloat16)
        )
        d_value = (
            back_kv[..., HEAD_DIM:].reshape(per_device, KV_HEADS * HEAD_DIM).astype(jnp.bfloat16)
        )
        d_normed_one = (
            plain_dot(d_query, wq_full) + plain_dot(d_key, wk_full) + plain_dot(d_value, wv_full)
        )
        grad_ga, d_input = norm_back(values_in, gain_a, d_normed_one)
        d_input = d_input + d_hidden
        gain_terms = (grad_ga, grad_gf)
        row_terms = (d_query, d_key, d_value, normed_one, mixed_tok, d_branch)
        d_input, gain_terms, row_terms, ffn_terms = (
            d_input.astype(jnp.bfloat16),
            gain_terms,
            row_terms,
            ffn_terms,
        )
        grads_back.append(d_input)
        row_lists.append(row_terms)
        if tick_index < n_micro:
            returned = shifted(d_input, "section", -1)
        if gain_total is None:
            gain_total = gain_terms
            ffn_total = ffn_terms
        else:
            gain_total = jax.tree.map(jnp.add, gain_total, gain_terms)
            ffn_total = jax.tree.map(jnp.add, ffn_total, ffn_terms)
    joined = [
        jnp.concatenate([row_set[index_val] for row_set in row_lists], 0) for index_val in range(6)
    ]
    grad_wq = outer_sum(joined[0], joined[3])
    grad_wk = outer_sum(joined[1], joined[3])
    grad_wv = outer_sum(joined[2], joined[3])
    grad_wo = outer_sum(joined[4], joined[5])
    attn_owned = (
        lax.psum_scatter(gain_total[0], ("shard", "seq"), scatter_dimension=0, tiled=True),
        lax.psum_scatter(gain_total[1], ("shard", "seq"), scatter_dimension=0, tiled=True),
        lax.psum_scatter(grad_wq, ("shard", "seq"), scatter_dimension=0, tiled=True),
        lax.psum_scatter(grad_wk, ("shard", "seq"), scatter_dimension=0, tiled=True),
        lax.psum_scatter(grad_wv, ("shard", "seq"), scatter_dimension=0, tiled=True),
        lax.psum_scatter(grad_wo, ("shard", "seq"), scatter_dimension=0, tiled=True),
    )
    outputs = lax.dynamic_slice_in_dim(jnp.stack(results), section_idx, n_micro, 0)[None]
    input_grads = lax.dynamic_slice_in_dim(jnp.stack(grads_back), 1 - section_idx, n_micro, 0)[None]
    return (
        outputs,
        input_grads,
        attn_owned[0][None],
        attn_owned[2][None],
        attn_owned[3][None],
        attn_owned[4][None],
        attn_owned[5][None],
        attn_owned[1][None],
        ffn_total[0][None],
        ffn_total[1][None],
        ffn_total[2][None],
    )


LOW = jnp.bfloat16
FULL = jnp.float32
MESH = pl.DeviceIdType.MESH
RING = 4
CHIPS = 2 * RING
SPLIT = 2
LAG = (0, 0, 1, 2, 3)
PLACE = 128
ORDER = ((2, 1), (1, 1), (3, 1), (0, 1), (2, 0), (1, 0), (3, 0), (0, 0))
IN_VMEM = pl.BlockSpec(memory_space=pltpu.VMEM)
IN_HBM = pl.BlockSpec(memory_space=pltpu.HBM)
IN_SMEM = pl.BlockSpec(memory_space=pltpu.SMEM)


class Site:
    def __init__(self):
        self.section = lax.axis_index("section")
        self.z = lax.axis_index("shard")
        member = lax.axis_index("seq")
        self.y = lax.div(member, 2)
        self.core = lax.rem(member, 2)
        self.up = (self.section, lax.rem(self.z + 1, RING), member)
        self.down = (self.section, lax.rem(self.z + RING - 1, RING), member)
        self.across = (self.section, self.z, (1 - self.y) * 2 + self.core)
        self.sibling = (self.section, self.z, self.y * 2 + 1 - self.core)
        self.corner = (self.section, self.z, (1 - self.y) * 2 + 1 - self.core)
        self.opposite = (self.section, lax.rem(self.z + 2, RING), member)
        self.partner = (1 - self.section, self.z, member)
        self.member = member

    def chip(self, along_z, along_y):
        return lax.rem(self.z + along_z, RING) * 2 + lax.rem(self.y + along_y, 2)


class Links:
    def __init__(self, send, recv, site):
        self.send, self.recv, self.site = send, recv, site
        self.sent = []

    def copy(self, index, src, dst, device):
        return pltpu.make_async_remote_copy(
            src_ref=src,
            dst_ref=dst,
            send_sem=self.send.at[index],
            recv_sem=self.recv.at[index],
            device_id=device,
            device_id_type=MESH,
        )

    def go(self, index, src, dst, device):
        copy = self.copy(index, src, dst, device)
        copy.start()
        self.sent.append(copy)

    def got(self, index, where):
        self.copy(index, where, where, self.site.sibling).wait_recv()
        return where

    def close(self):
        for copy in self.sent:
            copy.wait_send()


def greet(site):
    barrier = pltpu.get_barrier_semaphore()
    devices = (
        site.up, site.down, site.across, site.sibling, site.corner, site.opposite, site.partner
    )
    for device in devices:
        pl.semaphore_signal(barrier, inc=1, device_id=device, device_id_type=MESH)
    pl.semaphore_wait(barrier, len(devices))


SPREAD_SEMS = 7 * SPLIT + CHIPS
FOLD_SEMS = 7 * SPLIT + CHIPS
SMALL_SEMS = 11
COPY_SEMS = 64
CROSS_SEMS = 40
PIECE = 128


class Spread:
    def __init__(self, site, held, links, use):
        self.site, self.held, self.links, self.use = site, held, links, use
        self.size = held.shape[2] // SPLIT
        self.up, self.down, self.over, self.relay, self.y_below, self.y_above, self.y_far = (
            k * SPLIT for k in range(7)
        )
        self.along = ((0, 0), (3, 0), (1, 0), (0, 1), (2, 0), (3, 1), (1, 1), (2, 1))

    def piece(self, slot, part):
        site = self.site
        rows = pl.ds(part * self.size, self.size)
        return self.held.at[site.chip(*self.along[slot]), site.core, rows]

    def block(self, slot, core):
        return self.held.at[self.site.chip(*self.along[slot]), core]

    def go(self, index, where, device):
        self.links.go(index, where, where, device)

    def share(self, slot):
        self.go(7 * SPLIT + slot, self.block(slot, self.site.core), self.site.sibling)

    def consume(self, *slots):
        for slot in slots:
            self.links.got(7 * SPLIT + slot, self.block(slot, 1 - self.site.core))
            self.use(self.site.chip(*self.along[slot]))

    def ways(self, part):
        ways = (
            (self.up + part, 1, self.site.up, self.y_below + part),
            (self.down + part, 2, self.site.down, self.y_above + part),
        )
        return ways if part % 2 == 0 else ways[::-1]

    def own(self, part):
        where = self.piece(0, part)
        for index, _, device, _ in self.ways(part):
            self.go(index, where, device)
        self.go(self.over + part, where, self.site.across)

    def relays(self, part):
        for turn, (index, slot, device, over) in enumerate(self.ways(part)):
            came = self.links.got(index, self.piece(slot, part))
            if turn == 0:
                self.go(self.relay + part, came, device)
            self.go(over, came, self.site.across)

    def far(self, part):
        came = self.links.got(self.relay + part, self.piece(4, part))
        self.go(self.y_far + part, came, self.site.across)

    def after_relays(self):
        self.share(1)
        self.share(2)
        for part in range(SPLIT):
            self.links.got(self.over + part, self.piece(3, part))
        self.share(3)

    def tail(self, consume=True, first=0):
        def take(*slots):
            if consume:
                self.consume(*slots)

        self.share(4)
        take(*range(first, 3))
        for part in range(SPLIT):
            self.links.got(self.y_below + part, self.piece(5, part))
            self.links.got(self.y_above + part, self.piece(6, part))
        self.share(5)
        self.share(6)
        take(3, 4)
        for part in range(SPLIT):
            self.links.got(self.y_far + part, self.piece(7, part))
        self.share(7)
        take(5, 6, 7)
        if not consume:
            for slot in range(CHIPS):
                self.links.got(7 * SPLIT + slot, self.block(slot, 1 - self.site.core))

    def rest(self, consume=True):
        self.after_relays()
        for part in range(SPLIT):
            self.far(part)
        self.tail(consume)


class Fold:
    def __init__(self, site, part_of, buffers, links):
        self.site, self.part_of, self.links = site, part_of, links
        self.mine, self.pass_out, self.pass_in, self.stage, self.land = buffers
        self.rows = self.mine.shape[1]
        self.size = self.rows // SPLIT
        self.over = CHIPS
        self.relay, self.up, self.down = (CHIPS + (4 + k) * SPLIT for k in range(3))

    def where(self, part):
        return pl.ds(part * self.size, self.size)

    def came(self, index, where):
        return self.links.got(index, where)[...].astype(FULL)

    def compute(self, step):
        both = self.part_of(self.site.chip(*ORDER[step]))
        self.pass_out[step] = both[: self.rows].astype(LOW)
        self.links.go(step, self.pass_out.at[step], self.pass_in.at[step], self.site.sibling)
        self.mine[step] = both[self.rows :]

    def settle(self, step):
        self.mine[step] += self.came(step, self.pass_in.at[step])

    def send(self, index, slot, part, value, device):
        where = self.where(part)
        self.stage[slot, where] = value.astype(LOW)
        self.links.go(index, self.stage.at[slot, where], self.land.at[slot, where], device)

    def send_over(self, step, part):
        value = self.mine[step, self.where(part)]
        self.send(self.over + step * SPLIT + part, step, part, value, self.site.across)

    def start(self):
        self.compute(0)
        self.compute(1)
        for step in range(4):
            self.settle(step)
            self.send_over(step, 0)
            self.compute(step + 2)
        for part in range(1, SPLIT):
            for step in range(4):
                self.send_over(step, part)
        self.compute(6)
        self.compute(7)
        for step in range(4, CHIPS):
            self.settle(step)

    def pass_on(self, part):
        where = self.where(part)
        value = self.mine[4, where] + self.came(self.over + part, self.land.at[0, where])
        device = self.site.up if part % 2 == 0 else self.site.down
        self.send(self.relay + part, 4, part, value, device)

    def up_down(self, part):
        where = self.where(part)
        ways = ((5, self.up, self.site.up), (6, self.down, self.site.down))
        for step, base, device in ways if part % 2 else ways[::-1]:
            from_y = self.over + (step - 4) * SPLIT + part
            value = self.mine[step, where] + self.came(from_y, self.land.at[step - 4, where])
            if part % 2 == step - 5:
                value = value + self.came(self.relay + part, self.land.at[4, where])
            self.send(base + part, step, part, value, device)

    def final(self, part):
        where = self.where(part)
        value = self.mine[7, where] + self.came(
            self.over + 3 * SPLIT + part, self.land.at[3, where]
        )
        value = value + self.came(self.up + part, self.land.at[5, where])
        return value + self.came(self.down + part, self.land.at[6, where])


def fold_spread(fold, spread, local, idle):
    def finish(part):
        rows = local(fold.final(part), fold.where(part))
        if spread is not None:
            site = spread.site
            spread.held[site.chip(0, 0), site.core, fold.where(part)] = rows
            spread.own(part)

    fold.start()
    idle(3)
    last = SPLIT - 1
    for tick in range(SPLIT + LAG[-1]):
        steps = [tick - lag for lag in LAG]
        if 0 <= steps[0] < SPLIT:
            fold.pass_on(steps[0])
        if 0 <= steps[1] < SPLIT:
            fold.up_down(steps[1])
        if 0 <= steps[2] < SPLIT:
            finish(steps[2])
        if spread is not None:
            if steps[2] == last:
                spread.share(0)
            if 0 <= steps[3] < SPLIT:
                spread.relays(steps[3])
            if steps[3] == last:
                spread.after_relays()
            if 0 <= steps[4] < SPLIT:
                spread.far(steps[4])
            if steps[2] == last + 1:
                spread.consume(0)
        idle(3)
    if spread is not None:
        idle(10)
        spread.tail(first=1)
        spread.links.close()
    else:
        idle(10)
    fold.links.close()


class Cross:
    def __init__(self, n):
        self.site = n.site
        self.links = Links(n.cross_send, n.cross_recv, n.site)
        self.begun = []
        self.count = 0

    def where(self, layer, receives, action):
        if layer is None:
            action()
        else:
            pl.when((self.site.section == layer) == receives)(action)

    def send(self, src, dst, layer=None):
        rows = src.shape[0]
        pieces = []
        start = 0
        while start < rows:
            size = min(PIECE, rows - start)
            where = pl.ds(start, size)
            pieces.append(
                self.links.copy(self.count, src.at[where], dst.at[where], self.site.partner)
            )
            self.count += 1
            start += size

        def begin():
            for copy in pieces:
                copy.start()

        self.where(layer, False, begin)
        self.begun.append([pieces, layer, False])
        return len(self.begun) - 1

    def wait(self, index):
        pieces, layer, landed = self.begun[index]

        def arrive():
            for copy in pieces:
                copy.wait_recv()

        if not landed:
            self.begun[index][2] = True
            self.where(layer, True, arrive)

    def close(self):
        for index in range(len(self.begun)):
            self.wait(index)
        for pieces, layer, _ in self.begun:

            def leave():
                for copy in pieces:
                    copy.wait_send()

            self.where(layer, False, leave)
        self.begun = []


class Copies:
    def __init__(self, n):
        self.n, self.count, self.open = n, 0, []

    def sem(self):
        self.count += 1
        return self.n.copy_sem.at[self.count - 1]

    def start(self, src, dst):
        copy = pltpu.make_async_copy(src, dst, self.sem())
        copy.start()
        self.open.append(copy)
        return copy

    def pick(self, own, other, dst, layer):
        sem = self.sem()
        from_own = pltpu.make_async_copy(own, dst, sem)
        from_other = pltpu.make_async_copy(other, dst, sem)
        pl.when(self.n.site.section == layer)(from_own.start)
        pl.when(self.n.site.section != layer)(from_other.start)
        self.open.append(from_own)
        return from_own

    def wait(self, *copies):
        for copy in copies:
            if any(copy is other for other in self.open):
                self.open = [other for other in self.open if other is not copy]
                copy.wait()

    def close(self):
        self.wait(*list(self.open))


def kernel_of(body, names, *refs):
    n = types.SimpleNamespace(**dict(zip(names, refs)))
    n.site = Site()
    n.copies = Copies(n)
    n.cross = Cross(n)
    body(n)
    n.cross.close()
    n.copies.close()


def launch(name, ident, body, scalars, inputs, outputs, scratch):
    scratch = dict(
        scratch,
        copy_sem=pltpu.SemaphoreType.DMA((COPY_SEMS,)),
        cross_send=pltpu.SemaphoreType.DMA((CROSS_SEMS,)),
        cross_recv=pltpu.SemaphoreType.DMA((CROSS_SEMS,)),
    )
    names = [*scalars, *inputs, *outputs, *scratch]
    results = pl.pallas_call(
        functools.partial(kernel_of, body, names),
        out_shape=[jax.ShapeDtypeStruct(*value) for value in outputs.values()],
        in_specs=[IN_SMEM] * len(scalars) + [IN_HBM] * len(inputs),
        out_specs=[IN_HBM] * len(outputs),
        scratch_shapes=list(scratch.values()),
        compiler_params=pltpu.CompilerParams(
            collective_id=ident, has_side_effects=True, vmem_limit_bytes=60 * 2**20
        ),
        cost_estimate=pl.CostEstimate(flops=2**37, bytes_accessed=2**23, transcendentals=0),
        name=name,
    )(*scalars.values(), *inputs.values())
    return types.SimpleNamespace(**dict(zip(outputs, results)))


def fold_buffers(full):
    return dict(
        mine=pltpu.VMEM((CHIPS, *full), FULL),
        pass_out=pltpu.VMEM((CHIPS, *full), LOW),
        pass_in=pltpu.VMEM((CHIPS, *full), LOW),
        stage=pltpu.VMEM((CHIPS - 1, *full), LOW),
        land=pltpu.VMEM((CHIPS - 1, *full), LOW),
        fold_send=pltpu.SemaphoreType.DMA((FOLD_SEMS,)),
        fold_recv=pltpu.SemaphoreType.DMA((FOLD_SEMS,)),
    )


def fold_of(n, part_of):
    buffers = (n.mine, n.pass_out, n.pass_in, n.stage, n.land)
    return Fold(n.site, part_of, buffers, Links(n.fold_send, n.fold_recv, n.site))


def spread_of(n, held, send, recv, use, kept=None):
    def take(chip):
        block = held[chip]
        use(chip, block.reshape(block.shape[0] * block.shape[1], block.shape[2]))
        if kept is not None:
            n.copies.start(held.at[chip], kept.at[chip])

    return Spread(n.site, held, Links(send, recv, n.site), take)


def spread_sems(*names):
    return {name: pltpu.SemaphoreType.DMA((SPREAD_SEMS,)) for name in names}


def no_idle(count):
    pass


def rows_of(ref, chip, site):
    return jnp.concatenate([ref[chip, 1 - site.core], ref[chip, site.core]], 0)


def put(ref, chip, value):
    ref[chip] = value.astype(LOW).reshape(ref.shape[1:])


def gate_chunk(n, chip, rows):
    gate_pre = times_trans(rows, n.w_g[...])
    up_pre = times_trans(rows, n.w_u[...])
    sig = jax.nn.sigmoid(gate_pre)
    silu_val = gate_pre * sig
    put(n.act, chip, silu_val * up_pre)
    return up_pre * sig * (1.0 + gate_pre * (1.0 - sig)), silu_val


def norm_back_rows(values, gain_vec, grad_in):
    factor = lax.rsqrt(jnp.mean(values * values, -1, keepdims=True) + EPSILON)
    gain_grad = jnp.sum(grad_in * values * factor, 0, keepdims=True)
    mean_term = jnp.mean(grad_in * gain_vec * values, -1, keepdims=True)
    return (
        gain_grad,
        factor * gain_vec * grad_in - values * (factor * factor * factor) * mean_term,
    )


def swap_halves(value):
    width = value.shape[1]
    half = HEAD_DIM // 2
    lane = lax.broadcasted_iota(jnp.int32, value.shape, 1)
    return jnp.where(
        lax.rem(lane, HEAD_DIM) < half,
        pltpu.roll(value, width - half, 1),
        pltpu.roll(value, half, 1),
    )


def stacked(pair):
    return jnp.concatenate([pair[:, :HEAD_DIM], pair[:, HEAD_DIM:]], 0)


def side_by_side(turned):
    return jnp.concatenate([turned[:, :PLACE], turned[:, PLACE:]], 0).T


def hide_later(scores, fill):
    last = scores[-PLACE:]
    key = lax.broadcasted_iota(jnp.int32, last.shape, 0)
    query = lax.rem(lax.broadcasted_iota(jnp.int32, last.shape, 1), PLACE)
    last = jnp.where(key <= query, last, fill)
    if scores.shape[0] == PLACE:
        return last
    return jnp.concatenate([scores[:-PLACE], last], 0)


def turn_of(turns, place):
    near, far = pl.ds(0, PLACE), pl.ds(PLACE + place, 1)
    cos_near, sin_near = turns[0, near], turns[1, near]
    cos_far, sin_far = turns[0, far], turns[1, far]
    cosine = cos_near * cos_far - sin_near * sin_far
    sine = sin_near * cos_far + cos_near * sin_far
    lane = lax.broadcasted_iota(jnp.int32, cosine.shape, 1)
    sine = jnp.where(lax.rem(lane, HEAD_DIM) < HEAD_DIM // 2, -sine, sine)
    keyed = lane < HEAD_DIM
    return (
        jnp.concatenate([cosine, jnp.where(keyed, cosine, 1.0)], 1),
        jnp.concatenate([sine, jnp.where(keyed, sine, 0.0)], 1),
    )


def attend(n):
    q_width = 2 * HEAD_DIM
    scale = jnp.asarray(1.0 / math.sqrt(HEAD_DIM), LOW)
    for place in range(CHIPS):
        at = pl.ds(place * PLACE, PLACE)
        value = n.qkv[n.block_at[place]]
        cosine, sine = turn_of(n.turns_v, place)
        value = (value * cosine + swap_halves(value) * sine).astype(LOW)
        n.turned_v[at, :q_width] = value[:, :q_width] * scale
        n.turned_v[at, q_width:] = value[:, q_width:]
        n.values_t[:, at] = value[:, q_width:].astype(FULL).T[HEAD_DIM:].astype(LOW)
    for place in range(CHIPS):
        at = pl.ds(place * PLACE, PLACE)
        keys = pl.ds(0, (place + 1) * PLACE)
        query = stacked(n.turned_v[at, :q_width])
        scores = times_trans(n.turned_v[keys, q_width : q_width + HEAD_DIM], query)
        scores = hide_later(scores, NEG_LARGE)
        top = jnp.max(scores, 0, keepdims=True)
        weight = jnp.exp(scores - top)
        total = jnp.sum(weight, 0, keepdims=True)
        out = plain_dot(n.values_t[:, keys], weight.astype(LOW)) / total
        n.attended_v[place] = side_by_side(out)
        n.spread_v[pl.ds(place, 1)] = top + jnp.log(total)
    for block in range(CHIPS):
        put(n.mixed_v, block, n.attended_v[n.order[block]])


def keep_attention(n):
    n.copies.start(n.turned_v, n.turned)
    n.copies.start(n.attended_v, n.attended)
    n.copies.start(n.spread_v, n.spread)
    n.copies.start(n.mixed_v, n.mixed)


def attend_back(n):
    q_width = 2 * HEAD_DIM
    n.d_key[...] = jnp.zeros_like(n.d_key)
    n.d_value[...] = jnp.zeros_like(n.d_value)
    for place in range(CHIPS):
        at = pl.ds(place * PLACE, PLACE)
        n.keys_t[:, at] = n.turned_v[at, q_width:].astype(FULL).T[:HEAD_DIM].astype(LOW)
    for place in range(CHIPS):
        at = pl.ds(place * PLACE, PLACE)
        keys = pl.ds(0, (place + 1) * PLACE)
        d_out = n.d_mixed[n.block_at[place]]
        product = (d_out.astype(FULL) * n.attended_v[place]).T
        offset = jnp.concatenate(
            [
                jnp.sum(product[:HEAD_DIM], 0, keepdims=True),
                jnp.sum(product[HEAD_DIM:], 0, keepdims=True),
            ],
            1,
        )
        d_out = stacked(d_out)
        query = stacked(n.turned_v[at, :q_width])
        scores = times_trans(n.turned_v[keys, q_width : q_width + HEAD_DIM], query)
        scores = hide_later(scores, NEG_LARGE)
        probs = jnp.exp(scores - n.spread_v[pl.ds(place, 1)])
        d_probs = times_trans(n.turned_v[keys, q_width + HEAD_DIM :], d_out)
        d_scores = (probs * (d_probs - offset)).astype(LOW)
        n.d_key[keys] += plain_dot(d_scores, query)
        n.d_value[keys] += plain_dot(probs.astype(LOW), d_out)
        n.d_query[at] = side_by_side(plain_dot(n.keys_t[:, keys], d_scores)) * (
            1.0 / math.sqrt(HEAD_DIM)
        )
    for place in range(CHIPS):
        at = pl.ds(place * PLACE, PLACE)
        value = jnp.concatenate([n.d_query[at], n.d_key[at], n.d_value[at]], 1)
        cosine, sine = turn_of(n.turns_v, place)
        value = value * cosine - swap_halves(value) * sine
        n.d_turned[place] = value.astype(LOW)
    for block in range(CHIPS):
        put(n.d_qkv, block, n.d_turned[n.order[block]])


def gather_small(n):
    site = n.site
    links = n.links_small = Links(n.small_send, n.small_recv, site)
    links.go(0, n.gains_mine, n.gains_x, site.partner)
    links.go(1, n.kv_mine, n.kv_x, site.partner)
    links.got(0, n.gains_x)
    own, came = n.gains_mine[...], n.gains_x[...]
    first = site.section == 0
    n.gains_all[site.z, site.member] = jnp.concatenate(
        [
            jnp.where(first, own, came)[:2],
            jnp.where(first, came, own)[:2],
            jnp.zeros((4, own.shape[1]), FULL),
        ],
        0,
    )
    peers = (site.sibling, site.across, site.corner)
    mine = n.gains_all.at[site.z, site.member]
    for index, device in enumerate(peers):
        links.go(2 + index, mine, mine, device)
    for index, device in enumerate(peers):
        links.got(2 + index, n.gains_all.at[site.z, device[2]])
    shard = n.gains_all.at[site.z]
    for index, device in enumerate((site.up, site.down, site.opposite)):
        links.go(5 + index, shard, shard, device)


def gather_small_keys(n):
    site, links = n.site, n.links_small
    links.got(1, n.kv_x)
    n.kv_all[site.member, site.section] = n.kv_mine[...]
    n.kv_all[site.member, 1 - site.section] = n.kv_x[...]
    mine = n.kv_all.at[site.member]
    for index, device in enumerate((site.sibling, site.across, site.corner)):
        links.go(8 + index, mine, mine, device)


def gather_small_end(n):
    site, links = n.site, n.links_small
    for index, along_z in enumerate((RING - 1, 1, 2)):
        links.got(5 + index, n.gains_all.at[lax.rem(site.z + along_z, RING)])
    for index, device in enumerate((site.sibling, site.across, site.corner)):
        links.got(8 + index, n.kv_all.at[device[2]])
    links.close()
    n.gains_v[...] = jnp.concatenate(
        [n.gains_all[shard, seq] for shard in range(RING) for seq in range(RING)], 1
    )
    for layer in range(2):
        for index in range(2):
            rows = n.kv_all[:, layer, index]
            n.w_kv[layer, pl.ds(index * HEAD_DIM, HEAD_DIM)] = rows.reshape(
                HEAD_DIM, rows.shape[-1]
            )
    n.copies.start(n.gains_v, n.gains)
    n.copies.start(n.w_kv, n.kv_rows)


def forward_first(n):
    site, copies, cross = n.site, n.copies, n.cross
    own = (site.chip(0, 0), site.core)
    small = [
        copies.start(n.gains_own, n.gains_mine),
        copies.start(n.w_key, n.kv_mine.at[0]),
        copies.start(n.w_value, n.kv_mine.at[1]),
    ]
    rows_copy = copies.pick(n.inputs.at[0], n.inputs.at[1], n.held.at[own], 0)
    top_copy = copies.pick(n.cotangent.at[0], n.cotangent.at[1], n.top_v, 0)
    turns_copy = copies.start(n.turns, n.turns_v)
    greet(site)
    copies.wait(*small)
    gather_small(n)
    at_query, at_out, at_gate, at_up, _ = (
        cross.send(*pair)
        for pair in (
            (n.w_query, n.x_query),
            (n.w_out, n.x_out),
            (n.w_gate, n.x_gate),
            (n.w_up, n.x_up),
            (n.w_down, n.x_down),
        )
    )
    copies.wait(rows_copy)

    def use_first(chip, rows):
        normed = scaled(rows.astype(FULL), n.gains_v[:1]).astype(LOW)
        n.normed[chip] = normed.reshape(n.normed.shape[1:])
        n.qkv[chip] = jnp.concatenate(
            [times_trans(normed, n.w_q[...]), times_trans(normed, n.w_kv[0])], 1
        )
        copies.start(n.normed.at[chip], n.rows_one.at[chip])

    spread = spread_of(n, n.held, n.spread_send, n.spread_recv, use_first)
    for part in range(SPLIT):
        spread.own(part)
    spread.share(0)
    gather_small_keys(n)
    for part in range(SPLIT):
        spread.relays(part)
    gather_small_end(n)
    spread.after_relays()
    cross.wait(at_query)
    query_copy = copies.pick(n.w_query, n.x_query, n.w_q, 0)
    for part in range(SPLIT):
        spread.far(part)
    copies.wait(query_copy)
    copies.wait(top_copy, turns_copy)
    top_copy = copies.start(n.top_v, n.top_all.at[own])
    spread.tail()
    spread.links.close()
    copies.wait(top_copy)
    top = spread_of(n, n.top_all, n.top_send, n.top_recv, None)
    for part in range(SPLIT):
        top.own(part)
    cross.wait(at_out)
    out_copy = copies.pick(n.w_out, n.x_out, n.w_o, 0)
    attend(n)
    keep_attention(n)
    top.share(0)
    copies.wait(out_copy)

    def part_of(chip):
        return plain_dot(rows_of(n.mixed_v, chip, site), n.w_o[...])

    def local(total, where):
        hidden_in = n.held[(*own, where)].astype(FULL) + total
        n.hidden_v[where] = hidden_in
        return scaled(hidden_in, n.gains_v[1:2]).astype(LOW)

    waiting = []

    def use_later(chip, rows):
        waiting.append(chip)

    def use_gate(chip):
        rows = n.held_two[chip].reshape(-1, n.held_two.shape[-1])
        gate_slope, up_slope = gate_chunk(n, chip, rows)
        put(n.gate_slope_v, chip, gate_slope)
        put(n.up_slope_v, chip, up_slope)

    def idle(count):
        if count == 10:
            for part in range(SPLIT):
                top.relays(part)

    spread = spread_of(
        n, n.held_two, n.spread_two_send, n.spread_two_recv, use_later, n.rows_two
    )
    fold_spread(fold_of(n, part_of), spread, local, idle)
    copies.start(n.hidden_v, n.hidden)
    top.after_relays()
    for part in range(SPLIT):
        top.far(part)
    cross.wait(at_gate)
    cross.wait(at_up)
    copies.wait(
        copies.pick(n.w_gate, n.x_gate, n.w_g, 0), copies.pick(n.w_up, n.x_up, n.w_u, 0)
    )
    for chip in waiting:
        use_gate(chip)
    for source, target in (
        (n.act, n.act_all), (n.gate_slope_v, n.gate_slope), (n.up_slope_v, n.up_slope)
    ):
        copies.start(source, target)
    top.tail(consume=False)
    top.links.close()


def second_layer(n):
    site, copies = n.site, n.copies
    first = [
        copies.start(n.act_prev, n.act_prev_v),
        copies.pick(n.w_down, n.x_down, n.w_d_prev, 0),
    ]
    rows_copies = [copies.start(n.hidden_prev, n.hidden_prev_v), copies.start(n.gains, n.gains_v)]
    qkv_copies = [
        copies.pick(n.w_query, n.x_query, n.w_in.at[pl.ds(0, 2 * HEAD_DIM)], 1),
        copies.start(n.kv_rows.at[1], n.w_in.at[pl.ds(2 * HEAD_DIM, 2 * HEAD_DIM)]),
        copies.start(n.turns, n.turns_v),
    ]
    later = [
        copies.pick(n.w_out, n.x_out, n.w_o, 1),
        copies.pick(n.w_gate, n.x_gate, n.w_g, 1),
        copies.pick(n.w_up, n.x_up, n.w_u, 1),
        copies.pick(n.w_down, n.x_down, n.w_d, 1),
        copies.start(n.top_all, n.top_held),
    ]
    back_copies = [copies.pick(n.cotangent.at[0], n.cotangent.at[1], n.top_v, 0)]
    next_copies = [
        copies.start(n.gate_slope, n.gate_slope_v),
        copies.start(n.up_slope, n.up_slope_v),
    ]
    greet(site)
    copies.wait(*first, *rows_copies)

    def part_of(chip):
        return plain_dot(rows_of(n.act_prev_v, chip, site), n.w_d_prev[...])

    def local(total, where):
        result = (n.hidden_prev_v[where] + total).astype(LOW)
        n.result_v[where] = result
        return scaled(result.astype(FULL), n.gains_v[2:3]).astype(LOW)

    def use_qkv(chip, rows):
        n.qkv[chip] = times_trans(rows, n.w_in[...])

    def settle(count):
        copies.wait(*qkv_copies)

    spread = spread_of(n, n.held, n.spread_send, n.spread_recv, use_qkv)
    fold_spread(fold_of(n, part_of), spread, local, settle)
    copies.start(n.result_v, n.result_a)
    n.cross.send(n.result_v, n.came_result_a, 0)
    attend(n)
    copies.wait(*later)

    def part_of_two(chip):
        return plain_dot(rows_of(n.mixed_v, chip, site), n.w_o[...])

    def local_two(total, where):
        hidden_in = n.result_v[where].astype(FULL) + total
        n.hidden_v[where] = hidden_in
        return scaled(hidden_in, n.gains_v[3:4]).astype(LOW)

    def use_gate(chip, rows):
        gate_slope, up_slope = gate_chunk(n, chip, rows)
        d_act = times_trans(n.top_held[chip].reshape(rows.shape), n.w_d[...])
        put(n.d_gate_v, chip, d_act * gate_slope)
        put(n.d_up_v, chip, d_act * up_slope)

    spread = spread_of(
        n, n.held_two, n.spread_two_send, n.spread_two_recv, use_gate
    )
    fold_spread(fold_of(n, part_of_two), spread, local_two, no_idle)
    copies.wait(*back_copies)
    cross = n.cross
    first_copies = []

    def preload():
        first_copies.append(copies.pick(n.w_gate, n.x_gate, n.w_g, 0))
        first_copies.append(copies.pick(n.w_up, n.x_up, n.w_u, 0))
        first_copies.append(copies.pick(n.w_out, n.x_out, n.w_o, 0))
        first_copies.append(copies.start(n.rows_two, n.top_held))

    backward(
        n,
        types.SimpleNamespace(
            layer=1, attn_copies=[], one_copies=[], next_copies=next_copies, act=n.act,
            top_all=n.top_held, normed_two=n.held_two, normed_one=n.held, branch=n.normed,
            hidden=n.hidden_v, top=n.top_v, x_rows=n.result_v, d_input=n.d_input_v,
            w_next=n.w_d_prev, after_first=preload, send=n.back_send, recv=n.back_recv,
            sums=[
                (n.g_down_v, n.own_down_b, n.came_down_b),
                (n.g_gate_v, n.own_gate_b, n.came_gate_b),
                (n.g_up_v, n.own_up_b, None),
                (n.g_out_v, n.own_out_b, n.came_out_b),
                (n.g_query_v, n.own_query_b, n.came_query_b),
                (n.g_kv_v, n.own_kv_b, n.came_kv_b),
            ],
        ),
    )
    copies.start(n.d_input_v, n.d_input_b)
    n.gain_later_v[...] = n.gain_grads[...]
    copies.wait(*first_copies)
    copies.close()
    cross.close()
    attn_copies = [
        copies.start(n.turned, n.turned_v),
        copies.start(n.attended, n.attended_v),
        copies.start(n.spread, n.spread_v),
        copies.start(n.mixed, n.mixed_v),
        copies.pick(n.w_query, n.x_query, n.w_in.at[pl.ds(0, 2 * HEAD_DIM)], 0),
        copies.start(n.kv_rows.at[0], n.w_in.at[pl.ds(2 * HEAD_DIM, 2 * HEAD_DIM)]),
        copies.pick(n.inputs.at[0], n.inputs.at[1], n.x_v, 0),
    ]
    one_copies = [copies.start(n.rows_one, n.held)]
    cross.send(n.own_up_b, n.came_up_b, 1)
    cross.send(n.d_input_v, n.came_input_b, 1)
    backward(
        n,
        types.SimpleNamespace(
            layer=0, attn_copies=attn_copies, one_copies=one_copies, next_copies=[],
            act=n.act_prev_v, top_all=n.held_two, normed_two=n.top_held, normed_one=n.held,
            branch=n.normed, hidden=n.hidden_prev_v, top=n.d_input_v, x_rows=n.x_v,
            d_input=n.d_input_two, w_next=n.w_d, after_first=lambda: None, send=n.last_back_send,
            recv=n.last_back_recv,
            sums=[
                (n.g_down_v, n.own_down_a, n.came_down_a),
                (n.g_gate_v, n.own_gate_a, n.came_gate_a),
                (n.g_up_v, n.own_up_a, n.came_up_a),
                (n.g_out_v, n.own_out_a, n.came_out_a),
                (n.g_query_v, n.own_query_a, n.came_query_a),
                (n.g_kv_v, n.own_kv_a, n.came_kv_a),
            ],
        ),
    )


def products(n, left, right, store, tile=512):
    count = math.prod(left.shape[:-1])
    for start in range(0, right.shape[-1], tile):
        where = pl.ds(start, tile)
        value = outer_sum(
            left[...].reshape(count, left.shape[-1]), right[:, :, :, where].reshape(count, tile)
        )
        store(where, value.astype(LOW))
        yield


def ffn_products(n, k, made):
    for left, right, out in (
        (k.act, k.top_all, n.g_down_v),
        (n.d_gate_v, k.normed_two, n.g_gate_v),
        (n.d_up_v, k.normed_two, n.g_up_v),
    ):

        def store(where, value):
            out[:, where] = value

        yield from products(n, left, right, store)
        made(out)


def in_products(n, loads, made, normed_one, branch):
    site = n.site
    n.copies.wait(*loads)

    def store_out(where, value):
        n.g_out_v[:, where] = value

    def store_in(where, value):
        query = n.g_query_v.shape[0]
        n.g_query_v[:, where] = value[:query]
        n.kv_mine[:, :, :, where] = value[query:].reshape(
            *n.kv_mine.shape[:3], value.shape[1]
        )

    yield from products(n, n.d_qkv, normed_one, store_in)
    made(n.g_query_v)
    peers = (site.sibling, site.across, site.corner)
    links = Links(n.kv_send, n.kv_recv, site)
    for index, device in enumerate(peers):
        links.go(index, n.kv_mine.at[:, device[2]], n.kv_came.at[index], device)
    yield from products(n, n.mixed_v, branch, store_out)
    made(n.g_out_v)
    total = n.kv_mine[:, site.member].astype(FULL)
    for index in range(len(peers)):
        total = total + links.got(index, n.kv_came.at[index])[...].astype(FULL)
    n.g_kv_v[...] = total.astype(LOW)
    made(n.g_kv_v)
    links.close()


def fold_gains(n):
    site = n.site
    links = Links(n.gain_send, n.gain_recv, site)
    own = jnp.concatenate(
        [n.gain_grads[...], n.gain_later_v[...], jnp.zeros((4, n.gain_grads.shape[1]), FULL)], 0
    )
    width = n.gain_parts.shape[-1]
    for shard in range(RING):
        for seq in range(RING):
            start = (shard * RING + seq) * width
            n.gain_parts[seq, shard] = own[:, start : start + width]
    peers = (site.sibling, site.across, site.corner)
    for index, device in enumerate(peers):
        links.go(index, n.gain_parts.at[device[2]], n.gain_came.at[index], device)
    yield
    total = n.gain_parts[site.member]
    for index in range(3):
        total = total + links.got(index, n.gain_came.at[index])[...]
    n.gain_shards[...] = total
    for index, device in enumerate((site.up, site.down, site.opposite)):
        links.go(
            3 + index, n.gain_shards.at[device[1]], n.gain_last.at[index], device
        )
    yield
    total = n.gain_shards[site.z]
    for index in range(3):
        total = total + links.got(3 + index, n.gain_last.at[index])[...]
    n.gain_own[...] = total
    links.go(6, n.gain_own, n.gain_other, site.partner)
    yield
    total = n.gain_own[...] + links.got(6, n.gain_other)[...]
    n.gain_sums_v[...] = jnp.where(site.section == 0, total[:2], total[2:4])
    links.close()
    n.copies.start(n.gain_sums_v, n.gain_sums)


def backward(n, k):
    site, copies, cross = n.site, n.copies, n.cross
    layer = k.layer

    def made(out):
        for value, target, came in k.sums:
            if value is out:
                break
        copies.start(out, target)
        if came is not None:
            cross.send(out, came, layer)

    def step_on(working):
        def idle(count):
            for _ in range(count):
                next(working, None)

        return idle

    def part_of(chip):
        return plain_dot(rows_of(n.d_gate_v, chip, site), n.w_g[...]) + plain_dot(
            rows_of(n.d_up_v, chip, site), n.w_u[...]
        )

    def add_gain(row, value, where):
        row = pl.ds(row, 1)
        n.gain_grads[row] = value if where.start == 0 else n.gain_grads[row] + value

    def local(total, where):
        gain_grad, d_hidden = norm_back_rows(
            k.hidden[where], n.gains_v[2 * layer + 1 : 2 * layer + 2], total
        )
        d_hidden = d_hidden + k.top[where].astype(FULL)
        add_gain(1, gain_grad, where)
        n.d_hidden[where] = d_hidden
        return d_hidden.astype(LOW)

    def use_d_mixed(chip, rows):
        n.d_mixed[chip] = times_trans(rows, n.w_o[...]).astype(LOW)

    working = ffn_products(n, k, made)
    if layer == 0:
        step_on(working)(5)
    spread = spread_of(n, k.branch, k.send, k.recv, use_d_mixed)
    fold_spread(fold_of(n, part_of), spread, local, step_on(working))
    for _ in working:
        pass
    k.after_first()
    copies.wait(*k.attn_copies)
    attend_back(n)
    copies.wait(*k.next_copies)

    def part_of_two(chip):
        return plain_dot(rows_of(n.d_qkv, chip, site), n.w_in[...])

    def local_two(total, where):
        gain_grad, d_input = norm_back_rows(
            k.x_rows[where].astype(FULL), n.gains_v[2 * layer : 2 * layer + 1], total
        )
        d_input = (d_input + n.d_hidden[where]).astype(LOW)
        add_gain(0, gain_grad, where)
        k.d_input[where] = d_input
        return d_input

    working = in_products(n, k.one_copies, made, k.normed_one, k.branch)
    if layer == 1:

        def use_d_act(chip, rows):
            d_act = times_trans(rows, k.w_next[...])
            for out, slope in ((n.d_gate_v, n.gate_slope_v), (n.d_up_v, n.up_slope_v)):
                put(out, chip, d_act * slope[chip].astype(FULL).reshape(d_act.shape))

        spread = spread_of(n, n.held_two, n.back_two_send, n.back_two_recv, use_d_act)
        fold_spread(fold_of(n, part_of_two), spread, local_two, step_on(working))
        for _ in working:
            pass
        return
    fold_spread(fold_of(n, part_of_two), None, local_two, step_on(working))
    for _ in working:
        pass
    copies.start(k.d_input, n.d_input_a)
    cross.send(k.d_input, n.came_input_a, 0)

    def part_of_last(chip):
        return plain_dot(rows_of(n.act, chip, site), k.w_next[...])

    def local_last(total, where):
        n.result_two[where] = (n.hidden_v[where] + total).astype(LOW)

    buffers = (n.mine, n.pass_out, n.held_two.at[:, 0], n.stage, n.held_two.at[:, 1])
    links = Links(n.last_send, n.last_recv, site)
    gains_on = fold_gains(n)
    next(gains_on)
    fold_spread(
        Fold(site, part_of_last, buffers, links), None, local_last,
        lambda count: next(gains_on, None),
    )
    for _ in gains_on:
        pass
    copies.start(n.result_two, n.result_b)
    cross.send(n.result_two, n.came_result_b, 1)


def join_kernel(count, *refs):
    def take(number):
        nonlocal refs
        taken, refs = refs[:number], refs[number:]
        return taken

    own, came = (take(count), take(count)), (take(count), take(count))
    rows = (take(4), take(4))
    outs, row_outs = take(count + 1), take(2)
    own_at, came_at, sums = take(count), take(count), take(count)
    row_at, sems, out_sem, row_sem = refs
    section = lax.axis_index("section")

    def either(first, second):
        pl.when(section == 0)(first.start)
        pl.when(section != 0)(second.start)
        return first

    waits = []
    for index in range(count):
        for slot, (pair, target) in enumerate(((own, own_at), (came, came_at))):
            waits.append(
                either(
                    *(
                        pltpu.make_async_copy(
                            pair[layer][index], target[index], sems.at[2 * index + slot]
                        )
                        for layer in range(2)
                    )
                )
            )
    done = []
    row_waits = []
    for index, (own_a, own_b, came_a, came_b) in enumerate(rows):
        for slot, (first, second) in enumerate(((own_a, came_b), (came_a, own_b))):
            target, sem = row_at.at[index, slot], row_sem.at[2 * index + slot]
            row_waits.append(
                either(
                    pltpu.make_async_copy(first, target, sem),
                    pltpu.make_async_copy(second, target, sem),
                )
            )
    for copy in row_waits:
        copy.wait()
    for index, out in enumerate(row_outs):
        copy = pltpu.make_async_copy(row_at.at[index], out, row_sem.at[index])
        copy.start()
        done.append(copy)
    for index in range(count):
        waits[2 * index].wait()
        waits[2 * index + 1].wait()
        sums[index][...] = own_at[index][...].astype(FULL) + came_at[index][...].astype(FULL)
        if index < count - 1:
            parts = [(sums[index], outs[index])]
        else:
            parts = [(sums[index].at[pl.ds(k, 1)], outs[index + k]) for k in range(2)]
        for source, target in parts:
            copy = pltpu.make_async_copy(source, target, out_sem.at[len(done) - 2])
            copy.start()
            done.append(copy)
    for copy in done:
        copy.wait()


def join_all(own_a, own_b, came_a, came_b, results, input_grads):
    count = len(own_a)
    kept = [pltpu.VMEM(value.shape, LOW) for value in own_a]
    shapes = [value.shape for value in own_a]
    shapes = shapes[:-1] + [(1, *shapes[-1][1:])] * 2
    row_shape = jax.ShapeDtypeStruct((2, *results[0].shape), LOW)
    return pl.pallas_call(
        functools.partial(join_kernel, count),
        out_shape=[jax.ShapeDtypeStruct(value, FULL) for value in shapes] + [row_shape] * 2,
        in_specs=[IN_HBM] * (4 * count + 8),
        out_specs=[IN_HBM] * (count + 3),
        scratch_shapes=kept
        + kept
        + [pltpu.VMEM(value.shape, FULL) for value in own_a]
        + [
            pltpu.VMEM((2, *row_shape.shape), LOW),
            pltpu.SemaphoreType.DMA((2 * count,)),
            pltpu.SemaphoreType.DMA((count + 1,)),
            pltpu.SemaphoreType.DMA((4,)),
        ],
        compiler_params=pltpu.CompilerParams(vmem_limit_bytes=58 * 2**20),
        cost_estimate=pl.CostEstimate(flops=2**32, bytes_accessed=2**24, transcendentals=0),
        name="join_all",
    )(*own_a, *own_b, *came_a, *came_b, *results, *input_grads)


def relay_body(
    inputs,
    cotangent,
    positions,
    gain_attn,
    w_query,
    w_key,
    w_value,
    w_out,
    gain_ffn,
    w_gate,
    w_up,
    w_down,
):
    n_micro, per_device, model_width = inputs.shape
    n_seq = lax.axis_size("seq")
    n_shard = lax.axis_size("shard")
    members = n_seq * n_shard
    total_len = members * per_device
    section_idx = lax.axis_index("section")
    q_width = HEADS // members * HEAD_DIM
    in_width = q_width + 2 * HEAD_DIM
    hidden = w_down.shape[1]
    vmem = pltpu.VMEM

    def pick(first, second):
        return jnp.where(section_idx == 0, first, second)

    places = pick(positions[0], positions[1])
    gains_own = jnp.concatenate(
        [gain_attn, gain_ffn, jnp.zeros((6, gain_attn.shape[1]), gain_attn.dtype)], 0
    ).astype(FULL)
    own = dict(
        w_query=w_query[0], w_out=w_out[0], w_gate=w_gate[0], w_up=w_up[0], w_down=w_down[0]
    )

    order = (places.reshape(CHIPS, PLACE)[:, 0] // PLACE).astype(jnp.int32)
    numbers = jnp.arange(CHIPS, dtype=jnp.int32)
    block_at = jnp.sum(
        jnp.where(order[None, :] == numbers[:, None], numbers[None, :], 0), 1
    ).astype(jnp.int32)
    scalars = dict(block_at=block_at, order=order)
    half_dim = HEAD_DIM // 2
    inv_freq = THETA_BASE ** (-jnp.arange(half_dim, dtype=FULL) * (2.0 / HEAD_DIM))
    steps = jnp.concatenate([jnp.arange(PLACE), PLACE * jnp.arange(CHIPS)]).astype(FULL)
    angles = steps[:, None] * jnp.tile(inv_freq, 2 * q_width // HEAD_DIM)[None, :]
    turns = jnp.stack([jnp.cos(angles), jnp.sin(angles)])

    rows = (per_device, model_width)
    row_low, row_full = (rows, LOW), (rows, FULL)
    all_rows = ((CHIPS, 2, *rows), LOW)
    narrow = ((CHIPS, 2, per_device, hidden), LOW)
    wide = ((hidden, model_width), LOW)
    quarter = ((q_width, model_width), LOW)
    gain_row = ((8, model_width), FULL)
    kv_shape = (2, w_key.shape[1], model_width)
    small = gains_own.shape
    saved = dict(
        turned=((total_len, in_width), LOW),
        attended=((CHIPS, PLACE, q_width), FULL),
        spread=((CHIPS, 2 * PLACE), FULL),
        mixed=((CHIPS, 2, per_device, q_width), LOW),
    )
    saved_v = dict(
        turned_v=vmem(*saved["turned"]),
        attended_v=vmem(*saved["attended"]),
        spread_v=vmem(*saved["spread"]),
        mixed_v=vmem(*saved["mixed"]),
        turns_v=vmem(turns.shape, FULL),
    )
    attend_v_only = dict(
        qkv=vmem((CHIPS, PLACE, in_width), FULL),
        values_t=vmem((HEAD_DIM, total_len), LOW),
    )
    attend_v = dict(**saved_v, **attend_v_only)
    gates_v = dict(w_g=vmem(*wide), w_u=vmem(*wide))

    first = launch(
        "forward_first",
        0,
        forward_first,
        scalars,
        dict(
            inputs=inputs, cotangent=cotangent, gains_own=gains_own, w_key=w_key[0],
            w_value=w_value[0], turns=turns, **own,
        ),
        dict(
            x_query=quarter,
            x_out=quarter,
            x_gate=wide,
            x_up=wide,
            x_down=wide,
            gains=gain_row,
            kv_rows=((2, 2 * HEAD_DIM, model_width), LOW),
            top_all=all_rows,
            rows_one=all_rows,
            rows_two=all_rows,
            hidden=row_full,
            act_all=narrow,
            gate_slope=narrow,
            up_slope=narrow,
            **saved,
        ),
        dict(
            gains_mine=vmem(small, FULL),
            gains_x=vmem(small, FULL),
            gains_all=vmem((n_shard, n_seq, *small), FULL),
            gains_v=vmem(*gain_row),
            kv_mine=vmem(kv_shape, LOW),
            kv_x=vmem(kv_shape, LOW),
            kv_all=vmem((n_seq, 2, *kv_shape), LOW),
            w_kv=vmem((2, 2 * HEAD_DIM, model_width), LOW),
            small_send=pltpu.SemaphoreType.DMA((SMALL_SEMS,)),
            small_recv=pltpu.SemaphoreType.DMA((SMALL_SEMS,)),
            held=vmem(*all_rows),
            held_two=vmem(*all_rows),
            normed=vmem(*all_rows),
            w_q=vmem(*quarter),
            w_o=vmem(*quarter),
            hidden_v=vmem(*row_full),
            top_v=vmem(*row_low),
            act=vmem(*narrow),
            gate_slope_v=vmem(*narrow),
            up_slope_v=vmem(*narrow),
            **gates_v,
            **attend_v,
            **fold_buffers(rows),
            **spread_sems(
                "spread_send", "spread_recv", "spread_two_send", "spread_two_recv", "top_send",
                "top_recv",
            ),
        ),
    )
    crossed = dict(
        **own,
        x_query=first.x_query,
        x_out=first.x_out,
        x_gate=first.x_gate,
        x_up=first.x_up,
        x_down=first.x_down,
        gains=first.gains,
        kv_rows=first.kv_rows,
        turns=turns,
    )
    kv_pair = ((2, *kv_shape[1:]), LOW)
    sums_out = dict(down=wide, gate=wide, up=wide, out=quarter, query=quarter, kv=kv_pair)
    layers = dict(a=0, b=1)
    second = launch(
        "second_layer_and_back",
        1,
        second_layer,
        scalars,
        dict(
            act_prev=first.act_all,
            hidden_prev=first.hidden,
            inputs=inputs,
            cotangent=cotangent,
            top_all=first.top_all,
            rows_one=first.rows_one,
            rows_two=first.rows_two,
            gate_slope=first.gate_slope,
            up_slope=first.up_slope,
            **{key: getattr(first, key) for key in saved},
            **crossed,
        ),
        dict(
            gain_sums=((2, small[1]), FULL),
            **{
                f"{of}_{key}_{layer}": value
                for layer in layers
                for of in ("own", "came")
                for key, value in sums_out.items()
            },
            **{
                f"{of}_{layer}": row_low
                for layer in layers
                for of in ("result", "d_input", "came_result", "came_input")
            },
        ),
        dict(
            act_prev_v=vmem(*narrow),
            act=vmem(*narrow),
            d_gate_v=vmem(*narrow),
            d_up_v=vmem(*narrow),
            gate_slope_v=vmem(*narrow),
            up_slope_v=vmem(*narrow),
            hidden_prev_v=vmem(*row_full),
            hidden_v=vmem(*row_full),
            d_hidden=vmem(*row_full),
            result_v=vmem(*row_low),
            result_two=vmem(*row_low),
            top_v=vmem(*row_low),
            x_v=vmem(*row_low),
            d_input_v=vmem(*row_low),
            d_input_two=vmem(*row_low),
            gains_v=vmem(*gain_row),
            gain_grads=vmem((2, model_width), FULL),
            gain_later_v=vmem((2, model_width), FULL),
            w_d_prev=vmem(*wide),
            w_d=vmem(*wide),
            w_o=vmem(*quarter),
            w_in=vmem((in_width, model_width), LOW),
            top_held=vmem(*all_rows),
            normed=vmem(*all_rows),
            held=vmem(*all_rows),
            held_two=vmem(*all_rows),
            d_mixed=vmem((CHIPS, PLACE, q_width), LOW),
            d_qkv=vmem((CHIPS, 2, per_device, in_width), LOW),
            d_turned=vmem((CHIPS, PLACE, in_width), LOW),
            d_query=vmem((total_len, q_width), FULL),
            d_key=vmem((total_len, HEAD_DIM), FULL),
            d_value=vmem((total_len, HEAD_DIM), FULL),
            keys_t=vmem((HEAD_DIM, total_len), LOW),
            g_down_v=vmem(*wide),
            g_gate_v=vmem(*wide),
            g_up_v=vmem(*wide),
            g_out_v=vmem(*quarter),
            g_query_v=vmem(*quarter),
            g_kv_v=vmem(*kv_pair),
            kv_mine=vmem((2, n_seq, *kv_shape[1:]), LOW),
            kv_came=vmem((n_seq - 1, 2, *kv_shape[1:]), LOW),
            kv_send=pltpu.SemaphoreType.DMA((n_seq - 1,)),
            kv_recv=pltpu.SemaphoreType.DMA((n_seq - 1,)),
            last_send=pltpu.SemaphoreType.DMA((FOLD_SEMS,)),
            last_recv=pltpu.SemaphoreType.DMA((FOLD_SEMS,)),
            gain_parts=vmem((n_seq, n_shard, *small), FULL),
            gain_came=vmem((n_seq - 1, n_shard, *small), FULL),
            gain_shards=vmem((n_shard, *small), FULL),
            gain_last=vmem((n_shard - 1, *small), FULL),
            gain_own=vmem(small, FULL),
            gain_other=vmem(small, FULL),
            gain_sums_v=vmem((2, small[1]), FULL),
            gain_send=pltpu.SemaphoreType.DMA((7,)),
            gain_recv=pltpu.SemaphoreType.DMA((7,)),
            **gates_v,
            **attend_v,
            **fold_buffers(rows),
            **spread_sems(
                "spread_send", "spread_recv", "spread_two_send", "spread_two_recv", "back_send",
                "back_recv", "back_two_send", "back_two_recv", "last_back_send",
                "last_back_recv",
            ),
        ),
    )

    def sums(of, layer):
        return [getattr(second, f"{of}_{key}_{layer}") for key in sums_out]

    g_down, g_gate, g_up, g_out, g_query, g_key, g_value, outputs, input_grads = join_all(
        *(sums(of, layer) for of in ("own", "came") for layer in layers),
        (second.result_a, second.result_b, second.came_result_a, second.came_result_b),
        (second.d_input_a, second.d_input_b, second.came_input_a, second.came_input_b),
    )
    return (
        outputs[None],
        input_grads[None],
        second.gain_sums[:1],
        g_query[None],
        g_key,
        g_value,
        g_out[None],
        second.gain_sums[1:],
        g_gate[None],
        g_up[None],
        g_down[None],
    )


def fits_relay(mesh):
    shape = mesh.shape
    return shape["section"] == 2 and shape["shard"] == KV_HEADS == RING and shape["seq"] == 4


def solution(mesh):
    in_specs = (
        P(None, ("shard", "seq"), None),
        P(None, ("shard", "seq"), None),
        P(),
        P("section", ("shard", "seq")),
        P("section", ("shard", "seq"), None),
        P("section", ("shard", "seq"), None),
        P("section", ("shard", "seq"), None),
        P("section", ("shard", "seq"), None),
        P("section", ("shard", "seq")),
        P("section", ("shard", "seq"), None),
        P("section", ("shard", "seq"), None),
        P("section", ("shard", "seq"), None),
    )
    out_specs = (
        P("section", None, ("shard", "seq"), None),
        P("section", None, ("shard", "seq"), None),
        P("section", ("shard", "seq")),
        P("section", ("shard", "seq"), None),
        P("section", ("shard", "seq"), None),
        P("section", ("shard", "seq"), None),
        P("section", ("shard", "seq"), None),
        P("section", ("shard", "seq")),
        P("section", ("shard", "seq"), None),
        P("section", ("shard", "seq"), None),
        P("section", ("shard", "seq"), None),
    )
    chosen = relay_body if fits_relay(mesh) else body
    return jax.shard_map(chosen, mesh=mesh, in_specs=in_specs, out_specs=out_specs, check_vma=False)
```

```python
import functools
import math
import types

import jax
import jax.numpy as jnp
from jax import lax
from jax.experimental import pallas as pl
from jax.experimental.pallas import tpu as pltpu
from jax.sharding import PartitionSpec as P

HEADS = 32
KV_HEADS = 4
HEAD_DIM = 64


EPSILON = 1e-05
THETA_BASE = 10000.0
NEG_LARGE = -1e30


def shifted(value, axis, by):
    count = lax.axis_size(axis)
    pairs = [(i, i + by) for i in range(count) if 0 <= i + by < count]
    return lax.ppermute(value, axis, pairs)


def times_trans(left, right):
    return lax.dot_general(
        left, right, (((1,), (1,)), ((), ())), preferred_element_type=jnp.float32
    )


def outer_sum(left, right):
    return lax.dot_general(
        left, right, (((0,), (0,)), ((), ())), preferred_element_type=jnp.float32
    )


def plain_dot(left, right):
    return jnp.dot(left, right, preferred_element_type=jnp.float32)


def rotate(values, places, direction):
    half_dim = values.shape[-1] // 2
    inv_freq = THETA_BASE ** (-jnp.arange(half_dim, dtype=jnp.float32) * (2.0 / values.shape[-1]))
    angles = places.astype(jnp.float32)[:, None] * inv_freq[None, :]
    cosine = jnp.cos(angles)[:, None, :]
    sine_val = direction * jnp.sin(angles)[:, None, :]
    first = values[..., :half_dim]
    second = values[..., half_dim:]
    return jnp.concatenate(
        [first * cosine - second * sine_val, second * cosine + first * sine_val], -1
    )


def scaled(values, gain_vec):
    factor = lax.rsqrt(jnp.mean(values * values, -1, keepdims=True) + EPSILON)
    return values * factor * gain_vec


def norm_back(values, gain_vec, grad_in):
    factor = lax.rsqrt(jnp.mean(values * values, -1, keepdims=True) + EPSILON)
    gain_grad = jnp.sum(grad_in * values * factor, 0)
    mean_term = jnp.mean(grad_in * gain_vec * values, -1, keepdims=True)
    return (
        gain_grad,
        factor * gain_vec * grad_in - values * (factor * factor * factor) * mean_term,
    )


def ffn_back(grad_rows, kept_rows, gate_pre, up_pre, wg_part, wu_part, wd_part):
    sigmoid_val = jax.nn.sigmoid(gate_pre)
    silu_val = gate_pre * sigmoid_val
    hidden_act = (silu_val * up_pre).astype(jnp.bfloat16)
    grad_down = outer_sum(hidden_act, grad_rows)
    d_act = times_trans(grad_rows, wd_part)
    d_gate = (d_act * up_pre * sigmoid_val * (1.0 + gate_pre * (1.0 - sigmoid_val))).astype(
        jnp.bfloat16
    )
    d_up = (d_act * silu_val).astype(jnp.bfloat16)
    grad_gate = outer_sum(d_gate, kept_rows)
    grad_up = outer_sum(d_up, kept_rows)
    d_normed = plain_dot(d_gate, wg_part) + plain_dot(d_up, wu_part)
    return ((grad_gate, grad_up, grad_down), d_normed)


def body(
    inputs,
    cotangent,
    positions,
    gain_attn,
    w_query,
    w_key,
    w_value,
    w_out,
    gain_ffn,
    w_gate,
    w_up,
    w_down,
):
    n_micro, per_device, model_width = inputs.shape
    n_seq = lax.axis_size("seq")
    n_shard = lax.axis_size("shard")
    section_idx = lax.axis_index("section")
    shard_pos = lax.axis_index("shard")
    member = shard_pos * n_seq + lax.axis_index("seq")
    span_rows = per_device * n_seq
    total_len = span_rows * n_shard
    local_heads = HEADS // n_seq
    kv_repeat = n_seq // KV_HEADS
    q_width = local_heads * HEAD_DIM
    attn_scale = 1.0 / math.sqrt(HEAD_DIM)
    gain_one, gain_two, wq_full, wk_full, wv_full, wo_full = (
        lax.all_gather(gain_attn[0], ("shard", "seq"), axis=0, tiled=True),
        lax.all_gather(gain_ffn[0], ("shard", "seq"), axis=0, tiled=True),
        lax.all_gather(w_query[0], ("shard", "seq"), axis=0, tiled=True),
        lax.all_gather(w_key[0], ("shard", "seq"), axis=0, tiled=True),
        lax.all_gather(w_value[0], ("shard", "seq"), axis=0, tiled=True),
        lax.all_gather(w_out[0], ("shard", "seq"), axis=0, tiled=True),
    )
    gain_a = gain_one.astype(jnp.float32)
    gain_f = gain_two.astype(jnp.float32)
    wg_use, wu_use, wd_use = (w_gate[0], w_up[0], w_down[0])

    def spread_rows(block_in):
        return lax.all_gather(block_in, ("shard", "seq"), axis=0, tiled=True)

    def fold_rows(block_in):
        return lax.psum_scatter(block_in, ("shard", "seq"), scatter_dimension=0, tiled=True)

    def to_heads(block_in):
        return lax.all_to_all(block_in, "seq", split_axis=1, concat_axis=0, tiled=True)

    def to_tokens(block_in):
        return lax.all_to_all(block_in, "seq", split_axis=0, concat_axis=1, tiled=True)

    def over_keys(head_keys, head_values, step_fn, init_state):
        return step_fn(
            init_state,
            (
                lax.all_gather(head_keys, "shard", axis=0, tiled=True),
                lax.all_gather(head_values, "shard", axis=0, tiled=True),
            ),
            jnp.int32(0),
        )

    def place_sets(batch_index):
        place_row = lax.dynamic_index_in_dim(positions, batch_index, 0, keepdims=False)
        token_places = lax.dynamic_slice_in_dim(place_row, member * per_device, per_device)
        span_places = lax.dynamic_slice_in_dim(place_row, shard_pos * span_rows, span_rows)
        return (place_row, token_places, span_places)

    zero_rows = jnp.zeros((per_device, model_width), jnp.bfloat16)
    arrived_x = zero_rows
    results = []
    stored = []
    for tick_index in range(n_micro + 1):
        own_rows = inputs[tick_index] if tick_index < n_micro else zero_rows
        input_now = jnp.where(section_idx == 0, own_rows, arrived_x)
        batch_index = jnp.clip(tick_index - section_idx, 0, n_micro - 1)
        forward_place_row, forward_token_places, forward_span_places = place_sets(batch_index)
        forward_values_in = input_now.astype(jnp.float32)
        forward_normed_one = scaled(forward_values_in, gain_a).astype(jnp.bfloat16)
        queries = rotate(
            times_trans(forward_normed_one, wq_full).reshape(per_device, HEADS, HEAD_DIM),
            forward_token_places,
            1.0,
        ).astype(jnp.bfloat16)
        key_rows = rotate(
            times_trans(forward_normed_one, wk_full).reshape(per_device, KV_HEADS, HEAD_DIM),
            forward_token_places,
            1.0,
        ).astype(jnp.bfloat16)
        value_rows = (
            times_trans(forward_normed_one, wv_full)
            .reshape(per_device, KV_HEADS, HEAD_DIM)
            .astype(jnp.bfloat16)
        )
        key_rows = jnp.repeat(key_rows, kv_repeat, axis=1)
        value_rows = jnp.repeat(value_rows, kv_repeat, axis=1)
        packed = jnp.concatenate(
            [queries.reshape(per_device, n_seq, q_width), key_rows, value_rows], -1
        )
        arrived = to_heads(packed)[:, 0]
        forward_head_query = arrived[:, :q_width].reshape(span_rows, local_heads, HEAD_DIM)
        forward_head_keys = arrived[:, q_width : q_width + HEAD_DIM]
        forward_head_values = arrived[:, q_width + HEAD_DIM :]

        def absorb(state_in, key_piece, start_row):
            run_max, run_total, run_acc = state_in
            piece_keys, piece_values = key_piece
            visible = forward_place_row[None, None, :] <= forward_span_places[None, :, None]
            scores = (
                jnp.einsum(
                    "qhd,kd->hqk",
                    forward_head_query,
                    piece_keys,
                    preferred_element_type=jnp.float32,
                )
                * attn_scale
            )
            scores = jnp.where(visible, scores, NEG_LARGE)
            new_max = jnp.maximum(run_max, jnp.max(scores, -1))
            weight = jnp.where(visible, jnp.exp(scores - new_max[..., None]), 0.0)
            rescale = jnp.exp(run_max - new_max)
            run_total = jnp.sum(weight, -1)
            run_acc = run_acc * rescale.T[..., None] + jnp.einsum(
                "hqk,kd->qhd",
                weight.astype(jnp.bfloat16),
                piece_values,
                preferred_element_type=jnp.float32,
            )
            return (new_max, run_total, run_acc)

        forward_start_state = (
            jnp.full((local_heads, span_rows), NEG_LARGE, jnp.float32),
            jnp.zeros((local_heads, span_rows), jnp.float32),
            jnp.zeros((span_rows, local_heads, HEAD_DIM), jnp.float32),
        )
        run_max, run_total, run_acc = over_keys(
            forward_head_keys, forward_head_values, absorb, forward_start_state
        )
        forward_attended = run_acc / run_total.T[..., None]
        forward_spread = run_max + jnp.log(run_total)
        forward_mixed_tok = to_tokens(
            forward_attended.astype(jnp.bfloat16).reshape(span_rows, 1, q_width)
        ).reshape(per_device, HEADS * HEAD_DIM)
        forward_hidden_in = forward_values_in + plain_dot(forward_mixed_tok, wo_full)
        normed_two = scaled(forward_hidden_in, gain_f).astype(jnp.bfloat16)
        forward_kept_rows = spread_rows(normed_two)
        forward_gate_pre = times_trans(forward_kept_rows, wg_use)
        forward_up_pre = times_trans(forward_kept_rows, wu_use)
        hidden_act = (jax.nn.silu(forward_gate_pre) * forward_up_pre).astype(jnp.bfloat16)
        branch = fold_rows(plain_dot(hidden_act, wd_use))
        result = (forward_hidden_in + branch).astype(jnp.bfloat16)
        forward_saved = (
            input_now,
            forward_head_query,
            forward_head_keys,
            forward_head_values,
            forward_attended,
            forward_spread,
            forward_mixed_tok,
            forward_hidden_in,
            forward_kept_rows,
            forward_gate_pre,
            forward_up_pre,
        )
        result, saved = (result, forward_saved)
        results.append(result)
        stored.append(saved)
        if tick_index < n_micro:
            arrived_x = shifted(result, "section", 1)
    returned = zero_rows
    grads_back = []
    row_lists = []
    gain_total = None
    ffn_total = None
    for tick_index in range(n_micro + 1):
        own_rows = cotangent[tick_index] if tick_index < n_micro else zero_rows
        grad_now = jnp.where(section_idx == 1, own_rows, returned)
        batch_index = jnp.clip(tick_index - 1 + section_idx, 0, n_micro - 1)
        early_saved = stored[max(tick_index - 1, 0)]
        late_saved = stored[min(tick_index + 1, n_micro)]
        saved = jax.tree.map(
            lambda early_val, late_val: jnp.where(section_idx == 0, early_val, late_val),
            early_saved,
            late_saved,
        )
        (
            input_bf,
            head_query,
            backward_head_keys,
            backward_head_values,
            attended,
            spread,
            mixed_tok,
            hidden_in,
            kept_rows,
            gate_pre,
            up_pre,
        ) = saved
        backward_place_row, backward_token_places, backward_span_places = place_sets(batch_index)
        values_in = input_bf.astype(jnp.float32)
        normed_one = scaled(values_in, gain_a).astype(jnp.bfloat16)
        grad_all = spread_rows(grad_now)
        ffn_terms, d_partial = ffn_back(
            grad_all, kept_rows, gate_pre, up_pre, wg_use, wu_use, wd_use
        )
        d_normed_two = fold_rows(d_partial)
        grad_gf, d_hidden = norm_back(hidden_in, gain_f, d_normed_two)
        d_hidden = d_hidden + grad_now.astype(jnp.float32)
        d_branch = d_hidden.astype(jnp.bfloat16)
        d_mixed = times_trans(d_branch, wo_full).astype(jnp.bfloat16)
        d_att = to_heads(d_mixed.reshape(per_device, n_seq, q_width))[:, 0].reshape(
            span_rows, local_heads, HEAD_DIM
        )
        offset = jnp.sum(d_att.astype(jnp.float32) * attended, -1).T

        def collect(state_in, key_piece, start_row):
            piece_keys, piece_values = key_piece
            visible = backward_place_row[None, None, :] <= backward_span_places[None, :, None]
            scores = (
                jnp.einsum(
                    "qhd,kd->hqk", head_query, piece_keys, preferred_element_type=jnp.float32
                )
                * attn_scale
            )
            probs = jnp.where(visible, jnp.exp(scores - spread[..., None]), 0.0)
            d_probs = jnp.einsum(
                "qhd,kd->hqk", d_att, piece_values, preferred_element_type=jnp.float32
            )
            d_score = (probs * (d_probs - offset[..., None]) * attn_scale).astype(jnp.bfloat16)
            d_query_acc = jnp.einsum(
                "hqk,kd->qhd", d_score, piece_keys, preferred_element_type=jnp.float32
            )
            key_part = jnp.einsum(
                "hqk,qhd->kd", d_score, head_query, preferred_element_type=jnp.float32
            )
            value_part = jnp.einsum(
                "hqk,qhd->kd", probs.astype(jnp.bfloat16), d_att, preferred_element_type=jnp.float32
            )
            return (d_query_acc, key_part, value_part)

        start_state = (
            jnp.zeros((span_rows, local_heads, HEAD_DIM), jnp.float32),
            jnp.zeros((total_len, HEAD_DIM), jnp.float32),
            jnp.zeros((total_len, HEAD_DIM), jnp.float32),
        )
        d_query_acc, d_keys_all, d_values_all = over_keys(
            backward_head_keys, backward_head_values, collect, start_state
        )
        own_keys = lax.psum_scatter(
            d_keys_all.astype(jnp.bfloat16), "shard", scatter_dimension=0, tiled=True
        ).astype(jnp.float32)
        own_values = lax.psum_scatter(
            d_values_all.astype(jnp.bfloat16), "shard", scatter_dimension=0, tiled=True
        ).astype(jnp.float32)
        d_query_head = rotate(d_query_acc, backward_span_places, -1.0).astype(jnp.bfloat16)
        d_query = to_tokens(d_query_head.reshape(span_rows, 1, q_width)).reshape(
            per_device, HEADS * HEAD_DIM
        )
        own_keys = rotate(own_keys[:, None, :], backward_span_places, -1.0)[:, 0]
        back_kv = lax.all_to_all(
            jnp.concatenate([own_keys, own_values], -1)[:, None, :].astype(jnp.bfloat16),
            "seq",
            split_axis=0,
            concat_axis=1,
            tiled=True,
        ).astype(jnp.float32)
        back_kv = jnp.sum(back_kv.reshape(per_device, KV_HEADS, kv_repeat, 2 * HEAD_DIM), 2)
        d_key = (
            back_kv[..., :HEAD_DIM].reshape(per_device, KV_HEADS * HEAD_DIM).astype(jnp.bfloat16)
        )
        d_value = (
            back_kv[..., HEAD_DIM:].reshape(per_device, KV_HEADS * HEAD_DIM).astype(jnp.bfloat16)
        )
        d_normed_one = (
            plain_dot(d_query, wq_full) + plain_dot(d_key, wk_full) + plain_dot(d_value, wv_full)
        )
        grad_ga, d_input = norm_back(values_in, gain_a, d_normed_one)
        d_input = d_input + d_hidden
        gain_terms = (grad_ga, grad_gf)
        row_terms = (d_query, d_key, d_value, normed_one, mixed_tok, d_branch)
        d_input, gain_terms, row_terms, ffn_terms = (
            d_input.astype(jnp.bfloat16),
            gain_terms,
            row_terms,
            ffn_terms,
        )
        grads_back.append(d_input)
        row_lists.append(row_terms)
        if tick_index < n_micro:
            returned = shifted(d_input, "section", -1)
        if gain_total is None:
            gain_total = gain_terms
            ffn_total = ffn_terms
        else:
            gain_total = jax.tree.map(jnp.add, gain_total, gain_terms)
            ffn_total = jax.tree.map(jnp.add, ffn_total, ffn_terms)
    joined = [
        jnp.concatenate([row_set[index_val] for row_set in row_lists], 0) for index_val in range(6)
    ]
    grad_wq = outer_sum(joined[0], joined[3])
    grad_wk = outer_sum(joined[1], joined[3])
    grad_wv = outer_sum(joined[2], joined[3])
    grad_wo = outer_sum(joined[4], joined[5])
    attn_owned = (
        lax.psum_scatter(gain_total[0], ("shard", "seq"), scatter_dimension=0, tiled=True),
        lax.psum_scatter(gain_total[1], ("shard", "seq"), scatter_dimension=0, tiled=True),
        lax.psum_scatter(grad_wq, ("shard", "seq"), scatter_dimension=0, tiled=True),
        lax.psum_scatter(grad_wk, ("shard", "seq"), scatter_dimension=0, tiled=True),
        lax.psum_scatter(grad_wv, ("shard", "seq"), scatter_dimension=0, tiled=True),
        lax.psum_scatter(grad_wo, ("shard", "seq"), scatter_dimension=0, tiled=True),
    )
    outputs = lax.dynamic_slice_in_dim(jnp.stack(results), section_idx, n_micro, 0)[None]
    input_grads = lax.dynamic_slice_in_dim(jnp.stack(grads_back), 1 - section_idx, n_micro, 0)[None]
    return (
        outputs,
        input_grads,
        attn_owned[0][None],
        attn_owned[2][None],
        attn_owned[3][None],
        attn_owned[4][None],
        attn_owned[5][None],
        attn_owned[1][None],
        ffn_total[0][None],
        ffn_total[1][None],
        ffn_total[2][None],
    )


LOW = jnp.bfloat16
FULL = jnp.float32
MESH = pl.DeviceIdType.MESH
RING = 4
CHIPS = 2 * RING
SPLIT = 2
LAG = (0, 0, 1, 2, 3)
PLACE = 128
ORDER = ((2, 1), (1, 1), (3, 1), (0, 1), (2, 0), (1, 0), (3, 0), (0, 0))
IN_VMEM = pl.BlockSpec(memory_space=pltpu.VMEM)
IN_HBM = pl.BlockSpec(memory_space=pltpu.HBM)
IN_SMEM = pl.BlockSpec(memory_space=pltpu.SMEM)


class Site:
    def __init__(self):
        self.section = lax.axis_index("section")
        self.z = lax.axis_index("shard")
        member = lax.axis_index("seq")
        self.y = lax.div(member, 2)
        self.core = lax.rem(member, 2)
        self.up = (self.section, lax.rem(self.z + 1, RING), member)
        self.down = (self.section, lax.rem(self.z + RING - 1, RING), member)
        self.across = (self.section, self.z, (1 - self.y) * 2 + self.core)
        self.sibling = (self.section, self.z, self.y * 2 + 1 - self.core)
        self.corner = (self.section, self.z, (1 - self.y) * 2 + 1 - self.core)
        self.opposite = (self.section, lax.rem(self.z + 2, RING), member)
        self.partner = (1 - self.section, self.z, member)
        self.member = member

    def chip(self, along_z, along_y):
        return lax.rem(self.z + along_z, RING) * 2 + lax.rem(self.y + along_y, 2)


class Links:
    def __init__(self, send, recv, site):
        self.send, self.recv, self.site = send, recv, site
        self.sent = []

    def copy(self, index, src, dst, device):
        return pltpu.make_async_remote_copy(
            src_ref=src,
            dst_ref=dst,
            send_sem=self.send.at[index],
            recv_sem=self.recv.at[index],
            device_id=device,
            device_id_type=MESH,
        )

    def go(self, index, src, dst, device):
        copy = self.copy(index, src, dst, device)
        copy.start()
        self.sent.append(copy)

    def got(self, index, where):
        self.copy(index, where, where, self.site.sibling).wait_recv()
        return where

    def close(self):
        for copy in self.sent:
            copy.wait_send()


def greet(site):
    barrier = pltpu.get_barrier_semaphore()
    devices = (
        site.up, site.down, site.across, site.sibling, site.corner, site.opposite, site.partner
    )
    for device in devices:
        pl.semaphore_signal(barrier, inc=1, device_id=device, device_id_type=MESH)
    pl.semaphore_wait(barrier, len(devices))


SPREAD_SEMS = 7 * SPLIT + CHIPS
FOLD_SEMS = 7 * SPLIT + CHIPS
SMALL_SEMS = 11
COPY_SEMS = 64
CROSS_SEMS = 40
PIECE = 128


class Spread:
    def __init__(self, site, held, links, use):
        self.site, self.held, self.links, self.use = site, held, links, use
        self.size = held.shape[2] // SPLIT
        self.up, self.down, self.over, self.relay, self.y_below, self.y_above, self.y_far = (
            k * SPLIT for k in range(7)
        )
        self.along = ((0, 0), (3, 0), (1, 0), (0, 1), (2, 0), (3, 1), (1, 1), (2, 1))

    def piece(self, slot, part):
        site = self.site
        rows = pl.ds(part * self.size, self.size)
        return self.held.at[site.chip(*self.along[slot]), site.core, rows]

    def block(self, slot, core):
        return self.held.at[self.site.chip(*self.along[slot]), core]

    def go(self, index, where, device):
        self.links.go(index, where, where, device)

    def share(self, slot):
        self.go(7 * SPLIT + slot, self.block(slot, self.site.core), self.site.sibling)

    def consume(self, *slots):
        for slot in slots:
            self.links.got(7 * SPLIT + slot, self.block(slot, 1 - self.site.core))
            self.use(self.site.chip(*self.along[slot]))

    def ways(self, part):
        ways = (
            (self.up + part, 1, self.site.up, self.y_below + part),
            (self.down + part, 2, self.site.down, self.y_above + part),
        )
        return ways if part % 2 == 0 else ways[::-1]

    def own(self, part):
        where = self.piece(0, part)
        for index, _, device, _ in self.ways(part):
            self.go(index, where, device)
        self.go(self.over + part, where, self.site.across)

    def relays(self, part):
        for turn, (index, slot, device, over) in enumerate(self.ways(part)):
            came = self.links.got(index, self.piece(slot, part))
            if turn == 0:
                self.go(self.relay + part, came, device)
            self.go(over, came, self.site.across)

    def far(self, part):
        came = self.links.got(self.relay + part, self.piece(4, part))
        self.go(self.y_far + part, came, self.site.across)

    def after_relays(self):
        self.share(1)
        self.share(2)
        for part in range(SPLIT):
            self.links.got(self.over + part, self.piece(3, part))
        self.share(3)

    def tail(self, consume=True, first=0):
        def take(*slots):
            if consume:
                self.consume(*slots)

        self.share(4)
        take(*range(first, 3))
        for part in range(SPLIT):
            self.links.got(self.y_below + part, self.piece(5, part))
            self.links.got(self.y_above + part, self.piece(6, part))
        self.share(5)
        self.share(6)
        take(3, 4)
        for part in range(SPLIT):
            self.links.got(self.y_far + part, self.piece(7, part))
        self.share(7)
        take(5, 6, 7)
        if not consume:
            for slot in range(CHIPS):
                self.links.got(7 * SPLIT + slot, self.block(slot, 1 - self.site.core))

    def rest(self, consume=True):
        self.after_relays()
        for part in range(SPLIT):
            self.far(part)
        self.tail(consume)


class Fold:
    def __init__(self, site, part_of, buffers, links):
        self.site, self.part_of, self.links = site, part_of, links
        self.mine, self.pass_out, self.pass_in, self.stage, self.land = buffers
        self.rows = self.mine.shape[1]
        self.size = self.rows // SPLIT
        self.over = CHIPS
        self.relay, self.up, self.down = (CHIPS + (4 + k) * SPLIT for k in range(3))

    def where(self, part):
        return pl.ds(part * self.size, self.size)

    def came(self, index, where):
        return self.links.got(index, where)[...].astype(FULL)

    def compute(self, step):
        both = self.part_of(self.site.chip(*ORDER[step]))
        self.pass_out[step] = both[: self.rows].astype(LOW)
        self.links.go(step, self.pass_out.at[step], self.pass_in.at[step], self.site.sibling)
        self.mine[step] = both[self.rows :]

    def settle(self, step):
        self.mine[step] += self.came(step, self.pass_in.at[step])

    def send(self, index, slot, part, value, device):
        where = self.where(part)
        self.stage[slot, where] = value.astype(LOW)
        self.links.go(index, self.stage.at[slot, where], self.land.at[slot, where], device)

    def send_over(self, step, part):
        value = self.mine[step, self.where(part)]
        self.send(self.over + step * SPLIT + part, step, part, value, self.site.across)

    def start(self):
        self.compute(0)
        self.compute(1)
        for step in range(4):
            self.settle(step)
            self.send_over(step, 0)
            self.compute(step + 2)
        for part in range(1, SPLIT):
            for step in range(4):
                self.send_over(step, part)
        self.compute(6)
        self.compute(7)
        for step in range(4, CHIPS):
            self.settle(step)

    def pass_on(self, part):
        where = self.where(part)
        value = self.mine[4, where] + self.came(self.over + part, self.land.at[0, where])
        device = self.site.up if part % 2 == 0 else self.site.down
        self.send(self.relay + part, 4, part, value, device)

    def up_down(self, part):
        where = self.where(part)
        ways = ((5, self.up, self.site.up), (6, self.down, self.site.down))
        for step, base, device in ways if part % 2 else ways[::-1]:
            from_y = self.over + (step - 4) * SPLIT + part
            value = self.mine[step, where] + self.came(from_y, self.land.at[step - 4, where])
            if part % 2 == step - 5:
                value = value + self.came(self.relay + part, self.land.at[4, where])
            self.send(base + part, step, part, value, device)

    def final(self, part):
        where = self.where(part)
        value = self.mine[7, where] + self.came(
            self.over + 3 * SPLIT + part, self.land.at[3, where]
        )
        value = value + self.came(self.up + part, self.land.at[5, where])
        return value + self.came(self.down + part, self.land.at[6, where])


def fold_spread(fold, spread, local, idle):
    def finish(part):
        rows = local(fold.final(part), fold.where(part))
        if spread is not None:
            site = spread.site
            spread.held[site.chip(0, 0), site.core, fold.where(part)] = rows
            spread.own(part)

    fold.start()
    idle(3)
    last = SPLIT - 1
    for tick in range(SPLIT + LAG[-1]):
        steps = [tick - lag for lag in LAG]
        if 0 <= steps[0] < SPLIT:
            fold.pass_on(steps[0])
        if 0 <= steps[1] < SPLIT:
            fold.up_down(steps[1])
        if 0 <= steps[2] < SPLIT:
            finish(steps[2])
        if spread is not None:
            if steps[2] == last:
                spread.share(0)
            if 0 <= steps[3] < SPLIT:
                spread.relays(steps[3])
            if steps[3] == last:
                spread.after_relays()
            if 0 <= steps[4] < SPLIT:
                spread.far(steps[4])
            if steps[2] == last + 1:
                spread.consume(0)
        idle(3)
    if spread is not None:
        idle(10)
        spread.tail(first=1)
        spread.links.close()
    else:
        idle(10)
    fold.links.close()


class Cross:
    def __init__(self, n):
        self.site = n.site
        self.links = Links(n.cross_send, n.cross_recv, n.site)
        self.begun = []
        self.count = 0

    def where(self, layer, receives, action):
        if layer is None:
            action()
        else:
            pl.when((self.site.section == layer) == receives)(action)

    def send(self, src, dst, layer=None):
        rows = src.shape[0]
        pieces = []
        start = 0
        while start < rows:
            size = min(PIECE, rows - start)
            where = pl.ds(start, size)
            pieces.append(
                self.links.copy(self.count, src.at[where], dst.at[where], self.site.partner)
            )
            self.count += 1
            start += size

        def begin():
            for copy in pieces:
                copy.start()

        self.where(layer, False, begin)
        self.begun.append([pieces, layer, False])
        return len(self.begun) - 1

    def wait(self, index):
        pieces, layer, landed = self.begun[index]

        def arrive():
            for copy in pieces:
                copy.wait_recv()

        if not landed:
            self.begun[index][2] = True
            self.where(layer, True, arrive)

    def close(self):
        for index in range(len(self.begun)):
            self.wait(index)
        for pieces, layer, _ in self.begun:

            def leave():
                for copy in pieces:
                    copy.wait_send()

            self.where(layer, False, leave)
        self.begun = []


class Copies:
    def __init__(self, n):
        self.n, self.count, self.open = n, 0, []

    def sem(self):
        self.count += 1
        return self.n.copy_sem.at[self.count - 1]

    def start(self, src, dst):
        copy = pltpu.make_async_copy(src, dst, self.sem())
        copy.start()
        self.open.append(copy)
        return copy

    def pick(self, own, other, dst, layer):
        sem = self.sem()
        from_own = pltpu.make_async_copy(own, dst, sem)
        from_other = pltpu.make_async_copy(other, dst, sem)
        pl.when(self.n.site.section == layer)(from_own.start)
        pl.when(self.n.site.section != layer)(from_other.start)
        self.open.append(from_own)
        return from_own

    def wait(self, *copies):
        for copy in copies:
            if any(copy is other for other in self.open):
                self.open = [other for other in self.open if other is not copy]
                copy.wait()

    def close(self):
        self.wait(*list(self.open))


def kernel_of(body, names, *refs):
    n = types.SimpleNamespace(**dict(zip(names, refs)))
    n.site = Site()
    n.copies = Copies(n)
    n.cross = Cross(n)
    body(n)
    n.cross.close()
    n.copies.close()


def launch(name, ident, body, scalars, inputs, outputs, scratch):
    scratch = dict(
        scratch,
        copy_sem=pltpu.SemaphoreType.DMA((COPY_SEMS,)),
        cross_send=pltpu.SemaphoreType.DMA((CROSS_SEMS,)),
        cross_recv=pltpu.SemaphoreType.DMA((CROSS_SEMS,)),
    )
    names = [*scalars, *inputs, *outputs, *scratch]
    results = pl.pallas_call(
        functools.partial(kernel_of, body, names),
        out_shape=[jax.ShapeDtypeStruct(*value) for value in outputs.values()],
        in_specs=[IN_SMEM] * len(scalars) + [IN_HBM] * len(inputs),
        out_specs=[IN_HBM] * len(outputs),
        scratch_shapes=list(scratch.values()),
        compiler_params=pltpu.CompilerParams(
            collective_id=ident, has_side_effects=True, vmem_limit_bytes=60 * 2**20
        ),
        cost_estimate=pl.CostEstimate(flops=2**37, bytes_accessed=2**23, transcendentals=0),
        name=name,
    )(*scalars.values(), *inputs.values())
    return types.SimpleNamespace(**dict(zip(outputs, results)))


def fold_buffers(full):
    return dict(
        mine=pltpu.VMEM((CHIPS, *full), FULL),
        pass_out=pltpu.VMEM((CHIPS, *full), LOW),
        pass_in=pltpu.VMEM((CHIPS, *full), LOW),
        stage=pltpu.VMEM((CHIPS - 1, *full), LOW),
        land=pltpu.VMEM((CHIPS - 1, *full), LOW),
        fold_send=pltpu.SemaphoreType.DMA((FOLD_SEMS,)),
        fold_recv=pltpu.SemaphoreType.DMA((FOLD_SEMS,)),
    )


def fold_of(n, part_of):
    buffers = (n.mine, n.pass_out, n.pass_in, n.stage, n.land)
    return Fold(n.site, part_of, buffers, Links(n.fold_send, n.fold_recv, n.site))


def spread_of(n, held, send, recv, use, kept=None):
    def take(chip):
        block = held[chip]
        use(chip, block.reshape(block.shape[0] * block.shape[1], block.shape[2]))
        if kept is not None:
            n.copies.start(held.at[chip], kept.at[chip])

    return Spread(n.site, held, Links(send, recv, n.site), take)


def spread_sems(*names):
    return {name: pltpu.SemaphoreType.DMA((SPREAD_SEMS,)) for name in names}


def no_idle(count):
    pass


def rows_of(ref, chip, site):
    return jnp.concatenate([ref[chip, 1 - site.core], ref[chip, site.core]], 0)


def put(ref, chip, value):
    ref[chip] = value.astype(LOW).reshape(ref.shape[1:])


def gate_chunk(n, chip, rows):
    gate_pre = times_trans(rows, n.w_g[...])
    up_pre = times_trans(rows, n.w_u[...])
    sig = jax.nn.sigmoid(gate_pre)
    silu_val = gate_pre * sig
    put(n.act, chip, silu_val * up_pre)
    return up_pre * sig * (1.0 + gate_pre * (1.0 - sig)), silu_val


def norm_back_rows(values, gain_vec, grad_in):
    factor = lax.rsqrt(jnp.mean(values * values, -1, keepdims=True) + EPSILON)
    gain_grad = jnp.sum(grad_in * values * factor, 0, keepdims=True)
    mean_term = jnp.mean(grad_in * gain_vec * values, -1, keepdims=True)
    return (
        gain_grad,
        factor * gain_vec * grad_in - values * (factor * factor * factor) * mean_term,
    )


def swap_halves(value):
    width = value.shape[1]
    half = HEAD_DIM // 2
    lane = lax.broadcasted_iota(jnp.int32, value.shape, 1)
    return jnp.where(
        lax.rem(lane, HEAD_DIM) < half,
        pltpu.roll(value, width - half, 1),
        pltpu.roll(value, half, 1),
    )


def stacked(pair):
    return jnp.concatenate([pair[:, :HEAD_DIM], pair[:, HEAD_DIM:]], 0)


def side_by_side(turned):
    return jnp.concatenate([turned[:, :PLACE], turned[:, PLACE:]], 0).T


def hide_later(scores, fill):
    last = scores[-PLACE:]
    key = lax.broadcasted_iota(jnp.int32, last.shape, 0)
    query = lax.rem(lax.broadcasted_iota(jnp.int32, last.shape, 1), PLACE)
    last = jnp.where(key <= query, last, fill)
    if scores.shape[0] == PLACE:
        return last
    return jnp.concatenate([scores[:-PLACE], last], 0)


def turn_of(turns, place):
    near, far = pl.ds(0, PLACE), pl.ds(PLACE + place, 1)
    cos_near, sin_near = turns[0, near], turns[1, near]
    cos_far, sin_far = turns[0, far], turns[1, far]
    cosine = cos_near * cos_far - sin_near * sin_far
    sine = sin_near * cos_far + cos_near * sin_far
    lane = lax.broadcasted_iota(jnp.int32, cosine.shape, 1)
    sine = jnp.where(lax.rem(lane, HEAD_DIM) < HEAD_DIM // 2, -sine, sine)
    keyed = lane < HEAD_DIM
    return (
        jnp.concatenate([cosine, jnp.where(keyed, cosine, 1.0)], 1),
        jnp.concatenate([sine, jnp.where(keyed, sine, 0.0)], 1),
    )


def attend(n):
    q_width = 2 * HEAD_DIM
    scale = jnp.asarray(1.0 / math.sqrt(HEAD_DIM), LOW)
    for place in range(CHIPS):
        at = pl.ds(place * PLACE, PLACE)
        value = n.qkv[n.block_at[place]]
        cosine, sine = turn_of(n.turns_v, place)
        value = (value * cosine + swap_halves(value) * sine).astype(LOW)
        n.turned_v[at, :q_width] = value[:, :q_width] * scale
        n.turned_v[at, q_width:] = value[:, q_width:]
        n.values_t[:, at] = value[:, q_width:].astype(FULL).T[HEAD_DIM:].astype(LOW)
    for place in range(CHIPS):
        at = pl.ds(place * PLACE, PLACE)
        keys = pl.ds(0, (place + 1) * PLACE)
        query = stacked(n.turned_v[at, :q_width])
        scores = times_trans(n.turned_v[keys, q_width : q_width + HEAD_DIM], query)
        scores = hide_later(scores, NEG_LARGE)
        top = jnp.max(scores, 0, keepdims=True)
        weight = jnp.exp(scores - top)
        total = jnp.sum(weight, 0, keepdims=True)
        out = plain_dot(n.values_t[:, keys], weight.astype(LOW)) / total
        n.attended_v[place] = side_by_side(out)
        n.spread_v[pl.ds(place, 1)] = top + jnp.log(total)
    for block in range(CHIPS):
        put(n.mixed_v, block, n.attended_v[n.order[block]])


def keep_attention(n):
    n.copies.start(n.turned_v, n.turned)
    n.copies.start(n.attended_v, n.attended)
    n.copies.start(n.spread_v, n.spread)
    n.copies.start(n.mixed_v, n.mixed)


def attend_back(n):
    q_width = 2 * HEAD_DIM
    n.d_key[...] = jnp.zeros_like(n.d_key)
    n.d_value[...] = jnp.zeros_like(n.d_value)
    for place in range(CHIPS):
        at = pl.ds(place * PLACE, PLACE)
        n.keys_t[:, at] = n.turned_v[at, q_width:].astype(FULL).T[:HEAD_DIM].astype(LOW)
    for place in range(CHIPS):
        at = pl.ds(place * PLACE, PLACE)
        keys = pl.ds(0, (place + 1) * PLACE)
        d_out = n.d_mixed[n.block_at[place]]
        product = (d_out.astype(FULL) * n.attended_v[place]).T
        offset = jnp.concatenate(
            [
                jnp.sum(product[:HEAD_DIM], 0, keepdims=True),
                jnp.sum(product[HEAD_DIM:], 0, keepdims=True),
            ],
            1,
        )
        d_out = stacked(d_out)
        query = stacked(n.turned_v[at, :q_width])
        scores = times_trans(n.turned_v[keys, q_width : q_width + HEAD_DIM], query)
        scores = hide_later(scores, NEG_LARGE)
        probs = jnp.exp(scores - n.spread_v[pl.ds(place, 1)])
        d_probs = times_trans(n.turned_v[keys, q_width + HEAD_DIM :], d_out)
        d_scores = (probs * (d_probs - offset)).astype(LOW)
        n.d_key[keys] += plain_dot(d_scores, query)
        n.d_value[keys] += plain_dot(probs.astype(LOW), d_out)
        n.d_query[at] = side_by_side(plain_dot(n.keys_t[:, keys], d_scores)) * (
            1.0 / math.sqrt(HEAD_DIM)
        )
    for place in range(CHIPS):
        at = pl.ds(place * PLACE, PLACE)
        value = jnp.concatenate([n.d_query[at], n.d_key[at], n.d_value[at]], 1)
        cosine, sine = turn_of(n.turns_v, place)
        value = value * cosine - swap_halves(value) * sine
        n.d_turned[place] = value.astype(LOW)
    for block in range(CHIPS):
        put(n.d_qkv, block, n.d_turned[n.order[block]])


def gather_small_start(n):
    links = n.links_small = Links(n.small_send, n.small_recv, n.site)
    links.go(0, n.gains_mine, n.gains_x, n.site.partner)
    links.go(1, n.kv_mine, n.kv_x, n.site.partner)


def gather_small(n):
    site, links = n.site, n.links_small
    links.got(0, n.gains_x)
    own, came = n.gains_mine[...], n.gains_x[...]
    first = site.section == 0
    n.gains_all[site.z, site.member] = jnp.concatenate(
        [
            jnp.where(first, own, came)[:2],
            jnp.where(first, came, own)[:2],
            jnp.zeros((4, own.shape[1]), FULL),
        ],
        0,
    )
    peers = (site.sibling, site.across, site.corner)
    mine = n.gains_all.at[site.z, site.member]
    for index, device in enumerate(peers):
        links.go(2 + index, mine, mine, device)
    for index, device in enumerate(peers):
        links.got(2 + index, n.gains_all.at[site.z, device[2]])
    shard = n.gains_all.at[site.z]
    for index, device in enumerate((site.up, site.down, site.opposite)):
        links.go(5 + index, shard, shard, device)


def gather_small_keys(n):
    site, links = n.site, n.links_small
    links.got(1, n.kv_x)
    n.kv_all[site.member, site.section] = n.kv_mine[...]
    n.kv_all[site.member, 1 - site.section] = n.kv_x[...]
    mine = n.kv_all.at[site.member]
    for index, device in enumerate((site.sibling, site.across, site.corner)):
        links.go(8 + index, mine, mine, device)


def gather_small_end(n):
    site, links = n.site, n.links_small
    for index, along_z in enumerate((RING - 1, 1, 2)):
        links.got(5 + index, n.gains_all.at[lax.rem(site.z + along_z, RING)])
    for index, device in enumerate((site.sibling, site.across, site.corner)):
        links.got(8 + index, n.kv_all.at[device[2]])
    links.close()
    n.gains_v[...] = jnp.concatenate(
        [n.gains_all[shard, seq] for shard in range(RING) for seq in range(RING)], 1
    )
    for layer in range(2):
        for index in range(2):
            rows = n.kv_all[:, layer, index]
            n.w_kv[layer, pl.ds(index * HEAD_DIM, HEAD_DIM)] = rows.reshape(
                HEAD_DIM, rows.shape[-1]
            )
    n.copies.start(n.gains_v, n.gains)
    n.copies.start(n.w_kv, n.kv_rows)


def forward_first(n):
    site, copies, cross = n.site, n.copies, n.cross
    own = (site.chip(0, 0), site.core)
    small = [
        copies.start(n.gains_own, n.gains_mine),
        copies.start(n.w_key, n.kv_mine.at[0]),
        copies.start(n.w_value, n.kv_mine.at[1]),
    ]
    rows_copy = copies.pick(n.inputs.at[0], n.inputs.at[1], n.held.at[own], 0)
    top_copy = copies.pick(n.cotangent.at[0], n.cotangent.at[1], n.top_v, 0)
    turns_copy = copies.start(n.turns, n.turns_v)
    def use_first(chip, rows):
        normed = scaled(rows.astype(FULL), n.gains_v[:1]).astype(LOW)
        n.normed[chip] = normed.reshape(n.normed.shape[1:])
        n.qkv[chip] = jnp.concatenate(
            [times_trans(normed, n.w_q[...]), times_trans(normed, n.w_kv[0])], 1
        )
        copies.start(n.normed.at[chip], n.rows_one.at[chip])

    greet(site)
    copies.wait(*small)
    gather_small_start(n)
    at_query, at_out, at_gate, at_up, _ = (
        cross.send(*pair)
        for pair in (
            (n.w_query, n.x_query),
            (n.w_out, n.x_out),
            (n.w_gate, n.x_gate),
            (n.w_up, n.x_up),
            (n.w_down, n.x_down),
        )
    )
    copies.wait(rows_copy)
    spread = spread_of(n, n.held, n.spread_send, n.spread_recv, use_first)
    spread.own(0)
    gather_small(n)
    for part in range(1, SPLIT):
        spread.own(part)
    spread.share(0)
    gather_small_keys(n)
    for part in range(SPLIT):
        spread.relays(part)
    gather_small_end(n)
    spread.after_relays()
    cross.wait(at_query)
    query_copy = copies.pick(n.w_query, n.x_query, n.w_q, 0)
    for part in range(SPLIT):
        spread.far(part)
    copies.wait(query_copy)
    copies.wait(top_copy, turns_copy)
    top_copy = copies.start(n.top_v, n.top_all.at[own])
    spread.tail()
    spread.links.close()
    copies.wait(top_copy)
    top = spread_of(n, n.top_all, n.top_send, n.top_recv, None)
    for part in range(SPLIT):
        top.own(part)
    cross.wait(at_out)
    out_copy = copies.pick(n.w_out, n.x_out, n.w_o, 0)
    attend(n)
    keep_attention(n)
    top.share(0)
    copies.wait(out_copy)

    def part_of(chip):
        return plain_dot(rows_of(n.mixed_v, chip, site), n.w_o[...])

    def local(total, where):
        hidden_in = n.held[(*own, where)].astype(FULL) + total
        n.hidden_v[where] = hidden_in
        return scaled(hidden_in, n.gains_v[1:2]).astype(LOW)

    waiting = []

    def use_later(chip, rows):
        waiting.append(chip)

    def use_gate(chip):
        rows = n.held_two[chip].reshape(-1, n.held_two.shape[-1])
        gate_slope, up_slope = gate_chunk(n, chip, rows)
        put(n.gate_slope_v, chip, gate_slope)
        put(n.up_slope_v, chip, up_slope)

    def idle(count):
        if count == 10:
            for part in range(SPLIT):
                top.relays(part)

    spread = spread_of(
        n, n.held_two, n.spread_two_send, n.spread_two_recv, use_later, n.rows_two
    )
    fold_spread(fold_of(n, part_of), spread, local, idle)
    copies.start(n.hidden_v, n.hidden)
    top.after_relays()
    for part in range(SPLIT):
        top.far(part)
    cross.wait(at_gate)
    cross.wait(at_up)
    copies.wait(
        copies.pick(n.w_gate, n.x_gate, n.w_g, 0), copies.pick(n.w_up, n.x_up, n.w_u, 0)
    )
    for chip in waiting:
        use_gate(chip)
    for source, target in (
        (n.act, n.act_all), (n.gate_slope_v, n.gate_slope), (n.up_slope_v, n.up_slope)
    ):
        copies.start(source, target)
    top.tail(consume=False)
    top.links.close()


def second_layer(n):
    site, copies = n.site, n.copies
    first = [
        copies.start(n.act_prev, n.act_prev_v),
        copies.pick(n.w_down, n.x_down, n.w_d_prev, 0),
    ]
    rows_copies = [copies.start(n.hidden_prev, n.hidden_prev_v), copies.start(n.gains, n.gains_v)]
    qkv_copies = [
        copies.pick(n.w_query, n.x_query, n.w_in.at[pl.ds(0, 2 * HEAD_DIM)], 1),
        copies.start(n.kv_rows.at[1], n.w_in.at[pl.ds(2 * HEAD_DIM, 2 * HEAD_DIM)]),
        copies.start(n.turns, n.turns_v),
    ]
    later = [
        copies.pick(n.w_out, n.x_out, n.w_o, 1),
        copies.pick(n.w_gate, n.x_gate, n.w_g, 1),
        copies.pick(n.w_up, n.x_up, n.w_u, 1),
        copies.pick(n.w_down, n.x_down, n.w_d, 1),
        copies.start(n.top_all, n.top_held),
    ]
    back_copies = [copies.pick(n.cotangent.at[0], n.cotangent.at[1], n.top_v, 0)]
    next_copies = [
        copies.start(n.gate_slope, n.gate_slope_v),
        copies.start(n.up_slope, n.up_slope_v),
    ]
    greet(site)
    copies.wait(*first, *rows_copies)

    def part_of(chip):
        return plain_dot(rows_of(n.act_prev_v, chip, site), n.w_d_prev[...])

    def local(total, where):
        result = (n.hidden_prev_v[where] + total).astype(LOW)
        n.result_v[where] = result
        return scaled(result.astype(FULL), n.gains_v[2:3]).astype(LOW)

    def use_qkv(chip, rows):
        n.qkv[chip] = times_trans(rows, n.w_in[...])

    def settle(count):
        copies.wait(*qkv_copies)

    spread = spread_of(n, n.held, n.spread_send, n.spread_recv, use_qkv)
    fold_spread(fold_of(n, part_of), spread, local, settle)
    copies.start(n.result_v, n.result_a)
    n.cross.send(n.result_v, n.came_result_a, 0)
    attend(n)
    copies.wait(*later)

    def part_of_two(chip):
        return plain_dot(rows_of(n.mixed_v, chip, site), n.w_o[...])

    def local_two(total, where):
        hidden_in = n.result_v[where].astype(FULL) + total
        n.hidden_v[where] = hidden_in
        return scaled(hidden_in, n.gains_v[3:4]).astype(LOW)

    def use_gate(chip, rows):
        gate_slope, up_slope = gate_chunk(n, chip, rows)
        d_act = times_trans(n.top_held[chip].reshape(rows.shape), n.w_d[...])
        put(n.d_gate_v, chip, d_act * gate_slope)
        put(n.d_up_v, chip, d_act * up_slope)

    spread = spread_of(
        n, n.held_two, n.spread_two_send, n.spread_two_recv, use_gate
    )
    fold_spread(fold_of(n, part_of_two), spread, local_two, no_idle)
    copies.wait(*back_copies)
    cross = n.cross
    first_copies = []

    def preload():
        first_copies.append(copies.pick(n.w_gate, n.x_gate, n.w_g, 0))
        first_copies.append(copies.pick(n.w_up, n.x_up, n.w_u, 0))
        first_copies.append(copies.pick(n.w_out, n.x_out, n.w_o, 0))
        first_copies.append(copies.start(n.rows_two, n.top_held))

    backward(
        n,
        types.SimpleNamespace(
            layer=1, attn_copies=[], one_copies=[], next_copies=next_copies, act=n.act,
            top_all=n.top_held, normed_two=n.held_two, normed_one=n.held, branch=n.normed,
            hidden=n.hidden_v, top=n.top_v, x_rows=n.result_v, d_input=n.d_input_v,
            w_next=n.w_d_prev, after_first=preload, send=n.back_send, recv=n.back_recv,
            sums=[
                (n.g_down_v, n.own_down_b, n.came_down_b),
                (n.g_gate_v, n.own_gate_b, n.came_gate_b),
                (n.g_up_v, n.own_up_b, None),
                (n.g_out_v, n.own_out_b, n.came_out_b),
                (n.g_query_v, n.own_query_b, n.came_query_b),
                (n.g_kv_v, n.own_kv_b, n.came_kv_b),
            ],
        ),
    )
    copies.start(n.d_input_v, n.d_input_b)
    n.gain_later_v[...] = n.gain_grads[...]
    copies.wait(*first_copies)
    copies.close()
    cross.close()
    attn_copies = [
        copies.start(n.turned, n.turned_v),
        copies.start(n.attended, n.attended_v),
        copies.start(n.spread, n.spread_v),
        copies.start(n.mixed, n.mixed_v),
        copies.pick(n.w_query, n.x_query, n.w_in.at[pl.ds(0, 2 * HEAD_DIM)], 0),
        copies.start(n.kv_rows.at[0], n.w_in.at[pl.ds(2 * HEAD_DIM, 2 * HEAD_DIM)]),
        copies.pick(n.inputs.at[0], n.inputs.at[1], n.x_v, 0),
    ]
    one_copies = [copies.start(n.rows_one, n.held)]
    cross.send(n.own_up_b, n.came_up_b, 1)
    cross.send(n.d_input_v, n.came_input_b, 1)
    backward(
        n,
        types.SimpleNamespace(
            layer=0, attn_copies=attn_copies, one_copies=one_copies, next_copies=[],
            act=n.act_prev_v, top_all=n.held_two, normed_two=n.top_held, normed_one=n.held,
            branch=n.normed, hidden=n.hidden_prev_v, top=n.d_input_v, x_rows=n.x_v,
            d_input=n.d_input_two, w_next=n.w_d, after_first=lambda: None, send=n.last_back_send,
            recv=n.last_back_recv,
            sums=[
                (n.g_down_v, n.own_down_a, n.came_down_a),
                (n.g_gate_v, n.own_gate_a, n.came_gate_a),
                (n.g_up_v, n.own_up_a, n.came_up_a),
                (n.g_out_v, n.own_out_a, n.came_out_a),
                (n.g_query_v, n.own_query_a, n.came_query_a),
                (n.g_kv_v, n.own_kv_a, n.came_kv_a),
            ],
        ),
    )


def products(n, left, right, store, tile=512):
    count = math.prod(left.shape[:-1])
    for start in range(0, right.shape[-1], tile):
        where = pl.ds(start, tile)
        value = outer_sum(
            left[...].reshape(count, left.shape[-1]), right[:, :, :, where].reshape(count, tile)
        )
        store(where, value.astype(LOW))
        yield


def ffn_products(n, k, made):
    for left, right, out in (
        (k.act, k.top_all, n.g_down_v),
        (n.d_gate_v, k.normed_two, n.g_gate_v),
        (n.d_up_v, k.normed_two, n.g_up_v),
    ):

        def store(where, value):
            out[:, where] = value

        yield from products(n, left, right, store)
        made(out)


def in_products(n, loads, made, normed_one, branch):
    site = n.site
    n.copies.wait(*loads)

    def store_out(where, value):
        n.g_out_v[:, where] = value

    def store_in(where, value):
        query = n.g_query_v.shape[0]
        n.g_query_v[:, where] = value[:query]
        n.kv_mine[:, :, :, where] = value[query:].reshape(
            *n.kv_mine.shape[:3], value.shape[1]
        )

    yield from products(n, n.d_qkv, normed_one, store_in)
    made(n.g_query_v)
    peers = (site.sibling, site.across, site.corner)
    links = Links(n.kv_send, n.kv_recv, site)
    for index, device in enumerate(peers):
        links.go(index, n.kv_mine.at[:, device[2]], n.kv_came.at[index], device)
    yield from products(n, n.mixed_v, branch, store_out)
    made(n.g_out_v)
    total = n.kv_mine[:, site.member].astype(FULL)
    for index in range(len(peers)):
        total = total + links.got(index, n.kv_came.at[index])[...].astype(FULL)
    n.g_kv_v[...] = total.astype(LOW)
    made(n.g_kv_v)
    links.close()


def fold_gains(n):
    site = n.site
    links = Links(n.gain_send, n.gain_recv, site)
    own = jnp.concatenate(
        [n.gain_grads[...], n.gain_later_v[...], jnp.zeros((4, n.gain_grads.shape[1]), FULL)], 0
    )
    width = n.gain_parts.shape[-1]
    for shard in range(RING):
        for seq in range(RING):
            start = (shard * RING + seq) * width
            n.gain_parts[seq, shard] = own[:, start : start + width]
    peers = (site.sibling, site.across, site.corner)
    for index, device in enumerate(peers):
        links.go(index, n.gain_parts.at[device[2]], n.gain_came.at[index], device)
    yield
    total = n.gain_parts[site.member]
    for index in range(3):
        total = total + links.got(index, n.gain_came.at[index])[...]
    n.gain_shards[...] = total
    for index, device in enumerate((site.up, site.down, site.opposite)):
        links.go(
            3 + index, n.gain_shards.at[device[1]], n.gain_last.at[index], device
        )
    yield
    total = n.gain_shards[site.z]
    for index in range(3):
        total = total + links.got(3 + index, n.gain_last.at[index])[...]
    n.gain_own[...] = total
    links.go(6, n.gain_own, n.gain_other, site.partner)
    yield
    total = n.gain_own[...] + links.got(6, n.gain_other)[...]
    n.gain_sums_v[...] = jnp.where(site.section == 0, total[:2], total[2:4])
    links.close()
    n.copies.start(n.gain_sums_v, n.gain_sums)


def backward(n, k):
    site, copies, cross = n.site, n.copies, n.cross
    layer = k.layer

    def made(out):
        for value, target, came in k.sums:
            if value is out:
                break
        copies.start(out, target)
        if came is not None:
            cross.send(out, came, layer)

    def step_on(working):
        def idle(count):
            for _ in range(count):
                next(working, None)

        return idle

    def part_of(chip):
        return plain_dot(rows_of(n.d_gate_v, chip, site), n.w_g[...]) + plain_dot(
            rows_of(n.d_up_v, chip, site), n.w_u[...]
        )

    def add_gain(row, value, where):
        row = pl.ds(row, 1)
        n.gain_grads[row] = value if where.start == 0 else n.gain_grads[row] + value

    def local(total, where):
        gain_grad, d_hidden = norm_back_rows(
            k.hidden[where], n.gains_v[2 * layer + 1 : 2 * layer + 2], total
        )
        d_hidden = d_hidden + k.top[where].astype(FULL)
        add_gain(1, gain_grad, where)
        n.d_hidden[where] = d_hidden
        return d_hidden.astype(LOW)

    def use_d_mixed(chip, rows):
        n.d_mixed[chip] = times_trans(rows, n.w_o[...]).astype(LOW)

    working = ffn_products(n, k, made)
    if layer == 0:
        step_on(working)(5)
    spread = spread_of(n, k.branch, k.send, k.recv, use_d_mixed)
    fold_spread(fold_of(n, part_of), spread, local, step_on(working))
    for _ in working:
        pass
    k.after_first()
    copies.wait(*k.attn_copies)
    attend_back(n)
    copies.wait(*k.next_copies)

    def part_of_two(chip):
        return plain_dot(rows_of(n.d_qkv, chip, site), n.w_in[...])

    def local_two(total, where):
        gain_grad, d_input = norm_back_rows(
            k.x_rows[where].astype(FULL), n.gains_v[2 * layer : 2 * layer + 1], total
        )
        d_input = (d_input + n.d_hidden[where]).astype(LOW)
        add_gain(0, gain_grad, where)
        k.d_input[where] = d_input
        return d_input

    working = in_products(n, k.one_copies, made, k.normed_one, k.branch)
    if layer == 1:

        def use_d_act(chip, rows):
            d_act = times_trans(rows, k.w_next[...])
            for out, slope in ((n.d_gate_v, n.gate_slope_v), (n.d_up_v, n.up_slope_v)):
                put(out, chip, d_act * slope[chip].astype(FULL).reshape(d_act.shape))

        spread = spread_of(n, n.held_two, n.back_two_send, n.back_two_recv, use_d_act)
        fold_spread(fold_of(n, part_of_two), spread, local_two, step_on(working))
        for _ in working:
            pass
        return
    fold_spread(fold_of(n, part_of_two), None, local_two, step_on(working))
    for _ in working:
        pass
    copies.start(k.d_input, n.d_input_a)
    cross.send(k.d_input, n.came_input_a, 0)

    def part_of_last(chip):
        return plain_dot(rows_of(n.act, chip, site), k.w_next[...])

    def local_last(total, where):
        n.result_two[where] = (n.hidden_v[where] + total).astype(LOW)

    buffers = (n.mine, n.pass_out, n.held_two.at[:, 0], n.stage, n.held_two.at[:, 1])
    links = Links(n.last_send, n.last_recv, site)
    gains_on = fold_gains(n)
    next(gains_on)
    fold_spread(
        Fold(site, part_of_last, buffers, links), None, local_last,
        lambda count: next(gains_on, None),
    )
    for _ in gains_on:
        pass
    copies.start(n.result_two, n.result_b)
    cross.send(n.result_two, n.came_result_b, 1)


def join_kernel(count, *refs):
    def take(number):
        nonlocal refs
        taken, refs = refs[:number], refs[number:]
        return taken

    own, came = (take(count), take(count)), (take(count), take(count))
    rows = (take(4), take(4))
    outs, row_outs = take(count + 1), take(2)
    own_at, came_at, sums = take(count), take(count), take(count)
    row_at, sems, out_sem, row_sem = refs
    section = lax.axis_index("section")

    def either(first, second):
        pl.when(section == 0)(first.start)
        pl.when(section != 0)(second.start)
        return first

    waits = []
    for index in range(count):
        for slot, (pair, target) in enumerate(((own, own_at), (came, came_at))):
            waits.append(
                either(
                    *(
                        pltpu.make_async_copy(
                            pair[layer][index], target[index], sems.at[2 * index + slot]
                        )
                        for layer in range(2)
                    )
                )
            )
    done = []
    row_waits = []
    for index, (own_a, own_b, came_a, came_b) in enumerate(rows):
        for slot, (first, second) in enumerate(((own_a, came_b), (came_a, own_b))):
            target, sem = row_at.at[index, slot], row_sem.at[2 * index + slot]
            row_waits.append(
                either(
                    pltpu.make_async_copy(first, target, sem),
                    pltpu.make_async_copy(second, target, sem),
                )
            )
    for copy in row_waits:
        copy.wait()
    for index, out in enumerate(row_outs):
        copy = pltpu.make_async_copy(row_at.at[index], out, row_sem.at[index])
        copy.start()
        done.append(copy)
    for index in range(count):
        waits[2 * index].wait()
        waits[2 * index + 1].wait()
        sums[index][...] = own_at[index][...].astype(FULL) + came_at[index][...].astype(FULL)
        if index < count - 1:
            parts = [(sums[index], outs[index])]
        else:
            parts = [(sums[index].at[pl.ds(k, 1)], outs[index + k]) for k in range(2)]
        for source, target in parts:
            copy = pltpu.make_async_copy(source, target, out_sem.at[len(done) - 2])
            copy.start()
            done.append(copy)
    for copy in done:
        copy.wait()


def join_all(own_a, own_b, came_a, came_b, results, input_grads):
    count = len(own_a)
    kept = [pltpu.VMEM(value.shape, LOW) for value in own_a]
    shapes = [value.shape for value in own_a]
    shapes = shapes[:-1] + [(1, *shapes[-1][1:])] * 2
    row_shape = jax.ShapeDtypeStruct((2, *results[0].shape), LOW)
    return pl.pallas_call(
        functools.partial(join_kernel, count),
        out_shape=[jax.ShapeDtypeStruct(value, FULL) for value in shapes] + [row_shape] * 2,
        in_specs=[IN_HBM] * (4 * count + 8),
        out_specs=[IN_HBM] * (count + 3),
        scratch_shapes=kept
        + kept
        + [pltpu.VMEM(value.shape, FULL) for value in own_a]
        + [
            pltpu.VMEM((2, *row_shape.shape), LOW),
            pltpu.SemaphoreType.DMA((2 * count,)),
            pltpu.SemaphoreType.DMA((count + 1,)),
            pltpu.SemaphoreType.DMA((4,)),
        ],
        compiler_params=pltpu.CompilerParams(vmem_limit_bytes=58 * 2**20),
        cost_estimate=pl.CostEstimate(flops=2**32, bytes_accessed=2**24, transcendentals=0),
        name="join_all",
    )(*own_a, *own_b, *came_a, *came_b, *results, *input_grads)


def relay_body(
    inputs,
    cotangent,
    positions,
    gain_attn,
    w_query,
    w_key,
    w_value,
    w_out,
    gain_ffn,
    w_gate,
    w_up,
    w_down,
):
    n_micro, per_device, model_width = inputs.shape
    n_seq = lax.axis_size("seq")
    n_shard = lax.axis_size("shard")
    members = n_seq * n_shard
    total_len = members * per_device
    section_idx = lax.axis_index("section")
    q_width = HEADS // members * HEAD_DIM
    in_width = q_width + 2 * HEAD_DIM
    hidden = w_down.shape[1]
    vmem = pltpu.VMEM

    def pick(first, second):
        return jnp.where(section_idx == 0, first, second)

    places = pick(positions[0], positions[1])
    gains_own = jnp.concatenate(
        [gain_attn, gain_ffn, jnp.zeros((6, gain_attn.shape[1]), gain_attn.dtype)], 0
    ).astype(FULL)
    own = dict(
        w_query=w_query[0], w_out=w_out[0], w_gate=w_gate[0], w_up=w_up[0], w_down=w_down[0]
    )

    order = (places.reshape(CHIPS, PLACE)[:, 0] // PLACE).astype(jnp.int32)
    numbers = jnp.arange(CHIPS, dtype=jnp.int32)
    block_at = jnp.sum(
        jnp.where(order[None, :] == numbers[:, None], numbers[None, :], 0), 1
    ).astype(jnp.int32)
    scalars = dict(block_at=block_at, order=order)
    half_dim = HEAD_DIM // 2
    inv_freq = THETA_BASE ** (-jnp.arange(half_dim, dtype=FULL) * (2.0 / HEAD_DIM))
    steps = jnp.concatenate([jnp.arange(PLACE), PLACE * jnp.arange(CHIPS)]).astype(FULL)
    angles = steps[:, None] * jnp.tile(inv_freq, 2 * q_width // HEAD_DIM)[None, :]
    turns = jnp.stack([jnp.cos(angles), jnp.sin(angles)])

    rows = (per_device, model_width)
    row_low, row_full = (rows, LOW), (rows, FULL)
    all_rows = ((CHIPS, 2, *rows), LOW)
    narrow = ((CHIPS, 2, per_device, hidden), LOW)
    wide = ((hidden, model_width), LOW)
    quarter = ((q_width, model_width), LOW)
    gain_row = ((8, model_width), FULL)
    kv_shape = (2, w_key.shape[1], model_width)
    small = gains_own.shape
    saved = dict(
        turned=((total_len, in_width), LOW),
        attended=((CHIPS, PLACE, q_width), FULL),
        spread=((CHIPS, 2 * PLACE), FULL),
        mixed=((CHIPS, 2, per_device, q_width), LOW),
    )
    saved_v = dict(
        turned_v=vmem(*saved["turned"]),
        attended_v=vmem(*saved["attended"]),
        spread_v=vmem(*saved["spread"]),
        mixed_v=vmem(*saved["mixed"]),
        turns_v=vmem(turns.shape, FULL),
    )
    attend_v_only = dict(
        qkv=vmem((CHIPS, PLACE, in_width), FULL),
        values_t=vmem((HEAD_DIM, total_len), LOW),
    )
    attend_v = dict(**saved_v, **attend_v_only)
    gates_v = dict(w_g=vmem(*wide), w_u=vmem(*wide))

    first = launch(
        "forward_first",
        0,
        forward_first,
        scalars,
        dict(
            inputs=inputs, cotangent=cotangent, gains_own=gains_own, w_key=w_key[0],
            w_value=w_value[0], turns=turns, **own,
        ),
        dict(
            x_query=quarter,
            x_out=quarter,
            x_gate=wide,
            x_up=wide,
            x_down=wide,
            gains=gain_row,
            kv_rows=((2, 2 * HEAD_DIM, model_width), LOW),
            top_all=all_rows,
            rows_one=all_rows,
            rows_two=all_rows,
            hidden=row_full,
            act_all=narrow,
            gate_slope=narrow,
            up_slope=narrow,
            **saved,
        ),
        dict(
            gains_mine=vmem(small, FULL),
            gains_x=vmem(small, FULL),
            gains_all=vmem((n_shard, n_seq, *small), FULL),
            gains_v=vmem(*gain_row),
            kv_mine=vmem(kv_shape, LOW),
            kv_x=vmem(kv_shape, LOW),
            kv_all=vmem((n_seq, 2, *kv_shape), LOW),
            w_kv=vmem((2, 2 * HEAD_DIM, model_width), LOW),
            small_send=pltpu.SemaphoreType.DMA((SMALL_SEMS,)),
            small_recv=pltpu.SemaphoreType.DMA((SMALL_SEMS,)),
            held=vmem(*all_rows),
            held_two=vmem(*all_rows),
            normed=vmem(*all_rows),
            w_q=vmem(*quarter),
            w_o=vmem(*quarter),
            hidden_v=vmem(*row_full),
            top_v=vmem(*row_low),
            act=vmem(*narrow),
            gate_slope_v=vmem(*narrow),
            up_slope_v=vmem(*narrow),
            **gates_v,
            **attend_v,
            **fold_buffers(rows),
            **spread_sems(
                "spread_send", "spread_recv", "spread_two_send", "spread_two_recv", "top_send",
                "top_recv",
            ),
        ),
    )
    crossed = dict(
        **own,
        x_query=first.x_query,
        x_out=first.x_out,
        x_gate=first.x_gate,
        x_up=first.x_up,
        x_down=first.x_down,
        gains=first.gains,
        kv_rows=first.kv_rows,
        turns=turns,
    )
    kv_pair = ((2, *kv_shape[1:]), LOW)
    sums_out = dict(down=wide, gate=wide, up=wide, out=quarter, query=quarter, kv=kv_pair)
    layers = dict(a=0, b=1)
    second = launch(
        "second_layer_and_back",
        1,
        second_layer,
        scalars,
        dict(
            act_prev=first.act_all,
            hidden_prev=first.hidden,
            inputs=inputs,
            cotangent=cotangent,
            top_all=first.top_all,
            rows_one=first.rows_one,
            rows_two=first.rows_two,
            gate_slope=first.gate_slope,
            up_slope=first.up_slope,
            **{key: getattr(first, key) for key in saved},
            **crossed,
        ),
        dict(
            gain_sums=((2, small[1]), FULL),
            **{
                f"{of}_{key}_{layer}": value
                for layer in layers
                for of in ("own", "came")
                for key, value in sums_out.items()
            },
            **{
                f"{of}_{layer}": row_low
                for layer in layers
                for of in ("result", "d_input", "came_result", "came_input")
            },
        ),
        dict(
            act_prev_v=vmem(*narrow),
            act=vmem(*narrow),
            d_gate_v=vmem(*narrow),
            d_up_v=vmem(*narrow),
            gate_slope_v=vmem(*narrow),
            up_slope_v=vmem(*narrow),
            hidden_prev_v=vmem(*row_full),
            hidden_v=vmem(*row_full),
            d_hidden=vmem(*row_full),
            result_v=vmem(*row_low),
            result_two=vmem(*row_low),
            top_v=vmem(*row_low),
            x_v=vmem(*row_low),
            d_input_v=vmem(*row_low),
            d_input_two=vmem(*row_low),
            gains_v=vmem(*gain_row),
            gain_grads=vmem((2, model_width), FULL),
            gain_later_v=vmem((2, model_width), FULL),
            w_d_prev=vmem(*wide),
            w_d=vmem(*wide),
            w_o=vmem(*quarter),
            w_in=vmem((in_width, model_width), LOW),
            top_held=vmem(*all_rows),
            normed=vmem(*all_rows),
            held=vmem(*all_rows),
            held_two=vmem(*all_rows),
            d_mixed=vmem((CHIPS, PLACE, q_width), LOW),
            d_qkv=vmem((CHIPS, 2, per_device, in_width), LOW),
            d_turned=vmem((CHIPS, PLACE, in_width), LOW),
            d_query=vmem((total_len, q_width), FULL),
            d_key=vmem((total_len, HEAD_DIM), FULL),
            d_value=vmem((total_len, HEAD_DIM), FULL),
            keys_t=vmem((HEAD_DIM, total_len), LOW),
            g_down_v=vmem(*wide),
            g_gate_v=vmem(*wide),
            g_up_v=vmem(*wide),
            g_out_v=vmem(*quarter),
            g_query_v=vmem(*quarter),
            g_kv_v=vmem(*kv_pair),
            kv_mine=vmem((2, n_seq, *kv_shape[1:]), LOW),
            kv_came=vmem((n_seq - 1, 2, *kv_shape[1:]), LOW),
            kv_send=pltpu.SemaphoreType.DMA((n_seq - 1,)),
            kv_recv=pltpu.SemaphoreType.DMA((n_seq - 1,)),
            last_send=pltpu.SemaphoreType.DMA((FOLD_SEMS,)),
            last_recv=pltpu.SemaphoreType.DMA((FOLD_SEMS,)),
            gain_parts=vmem((n_seq, n_shard, *small), FULL),
            gain_came=vmem((n_seq - 1, n_shard, *small), FULL),
            gain_shards=vmem((n_shard, *small), FULL),
            gain_last=vmem((n_shard - 1, *small), FULL),
            gain_own=vmem(small, FULL),
            gain_other=vmem(small, FULL),
            gain_sums_v=vmem((2, small[1]), FULL),
            gain_send=pltpu.SemaphoreType.DMA((7,)),
            gain_recv=pltpu.SemaphoreType.DMA((7,)),
            **gates_v,
            **attend_v,
            **fold_buffers(rows),
            **spread_sems(
                "spread_send", "spread_recv", "spread_two_send", "spread_two_recv", "back_send",
                "back_recv", "back_two_send", "back_two_recv", "last_back_send",
                "last_back_recv",
            ),
        ),
    )

    def sums(of, layer):
        return [getattr(second, f"{of}_{key}_{layer}") for key in sums_out]

    g_down, g_gate, g_up, g_out, g_query, g_key, g_value, outputs, input_grads = join_all(
        *(sums(of, layer) for of in ("own", "came") for layer in layers),
        (second.result_a, second.result_b, second.came_result_a, second.came_result_b),
        (second.d_input_a, second.d_input_b, second.came_input_a, second.came_input_b),
    )
    return (
        outputs[None],
        input_grads[None],
        second.gain_sums[:1],
        g_query[None],
        g_key,
        g_value,
        g_out[None],
        second.gain_sums[1:],
        g_gate[None],
        g_up[None],
        g_down[None],
    )


def fits_relay(mesh):
    shape = mesh.shape
    return shape["section"] == 2 and shape["shard"] == KV_HEADS == RING and shape["seq"] == 4


def solution(mesh):
    in_specs = (
        P(None, ("shard", "seq"), None),
        P(None, ("shard", "seq"), None),
        P(),
        P("section", ("shard", "seq")),
        P("section", ("shard", "seq"), None),
        P("section", ("shard", "seq"), None),
        P("section", ("shard", "seq"), None),
        P("section", ("shard", "seq"), None),
        P("section", ("shard", "seq")),
        P("section", ("shard", "seq"), None),
        P("section", ("shard", "seq"), None),
        P("section", ("shard", "seq"), None),
    )
    out_specs = (
        P("section", None, ("shard", "seq"), None),
        P("section", None, ("shard", "seq"), None),
        P("section", ("shard", "seq")),
        P("section", ("shard", "seq"), None),
        P("section", ("shard", "seq"), None),
        P("section", ("shard", "seq"), None),
        P("section", ("shard", "seq"), None),
        P("section", ("shard", "seq")),
        P("section", ("shard", "seq"), None),
        P("section", ("shard", "seq"), None),
        P("section", ("shard", "seq"), None),
    )
    chosen = relay_body if fits_relay(mesh) else body
    return jax.shard_map(chosen, mesh=mesh, in_specs=in_specs, out_specs=out_specs, check_vma=False)
```

```python
import functools
import math
import types

import jax
import jax.numpy as jnp
from jax import lax
from jax.experimental import pallas as pl
from jax.experimental.pallas import tpu as pltpu
from jax.sharding import PartitionSpec as P

HEADS = 32
KV_HEADS = 4
HEAD_DIM = 64


EPSILON = 1e-05
THETA_BASE = 10000.0
NEG_LARGE = -1e30


def shifted(value, axis, by):
    count = lax.axis_size(axis)
    pairs = [(i, i + by) for i in range(count) if 0 <= i + by < count]
    return lax.ppermute(value, axis, pairs)


def times_trans(left, right):
    return lax.dot_general(
        left, right, (((1,), (1,)), ((), ())), preferred_element_type=jnp.float32
    )


def outer_sum(left, right):
    return lax.dot_general(
        left, right, (((0,), (0,)), ((), ())), preferred_element_type=jnp.float32
    )


def plain_dot(left, right):
    return jnp.dot(left, right, preferred_element_type=jnp.float32)


def rotate(values, places, direction):
    half_dim = values.shape[-1] // 2
    inv_freq = THETA_BASE ** (-jnp.arange(half_dim, dtype=jnp.float32) * (2.0 / values.shape[-1]))
    angles = places.astype(jnp.float32)[:, None] * inv_freq[None, :]
    cosine = jnp.cos(angles)[:, None, :]
    sine_val = direction * jnp.sin(angles)[:, None, :]
    first = values[..., :half_dim]
    second = values[..., half_dim:]
    return jnp.concatenate(
        [first * cosine - second * sine_val, second * cosine + first * sine_val], -1
    )


def scaled(values, gain_vec):
    factor = lax.rsqrt(jnp.mean(values * values, -1, keepdims=True) + EPSILON)
    return values * factor * gain_vec


def norm_back(values, gain_vec, grad_in):
    factor = lax.rsqrt(jnp.mean(values * values, -1, keepdims=True) + EPSILON)
    gain_grad = jnp.sum(grad_in * values * factor, 0)
    mean_term = jnp.mean(grad_in * gain_vec * values, -1, keepdims=True)
    return (
        gain_grad,
        factor * gain_vec * grad_in - values * (factor * factor * factor) * mean_term,
    )


def ffn_back(grad_rows, kept_rows, gate_pre, up_pre, wg_part, wu_part, wd_part):
    sigmoid_val = jax.nn.sigmoid(gate_pre)
    silu_val = gate_pre * sigmoid_val
    hidden_act = (silu_val * up_pre).astype(jnp.bfloat16)
    grad_down = outer_sum(hidden_act, grad_rows)
    d_act = times_trans(grad_rows, wd_part)
    d_gate = (d_act * up_pre * sigmoid_val * (1.0 + gate_pre * (1.0 - sigmoid_val))).astype(
        jnp.bfloat16
    )
    d_up = (d_act * silu_val).astype(jnp.bfloat16)
    grad_gate = outer_sum(d_gate, kept_rows)
    grad_up = outer_sum(d_up, kept_rows)
    d_normed = plain_dot(d_gate, wg_part) + plain_dot(d_up, wu_part)
    return ((grad_gate, grad_up, grad_down), d_normed)


def body(
    inputs,
    cotangent,
    positions,
    gain_attn,
    w_query,
    w_key,
    w_value,
    w_out,
    gain_ffn,
    w_gate,
    w_up,
    w_down,
):
    n_micro, per_device, model_width = inputs.shape
    n_seq = lax.axis_size("seq")
    n_shard = lax.axis_size("shard")
    section_idx = lax.axis_index("section")
    shard_pos = lax.axis_index("shard")
    member = shard_pos * n_seq + lax.axis_index("seq")
    span_rows = per_device * n_seq
    total_len = span_rows * n_shard
    local_heads = HEADS // n_seq
    kv_repeat = n_seq // KV_HEADS
    q_width = local_heads * HEAD_DIM
    attn_scale = 1.0 / math.sqrt(HEAD_DIM)
    gain_one, gain_two, wq_full, wk_full, wv_full, wo_full = (
        lax.all_gather(gain_attn[0], ("shard", "seq"), axis=0, tiled=True),
        lax.all_gather(gain_ffn[0], ("shard", "seq"), axis=0, tiled=True),
        lax.all_gather(w_query[0], ("shard", "seq"), axis=0, tiled=True),
        lax.all_gather(w_key[0], ("shard", "seq"), axis=0, tiled=True),
        lax.all_gather(w_value[0], ("shard", "seq"), axis=0, tiled=True),
        lax.all_gather(w_out[0], ("shard", "seq"), axis=0, tiled=True),
    )
    gain_a = gain_one.astype(jnp.float32)
    gain_f = gain_two.astype(jnp.float32)
    wg_use, wu_use, wd_use = (w_gate[0], w_up[0], w_down[0])

    def spread_rows(block_in):
        return lax.all_gather(block_in, ("shard", "seq"), axis=0, tiled=True)

    def fold_rows(block_in):
        return lax.psum_scatter(block_in, ("shard", "seq"), scatter_dimension=0, tiled=True)

    def to_heads(block_in):
        return lax.all_to_all(block_in, "seq", split_axis=1, concat_axis=0, tiled=True)

    def to_tokens(block_in):
        return lax.all_to_all(block_in, "seq", split_axis=0, concat_axis=1, tiled=True)

    def over_keys(head_keys, head_values, step_fn, init_state):
        return step_fn(
            init_state,
            (
                lax.all_gather(head_keys, "shard", axis=0, tiled=True),
                lax.all_gather(head_values, "shard", axis=0, tiled=True),
            ),
            jnp.int32(0),
        )

    def place_sets(batch_index):
        place_row = lax.dynamic_index_in_dim(positions, batch_index, 0, keepdims=False)
        token_places = lax.dynamic_slice_in_dim(place_row, member * per_device, per_device)
        span_places = lax.dynamic_slice_in_dim(place_row, shard_pos * span_rows, span_rows)
        return (place_row, token_places, span_places)

    zero_rows = jnp.zeros((per_device, model_width), jnp.bfloat16)
    arrived_x = zero_rows
    results = []
    stored = []
    for tick_index in range(n_micro + 1):
        own_rows = inputs[tick_index] if tick_index < n_micro else zero_rows
        input_now = jnp.where(section_idx == 0, own_rows, arrived_x)
        batch_index = jnp.clip(tick_index - section_idx, 0, n_micro - 1)
        forward_place_row, forward_token_places, forward_span_places = place_sets(batch_index)
        forward_values_in = input_now.astype(jnp.float32)
        forward_normed_one = scaled(forward_values_in, gain_a).astype(jnp.bfloat16)
        queries = rotate(
            times_trans(forward_normed_one, wq_full).reshape(per_device, HEADS, HEAD_DIM),
            forward_token_places,
            1.0,
        ).astype(jnp.bfloat16)
        key_rows = rotate(
            times_trans(forward_normed_one, wk_full).reshape(per_device, KV_HEADS, HEAD_DIM),
            forward_token_places,
            1.0,
        ).astype(jnp.bfloat16)
        value_rows = (
            times_trans(forward_normed_one, wv_full)
            .reshape(per_device, KV_HEADS, HEAD_DIM)
            .astype(jnp.bfloat16)
        )
        key_rows = jnp.repeat(key_rows, kv_repeat, axis=1)
        value_rows = jnp.repeat(value_rows, kv_repeat, axis=1)
        packed = jnp.concatenate(
            [queries.reshape(per_device, n_seq, q_width), key_rows, value_rows], -1
        )
        arrived = to_heads(packed)[:, 0]
        forward_head_query = arrived[:, :q_width].reshape(span_rows, local_heads, HEAD_DIM)
        forward_head_keys = arrived[:, q_width : q_width + HEAD_DIM]
        forward_head_values = arrived[:, q_width + HEAD_DIM :]

        def absorb(state_in, key_piece, start_row):
            run_max, run_total, run_acc = state_in
            piece_keys, piece_values = key_piece
            visible = forward_place_row[None, None, :] <= forward_span_places[None, :, None]
            scores = (
                jnp.einsum(
                    "qhd,kd->hqk",
                    forward_head_query,
                    piece_keys,
                    preferred_element_type=jnp.float32,
                )
                * attn_scale
            )
            scores = jnp.where(visible, scores, NEG_LARGE)
            new_max = jnp.maximum(run_max, jnp.max(scores, -1))
            weight = jnp.where(visible, jnp.exp(scores - new_max[..., None]), 0.0)
            rescale = jnp.exp(run_max - new_max)
            run_total = jnp.sum(weight, -1)
            run_acc = run_acc * rescale.T[..., None] + jnp.einsum(
                "hqk,kd->qhd",
                weight.astype(jnp.bfloat16),
                piece_values,
                preferred_element_type=jnp.float32,
            )
            return (new_max, run_total, run_acc)

        forward_start_state = (
            jnp.full((local_heads, span_rows), NEG_LARGE, jnp.float32),
            jnp.zeros((local_heads, span_rows), jnp.float32),
            jnp.zeros((span_rows, local_heads, HEAD_DIM), jnp.float32),
        )
        run_max, run_total, run_acc = over_keys(
            forward_head_keys, forward_head_values, absorb, forward_start_state
        )
        forward_attended = run_acc / run_total.T[..., None]
        forward_spread = run_max + jnp.log(run_total)
        forward_mixed_tok = to_tokens(
            forward_attended.astype(jnp.bfloat16).reshape(span_rows, 1, q_width)
        ).reshape(per_device, HEADS * HEAD_DIM)
        forward_hidden_in = forward_values_in + plain_dot(forward_mixed_tok, wo_full)
        normed_two = scaled(forward_hidden_in, gain_f).astype(jnp.bfloat16)
        forward_kept_rows = spread_rows(normed_two)
        forward_gate_pre = times_trans(forward_kept_rows, wg_use)
        forward_up_pre = times_trans(forward_kept_rows, wu_use)
        hidden_act = (jax.nn.silu(forward_gate_pre) * forward_up_pre).astype(jnp.bfloat16)
        branch = fold_rows(plain_dot(hidden_act, wd_use))
        result = (forward_hidden_in + branch).astype(jnp.bfloat16)
        forward_saved = (
            input_now,
            forward_head_query,
            forward_head_keys,
            forward_head_values,
            forward_attended,
            forward_spread,
            forward_mixed_tok,
            forward_hidden_in,
            forward_kept_rows,
            forward_gate_pre,
            forward_up_pre,
        )
        result, saved = (result, forward_saved)
        results.append(result)
        stored.append(saved)
        if tick_index < n_micro:
            arrived_x = shifted(result, "section", 1)
    returned = zero_rows
    grads_back = []
    row_lists = []
    gain_total = None
    ffn_total = None
    for tick_index in range(n_micro + 1):
        own_rows = cotangent[tick_index] if tick_index < n_micro else zero_rows
        grad_now = jnp.where(section_idx == 1, own_rows, returned)
        batch_index = jnp.clip(tick_index - 1 + section_idx, 0, n_micro - 1)
        early_saved = stored[max(tick_index - 1, 0)]
        late_saved = stored[min(tick_index + 1, n_micro)]
        saved = jax.tree.map(
            lambda early_val, late_val: jnp.where(section_idx == 0, early_val, late_val),
            early_saved,
            late_saved,
        )
        (
            input_bf,
            head_query,
            backward_head_keys,
            backward_head_values,
            attended,
            spread,
            mixed_tok,
            hidden_in,
            kept_rows,
            gate_pre,
            up_pre,
        ) = saved
        backward_place_row, backward_token_places, backward_span_places = place_sets(batch_index)
        values_in = input_bf.astype(jnp.float32)
        normed_one = scaled(values_in, gain_a).astype(jnp.bfloat16)
        grad_all = spread_rows(grad_now)
        ffn_terms, d_partial = ffn_back(
            grad_all, kept_rows, gate_pre, up_pre, wg_use, wu_use, wd_use
        )
        d_normed_two = fold_rows(d_partial)
        grad_gf, d_hidden = norm_back(hidden_in, gain_f, d_normed_two)
        d_hidden = d_hidden + grad_now.astype(jnp.float32)
        d_branch = d_hidden.astype(jnp.bfloat16)
        d_mixed = times_trans(d_branch, wo_full).astype(jnp.bfloat16)
        d_att = to_heads(d_mixed.reshape(per_device, n_seq, q_width))[:, 0].reshape(
            span_rows, local_heads, HEAD_DIM
        )
        offset = jnp.sum(d_att.astype(jnp.float32) * attended, -1).T

        def collect(state_in, key_piece, start_row):
            piece_keys, piece_values = key_piece
            visible = backward_place_row[None, None, :] <= backward_span_places[None, :, None]
            scores = (
                jnp.einsum(
                    "qhd,kd->hqk", head_query, piece_keys, preferred_element_type=jnp.float32
                )
                * attn_scale
            )
            probs = jnp.where(visible, jnp.exp(scores - spread[..., None]), 0.0)
            d_probs = jnp.einsum(
                "qhd,kd->hqk", d_att, piece_values, preferred_element_type=jnp.float32
            )
            d_score = (probs * (d_probs - offset[..., None]) * attn_scale).astype(jnp.bfloat16)
            d_query_acc = jnp.einsum(
                "hqk,kd->qhd", d_score, piece_keys, preferred_element_type=jnp.float32
            )
            key_part = jnp.einsum(
                "hqk,qhd->kd", d_score, head_query, preferred_element_type=jnp.float32
            )
            value_part = jnp.einsum(
                "hqk,qhd->kd", probs.astype(jnp.bfloat16), d_att, preferred_element_type=jnp.float32
            )
            return (d_query_acc, key_part, value_part)

        start_state = (
            jnp.zeros((span_rows, local_heads, HEAD_DIM), jnp.float32),
            jnp.zeros((total_len, HEAD_DIM), jnp.float32),
            jnp.zeros((total_len, HEAD_DIM), jnp.float32),
        )
        d_query_acc, d_keys_all, d_values_all = over_keys(
            backward_head_keys, backward_head_values, collect, start_state
        )
        own_keys = lax.psum_scatter(
            d_keys_all.astype(jnp.bfloat16), "shard", scatter_dimension=0, tiled=True
        ).astype(jnp.float32)
        own_values = lax.psum_scatter(
            d_values_all.astype(jnp.bfloat16), "shard", scatter_dimension=0, tiled=True
        ).astype(jnp.float32)
        d_query_head = rotate(d_query_acc, backward_span_places, -1.0).astype(jnp.bfloat16)
        d_query = to_tokens(d_query_head.reshape(span_rows, 1, q_width)).reshape(
            per_device, HEADS * HEAD_DIM
        )
        own_keys = rotate(own_keys[:, None, :], backward_span_places, -1.0)[:, 0]
        back_kv = lax.all_to_all(
            jnp.concatenate([own_keys, own_values], -1)[:, None, :].astype(jnp.bfloat16),
            "seq",
            split_axis=0,
            concat_axis=1,
            tiled=True,
        ).astype(jnp.float32)
        back_kv = jnp.sum(back_kv.reshape(per_device, KV_HEADS, kv_repeat, 2 * HEAD_DIM), 2)
        d_key = (
            back_kv[..., :HEAD_DIM].reshape(per_device, KV_HEADS * HEAD_DIM).astype(jnp.bfloat16)
        )
        d_value = (
            back_kv[..., HEAD_DIM:].reshape(per_device, KV_HEADS * HEAD_DIM).astype(jnp.bfloat16)
        )
        d_normed_one = (
            plain_dot(d_query, wq_full) + plain_dot(d_key, wk_full) + plain_dot(d_value, wv_full)
        )
        grad_ga, d_input = norm_back(values_in, gain_a, d_normed_one)
        d_input = d_input + d_hidden
        gain_terms = (grad_ga, grad_gf)
        row_terms = (d_query, d_key, d_value, normed_one, mixed_tok, d_branch)
        d_input, gain_terms, row_terms, ffn_terms = (
            d_input.astype(jnp.bfloat16),
            gain_terms,
            row_terms,
            ffn_terms,
        )
        grads_back.append(d_input)
        row_lists.append(row_terms)
        if tick_index < n_micro:
            returned = shifted(d_input, "section", -1)
        if gain_total is None:
            gain_total = gain_terms
            ffn_total = ffn_terms
        else:
            gain_total = jax.tree.map(jnp.add, gain_total, gain_terms)
            ffn_total = jax.tree.map(jnp.add, ffn_total, ffn_terms)
    joined = [
        jnp.concatenate([row_set[index_val] for row_set in row_lists], 0) for index_val in range(6)
    ]
    grad_wq = outer_sum(joined[0], joined[3])
    grad_wk = outer_sum(joined[1], joined[3])
    grad_wv = outer_sum(joined[2], joined[3])
    grad_wo = outer_sum(joined[4], joined[5])
    attn_owned = (
        lax.psum_scatter(gain_total[0], ("shard", "seq"), scatter_dimension=0, tiled=True),
        lax.psum_scatter(gain_total[1], ("shard", "seq"), scatter_dimension=0, tiled=True),
        lax.psum_scatter(grad_wq, ("shard", "seq"), scatter_dimension=0, tiled=True),
        lax.psum_scatter(grad_wk, ("shard", "seq"), scatter_dimension=0, tiled=True),
        lax.psum_scatter(grad_wv, ("shard", "seq"), scatter_dimension=0, tiled=True),
        lax.psum_scatter(grad_wo, ("shard", "seq"), scatter_dimension=0, tiled=True),
    )
    outputs = lax.dynamic_slice_in_dim(jnp.stack(results), section_idx, n_micro, 0)[None]
    input_grads = lax.dynamic_slice_in_dim(jnp.stack(grads_back), 1 - section_idx, n_micro, 0)[None]
    return (
        outputs,
        input_grads,
        attn_owned[0][None],
        attn_owned[2][None],
        attn_owned[3][None],
        attn_owned[4][None],
        attn_owned[5][None],
        attn_owned[1][None],
        ffn_total[0][None],
        ffn_total[1][None],
        ffn_total[2][None],
    )


LOW = jnp.bfloat16
FULL = jnp.float32
MESH = pl.DeviceIdType.MESH
RING = 4
CHIPS = 2 * RING
SPLIT = 2
LAG = (0, 0, 1, 2, 3)
PLACE = 128
ORDER = ((2, 1), (1, 1), (3, 1), (0, 1), (2, 0), (1, 0), (3, 0), (0, 0))
IN_VMEM = pl.BlockSpec(memory_space=pltpu.VMEM)
IN_HBM = pl.BlockSpec(memory_space=pltpu.HBM)
IN_SMEM = pl.BlockSpec(memory_space=pltpu.SMEM)


class Site:
    def __init__(self):
        self.section = lax.axis_index("section")
        self.z = lax.axis_index("shard")
        member = lax.axis_index("seq")
        self.y = lax.div(member, 2)
        self.core = lax.rem(member, 2)
        self.up = (self.section, lax.rem(self.z + 1, RING), member)
        self.down = (self.section, lax.rem(self.z + RING - 1, RING), member)
        self.across = (self.section, self.z, (1 - self.y) * 2 + self.core)
        self.sibling = (self.section, self.z, self.y * 2 + 1 - self.core)
        self.corner = (self.section, self.z, (1 - self.y) * 2 + 1 - self.core)
        self.opposite = (self.section, lax.rem(self.z + 2, RING), member)
        self.partner = (1 - self.section, self.z, member)
        self.member = member

    def chip(self, along_z, along_y):
        return lax.rem(self.z + along_z, RING) * 2 + lax.rem(self.y + along_y, 2)


class Links:
    def __init__(self, send, recv, site):
        self.send, self.recv, self.site = send, recv, site
        self.sent = []

    def copy(self, index, src, dst, device):
        return pltpu.make_async_remote_copy(
            src_ref=src,
            dst_ref=dst,
            send_sem=self.send.at[index],
            recv_sem=self.recv.at[index],
            device_id=device,
            device_id_type=MESH,
        )

    def go(self, index, src, dst, device):
        copy = self.copy(index, src, dst, device)
        copy.start()
        self.sent.append(copy)

    def got(self, index, where):
        self.copy(index, where, where, self.site.sibling).wait_recv()
        return where

    def close(self):
        for copy in self.sent:
            copy.wait_send()


def greet(site):
    barrier = pltpu.get_barrier_semaphore()
    devices = (
        site.up, site.down, site.across, site.sibling, site.corner, site.opposite, site.partner
    )
    for device in devices:
        pl.semaphore_signal(barrier, inc=1, device_id=device, device_id_type=MESH)
    pl.semaphore_wait(barrier, len(devices))


SPREAD_SEMS = 7 * SPLIT + CHIPS
FOLD_SEMS = 7 * SPLIT + CHIPS
SMALL_SEMS = 11
COPY_SEMS = 64
CROSS_SEMS = 40
PIECE = 128


class Spread:
    def __init__(self, site, held, links, use):
        self.site, self.held, self.links, self.use = site, held, links, use
        self.size = held.shape[2] // SPLIT
        self.up, self.down, self.over, self.relay, self.y_below, self.y_above, self.y_far = (
            k * SPLIT for k in range(7)
        )
        self.along = ((0, 0), (3, 0), (1, 0), (0, 1), (2, 0), (3, 1), (1, 1), (2, 1))

    def piece(self, slot, part):
        site = self.site
        rows = pl.ds(part * self.size, self.size)
        return self.held.at[site.chip(*self.along[slot]), site.core, rows]

    def block(self, slot, core):
        return self.held.at[self.site.chip(*self.along[slot]), core]

    def go(self, index, where, device):
        self.links.go(index, where, where, device)

    def share(self, slot):
        self.go(7 * SPLIT + slot, self.block(slot, self.site.core), self.site.sibling)

    def consume(self, *slots):
        for slot in slots:
            self.links.got(7 * SPLIT + slot, self.block(slot, 1 - self.site.core))
            self.use(self.site.chip(*self.along[slot]))

    def ways(self, part):
        ways = (
            (self.up + part, 1, self.site.up, self.y_below + part),
            (self.down + part, 2, self.site.down, self.y_above + part),
        )
        return ways if part % 2 == 0 else ways[::-1]

    def own(self, part):
        where = self.piece(0, part)
        for index, _, device, _ in self.ways(part):
            self.go(index, where, device)
        self.go(self.over + part, where, self.site.across)

    def relays(self, part):
        for turn, (index, slot, device, over) in enumerate(self.ways(part)):
            came = self.links.got(index, self.piece(slot, part))
            if turn == 0:
                self.go(self.relay + part, came, device)
            self.go(over, came, self.site.across)

    def far(self, part):
        came = self.links.got(self.relay + part, self.piece(4, part))
        self.go(self.y_far + part, came, self.site.across)

    def after_relays(self):
        self.share(1)
        self.share(2)
        for part in range(SPLIT):
            self.links.got(self.over + part, self.piece(3, part))
        self.share(3)

    def tail(self, consume=True, first=0):
        def take(*slots):
            if consume:
                self.consume(*slots)

        self.share(4)
        take(*range(first, 3))
        for part in range(SPLIT):
            self.links.got(self.y_below + part, self.piece(5, part))
            self.links.got(self.y_above + part, self.piece(6, part))
        self.share(5)
        self.share(6)
        take(3, 4)
        for part in range(SPLIT):
            self.links.got(self.y_far + part, self.piece(7, part))
        self.share(7)
        take(5, 6, 7)
        if not consume:
            for slot in range(CHIPS):
                self.links.got(7 * SPLIT + slot, self.block(slot, 1 - self.site.core))

    def rest(self, consume=True):
        self.after_relays()
        for part in range(SPLIT):
            self.far(part)
        self.tail(consume)


class Fold:
    def __init__(self, site, part_of, buffers, links):
        self.site, self.part_of, self.links = site, part_of, links
        self.mine, self.pass_out, self.pass_in, self.stage, self.land = buffers
        self.rows = self.mine.shape[1]
        self.size = self.rows // SPLIT
        self.over = CHIPS
        self.relay, self.up, self.down = (CHIPS + (4 + k) * SPLIT for k in range(3))

    def where(self, part):
        return pl.ds(part * self.size, self.size)

    def came(self, index, where):
        return self.links.got(index, where)[...].astype(FULL)

    def compute(self, step):
        both = self.part_of(self.site.chip(*ORDER[step]))
        self.pass_out[step] = both[: self.rows].astype(LOW)
        self.links.go(step, self.pass_out.at[step], self.pass_in.at[step], self.site.sibling)
        self.mine[step] = both[self.rows :]

    def settle(self, step):
        self.mine[step] += self.came(step, self.pass_in.at[step])

    def send(self, index, slot, part, value, device):
        where = self.where(part)
        self.stage[slot, where] = value.astype(LOW)
        self.links.go(index, self.stage.at[slot, where], self.land.at[slot, where], device)

    def send_over(self, step, part):
        value = self.mine[step, self.where(part)]
        self.send(self.over + step * SPLIT + part, step, part, value, self.site.across)

    def start(self):
        self.compute(0)
        self.compute(1)
        for step in range(4):
            self.settle(step)
            self.send_over(step, 0)
            self.compute(step + 2)
        for part in range(1, SPLIT):
            for step in range(4):
                self.send_over(step, part)
        self.compute(6)
        self.compute(7)
        for step in range(4, CHIPS):
            self.settle(step)

    def pass_on(self, part):
        where = self.where(part)
        value = self.mine[4, where] + self.came(self.over + part, self.land.at[0, where])
        device = self.site.up if part % 2 == 0 else self.site.down
        self.send(self.relay + part, 4, part, value, device)

    def up_down(self, part):
        where = self.where(part)
        ways = ((5, self.up, self.site.up), (6, self.down, self.site.down))
        for step, base, device in ways if part % 2 else ways[::-1]:
            from_y = self.over + (step - 4) * SPLIT + part
            value = self.mine[step, where] + self.came(from_y, self.land.at[step - 4, where])
            if part % 2 == step - 5:
                value = value + self.came(self.relay + part, self.land.at[4, where])
            self.send(base + part, step, part, value, device)

    def final(self, part):
        where = self.where(part)
        value = self.mine[7, where] + self.came(
            self.over + 3 * SPLIT + part, self.land.at[3, where]
        )
        value = value + self.came(self.up + part, self.land.at[5, where])
        return value + self.came(self.down + part, self.land.at[6, where])


def fold_spread(fold, spread, local, idle):
    def finish(part):
        rows = local(fold.final(part), fold.where(part))
        if spread is not None:
            site = spread.site
            spread.held[site.chip(0, 0), site.core, fold.where(part)] = rows
            spread.own(part)

    fold.start()
    idle(3)
    last = SPLIT - 1
    for tick in range(SPLIT + LAG[-1]):
        steps = [tick - lag for lag in LAG]
        if 0 <= steps[0] < SPLIT:
            fold.pass_on(steps[0])
        if 0 <= steps[1] < SPLIT:
            fold.up_down(steps[1])
        if 0 <= steps[2] < SPLIT:
            finish(steps[2])
        if spread is not None:
            if steps[2] == last:
                spread.share(0)
            if 0 <= steps[3] < SPLIT:
                spread.relays(steps[3])
            if steps[3] == last:
                spread.after_relays()
            if 0 <= steps[4] < SPLIT:
                spread.far(steps[4])
            if steps[2] == last + 1:
                spread.consume(0)
        idle(3)
    if spread is not None:
        idle(10)
        spread.tail(first=1)
        spread.links.close()
    else:
        idle(10)
    fold.links.close()


class Cross:
    def __init__(self, n):
        self.site = n.site
        self.links = Links(n.cross_send, n.cross_recv, n.site)
        self.begun = []
        self.count = 0

    def where(self, layer, receives, action):
        if layer is None:
            action()
        else:
            pl.when((self.site.section == layer) == receives)(action)

    def send(self, src, dst, layer=None):
        rows = src.shape[0]
        pieces = []
        start = 0
        while start < rows:
            size = min(PIECE, rows - start)
            where = pl.ds(start, size)
            pieces.append(
                self.links.copy(self.count, src.at[where], dst.at[where], self.site.partner)
            )
            self.count += 1
            start += size

        def begin():
            for copy in pieces:
                copy.start()

        self.where(layer, False, begin)
        self.begun.append([pieces, layer, False])
        return len(self.begun) - 1

    def wait(self, index):
        pieces, layer, landed = self.begun[index]

        def arrive():
            for copy in pieces:
                copy.wait_recv()

        if not landed:
            self.begun[index][2] = True
            self.where(layer, True, arrive)

    def close(self):
        for index in range(len(self.begun)):
            self.wait(index)
        for pieces, layer, _ in self.begun:

            def leave():
                for copy in pieces:
                    copy.wait_send()

            self.where(layer, False, leave)
        self.begun = []


class Copies:
    def __init__(self, n):
        self.n, self.count, self.open = n, 0, []

    def sem(self):
        self.count += 1
        return self.n.copy_sem.at[self.count - 1]

    def start(self, src, dst):
        copy = pltpu.make_async_copy(src, dst, self.sem())
        copy.start()
        self.open.append(copy)
        return copy

    def pick(self, own, other, dst, layer):
        sem = self.sem()
        from_own = pltpu.make_async_copy(own, dst, sem)
        from_other = pltpu.make_async_copy(other, dst, sem)
        pl.when(self.n.site.section == layer)(from_own.start)
        pl.when(self.n.site.section != layer)(from_other.start)
        self.open.append(from_own)
        return from_own

    def wait(self, *copies):
        for copy in copies:
            if any(copy is other for other in self.open):
                self.open = [other for other in self.open if other is not copy]
                copy.wait()

    def close(self):
        self.wait(*list(self.open))


def kernel_of(body, names, *refs):
    n = types.SimpleNamespace(**dict(zip(names, refs)))
    n.site = Site()
    n.copies = Copies(n)
    n.cross = Cross(n)
    body(n)
    n.cross.close()
    n.copies.close()


def launch(name, ident, body, scalars, inputs, outputs, scratch):
    scratch = dict(
        scratch,
        copy_sem=pltpu.SemaphoreType.DMA((COPY_SEMS,)),
        cross_send=pltpu.SemaphoreType.DMA((CROSS_SEMS,)),
        cross_recv=pltpu.SemaphoreType.DMA((CROSS_SEMS,)),
    )
    names = [*scalars, *inputs, *outputs, *scratch]
    results = pl.pallas_call(
        functools.partial(kernel_of, body, names),
        out_shape=[jax.ShapeDtypeStruct(*value) for value in outputs.values()],
        in_specs=[IN_SMEM] * len(scalars) + [IN_HBM] * len(inputs),
        out_specs=[IN_HBM] * len(outputs),
        scratch_shapes=list(scratch.values()),
        compiler_params=pltpu.CompilerParams(
            collective_id=ident, has_side_effects=True, vmem_limit_bytes=60 * 2**20
        ),
        cost_estimate=pl.CostEstimate(flops=2**37, bytes_accessed=2**23, transcendentals=0),
        name=name,
    )(*scalars.values(), *inputs.values())
    return types.SimpleNamespace(**dict(zip(outputs, results)))


def fold_buffers(full):
    return dict(
        mine=pltpu.VMEM((CHIPS, *full), FULL),
        pass_out=pltpu.VMEM((CHIPS, *full), LOW),
        pass_in=pltpu.VMEM((CHIPS, *full), LOW),
        stage=pltpu.VMEM((CHIPS - 1, *full), LOW),
        land=pltpu.VMEM((CHIPS - 1, *full), LOW),
        fold_send=pltpu.SemaphoreType.DMA((FOLD_SEMS,)),
        fold_recv=pltpu.SemaphoreType.DMA((FOLD_SEMS,)),
    )


def fold_of(n, part_of):
    buffers = (n.mine, n.pass_out, n.pass_in, n.stage, n.land)
    return Fold(n.site, part_of, buffers, Links(n.fold_send, n.fold_recv, n.site))


def spread_of(n, held, send, recv, use, kept=None):
    def take(chip):
        block = held[chip]
        use(chip, block.reshape(block.shape[0] * block.shape[1], block.shape[2]))
        if kept is not None:
            n.copies.start(held.at[chip], kept.at[chip])

    return Spread(n.site, held, Links(send, recv, n.site), take)


def spread_sems(*names):
    return {name: pltpu.SemaphoreType.DMA((SPREAD_SEMS,)) for name in names}


def no_idle(count):
    pass


def rows_of(ref, chip, site):
    return jnp.concatenate([ref[chip, 1 - site.core], ref[chip, site.core]], 0)


def put(ref, chip, value):
    ref[chip] = value.astype(LOW).reshape(ref.shape[1:])


def gate_chunk(n, chip, rows):
    gate_pre = times_trans(rows, n.w_g[...])
    up_pre = times_trans(rows, n.w_u[...])
    sig = jax.nn.sigmoid(gate_pre)
    silu_val = gate_pre * sig
    put(n.act, chip, silu_val * up_pre)
    return up_pre * sig * (1.0 + gate_pre * (1.0 - sig)), silu_val


def norm_back_rows(values, gain_vec, grad_in):
    factor = lax.rsqrt(jnp.mean(values * values, -1, keepdims=True) + EPSILON)
    gain_grad = jnp.sum(grad_in * values * factor, 0, keepdims=True)
    mean_term = jnp.mean(grad_in * gain_vec * values, -1, keepdims=True)
    return (
        gain_grad,
        factor * gain_vec * grad_in - values * (factor * factor * factor) * mean_term,
    )


def swap_halves(value):
    width = value.shape[1]
    half = HEAD_DIM // 2
    lane = lax.broadcasted_iota(jnp.int32, value.shape, 1)
    return jnp.where(
        lax.rem(lane, HEAD_DIM) < half,
        pltpu.roll(value, width - half, 1),
        pltpu.roll(value, half, 1),
    )


def stacked(pair):
    return jnp.concatenate([pair[:, :HEAD_DIM], pair[:, HEAD_DIM:]], 0)


def side_by_side(turned):
    return jnp.concatenate([turned[:, :PLACE], turned[:, PLACE:]], 0).T


def hide_later(scores, fill):
    last = scores[-PLACE:]
    key = lax.broadcasted_iota(jnp.int32, last.shape, 0)
    query = lax.rem(lax.broadcasted_iota(jnp.int32, last.shape, 1), PLACE)
    last = jnp.where(key <= query, last, fill)
    if scores.shape[0] == PLACE:
        return last
    return jnp.concatenate([scores[:-PLACE], last], 0)


def turn_of(turns, place):
    near, far = pl.ds(0, PLACE), pl.ds(PLACE + place, 1)
    cos_near, sin_near = turns[0, near], turns[1, near]
    cos_far, sin_far = turns[0, far], turns[1, far]
    cosine = cos_near * cos_far - sin_near * sin_far
    sine = sin_near * cos_far + cos_near * sin_far
    lane = lax.broadcasted_iota(jnp.int32, cosine.shape, 1)
    sine = jnp.where(lax.rem(lane, HEAD_DIM) < HEAD_DIM // 2, -sine, sine)
    keyed = lane < HEAD_DIM
    return (
        jnp.concatenate([cosine, jnp.where(keyed, cosine, 1.0)], 1),
        jnp.concatenate([sine, jnp.where(keyed, sine, 0.0)], 1),
    )


def attend(n):
    q_width = 2 * HEAD_DIM
    scale = jnp.asarray(1.0 / math.sqrt(HEAD_DIM), LOW)
    for place in range(CHIPS):
        at = pl.ds(place * PLACE, PLACE)
        value = n.qkv[n.block_at[place]]
        cosine, sine = turn_of(n.turns_v, place)
        value = (value * cosine + swap_halves(value) * sine).astype(LOW)
        n.turned_v[at, :q_width] = value[:, :q_width] * scale
        n.turned_v[at, q_width:] = value[:, q_width:]
        n.values_t[:, at] = value[:, q_width:].astype(FULL).T[HEAD_DIM:].astype(LOW)
    for place in range(CHIPS):
        at = pl.ds(place * PLACE, PLACE)
        keys = pl.ds(0, (place + 1) * PLACE)
        query = stacked(n.turned_v[at, :q_width])
        scores = times_trans(n.turned_v[keys, q_width : q_width + HEAD_DIM], query)
        scores = hide_later(scores, NEG_LARGE)
        top = jnp.max(scores, 0, keepdims=True)
        weight = jnp.exp(scores - top)
        total = jnp.sum(weight, 0, keepdims=True)
        out = plain_dot(n.values_t[:, keys], weight.astype(LOW)) / total
        n.attended_v[place] = side_by_side(out)
        n.spread_v[pl.ds(place, 1)] = top + jnp.log(total)
    for block in range(CHIPS):
        put(n.mixed_v, block, n.attended_v[n.order[block]])


def keep_attention(n):
    n.copies.start(n.turned_v, n.turned)
    n.copies.start(n.attended_v, n.attended)
    n.copies.start(n.spread_v, n.spread)
    n.copies.start(n.mixed_v, n.mixed)


def attend_back(n):
    q_width = 2 * HEAD_DIM
    n.d_key[...] = jnp.zeros_like(n.d_key)
    n.d_value[...] = jnp.zeros_like(n.d_value)
    for place in range(CHIPS):
        at = pl.ds(place * PLACE, PLACE)
        n.keys_t[:, at] = n.turned_v[at, q_width:].astype(FULL).T[:HEAD_DIM].astype(LOW)
    for place in range(CHIPS):
        at = pl.ds(place * PLACE, PLACE)
        keys = pl.ds(0, (place + 1) * PLACE)
        d_out = n.d_mixed[n.block_at[place]]
        product = (d_out.astype(FULL) * n.attended_v[place]).T
        offset = jnp.concatenate(
            [
                jnp.sum(product[:HEAD_DIM], 0, keepdims=True),
                jnp.sum(product[HEAD_DIM:], 0, keepdims=True),
            ],
            1,
        )
        d_out = stacked(d_out)
        query = stacked(n.turned_v[at, :q_width])
        scores = times_trans(n.turned_v[keys, q_width : q_width + HEAD_DIM], query)
        scores = hide_later(scores, NEG_LARGE)
        probs = jnp.exp(scores - n.spread_v[pl.ds(place, 1)])
        d_probs = times_trans(n.turned_v[keys, q_width + HEAD_DIM :], d_out)
        d_scores = (probs * (d_probs - offset)).astype(LOW)
        n.d_key[keys] += plain_dot(d_scores, query)
        n.d_value[keys] += plain_dot(probs.astype(LOW), d_out)
        n.d_query[at] = side_by_side(plain_dot(n.keys_t[:, keys], d_scores)) * (
            1.0 / math.sqrt(HEAD_DIM)
        )
    for place in range(CHIPS):
        at = pl.ds(place * PLACE, PLACE)
        value = jnp.concatenate([n.d_query[at], n.d_key[at], n.d_value[at]], 1)
        cosine, sine = turn_of(n.turns_v, place)
        value = value * cosine - swap_halves(value) * sine
        n.d_turned[place] = value.astype(LOW)
    for block in range(CHIPS):
        put(n.d_qkv, block, n.d_turned[n.order[block]])


def gather_small_start(n):
    links = n.links_small = Links(n.small_send, n.small_recv, n.site)
    links.go(0, n.gains_mine, n.gains_x, n.site.partner)
    links.go(1, n.kv_mine, n.kv_x, n.site.partner)


def gather_small(n):
    site, links = n.site, n.links_small
    links.got(0, n.gains_x)
    own, came = n.gains_mine[...], n.gains_x[...]
    first = site.section == 0
    n.gains_all[site.z, site.member] = jnp.concatenate(
        [
            jnp.where(first, own, came)[:2],
            jnp.where(first, came, own)[:2],
            jnp.zeros((4, own.shape[1]), FULL),
        ],
        0,
    )
    peers = (site.sibling, site.across, site.corner)
    mine = n.gains_all.at[site.z, site.member]
    for index, device in enumerate(peers):
        links.go(2 + index, mine, mine, device)
    for index, device in enumerate(peers):
        links.got(2 + index, n.gains_all.at[site.z, device[2]])
    shard = n.gains_all.at[site.z]
    for index, device in enumerate((site.up, site.down, site.opposite)):
        links.go(5 + index, shard, shard, device)


def gather_small_keys(n):
    site, links = n.site, n.links_small
    links.got(1, n.kv_x)
    n.kv_all[site.member, site.section] = n.kv_mine[...]
    n.kv_all[site.member, 1 - site.section] = n.kv_x[...]
    mine = n.kv_all.at[site.member]
    for index, device in enumerate((site.sibling, site.across, site.corner)):
        links.go(8 + index, mine, mine, device)


def gather_small_end(n):
    site, links = n.site, n.links_small
    for index, along_z in enumerate((RING - 1, 1, 2)):
        links.got(5 + index, n.gains_all.at[lax.rem(site.z + along_z, RING)])
    for index, device in enumerate((site.sibling, site.across, site.corner)):
        links.got(8 + index, n.kv_all.at[device[2]])
    links.close()
    n.gains_v[...] = jnp.concatenate(
        [n.gains_all[shard, seq] for shard in range(RING) for seq in range(RING)], 1
    )
    for layer in range(2):
        for index in range(2):
            rows = n.kv_all[:, layer, index]
            n.w_kv[layer, pl.ds(index * HEAD_DIM, HEAD_DIM)] = rows.reshape(
                HEAD_DIM, rows.shape[-1]
            )
    n.copies.start(n.gains_v, n.gains)
    n.copies.start(n.w_kv, n.kv_rows)


def forward_first(n):
    site, copies, cross = n.site, n.copies, n.cross
    own = (site.chip(0, 0), site.core)
    small = [
        copies.start(n.gains_own, n.gains_mine),
        copies.start(n.w_key, n.kv_mine.at[0]),
        copies.start(n.w_value, n.kv_mine.at[1]),
    ]
    rows_copy = copies.pick(n.inputs.at[0], n.inputs.at[1], n.held.at[own], 0)
    top_copy = copies.pick(n.cotangent.at[0], n.cotangent.at[1], n.top_v, 0)
    turns_copy = copies.start(n.turns, n.turns_v)
    def use_first(chip, rows):
        normed = scaled(rows.astype(FULL), n.gains_v[:1]).astype(LOW)
        n.normed[chip] = normed.reshape(n.normed.shape[1:])
        n.qkv[chip] = jnp.concatenate(
            [times_trans(normed, n.w_q[...]), times_trans(normed, n.w_kv[0])], 1
        )
        copies.start(n.normed.at[chip], n.rows_one.at[chip])

    greet(site)
    copies.wait(*small)
    gather_small_start(n)
    at_query, at_out, at_gate, at_up, _ = (
        cross.send(*pair)
        for pair in (
            (n.w_query, n.x_query),
            (n.w_out, n.x_out),
            (n.w_gate, n.x_gate),
            (n.w_up, n.x_up),
            (n.w_down, n.x_down),
        )
    )
    copies.wait(rows_copy)
    spread = spread_of(n, n.held, n.spread_send, n.spread_recv, use_first)
    spread.own(0)
    gather_small(n)
    for part in range(1, SPLIT):
        spread.own(part)
    spread.share(0)
    gather_small_keys(n)
    for part in range(SPLIT):
        spread.relays(part)
    gather_small_end(n)
    spread.after_relays()
    cross.wait(at_query)
    query_copy = copies.pick(n.w_query, n.x_query, n.w_q, 0)
    for part in range(SPLIT):
        spread.far(part)
    copies.wait(query_copy)
    copies.wait(top_copy, turns_copy)
    top_copy = copies.start(n.top_v, n.top_all.at[own])
    spread.tail()
    spread.links.close()
    copies.wait(top_copy)
    top = spread_of(n, n.top_all, n.top_send, n.top_recv, None)
    for part in range(SPLIT):
        top.own(part)
    cross.wait(at_out)
    out_copy = copies.pick(n.w_out, n.x_out, n.w_o, 0)
    attend(n)
    keep_attention(n)
    top.share(0)
    copies.wait(out_copy)

    def part_of(chip):
        return plain_dot(rows_of(n.mixed_v, chip, site), n.w_o[...])

    def local(total, where):
        hidden_in = n.held[(*own, where)].astype(FULL) + total
        n.hidden_v[where] = hidden_in
        return scaled(hidden_in, n.gains_v[1:2]).astype(LOW)

    waiting = []

    def use_later(chip, rows):
        waiting.append(chip)

    def use_gate(chip):
        rows = n.held_two[chip].reshape(-1, n.held_two.shape[-1])
        gate_slope, up_slope = gate_chunk(n, chip, rows)
        put(n.gate_slope_v, chip, gate_slope)
        put(n.up_slope_v, chip, up_slope)

    def idle(count):
        if count == 10:
            for part in range(SPLIT):
                top.relays(part)

    spread = spread_of(
        n, n.held_two, n.spread_two_send, n.spread_two_recv, use_later, n.rows_two
    )
    fold_spread(fold_of(n, part_of), spread, local, idle)
    copies.start(n.hidden_v, n.hidden)
    top.after_relays()
    for part in range(SPLIT):
        top.far(part)
    cross.wait(at_gate)
    cross.wait(at_up)
    copies.wait(
        copies.pick(n.w_gate, n.x_gate, n.w_g, 0), copies.pick(n.w_up, n.x_up, n.w_u, 0)
    )
    for chip in waiting:
        use_gate(chip)
    for source, target in (
        (n.act, n.act_all), (n.gate_slope_v, n.gate_slope), (n.up_slope_v, n.up_slope)
    ):
        copies.start(source, target)
    top.tail(consume=False)
    top.links.close()


def second_layer(n):
    site, copies = n.site, n.copies
    first = [
        copies.start(n.act_prev, n.act_prev_v),
        copies.pick(n.w_down, n.x_down, n.w_d_prev, 0),
    ]
    rows_copies = [copies.start(n.hidden_prev, n.hidden_prev_v), copies.start(n.gains, n.gains_v)]
    qkv_copies = [
        copies.pick(n.w_query, n.x_query, n.w_in.at[pl.ds(0, 2 * HEAD_DIM)], 1),
        copies.start(n.kv_rows.at[1], n.w_in.at[pl.ds(2 * HEAD_DIM, 2 * HEAD_DIM)]),
        copies.start(n.turns, n.turns_v),
    ]
    later = [
        copies.pick(n.w_out, n.x_out, n.w_o, 1),
        copies.pick(n.w_gate, n.x_gate, n.w_g, 1),
        copies.pick(n.w_up, n.x_up, n.w_u, 1),
        copies.pick(n.w_down, n.x_down, n.w_d, 1),
        copies.start(n.top_all, n.top_held),
    ]
    back_copies = [copies.pick(n.cotangent.at[0], n.cotangent.at[1], n.top_v, 0)]
    next_copies = [
        copies.start(n.gate_slope, n.gate_slope_v),
        copies.start(n.up_slope, n.up_slope_v),
    ]
    greet(site)
    copies.wait(*first, *rows_copies)

    def part_of(chip):
        return plain_dot(rows_of(n.act_prev_v, chip, site), n.w_d_prev[...])

    def local(total, where):
        result = (n.hidden_prev_v[where] + total).astype(LOW)
        n.result_v[where] = result
        return scaled(result.astype(FULL), n.gains_v[2:3]).astype(LOW)

    def use_qkv(chip, rows):
        n.qkv[chip] = times_trans(rows, n.w_in[...])

    def settle(count):
        copies.wait(*qkv_copies)

    spread = spread_of(n, n.held, n.spread_send, n.spread_recv, use_qkv)
    fold_spread(fold_of(n, part_of), spread, local, settle)
    copies.start(n.result_v, n.result_a)
    n.cross.send(n.result_v, n.came_result_a, 0)
    attend(n)
    copies.wait(*later)

    def part_of_two(chip):
        return plain_dot(rows_of(n.mixed_v, chip, site), n.w_o[...])

    def local_two(total, where):
        hidden_in = n.result_v[where].astype(FULL) + total
        n.hidden_v[where] = hidden_in
        return scaled(hidden_in, n.gains_v[3:4]).astype(LOW)

    def use_gate(chip, rows):
        gate_slope, up_slope = gate_chunk(n, chip, rows)
        d_act = times_trans(n.top_held[chip].reshape(rows.shape), n.w_d[...])
        put(n.d_gate_v, chip, d_act * gate_slope)
        put(n.d_up_v, chip, d_act * up_slope)

    spread = spread_of(
        n, n.held_two, n.spread_two_send, n.spread_two_recv, use_gate
    )
    fold_spread(fold_of(n, part_of_two), spread, local_two, no_idle)
    copies.wait(*back_copies)
    cross = n.cross
    first_copies = []

    def preload():
        first_copies.append(copies.pick(n.w_gate, n.x_gate, n.w_g, 0))
        first_copies.append(copies.pick(n.w_up, n.x_up, n.w_u, 0))
        first_copies.append(copies.pick(n.w_out, n.x_out, n.w_o, 0))
        first_copies.append(copies.start(n.rows_two, n.top_held))

    backward(
        n,
        types.SimpleNamespace(
            layer=1, attn_copies=[], one_copies=[], next_copies=next_copies, act=n.act,
            top_all=n.top_held, normed_two=n.held_two, normed_one=n.held, branch=n.normed,
            hidden=n.hidden_v, top=n.top_v, x_rows=n.result_v, d_input=n.d_input_v,
            w_next=n.w_d_prev, after_first=preload, send=n.back_send, recv=n.back_recv,
            sums=[
                (n.g_down_v, n.own_down_b, n.came_down_b),
                (n.g_gate_v, n.own_gate_b, n.came_gate_b),
                (n.g_up_v, n.own_up_b, None),
                (n.g_out_v, n.own_out_b, n.came_out_b),
                (n.g_query_v, n.own_query_b, n.came_query_b),
                (n.g_kv_v, n.own_kv_b, n.came_kv_b),
            ],
        ),
    )
    copies.start(n.d_input_v, n.d_input_b)
    n.gain_later_v[...] = n.gain_grads[...]
    copies.wait(*first_copies)
    copies.close()
    cross.close()
    attn_copies = [
        copies.start(n.turned, n.turned_v),
        copies.start(n.attended, n.attended_v),
        copies.start(n.spread, n.spread_v),
        copies.start(n.mixed, n.mixed_v),
        copies.pick(n.w_query, n.x_query, n.w_in.at[pl.ds(0, 2 * HEAD_DIM)], 0),
        copies.start(n.kv_rows.at[0], n.w_in.at[pl.ds(2 * HEAD_DIM, 2 * HEAD_DIM)]),
        copies.pick(n.inputs.at[0], n.inputs.at[1], n.x_v, 0),
    ]
    one_copies = [copies.start(n.rows_one, n.held)]
    cross.send(n.own_up_b, n.came_up_b, 1)
    cross.send(n.d_input_v, n.came_input_b, 1)
    backward(
        n,
        types.SimpleNamespace(
            layer=0, attn_copies=attn_copies, one_copies=one_copies, next_copies=[],
            act=n.act_prev_v, top_all=n.held_two, normed_two=n.top_held, normed_one=n.held,
            branch=n.normed, hidden=n.hidden_prev_v, top=n.d_input_v, x_rows=n.x_v,
            d_input=n.d_input_two, w_next=n.w_d, after_first=lambda: None, send=n.last_back_send,
            recv=n.last_back_recv,
            sums=[
                (n.g_down_v, n.own_down_a, n.came_down_a),
                (n.g_gate_v, n.own_gate_a, n.came_gate_a),
                (n.g_up_v, n.own_up_a, n.came_up_a),
                (n.g_out_v, n.own_out_a, n.came_out_a),
                (n.g_query_v, n.own_query_a, n.came_query_a),
                (n.g_kv_v, n.own_kv_a, n.came_kv_a),
            ],
        ),
    )


def products(n, left, right, store, tile=512):
    count = math.prod(left.shape[:-1])
    for start in range(0, right.shape[-1], tile):
        where = pl.ds(start, tile)
        value = outer_sum(
            left[...].reshape(count, left.shape[-1]), right[:, :, :, where].reshape(count, tile)
        )
        store(where, value.astype(LOW))
        yield


def ffn_products(n, k, made):
    for left, right, out in (
        (k.act, k.top_all, n.g_down_v),
        (n.d_gate_v, k.normed_two, n.g_gate_v),
        (n.d_up_v, k.normed_two, n.g_up_v),
    ):

        def store(where, value):
            out[:, where] = value

        yield from products(n, left, right, store)
        made(out)


def in_products(n, loads, made, normed_one, branch):
    site = n.site
    n.copies.wait(*loads)

    def store_out(where, value):
        n.g_out_v[:, where] = value

    def store_in(where, value):
        query = n.g_query_v.shape[0]
        n.g_query_v[:, where] = value[:query]
        n.kv_mine[:, :, :, where] = value[query:].reshape(
            *n.kv_mine.shape[:3], value.shape[1]
        )

    yield from products(n, n.d_qkv, normed_one, store_in)
    made(n.g_query_v)
    peers = (site.sibling, site.across, site.corner)
    links = Links(n.kv_send, n.kv_recv, site)
    for index, device in enumerate(peers):
        links.go(index, n.kv_mine.at[:, device[2]], n.kv_came.at[index], device)
    yield from products(n, n.mixed_v, branch, store_out)
    made(n.g_out_v)
    total = n.kv_mine[:, site.member].astype(FULL)
    for index in range(len(peers)):
        total = total + links.got(index, n.kv_came.at[index])[...].astype(FULL)
    n.g_kv_v[...] = total.astype(LOW)
    made(n.g_kv_v)
    links.close()


def fold_gains(n):
    site = n.site
    links = Links(n.gain_send, n.gain_recv, site)
    own = jnp.concatenate(
        [n.gain_grads[...], n.gain_later_v[...], jnp.zeros((4, n.gain_grads.shape[1]), FULL)], 0
    )
    width = n.gain_parts.shape[-1]
    for shard in range(RING):
        for seq in range(RING):
            start = (shard * RING + seq) * width
            n.gain_parts[seq, shard] = own[:, start : start + width]
    peers = (site.sibling, site.across, site.corner)
    for index, device in enumerate(peers):
        links.go(index, n.gain_parts.at[device[2]], n.gain_came.at[index], device)
    yield
    total = n.gain_parts[site.member]
    for index in range(3):
        total = total + links.got(index, n.gain_came.at[index])[...]
    n.gain_shards[...] = total
    for index, device in enumerate((site.up, site.down, site.opposite)):
        links.go(
            3 + index, n.gain_shards.at[device[1]], n.gain_last.at[index], device
        )
    yield
    total = n.gain_shards[site.z]
    for index in range(3):
        total = total + links.got(3 + index, n.gain_last.at[index])[...]
    n.gain_own[...] = total
    links.go(6, n.gain_own, n.gain_other, site.partner)
    yield
    total = n.gain_own[...] + links.got(6, n.gain_other)[...]
    n.gain_sums_v[...] = jnp.where(site.section == 0, total[:2], total[2:4])
    links.close()
    n.copies.start(n.gain_sums_v, n.gain_sums)


def backward(n, k):
    site, copies, cross = n.site, n.copies, n.cross
    layer = k.layer

    def made(out):
        for value, target, came in k.sums:
            if value is out:
                break
        copies.start(out, target)
        if came is not None:
            cross.send(out, came, layer)

    def step_on(working):
        def idle(count):
            for _ in range(count):
                next(working, None)

        return idle

    def part_of(chip):
        return plain_dot(rows_of(n.d_gate_v, chip, site), n.w_g[...]) + plain_dot(
            rows_of(n.d_up_v, chip, site), n.w_u[...]
        )

    def add_gain(row, value, where):
        row = pl.ds(row, 1)
        n.gain_grads[row] = value if where.start == 0 else n.gain_grads[row] + value

    def local(total, where):
        gain_grad, d_hidden = norm_back_rows(
            k.hidden[where], n.gains_v[2 * layer + 1 : 2 * layer + 2], total
        )
        d_hidden = d_hidden + k.top[where].astype(FULL)
        add_gain(1, gain_grad, where)
        n.d_hidden[where] = d_hidden
        return d_hidden.astype(LOW)

    def use_d_mixed(chip, rows):
        n.d_mixed[chip] = times_trans(rows, n.w_o[...]).astype(LOW)

    working = ffn_products(n, k, made)
    if layer == 0:
        step_on(working)(5)
    spread = spread_of(n, k.branch, k.send, k.recv, use_d_mixed)
    fold_spread(fold_of(n, part_of), spread, local, step_on(working))
    for _ in working:
        pass
    k.after_first()
    copies.wait(*k.attn_copies)
    attend_back(n)
    copies.wait(*k.next_copies)

    def part_of_two(chip):
        return plain_dot(rows_of(n.d_qkv, chip, site), n.w_in[...])

    def local_two(total, where):
        gain_grad, d_input = norm_back_rows(
            k.x_rows[where].astype(FULL), n.gains_v[2 * layer : 2 * layer + 1], total
        )
        d_input = (d_input + n.d_hidden[where]).astype(LOW)
        add_gain(0, gain_grad, where)
        k.d_input[where] = d_input
        return d_input

    working = in_products(n, k.one_copies, made, k.normed_one, k.branch)
    if layer == 1:

        def use_d_act(chip, rows):
            d_act = times_trans(rows, k.w_next[...])
            for out, slope in ((n.d_gate_v, n.gate_slope_v), (n.d_up_v, n.up_slope_v)):
                put(out, chip, d_act * slope[chip].astype(FULL).reshape(d_act.shape))

        spread = spread_of(n, n.held_two, n.back_two_send, n.back_two_recv, use_d_act)
        fold_spread(fold_of(n, part_of_two), spread, local_two, step_on(working))
        for _ in working:
            pass
        return
    fold_spread(fold_of(n, part_of_two), None, local_two, step_on(working))
    for _ in working:
        pass
    copies.start(k.d_input, n.d_input_a)
    cross.send(k.d_input, n.came_input_a, 0)

    def part_of_last(chip):
        return plain_dot(rows_of(n.act, chip, site), k.w_next[...])

    def local_last(total, where):
        n.result_two[where] = (n.hidden_v[where] + total).astype(LOW)

    buffers = (n.mine, n.pass_out, n.held_two.at[:, 0], n.stage, n.held_two.at[:, 1])
    links = Links(n.last_send, n.last_recv, site)
    gains_on = fold_gains(n)
    next(gains_on)
    fold_spread(
        Fold(site, part_of_last, buffers, links), None, local_last,
        lambda count: next(gains_on, None),
    )
    for _ in gains_on:
        pass
    copies.start(n.result_two, n.result_b)
    cross.send(n.result_two, n.came_result_b, 1)


def join_kernel(count, *refs):
    def take(number):
        nonlocal refs
        taken, refs = refs[:number], refs[number:]
        return taken

    own, came = (take(count), take(count)), (take(count), take(count))
    rows = (take(4), take(4))
    outs, row_outs = take(count + 1), take(2)
    own_at, came_at, sums = take(count), take(count), take(count)
    row_at, sems, out_sem, row_sem = refs
    section = lax.axis_index("section")

    def either(first, second):
        pl.when(section == 0)(first.start)
        pl.when(section != 0)(second.start)
        return first

    waits = []
    for index in range(count):
        for slot, (pair, target) in enumerate(((own, own_at), (came, came_at))):
            waits.append(
                either(
                    *(
                        pltpu.make_async_copy(
                            pair[layer][index], target[index], sems.at[2 * index + slot]
                        )
                        for layer in range(2)
                    )
                )
            )
    done = []
    row_waits = []
    for index, (own_a, own_b, came_a, came_b) in enumerate(rows):
        for slot, (first, second) in enumerate(((own_a, came_b), (came_a, own_b))):
            target, sem = row_at.at[index, slot], row_sem.at[2 * index + slot]
            row_waits.append(
                either(
                    pltpu.make_async_copy(first, target, sem),
                    pltpu.make_async_copy(second, target, sem),
                )
            )
    for index in range(count):
        waits[2 * index].wait()
        waits[2 * index + 1].wait()
        sums[index][...] = own_at[index][...].astype(FULL) + came_at[index][...].astype(FULL)
        if index < count - 1:
            parts = [(sums[index], outs[index])]
        else:
            parts = [(sums[index].at[pl.ds(k, 1)], outs[index + k]) for k in range(2)]
        for source, target in parts:
            copy = pltpu.make_async_copy(source, target, out_sem.at[len(done)])
            copy.start()
            done.append(copy)
    for copy in row_waits:
        copy.wait()
    for index, out in enumerate(row_outs):
        copy = pltpu.make_async_copy(row_at.at[index], out, row_sem.at[index])
        copy.start()
        done.append(copy)
    for copy in done:
        copy.wait()


def join_all(own_a, own_b, came_a, came_b, results, input_grads):
    count = len(own_a)
    kept = [pltpu.VMEM(value.shape, LOW) for value in own_a]
    shapes = [value.shape for value in own_a]
    shapes = shapes[:-1] + [(1, *shapes[-1][1:])] * 2
    row_shape = jax.ShapeDtypeStruct((2, *results[0].shape), LOW)
    return pl.pallas_call(
        functools.partial(join_kernel, count),
        out_shape=[jax.ShapeDtypeStruct(value, FULL) for value in shapes] + [row_shape] * 2,
        in_specs=[IN_HBM] * (4 * count + 8),
        out_specs=[IN_HBM] * (count + 3),
        scratch_shapes=kept
        + kept
        + [pltpu.VMEM(value.shape, FULL) for value in own_a]
        + [
            pltpu.VMEM((2, *row_shape.shape), LOW),
            pltpu.SemaphoreType.DMA((2 * count,)),
            pltpu.SemaphoreType.DMA((count + 1,)),
            pltpu.SemaphoreType.DMA((4,)),
        ],
        compiler_params=pltpu.CompilerParams(vmem_limit_bytes=58 * 2**20),
        cost_estimate=pl.CostEstimate(flops=2**32, bytes_accessed=2**24, transcendentals=0),
        name="join_all",
    )(*own_a, *own_b, *came_a, *came_b, *results, *input_grads)


def relay_body(
    inputs,
    cotangent,
    positions,
    gain_attn,
    w_query,
    w_key,
    w_value,
    w_out,
    gain_ffn,
    w_gate,
    w_up,
    w_down,
):
    n_micro, per_device, model_width = inputs.shape
    n_seq = lax.axis_size("seq")
    n_shard = lax.axis_size("shard")
    members = n_seq * n_shard
    total_len = members * per_device
    section_idx = lax.axis_index("section")
    q_width = HEADS // members * HEAD_DIM
    in_width = q_width + 2 * HEAD_DIM
    hidden = w_down.shape[1]
    vmem = pltpu.VMEM

    def pick(first, second):
        return jnp.where(section_idx == 0, first, second)

    places = pick(positions[0], positions[1])
    gains_own = jnp.concatenate(
        [gain_attn, gain_ffn, jnp.zeros((6, gain_attn.shape[1]), gain_attn.dtype)], 0
    ).astype(FULL)
    own = dict(
        w_query=w_query[0], w_out=w_out[0], w_gate=w_gate[0], w_up=w_up[0], w_down=w_down[0]
    )

    order = (places.reshape(CHIPS, PLACE)[:, 0] // PLACE).astype(jnp.int32)
    numbers = jnp.arange(CHIPS, dtype=jnp.int32)
    block_at = jnp.sum(
        jnp.where(order[None, :] == numbers[:, None], numbers[None, :], 0), 1
    ).astype(jnp.int32)
    scalars = dict(block_at=block_at, order=order)
    half_dim = HEAD_DIM // 2
    inv_freq = THETA_BASE ** (-jnp.arange(half_dim, dtype=FULL) * (2.0 / HEAD_DIM))
    steps = jnp.concatenate([jnp.arange(PLACE), PLACE * jnp.arange(CHIPS)]).astype(FULL)
    angles = steps[:, None] * jnp.tile(inv_freq, 2 * q_width // HEAD_DIM)[None, :]
    turns = jnp.stack([jnp.cos(angles), jnp.sin(angles)])

    rows = (per_device, model_width)
    row_low, row_full = (rows, LOW), (rows, FULL)
    all_rows = ((CHIPS, 2, *rows), LOW)
    narrow = ((CHIPS, 2, per_device, hidden), LOW)
    wide = ((hidden, model_width), LOW)
    quarter = ((q_width, model_width), LOW)
    gain_row = ((8, model_width), FULL)
    kv_shape = (2, w_key.shape[1], model_width)
    small = gains_own.shape
    saved = dict(
        turned=((total_len, in_width), LOW),
        attended=((CHIPS, PLACE, q_width), FULL),
        spread=((CHIPS, 2 * PLACE), FULL),
        mixed=((CHIPS, 2, per_device, q_width), LOW),
    )
    saved_v = dict(
        turned_v=vmem(*saved["turned"]),
        attended_v=vmem(*saved["attended"]),
        spread_v=vmem(*saved["spread"]),
        mixed_v=vmem(*saved["mixed"]),
        turns_v=vmem(turns.shape, FULL),
    )
    attend_v_only = dict(
        qkv=vmem((CHIPS, PLACE, in_width), FULL),
        values_t=vmem((HEAD_DIM, total_len), LOW),
    )
    attend_v = dict(**saved_v, **attend_v_only)
    gates_v = dict(w_g=vmem(*wide), w_u=vmem(*wide))

    first = launch(
        "forward_first",
        0,
        forward_first,
        scalars,
        dict(
            inputs=inputs, cotangent=cotangent, gains_own=gains_own, w_key=w_key[0],
            w_value=w_value[0], turns=turns, **own,
        ),
        dict(
            x_query=quarter,
            x_out=quarter,
            x_gate=wide,
            x_up=wide,
            x_down=wide,
            gains=gain_row,
            kv_rows=((2, 2 * HEAD_DIM, model_width), LOW),
            top_all=all_rows,
            rows_one=all_rows,
            rows_two=all_rows,
            hidden=row_full,
            act_all=narrow,
            gate_slope=narrow,
            up_slope=narrow,
            **saved,
        ),
        dict(
            gains_mine=vmem(small, FULL),
            gains_x=vmem(small, FULL),
            gains_all=vmem((n_shard, n_seq, *small), FULL),
            gains_v=vmem(*gain_row),
            kv_mine=vmem(kv_shape, LOW),
            kv_x=vmem(kv_shape, LOW),
            kv_all=vmem((n_seq, 2, *kv_shape), LOW),
            w_kv=vmem((2, 2 * HEAD_DIM, model_width), LOW),
            small_send=pltpu.SemaphoreType.DMA((SMALL_SEMS,)),
            small_recv=pltpu.SemaphoreType.DMA((SMALL_SEMS,)),
            held=vmem(*all_rows),
            held_two=vmem(*all_rows),
            normed=vmem(*all_rows),
            w_q=vmem(*quarter),
            w_o=vmem(*quarter),
            hidden_v=vmem(*row_full),
            top_v=vmem(*row_low),
            act=vmem(*narrow),
            gate_slope_v=vmem(*narrow),
            up_slope_v=vmem(*narrow),
            **gates_v,
            **attend_v,
            **fold_buffers(rows),
            **spread_sems(
                "spread_send", "spread_recv", "spread_two_send", "spread_two_recv", "top_send",
                "top_recv",
            ),
        ),
    )
    crossed = dict(
        **own,
        x_query=first.x_query,
        x_out=first.x_out,
        x_gate=first.x_gate,
        x_up=first.x_up,
        x_down=first.x_down,
        gains=first.gains,
        kv_rows=first.kv_rows,
        turns=turns,
    )
    kv_pair = ((2, *kv_shape[1:]), LOW)
    sums_out = dict(down=wide, gate=wide, up=wide, out=quarter, query=quarter, kv=kv_pair)
    layers = dict(a=0, b=1)
    second = launch(
        "second_layer_and_back",
        1,
        second_layer,
        scalars,
        dict(
            act_prev=first.act_all,
            hidden_prev=first.hidden,
            inputs=inputs,
            cotangent=cotangent,
            top_all=first.top_all,
            rows_one=first.rows_one,
            rows_two=first.rows_two,
            gate_slope=first.gate_slope,
            up_slope=first.up_slope,
            **{key: getattr(first, key) for key in saved},
            **crossed,
        ),
        dict(
            gain_sums=((2, small[1]), FULL),
            **{
                f"{of}_{key}_{layer}": value
                for layer in layers
                for of in ("own", "came")
                for key, value in sums_out.items()
            },
            **{
                f"{of}_{layer}": row_low
                for layer in layers
                for of in ("result", "d_input", "came_result", "came_input")
            },
        ),
        dict(
            act_prev_v=vmem(*narrow),
            act=vmem(*narrow),
            d_gate_v=vmem(*narrow),
            d_up_v=vmem(*narrow),
            gate_slope_v=vmem(*narrow),
            up_slope_v=vmem(*narrow),
            hidden_prev_v=vmem(*row_full),
            hidden_v=vmem(*row_full),
            d_hidden=vmem(*row_full),
            result_v=vmem(*row_low),
            result_two=vmem(*row_low),
            top_v=vmem(*row_low),
            x_v=vmem(*row_low),
            d_input_v=vmem(*row_low),
            d_input_two=vmem(*row_low),
            gains_v=vmem(*gain_row),
            gain_grads=vmem((2, model_width), FULL),
            gain_later_v=vmem((2, model_width), FULL),
            w_d_prev=vmem(*wide),
            w_d=vmem(*wide),
            w_o=vmem(*quarter),
            w_in=vmem((in_width, model_width), LOW),
            top_held=vmem(*all_rows),
            normed=vmem(*all_rows),
            held=vmem(*all_rows),
            held_two=vmem(*all_rows),
            d_mixed=vmem((CHIPS, PLACE, q_width), LOW),
            d_qkv=vmem((CHIPS, 2, per_device, in_width), LOW),
            d_turned=vmem((CHIPS, PLACE, in_width), LOW),
            d_query=vmem((total_len, q_width), FULL),
            d_key=vmem((total_len, HEAD_DIM), FULL),
            d_value=vmem((total_len, HEAD_DIM), FULL),
            keys_t=vmem((HEAD_DIM, total_len), LOW),
            g_down_v=vmem(*wide),
            g_gate_v=vmem(*wide),
            g_up_v=vmem(*wide),
            g_out_v=vmem(*quarter),
            g_query_v=vmem(*quarter),
            g_kv_v=vmem(*kv_pair),
            kv_mine=vmem((2, n_seq, *kv_shape[1:]), LOW),
            kv_came=vmem((n_seq - 1, 2, *kv_shape[1:]), LOW),
            kv_send=pltpu.SemaphoreType.DMA((n_seq - 1,)),
            kv_recv=pltpu.SemaphoreType.DMA((n_seq - 1,)),
            last_send=pltpu.SemaphoreType.DMA((FOLD_SEMS,)),
            last_recv=pltpu.SemaphoreType.DMA((FOLD_SEMS,)),
            gain_parts=vmem((n_seq, n_shard, *small), FULL),
            gain_came=vmem((n_seq - 1, n_shard, *small), FULL),
            gain_shards=vmem((n_shard, *small), FULL),
            gain_last=vmem((n_shard - 1, *small), FULL),
            gain_own=vmem(small, FULL),
            gain_other=vmem(small, FULL),
            gain_sums_v=vmem((2, small[1]), FULL),
            gain_send=pltpu.SemaphoreType.DMA((7,)),
            gain_recv=pltpu.SemaphoreType.DMA((7,)),
            **gates_v,
            **attend_v,
            **fold_buffers(rows),
            **spread_sems(
                "spread_send", "spread_recv", "spread_two_send", "spread_two_recv", "back_send",
                "back_recv", "back_two_send", "back_two_recv", "last_back_send",
                "last_back_recv",
            ),
        ),
    )

    def sums(of, layer):
        return [getattr(second, f"{of}_{key}_{layer}") for key in sums_out]

    g_down, g_gate, g_up, g_out, g_query, g_key, g_value, outputs, input_grads = join_all(
        *(sums(of, layer) for of in ("own", "came") for layer in layers),
        (second.result_a, second.result_b, second.came_result_a, second.came_result_b),
        (second.d_input_a, second.d_input_b, second.came_input_a, second.came_input_b),
    )
    return (
        outputs[None],
        input_grads[None],
        second.gain_sums[:1],
        g_query[None],
        g_key,
        g_value,
        g_out[None],
        second.gain_sums[1:],
        g_gate[None],
        g_up[None],
        g_down[None],
    )


def fits_relay(mesh):
    shape = mesh.shape
    return shape["section"] == 2 and shape["shard"] == KV_HEADS == RING and shape["seq"] == 4


def solution(mesh):
    in_specs = (
        P(None, ("shard", "seq"), None),
        P(None, ("shard", "seq"), None),
        P(),
        P("section", ("shard", "seq")),
        P("section", ("shard", "seq"), None),
        P("section", ("shard", "seq"), None),
        P("section", ("shard", "seq"), None),
        P("section", ("shard", "seq"), None),
        P("section", ("shard", "seq")),
        P("section", ("shard", "seq"), None),
        P("section", ("shard", "seq"), None),
        P("section", ("shard", "seq"), None),
    )
    out_specs = (
        P("section", None, ("shard", "seq"), None),
        P("section", None, ("shard", "seq"), None),
        P("section", ("shard", "seq")),
        P("section", ("shard", "seq"), None),
        P("section", ("shard", "seq"), None),
        P("section", ("shard", "seq"), None),
        P("section", ("shard", "seq"), None),
        P("section", ("shard", "seq")),
        P("section", ("shard", "seq"), None),
        P("section", ("shard", "seq"), None),
        P("section", ("shard", "seq"), None),
    )
    chosen = relay_body if fits_relay(mesh) else body
    return jax.shard_map(chosen, mesh=mesh, in_specs=in_specs, out_specs=out_specs, check_vma=False)
```
